32 devices in a mesh: date: 8 (over y, x, core), lat: 4 (over z).
Axes of the slice: x: 2, y: 2, z: 4, core: 2. Of those that a mesh axis runs over, the one named last changes fastest.
Arguments:
- inputs: bfloat16 [8, 2, 8, 720, 641], P('date', None, 'lat'), may hold values from -6 to 6
- noise: bfloat16 [8, 2, 8, 720, 8], P('date', None, 'lat'), may hold values from -6 to 6
- cotangent: bfloat16 [8, 2, 8, 720, 641], P('date', None, 'lat'), may hold values from -6 to 6
- params: bfloat16 [3313664], P(('date', 'lat')), as said below
- psi: float32 [8, 12], replicated, may hold values from 0.2 to 1
- step_counts: int32 [8], P('date'), may hold values from 1 to 2, as said below
- pixel_mask: int32 [8, 720], P('lat'), may hold values 0 or 1
- support_offsets: int32 [12, 2], replicated, may hold values from -2 to 2, as said below
- support_basis: int32 [12], replicated, may hold values from 0 to 3, as said below
Outputs:
- output: bfloat16 [8, 2, 8, 720, 641], P('date', None, 'lat')
- input_grad: bfloat16 [8, 2, 8, 720, 641], P('date', None, 'lat')
- param_grad: float32 [3313664], P(('date', 'lat'))
The draws below stay inside these ranges and needn't reach their ends.
Inputs may be any that keep to these rules, and one draw needn't show every extreme that they name: `support_offsets`: each row is a distinct latitude and longitude offset of the window of 3 latitudes and 5 longitudes; latitude offsets -1 and +1 both occur. `support_basis`: each basis function names 3 support points. `step_counts`: some sample has 2 given steps. `params`: the unused entries are zero.
All inputs are finite; a program needn't handle non-finite values. No bound on the sum of `pixel_mask` on one device may be relied on, other than what follows from the above.
Results may differ from the reference program's by a relative error of at most 0.0059.
Values may be sent and summed in bfloat16 or wider, within the bound.
A program may use at most 320 MiB of HBM per device.

```python
import math
import jax
import jax.numpy as jnp
from jax import lax

C = 641
NOISE = 8
HID = 1282
BASIS = 4
SUPPORT = 12
REACH = 2
LON = 720
STEPS = 2
CIN = 649
SAMPLES = 8
LAT = 8
FLAT_PAD = 3313664


def draw_params(key, part):
    key = jax.random.fold_in(key, 11)
    layout = [(BASIS * CIN * C, (BASIS * CIN) ** (-0.5), 0.0), (C, 0.3, 0.0), (CIN, 0.15, 1.0), (CIN, 0.3, 0.0), (C, 0.15, 1.0), (C, 0.3, 0.0), (C * HID, C ** (-0.5), 0.0), (HID, 0.3, 0.0), (HID * C, HID ** (-0.5), 0.0), (C, 0.3, 0.0)]
    pieces = []
    used = 0
    for position, entry in enumerate(layout):
        amount, spread_value, centre = entry
        subkey = jax.random.fold_in(key, position)
        values = jax.random.normal(subkey, (amount,), jnp.float32)
        pieces.append(centre + spread_value * values)
        used = used + amount
    pieces.append(jnp.zeros((FLAT_PAD - used,), jnp.float32))
    return jnp.concatenate(pieces).astype(jnp.bfloat16)


def draw_step_counts(key, part):
    key = jax.random.fold_in(key, 9)
    first_key, second_key = jax.random.split(key)
    counts = jax.random.randint(first_key, (SAMPLES,), 1, STEPS + 1, dtype=jnp.int32)
    chosen = jax.random.randint(second_key, (), 0, SAMPLES, dtype=jnp.int32)
    return counts.at[chosen].set(STEPS).astype(jnp.int32)


def draw_support_offsets(key, part):
    key = jax.random.fold_in(key, 5)
    window = 2 * REACH + 1
    picks = jax.random.permutation(key, 3 * window)[:SUPPORT].astype(jnp.int32)
    return jnp.stack([picks // window - 1, picks % window - REACH], axis=1).astype(jnp.int32)


def draw_support_basis(key, part):
    key = jax.random.fold_in(key, 7)
    ordering = jax.random.permutation(key, SUPPORT).astype(jnp.int32)
    return (ordering % BASIS).astype(jnp.int32)


def with_ends(array, rng, low, high):
    dims = array.shape
    index_at = [jax.random.randint(jax.random.fold_in(rng, axis), (), 0, dims[axis]) for axis in range(len(dims))]
    array = array.at[tuple(index_at)].set(low)
    longest = dims.index(max(dims))
    index_at[longest] = (index_at[longest] + 1) % dims[longest]
    return array.at[tuple(index_at)].set(high)


def levels(stream_key, shape, cuts, least, top_value):
    def one(dim, blocks):
        steps = jax.random.uniform(jax.random.fold_in(jax.random.fold_in(stream_key, 6), dim), (blocks,), jnp.float32, least / len(cuts), top_value / len(cuts))
        return jnp.repeat(jnp.exp(steps), shape[dim] // blocks).reshape((-1,) + (1,) * (len(shape) - dim - 1))

    loudness = one(*cuts[0])
    for cut in cuts[1:]:
        loudness = loudness * one(*cut)
    return loudness


def bell_draw(own_key, shape, deviation, reach, cuts=(), kind=jnp.bfloat16):
    array = jax.random.normal(own_key, shape, jnp.float32) * deviation
    if len(cuts) > 0:
        array = levels(own_key, shape, cuts, -0.22, 0.18) * array
    return jnp.clip(array, min=-reach, max=reach).astype(kind)


def setup_inputs(seed: int = 0) -> dict:
    seeds = jax.random.split(jax.random.key(seed), 10)
    inputs = bell_draw(seeds[0], (SAMPLES, STEPS, LAT, LON, C), 1.0, 6.0, ((0, 8), (2, 4)))
    noise = bell_draw(seeds[1], (SAMPLES, STEPS, LAT, LON, NOISE), 1.0, 6.0, ((0, 8), (2, 4)))
    cotangent = bell_draw(seeds[2], (SAMPLES, STEPS, LAT, LON, C), 1.0, 6.0, ((0, 8), (2, 4)))
    params = draw_params(jax.random.fold_in(seeds[9], 71), 0)
    psi = jnp.clip(jnp.exp(jax.random.uniform(seeds[4], (LAT, SUPPORT), jnp.float32, math.log(0.2), math.log(1.0))), 0.2, 1.0)
    step_counts = draw_step_counts(jax.random.fold_in(seeds[9], 71), 0)
    pixel_mask = with_ends((jax.random.randint(seeds[6], (LAT, LON), 0, 8) < 7).astype(jnp.int32), jax.random.fold_in(seeds[6], 1), 0, 1)
    support_offsets = draw_support_offsets(jax.random.fold_in(seeds[9], 71), 0)
    support_basis = draw_support_basis(jax.random.fold_in(seeds[9], 71), 0)
    return {"inputs": inputs, "noise": noise, "cotangent": cotangent, "params": params, "psi": psi, "step_counts": step_counts, "pixel_mask": pixel_mask, "support_offsets": support_offsets, "support_basis": support_basis}


@jax.custom_vjp
def low(v):
    return lax.optimization_barrier(v.astype(jnp.bfloat16)).astype(jnp.float32)

@jax.custom_vjp
def low_back(v):
    return v

def low_keep(v):
    return (low(v), None)

def low_pass(kept, grad):
    return (grad,)

def back_keep(v):
    return (v, None)

def back_low(kept, grad):
    return (low(grad),)
low.defvjp(low_keep, low_pass)
low_back.defvjp(back_keep, back_low)

def unpack(flat_params):
    layout = [(BASIS * CIN, C), (C,), (CIN,), (CIN,), (C,), (C,), (C, HID), (HID,), (HID, C), (C,)]
    pieces = []
    offset = 0
    for extent in layout:
        amount = math.prod(extent)
        pieces.append(flat_params[offset:offset + amount].reshape(extent))
        offset = offset + amount
    return pieces

def layer_norm(values, norm_gain, norm_shift):
    average = lax.optimization_barrier(jnp.mean(values, axis=-1, keepdims=True))
    centered = values - average
    variance = lax.optimization_barrier(jnp.mean(centered * centered, axis=-1, keepdims=True))
    return centered * lax.rsqrt(variance + 1e-05) * norm_gain + norm_shift

def matmul(left, right):
    return jnp.dot(left, right, precision=lax.Precision.HIGHEST, preferred_element_type=jnp.float32)

def disco_block(sample, noise_part, flat_params, psi, support_offsets, onehot):
    disco_weight, conv_bias, first_gain, first_shift, second_gain, second_shift, up_weight, up_bias, down_weight, down_bias = unpack(flat_params)
    stacked = jnp.concatenate([sample, noise_part], axis=-1)
    normed = low(layer_norm(stacked, first_gain, first_shift))
    padded = jnp.pad(normed, ((0, 0), (1, 1), (0, 0), (0, 0)))
    padded = jnp.concatenate([padded[:, :, -REACH:], padded, padded[:, :, :REACH]], axis=2)
    zero_index = jnp.zeros((), jnp.int32)
    terms = jnp.zeros((STEPS, LAT, LON, BASIS, CIN), jnp.float32)
    for point in range(SUPPORT):
        lat_start = (1 + support_offsets[point, 0]).astype(jnp.int32)
        lon_start = (REACH + support_offsets[point, 1]).astype(jnp.int32)
        window_part = lax.dynamic_slice(padded, (zero_index, lat_start, lon_start, zero_index), (STEPS, LAT, LON, CIN))
        weighting = psi[:, point][:, None] * onehot[point][None, :]
        terms = terms + weighting[None, :, None, :, None] * window_part[:, :, :, None, :]
    basis_terms = low(low_back(terms.reshape(-1, BASIS * CIN)))
    conv = low_back(matmul(basis_terms, disco_weight) + conv_bias)
    residual = sample.reshape(-1, C) + conv
    second = low(layer_norm(residual, second_gain, second_shift))
    pre_act = low_back(matmul(second, up_weight) + up_bias)
    activated = low(jax.nn.gelu(pre_act))
    branch = low_back(matmul(activated, down_weight) + down_bias)
    return (residual + branch).reshape(STEPS, LAT, LON, C)

def reference(inputs, noise, cotangent, params, psi, step_counts, pixel_mask, support_offsets, support_basis):
    weights = params.astype(jnp.float32)
    onehot = (support_basis[:, None] == jnp.arange(BASIS, dtype=jnp.int32)[None, :]).astype(jnp.float32)
    pixels = pixel_mask.astype(jnp.float32)

    def one_sample(summed, item):
        sample, noise_part, cotangent_part, given = item
        extra = noise_part.astype(jnp.float32)

        def forward(state, flat_params):
            return disco_block(state, extra, flat_params, psi, support_offsets, onehot)
        result, backward = jax.vjp(forward, sample.astype(jnp.float32), weights)
        active = (jnp.arange(STEPS, dtype=jnp.int32) < given).astype(jnp.float32)
        weighting = cotangent_part.astype(jnp.float32) * active[:, None, None, None] * pixels[None, :, :, None]
        grad_input, grad_weights = backward(weighting)
        return (summed + grad_weights, (result.astype(jnp.bfloat16), grad_input.astype(jnp.bfloat16)))
    summed, stacked_out = lax.scan(one_sample, jnp.zeros(params.shape, jnp.float32), (inputs, noise, cotangent, step_counts))
    return (stacked_out[0], stacked_out[1], summed)
```

```python
import functools
import math

import jax
import jax.numpy as jnp
from jax import lax
from jax.experimental import pallas as pl
from jax.experimental.pallas import tpu as pltpu
from jax.sharding import PartitionSpec as P

C = 641
HID = 1282
BASIS = 4
SUPPORT = 12
REACH = 2
CIN = 649
BF16, F32 = jnp.bfloat16, jnp.float32
MESH = pl.DeviceIdType.MESH
LANES = 128
STEP = 16
CP = 656
HP = 1296
WIDE = 768
HL = 1408
UNROLL = 4
VMEM = 60 << 20


OFF_G1=BASIS*CIN*C+C; OFF_S1=OFF_G1+CIN; OFF_G2=OFF_S1+CIN; OFF_S2=OFF_G2+C; OFF_UP=OFF_S2+C; OFF_DN=OFF_UP+(C+1)*HID;
SMALL=((OFF_G1,CIN),(OFF_S1,CIN),(OFF_G2,C),(OFF_S2,C))
MATS=((0,C,BASIS*CIN+1,128,3),(OFF_UP,HID,C+1,64,2),(OFF_DN,C,HID+1,128,2))
F_ROWS=29952
def lane_ids(): return lax.broadcasted_iota(jnp.int32,(8,LANES),1)
def place(base,cols,period,b):
    start=base+cols*b
    return start//LANES, start%LANES
def unpack_kernel(nrow,pad, g_ref, w_ref,wt_ref,up_ref,upt_ref,dn_ref,dnt_ref,small_ref,flat,chunks):
    def fill(s,_):
        flat[pl.ds(nrow*s,pad),:]=g_ref[s].astype(F32); return 0
    lax.fori_loop(0,g_ref.shape[0],fill,0)
    lane=lane_ids()
    def split(base,cols,period,groups):
        J=-(-cols//LANES); pitch=period+8; height=pitch*8*groups+8; last=cols-(J-1)*LANES
        def body(b,_):
            row,s=place(base,cols,period,b)
            back=(LANES-s)%LANES
            for g in range(groups):
                rolled=[pltpu.roll(flat[pl.ds(row+641*8*g+j,8,stride=641),:],back,axis=1) for j in range(J+1)]
                for j in range(J):
                    val=jnp.where(lane<LANES-s,rolled[j],rolled[j+1])
                    if j==J-1: val=jnp.where(lane<last,val,0.0)
                    chunks[pl.ds(j*height+8*g*pitch+b,8,stride=pitch),:]=val
            return 0
        lax.fori_loop(0,period,body,0,unroll=8)
        def border(a,_):
            for j in range(J): chunks[pl.ds(j*height+a*pitch-8,8),:]=chunks[pl.ds(j*height+a*pitch,8),:]
            return 0
        lax.fori_loop(1,8*groups,border,0)
        return J,height,period
    def convert(dst,dst_row,src_row,rows,pad_rows,J,height,period):
        full=rows//16
        def piece(j,r): return chunks[pl.ds(j*height+r//period*(period+8)+r%period,8),:]
        def pair(j,r): return jnp.concatenate([piece(j,r),piece(j,r+8)],axis=0)
        def body(m,_):
            for j in range(J):
                dst[pl.ds(pl.multiple_of(dst_row+16*m,16),16),j*LANES:(j+1)*LANES]=pair(j,src_row+16*m).astype(BF16)
            return 0
        lax.fori_loop(0,full,body,0,unroll=4)
        keep=lax.broadcasted_iota(jnp.int32,(16,LANES),0)<rows-16*full
        for m in range(full,pad_rows//16):
            for j in range(J):
                v=jnp.where(keep,pair(j,src_row+16*m),0.0) if m==full else jnp.zeros((16,LANES),F32)
                dst[dst_row+16*m:dst_row+16*m+16,j*LANES:(j+1)*LANES]=v.astype(BF16)
    J,h,p=split(*MATS[0][:2],*MATS[0][3:])
    for k in range(BASIS):
        convert(w_ref,k*CP,k*CIN,CIN+(k==BASIS-1),CP,J,h,p)
    J,h,p=split(*MATS[1][:2],*MATS[1][3:])
    convert(up_ref,0,0,C+1,CP,J,h,p)
    J,h,p=split(*MATS[2][:2],*MATS[2][3:])
    convert(dn_ref,0,0,HID+1,HP,J,h,p)
    wt_ref[...]=w_ref[:,:CP].T
    upt_ref[...]=up_ref[:,:HP].T
    dnt_ref[...]=dn_ref[:,:CP].T
    for i,(off,n) in enumerate(SMALL):
        row,s=divmod(off,LANES)
        r=pltpu.roll(flat[row:row+8,:],(LANES-s)%LANES,axis=1)
        v=jnp.where(lane<LANES-s,r,pltpu.roll(r,7,axis=0))
        sub=lax.broadcasted_iota(jnp.int32,(8,LANES),0)
        v=jnp.where(sub*LANES+lane<n,v,0.0)
        t=v.T
        for j in range(6):
            rows=min(LANES,CP-j*LANES)
            small_ref[i,j*LANES:j*LANES+rows,:]=jnp.broadcast_to(t[:rows,j:j+1],(rows,LANES))
def unpack(gathered,nrow):
    n,pad,_=gathered.shape
    return pl.pallas_call(functools.partial(unpack_kernel,nrow,pad),
        out_shape=(jax.ShapeDtypeStruct((BASIS*CP,WIDE),BF16),jax.ShapeDtypeStruct((CP,BASIS*CP),BF16),
            jax.ShapeDtypeStruct((CP,HL),BF16),jax.ShapeDtypeStruct((HP,CP),BF16),
            jax.ShapeDtypeStruct((HP,WIDE),BF16),jax.ShapeDtypeStruct((CP,HP),BF16),jax.ShapeDtypeStruct((4,CP,LANES),F32)),
        scratch_shapes=[pltpu.VMEM((F_ROWS,LANES),F32),pltpu.VMEM((6*(136*24+8),LANES),F32)],
        compiler_params=pltpu.CompilerParams(vmem_limit_bytes=VMEM),name="unpack")(gathered)
def pack_kernel(nrow,pad,gd_ref,gu_ref,gn_ref,sm_ref,out_ref,flat,chunks):
    lane=lane_ids(); sub=lax.broadcasted_iota(jnp.int32,(8,LANES),0)
    def gather(src,src_row,dst_row,rows,J,height,last,period):
        full=rows//8
        def cols(m,j):
            v=src[pl.ds(pl.multiple_of(src_row+8*m,8),8),j*LANES:(j+1)*LANES]
            return jnp.where(lane<last,v,0.0) if j==J-1 else v
        def body(m,_):
            r=dst_row+8*m; at=r//period*(period+8)+r%period
            for j in range(J):
                v=cols(m,j)
                chunks[pl.ds(j*height+at+8,8),:]=v
                chunks[pl.ds(j*height+at,8),:]=v
            return 0
        lax.fori_loop(0,full,body,0,unroll=4)
        if rows%8:
            r=dst_row+8*full; at=r//period*(period+8)+r%period
            for j in range(J):
                v=jnp.where(sub<rows-8*full,cols(full,j),0.0)
                chunks[pl.ds(j*height+at+8,8),:]=v
                chunks[pl.ds(j*height+at,8),:]=v
    def clear(J,height,row,period):
        row=row//period*(period+8)+row%period
        count=(height-row)//8
        def body(m,_):
            for j in range(J): chunks[pl.ds(j*height+row+8*m,8),:]=jnp.zeros((8,LANES),F32)
            return 0
        lax.fori_loop(0,count,body,0)
    def merge(base,cols,period,groups):
        J=-(-cols//LANES); pitch=period+8; height=pitch*8*groups+8
        def body(b,tails,rows=J):
            row,s=place(base,cols,period,b)
            new=[]
            for g in range(groups):
                x=[pltpu.roll(chunks[pl.ds(j*height+8*g*pitch+b,8,stride=pitch),:],s,axis=1) for j in range(J)]
                first=lane>=s
                for j in range(J):
                    v=jnp.where(first,x[j],tails[g] if j==0 else x[j-1])
                    if j<rows: flat[pl.ds(row+641*8*g+j,8,stride=641),:]=v
                new.append(jnp.where(s==LANES-1,jnp.where(first,0.0,x[J-1]),v))
            return tuple(new)
        row0=base//LANES
        init=[jnp.zeros((8,LANES),F32)]*groups
        if base%LANES:
            init[0]=jnp.where(sub==0,flat[row0:row0+8,:],0.0)
        tails=lax.fori_loop(0,period-8,body,tuple(init),unroll=8)
        for b in range(period-8,period):
            tails=body(b,tails,J-1 if base%LANES and b==period-1 else J)
        if base%LANES:
            for g in range(groups):
                at=pl.ds(row0+641*(8*g+1),8,stride=641)
                flat[at,:]=flat[at,:]+tails[g]
    h=136*24+8
    for k in range(BASIS): gather(gd_ref,k*CP,k*CIN,CIN+(k==BASIS-1),6,h,1,128)
    clear(6,h,2600,128)
    merge(0,C,128,3)
    h=72*16+8
    gather(gu_ref,0,0,C+1,11,h,2,64)
    clear(11,h,648,64)
    merge(OFF_UP,HID,64,2)
    h=136*16+8
    gather(gn_ref,0,0,HID+1,6,h,1,128)
    clear(6,h,1288,128)
    merge(OFF_DN,C,128,2)
    for i,(off,n) in enumerate(SMALL):
        row,s=divmod(off,LANES)
        r=pltpu.roll(sm_ref[i],s,axis=1)
        prev=pltpu.roll(r,1,axis=0)
        v=jnp.where(lane>=s,r,jnp.where(sub==0,0.0,prev))
        flat[row:row+8,:]=flat[row:row+8,:]+v
    def store(s,_):
        out_ref[s]=flat[pl.ds(nrow*s,pad),:].astype(BF16); return 0
    lax.fori_loop(0,out_ref.shape[0],store,0)
def pack(gd,gu,gn,sm,n,nrow,pad):
    return pl.pallas_call(functools.partial(pack_kernel,nrow,pad),
        out_shape=jax.ShapeDtypeStruct((n,pad,LANES),BF16),
        scratch_shapes=[pltpu.VMEM((F_ROWS,LANES),F32),pltpu.VMEM((6*(136*24+8),LANES),F32)],
        compiler_params=pltpu.CompilerParams(vmem_limit_bytes=VMEM),name="pack")(gd,gu,gn,sm)


def tiled(column):
    return jnp.concatenate([column] * (WIDE // LANES), axis=1)


def lane_of(rows, start=0):
    return lax.broadcasted_iota(jnp.int32, (rows, LANES), 1) + start


def wrapped(chunk, width):
    head, first, last = chunk[:, : WIDE - LANES], chunk[:, :LANES], chunk[:, WIDE - LANES :]
    edge = width - (WIDE - LANES)
    lane = lane_of(chunk.shape[0])
    beyond = jnp.where(
        lane < LANES - REACH, pltpu.roll(first, edge, axis=1), pltpu.roll(last, LANES - edge, axis=1)
    )
    return jnp.concatenate([head, jnp.where(lane < edge, last, beyond)], axis=1)


def cut(chunk, width):
    head, last = chunk[:, : WIDE - LANES], chunk[:, WIDE - LANES :]
    keep = lane_of(chunk.shape[0], WIDE - LANES) < width
    return jnp.concatenate([head, jnp.where(keep, last, 0.0)], axis=1)


def rows_below(count):
    return lax.broadcasted_iota(jnp.int32, (STEP, WIDE), 0) < count


def halves(chunk):
    return chunk[:8] + chunk[8:]


def column_sums(read, channels, count):
    whole = channels // STEP

    def body(m, sums):
        return tuple(a + halves(v) for a, v in zip(sums, read(m)))

    sums = lax.fori_loop(
        0, whole, body, tuple(jnp.zeros((8, WIDE), F32) for _ in range(count)), unroll=UNROLL
    )
    keep = rows_below(channels - whole * STEP)
    sums = [a + halves(jnp.where(keep, v, 0.0)) for a, v in zip(sums, read(whole))]
    return [jnp.sum(a, axis=0, keepdims=True) for a in sums]


def norm_stats(read, channels):
    (total,) = column_sums(lambda m: (read(m),), channels, 1)
    mean = total * (1.0 / channels)

    def squares(m):
        centered = read(m) - mean
        return (centered * centered,)

    (total,) = column_sums(squares, channels, 1)
    return mean, lax.rsqrt(total * (1.0 / channels) + 1e-05)


def each_chunk(body, unroll=None):
    def step(m, _):
        body(m, pl.ds(pl.multiple_of(m * STEP, STEP), STEP))
        return 0

    lax.fori_loop(0, CP // STEP, step, 0, unroll=unroll)


def lift_kernel(rows, lat, width, offsets, bases, psi, lo, own, hi, gain, shift, out, moved, table):
    first_row = lax.axis_index("lat") * rows
    for k in range(BASIS):
        table[SUPPORT + k] = 0
    for p in range(SUPPORT):
        k = bases[p]
        used = table[SUPPORT + k]
        table[k * 3 + used] = p
        table[SUPPORT + k] = used + 1
    for m in range(rows + 2):
        source = lo if m == 0 else hi if m == rows + 1 else own.at[:, m - 1]

        def read(c):
            return source[0, pl.ds(pl.multiple_of(c * STEP, STEP), STEP), :].astype(F32)

        mean, scale = norm_stats(read, CIN)

        def shifts(c, at):
            values = (source[0, at, :].astype(F32) - mean) * scale
            values = values * tiled(gain[at, :]) + tiled(shift[at, :])
            values = wrapped(values, width).astype(BF16)
            for d in range(-REACH, REACH + 1):
                moved[m, d + REACH, at, :] = pltpu.roll(values, -d % WIDE, axis=1) if d else values

        each_chunk(shifts, 1)
    for r in range(rows):
        for k in range(BASIS):
            parts = []
            for q in range(3):
                p = table[k * 3 + q]
                row = first_row + r + offsets[p, 0]
                inside = jnp.logical_and(row >= 0, row < lat)
                weight = jnp.where(inside, psi[first_row + r, p], 0.0)
                parts.append((weight, r + 1 + offsets[p, 0], offsets[p, 1] + REACH))

            def combine(c, at):
                total = None
                for weight, row, d in parts:
                    term = weight * moved[row, d, at, :].astype(F32)
                    total = term if total is None else total + term
                to = pl.ds(pl.multiple_of(k * CP + c * STEP, STEP), STEP)
                out[0, r, to, :] = cut(total, width).astype(BF16)

            each_chunk(combine, 1)
        last = slice(BASIS * CP - STEP, BASIS * CP)
        bias_row = CIN - (CP - STEP)
        sub = lax.broadcasted_iota(jnp.int32, (STEP, WIDE), 0)
        lane = lax.broadcasted_iota(jnp.int32, (STEP, WIDE), 1)
        ones = jnp.where(lane < width, 1.0, 0.0)
        out[0, r, last, :] = jnp.where(sub == bias_row, ones, out[0, r, last, :].astype(F32)).astype(BF16)


def lift(offsets, bases, psi, lo, own, hi, gain, shift, lat, width):
    slabs, rows = own.shape[:2]
    smem = pl.BlockSpec(memory_space=pltpu.SMEM)
    halo = pl.BlockSpec((1, CP, WIDE), lambda s: (s, 0, 0))
    column = pl.BlockSpec((CP, LANES), lambda s: (0, 0))
    return pl.pallas_call(
        functools.partial(lift_kernel, rows, lat, width),
        grid=(slabs,),
        in_specs=[
            smem,
            smem,
            smem,
            halo,
            pl.BlockSpec((1, rows, CP, WIDE), lambda s: (s, 0, 0, 0)),
            halo,
            column,
            column,
        ],
        out_specs=pl.BlockSpec((1, rows, BASIS * CP, WIDE), lambda s: (s, 0, 0, 0)),
        out_shape=jax.ShapeDtypeStruct((slabs, rows, BASIS * CP, WIDE), BF16),
        scratch_shapes=[
            pltpu.VMEM((rows + 2, 2 * REACH + 1, CP, WIDE), BF16),
            pltpu.SMEM((SUPPORT + BASIS,), jnp.int32),
        ],
        compiler_params=pltpu.CompilerParams(vmem_limit_bytes=VMEM),
        name="lift",
    )(offsets, bases, psi, lo, own, hi, gain, shift)


GELU_A = math.sqrt(2.0 / math.pi)
GELU_B = 0.044715


def block_kernel(
    width, basis, x, cot, mask, wt, upt, up, dnt, dn, gain, shift,
    out, gconv, gup, gdn, sums,
    res, second, pre, act, slope, gb, gpre, gsec,
):
    start = pl.program_id(0) == 0

    @pl.when(start)
    def _():
        gup[...] = jnp.zeros_like(gup)
        gdn[...] = jnp.zeros_like(gdn)
        sums[...] = jnp.zeros_like(sums)

    def dot(a, b):
        return jnp.dot(a, b, preferred_element_type=F32)

    res[...] = dot(wt[...], basis[0])

    def add_input(c, at):
        values = x[0, at, :].astype(F32)
        keep = lax.broadcasted_iota(jnp.int32, (STEP, WIDE), 0) + c * STEP < C
        res[at, :] = res[at, :] + jnp.where(keep, values, 0.0)
        gb[at, :] = (cot[0, at, :].astype(F32) * mask[0]).astype(BF16)

    each_chunk(add_input, 1)

    def read(c):
        return res[pl.ds(pl.multiple_of(c * STEP, STEP), STEP), :]

    mean, scale = norm_stats(read, C)

    def normalize(c, at):
        values = (res[at, :] - mean) * scale * tiled(gain[at, :]) + tiled(shift[at, :])
        row = lax.broadcasted_iota(jnp.int32, (STEP, WIDE), 0) + c * STEP
        second[at, :] = jnp.where(row == C, 1.0, values).astype(BF16)

    each_chunk(normalize, 1)
    pre[...] = dot(upt[...], second[...])

    def gelu(c, _):
        at = pl.ds(pl.multiple_of(c * STEP, STEP), STEP)
        v = pre[at, :]
        square = v * v
        bend = jnp.tanh(GELU_A * v * (1.0 + GELU_B * square))
        half = 0.5 * (1.0 + bend)
        row = lax.broadcasted_iota(jnp.int32, (STEP, WIDE), 0) + c * STEP
        act[at, :] = jnp.where(row == HID, 1.0, v * half).astype(BF16)
        rise = GELU_A * (1.0 + 3.0 * GELU_B * square)
        slope[at, :] = half + 0.5 * v * (1.0 - bend * bend) * rise
        return 0

    lax.fori_loop(0, HP // STEP, gelu, 0)
    pre[:CP, :] = dot(dnt[...], act[...])

    def finish(c, at):
        out[0, at, :] = (res[at, :] + pre[at, :]).astype(BF16)

    each_chunk(finish, 1)
    pre[...] = dot(dn[:, :CP], gb[...])

    def back(c, _):
        at = pl.ds(pl.multiple_of(c * STEP, STEP), STEP)
        gpre[at, :] = (pre[at, :] * slope[at, :]).astype(BF16)
        return 0

    lax.fori_loop(0, HP // STEP, back, 0)
    gsec[...] = dot(up[:, :HP], gpre[...])

    def means(c):
        at = pl.ds(pl.multiple_of(c * STEP, STEP), STEP)
        g = gsec[at, :] * tiled(gain[at, :])
        return g, g * ((res[at, :] - mean) * scale)

    flat, along = [v * (1.0 / C) for v in column_sums(means, C, 2)]

    def backward(c, at):
        dm = gsec[at, :]
        xhat = (res[at, :] - mean) * scale
        g = dm * tiled(gain[at, :])
        value = gb[at, :].astype(F32) + scale * (g - flat - xhat * along)
        row = lax.broadcasted_iota(jnp.int32, (STEP, WIDE), 0) + c * STEP
        value = jnp.where(row < C, value, 0.0)
        gconv[0, at, :] = wrapped(value, width).astype(BF16)
        along_lanes(sums.at[0], at, dm * xhat)
        along_lanes(sums.at[1], at, dm)

    each_chunk(backward, 1)

    def outer(a, b):
        return lax.dot_general(a, b, (((1,), (1,)), ((), ())), preferred_element_type=F32)

    gdn[:, :CP] += outer(act[...], gb[...])
    gup[:, :HP] += outer(second[...], gpre[...])


def along_lanes(ref, at, values):
    total = values[:, :LANES]
    for j in range(1, WIDE // LANES):
        total = total + values[:, j * LANES : (j + 1) * LANES]
    ref[at, :] = ref[at, :] + total


def block(basis, x, cot, mask, wt, upt, up, dnt, dn, gain, shift, width):
    count = x.shape[0]

    def per_row(height):
        return pl.BlockSpec((1, height, WIDE), lambda i: (i, 0, 0))

    def whole(a):
        return pl.BlockSpec(a.shape, lambda i: (0,) * len(a.shape), pipeline_mode=pl.Buffered(1))

    outs = (
        jax.ShapeDtypeStruct((count, CP, WIDE), BF16),
        jax.ShapeDtypeStruct((count, CP, WIDE), BF16),
        jax.ShapeDtypeStruct((CP, HL), F32),
        jax.ShapeDtypeStruct((HP, WIDE), F32),
        jax.ShapeDtypeStruct((2, CP, LANES), F32),
    )
    weights = (wt, upt, up, dnt, dn, gain, shift)
    return pl.pallas_call(
        functools.partial(block_kernel, width),
        grid=(count,),
        in_specs=[per_row(BASIS * CP), per_row(CP), per_row(CP), per_row(1)] + [whole(a) for a in weights],
        out_specs=[per_row(CP), per_row(CP)] + [whole(a) for a in outs[2:]],
        out_shape=outs,
        scratch_shapes=[
            pltpu.VMEM((CP, WIDE), F32),
            pltpu.VMEM((CP, WIDE), BF16),
            pltpu.VMEM((HP, WIDE), F32),
            pltpu.VMEM((HP, WIDE), BF16),
            pltpu.VMEM((HP, WIDE), F32),
            pltpu.VMEM((CP, WIDE), BF16),
            pltpu.VMEM((HP, WIDE), BF16),
            pltpu.VMEM((CP, WIDE), F32),
        ],
        compiler_params=pltpu.CompilerParams(vmem_limit_bytes=VMEM),
        name="block",
    )(basis, x, cot, mask, *weights)


def outer_kernel(basis, gconv, out):
    i = pl.program_id(0)
    term = lax.dot_general(basis[0], gconv[0], (((1,), (1,)), ((), ())), preferred_element_type=F32)

    @pl.when(i == 0)
    def _():
        out[:, :CP] = term

    @pl.when(i > 0)
    def _():
        out[:, :CP] += term


def weight_grad(basis, gconv):
    count = basis.shape[0]
    return pl.pallas_call(
        outer_kernel,
        grid=(count,),
        in_specs=[
            pl.BlockSpec((1, BASIS * CP, WIDE), lambda i: (i, 0, 0)),
            pl.BlockSpec((1, CP, WIDE), lambda i: (i, 0, 0)),
        ],
        out_specs=pl.BlockSpec((BASIS * CP, WIDE), lambda i: (0, 0)),
        out_shape=jax.ShapeDtypeStruct((BASIS * CP, WIDE), F32),
        compiler_params=pltpu.CompilerParams(vmem_limit_bytes=VMEM),
        name="weight_grad",
    )(basis, gconv)


def lower_kernel(rows, offsets, bases, psi, gconv, w, own, lo, hi, lifted, place, coef):
    first_row = lax.axis_index("lat") * rows
    span = 2 * REACH + 1
    for n in range(3 * span):
        place[n] = 0
        for r in range(rows):
            coef[r, n] = 0.0
    for p in range(SUPPORT):
        n = (offsets[p, 0] + 1) * span + offsets[p, 1] + REACH
        place[n] = bases[p]
        for r in range(rows):
            coef[r, n] = psi[first_row + r, p]
    for r in range(rows):
        lifted[r] = jnp.dot(w[:, :CP], gconv[0, r], preferred_element_type=F32).astype(BF16)
    for target in range(-1, rows + 1):
        terms = []
        for d in range(-REACH, REACH + 1):
            for o in (-1, 0, 1):
                r = target - o
                if 0 <= r < rows:
                    n = (o + 1) * span + d + REACH
                    terms.append((d, r, coef[r, n], place[n] * CP))

        def gather(c, at):
            total = None
            for d in range(-REACH, REACH + 1):
                part = None
                for e, r, weight, base in terms:
                    if e == d:
                        source = pl.ds(pl.multiple_of(base + c * STEP, STEP), STEP)
                        term = weight * lifted[r, source, :].astype(F32)
                        part = term if part is None else part + term
                if d:
                    part = pltpu.roll(part, d % WIDE, axis=1)
                total = part if total is None else total + part
            if target < 0:
                lo[0, at, :] = total.astype(BF16)
            elif target == rows:
                hi[0, at, :] = total.astype(BF16)
            else:
                own[0, target, at, :] = total

        each_chunk(gather, 1)


def lower(offsets, bases, psi, gconv, w):
    slabs, rows = gconv.shape[:2]
    smem = pl.BlockSpec(memory_space=pltpu.SMEM)
    halo = pl.BlockSpec((1, CP, WIDE), lambda s: (s, 0, 0))
    per_slab = pl.BlockSpec((1, rows, CP, WIDE), lambda s: (s, 0, 0, 0))
    edge = jax.ShapeDtypeStruct((slabs, CP, WIDE), BF16)
    return pl.pallas_call(
        functools.partial(lower_kernel, rows),
        grid=(slabs,),
        in_specs=[
            smem,
            smem,
            smem,
            per_slab,
            pl.BlockSpec(w.shape, lambda s: (0, 0), pipeline_mode=pl.Buffered(1)),
        ],
        out_specs=[per_slab, halo, halo],
        out_shape=(jax.ShapeDtypeStruct((slabs, rows, CP, WIDE), F32), edge, edge),
        scratch_shapes=[
            pltpu.VMEM((rows, BASIS * CP, WIDE), BF16),
            pltpu.SMEM((3 * (2 * REACH + 1),), jnp.int32),
            pltpu.SMEM((rows, 3 * (2 * REACH + 1)), F32),
        ],
        compiler_params=pltpu.CompilerParams(vmem_limit_bytes=VMEM),
        name="lower",
    )(offsets, bases, psi, gconv, w)


def input_kernel(rows, width, x, gconv, own, lo, hi, gain, out, sums, total):
    r = pl.program_id(1)

    @pl.when(jnp.logical_and(pl.program_id(0) == 0, r == 0))
    def _():
        sums[...] = jnp.zeros_like(sums)

    from_below = jnp.where(r == 0, 1.0, 0.0)
    from_above = jnp.where(r == rows - 1, 1.0, 0.0)

    def read(c):
        return x[0, 0, pl.ds(pl.multiple_of(c * STEP, STEP), STEP), :].astype(F32)

    mean, scale = norm_stats(read, CIN)

    def join(c, at):
        halo = lo[0, at, :].astype(F32) * from_below + hi[0, at, :].astype(F32) * from_above
        total[at, :] = own[0, 0, at, :] + halo

    each_chunk(join, 1)

    def means(c):
        at = pl.ds(pl.multiple_of(c * STEP, STEP), STEP)
        g = total[at, :] * tiled(gain[at, :])
        return g, g * ((read(c) - mean) * scale)

    flat, along = [v * (1.0 / CIN) for v in column_sums(means, CIN, 2)]

    def backward(c, at):
        dm = cut(total[at, :], width)
        xhat = (read(c) - mean) * scale
        g = dm * tiled(gain[at, :])
        value = scale * (g - flat - xhat * along) + gconv[0, 0, at, :].astype(F32)
        out[0, 0, at, :] = value.astype(BF16)
        along_lanes(sums.at[0], at, dm * xhat)
        along_lanes(sums.at[1], at, dm)

    each_chunk(backward, 1)


def input_grad(x, gconv, own, lo, hi, gain, width):
    slabs, rows = x.shape[:2]
    per_row = pl.BlockSpec((1, 1, CP, WIDE), lambda s, r: (s, r, 0, 0))
    halo = pl.BlockSpec((1, CP, WIDE), lambda s, r: (s, 0, 0))
    return pl.pallas_call(
        functools.partial(input_kernel, rows, width),
        grid=(slabs, rows),
        in_specs=[per_row, per_row, per_row, halo, halo, pl.BlockSpec((CP, LANES), lambda s, r: (0, 0))],
        out_specs=[per_row, pl.BlockSpec((2, CP, LANES), lambda s, r: (0, 0, 0))],
        out_shape=(
            jax.ShapeDtypeStruct((slabs, rows, CP, WIDE), BF16),
            jax.ShapeDtypeStruct((2, CP, LANES), F32),
        ),
        scratch_shapes=[pltpu.VMEM((CP, WIDE), F32)],
        compiler_params=pltpu.CompilerParams(vmem_limit_bytes=VMEM),
        name="input_grad",
    )(x, gconv, own, lo, hi, gain)


def flip(value, bit):
    return value + (1 - 2 * ((value // (1 << bit)) % 2)) * (1 << bit)


def flipped(value, mask):
    bit = 0
    while mask >> bit:
        if mask >> bit & 1:
            value = flip(value, bit)
        bit += 1
    return value


def span(bits):
    masks = [0]
    for b in bits:
        masks = masks + [m | 1 << b for m in masks]
    return masks


def orders(dates):
    bits = list(range(1, dates.bit_length() - 1))
    return bits + [0], bits[::-1] + [0]


def greet(dates, lats, d, l):
    barrier = pltpu.get_barrier_semaphore()
    count = 0
    for o in range(1, lats):
        pl.semaphore_signal(barrier, inc=1, device_id=(d, lax.rem(l + o, lats)), device_id_type=MESH)
        count += 1
    for b in range(dates.bit_length() - 1):
        pl.semaphore_signal(barrier, inc=1, device_id=(flip(d, b), l), device_id_type=MESH)
        count += 1
    pl.semaphore_wait(barrier, count)


def gather_kernel(dates, lats, src, out, local_sem, z_send, z_recv, send, recv):
    d, l = lax.axis_index("date"), lax.axis_index("lat")
    half = lats // 2
    greet(dates, lats, d, l)
    own = pltpu.make_async_copy(src, out.at[d, l], local_sem)
    own.start()
    z = []
    for o in range(1, lats):
        z.append(
            pltpu.make_async_remote_copy(
                src_ref=src,
                dst_ref=out.at[d, l],
                send_sem=z_send.at[o - 1],
                recv_sem=z_recv.at[o - 1],
                device_id=(d, lax.rem(l + o, lats)),
                device_id_type=MESH,
            )
        )
        z[-1].start()
    own.wait()
    for copy in z:
        copy.wait_recv()
    sent = []

    def cross(h, i, mask):
        order = orders(dates)[h]
        at = span(order[:i]).index(mask)
        block = out.at[flipped(d, mask), pl.ds(h * half, half)]
        slot = (1 << i) - 1 + at
        copy = pltpu.make_async_remote_copy(
            src_ref=block,
            dst_ref=block,
            send_sem=send.at[h, slot],
            recv_sem=recv.at[h, slot],
            device_id=(flip(d, order[i]), l),
            device_id_type=MESH,
        )
        copy.start()
        sent.append(copy)
        return copy

    flights = {}
    steps = dates.bit_length() - 1
    for i in range(steps):
        for h in range(2):
            flights[h, i, 0] = cross(h, i, 0)
    for i in range(steps):
        for at, mask in enumerate(span(orders(dates)[0][:i])):
            for h in range(2):
                order = orders(dates)[h]
                mask = span(order[:i])[at]
                flights[h, i, mask].wait_recv()
                for later in range(i + 1, steps):
                    reached = mask | 1 << order[i]
                    flights[h, later, reached] = cross(h, later, reached)
    for copy in z + sent:
        copy.wait_send()


def gather(shard, dates, lats):
    slots = dates - 1
    return pl.pallas_call(
        functools.partial(gather_kernel, dates, lats),
        in_specs=[pl.BlockSpec(memory_space=pl.ANY)],
        out_specs=pl.BlockSpec(memory_space=pl.ANY),
        out_shape=jax.ShapeDtypeStruct((dates, lats) + shard.shape, shard.dtype),
        scratch_shapes=[
            pltpu.SemaphoreType.DMA(()),
            pltpu.SemaphoreType.DMA((lats - 1,)),
            pltpu.SemaphoreType.DMA((lats - 1,)),
            pltpu.SemaphoreType.DMA((2, slots)),
            pltpu.SemaphoreType.DMA((2, slots)),
        ],
        compiler_params=pltpu.CompilerParams(collective_id=0, has_side_effects=True),
        name="gather_params",
    )(shard)


def scatter_kernel(dates, lats, src, out, parts, mine, others, z_send, z_recv, send, recv):
    d, l = lax.axis_index("date"), lax.axis_index("lat")
    half = lats // 2
    greet(dates, lats, d, l)
    steps = dates.bit_length() - 1
    sent = []
    paths = [order[::-1] for order in orders(dates)]

    def slot_of(h, i, mask):
        later = span(paths[h][i + 1 :][::-1])
        first = sum(1 << (steps - 1 - e) for e in range(i))
        return first + later.index(mask)

    def holder(h, i, mask):
        if i == 0:
            return src.at[flipped(d, mask), pl.ds(h * half, half)]
        return parts.at[h, slot_of(h, i - 1, mask)]

    def cross(h, i, mask):
        bit = paths[h][i]
        slot = slot_of(h, i, mask)
        copy = pltpu.make_async_remote_copy(
            src_ref=holder(h, i, mask | 1 << bit),
            dst_ref=parts.at[h, slot],
            send_sem=send.at[h, slot],
            recv_sem=recv.at[h, slot],
            device_id=(flip(d, bit), l),
            device_id_type=MESH,
        )
        copy.start()
        sent.append(copy)
        return copy

    def left(h, i):
        masks = span(paths[h][i + 1 :][::-1])
        return masks[::-1]

    flights = {}
    for n in range(len(left(0, 0))):
        for h in range(2):
            mask = left(h, 0)[n]
            flights[h, 0, mask] = cross(h, 0, mask)
    for i in range(steps):
        for n in range(len(left(0, i))):
            for h in range(2):
                mask = left(h, i)[n]
                flights[h, i, mask].wait_recv()
                have = holder(h, i, mask)
                got = parts.at[h, slot_of(h, i, mask)]
                for s in range(half):
                    total = have[s].astype(F32) + got[s].astype(F32)
                    if i == steps - 1:
                        mine[h * half + s] = total.astype(BF16)
                    else:
                        got[s] = total.astype(BF16)
                if i + 1 < steps and mask >> paths[h][i + 1] & 1:
                    ahead = mask & ~(1 << paths[h][i + 1])
                    flights[h, i + 1, ahead] = cross(h, i + 1, ahead)
    z = []
    for o in range(1, lats):
        to = lax.rem(l + o, lats)
        z.append(
            pltpu.make_async_remote_copy(
                src_ref=mine.at[to],
                dst_ref=others.at[o - 1],
                send_sem=z_send.at[o - 1],
                recv_sem=z_recv.at[o - 1],
                device_id=(d, to),
                device_id_type=MESH,
            )
        )
        z[-1].start()
    total = mine[l].astype(F32)
    for o in range(1, lats):
        z[o - 1].wait_recv()
        total = total + others[o - 1].astype(F32)
    out[...] = total
    for copy in z + sent:
        copy.wait_send()


def scatter(packed):
    dates, lats, rows, lanes = packed.shape
    slots = dates - 1
    return pl.pallas_call(
        functools.partial(scatter_kernel, dates, lats),
        in_specs=[pl.BlockSpec(memory_space=pltpu.VMEM)],
        out_specs=pl.BlockSpec(memory_space=pltpu.VMEM),
        out_shape=jax.ShapeDtypeStruct((rows, lanes), F32),
        scratch_shapes=[
            pltpu.VMEM((2, slots, lats // 2, rows, lanes), BF16),
            pltpu.VMEM((lats, rows, lanes), BF16),
            pltpu.VMEM((lats - 1, rows, lanes), BF16),
            pltpu.SemaphoreType.DMA((lats - 1,)),
            pltpu.SemaphoreType.DMA((lats - 1,)),
            pltpu.SemaphoreType.DMA((2, slots)),
            pltpu.SemaphoreType.DMA((2, slots)),
        ],
        compiler_params=pltpu.CompilerParams(
            collective_id=1, has_side_effects=True, vmem_limit_bytes=VMEM
        ),
        name="scatter_grads",
    )(packed)


def local(inputs, noise, cotangent, params, psi, step_counts, pixel_mask, offsets, bases):
    samples, steps, rows, width, _ = inputs.shape
    slabs = samples * steps
    dates, lats = lax.axis_size("date"), lax.axis_size("lat")
    lat = rows * lats

    def by_channel(values):
        return jnp.swapaxes(values, 3, 4).reshape(slabs, rows, -1, width)

    def padded(values):
        return jnp.pad(values, ((0, 0), (0, 0), (0, CP - values.shape[2]), (0, WIDE - width)))

    upward = [(i, i + 1) for i in range(lats - 1)]
    downward = [(i + 1, i) for i in range(lats - 1)]
    x = padded(jnp.concatenate([by_channel(inputs), by_channel(noise)], axis=2))
    below = lax.ppermute(x[:, rows - 1], "lat", upward)
    above = lax.ppermute(x[:, 0], "lat", downward)
    lines = params.shape[0] // LANES
    held = -(-lines // STEP) * STEP
    shard = jnp.pad(params.reshape(lines, LANES), ((0, held - lines), (0, 0)))
    gathered = gather(shard, dates, lats).reshape(dates * lats, held, LANES)
    w, wt, up, upt, dn, dnt, small = unpack(gathered, lines)
    cot = padded(by_channel(cotangent)).reshape(slabs * rows, CP, WIDE)
    active = jnp.arange(steps, dtype=jnp.int32)[None, :] < step_counts[:, None]
    mask = active.reshape(slabs, 1, 1) * pixel_mask[None]
    mask = jnp.pad(mask.astype(F32), ((0, 0), (0, 0), (0, WIDE - width)))
    basis = lift(offsets, bases, psi, below, x, above, small[0], small[1], lat, width)
    basis = basis.reshape(slabs * rows, BASIS * CP, WIDE)
    output, gconv, gup, gdn, second_sums = block(
        basis, x.reshape(slabs * rows, CP, WIDE), cot, mask.reshape(slabs * rows, 1, WIDE),
        wt, upt, up, dnt, dn, small[2], small[3], width,
    )
    gconv_rows = gconv.reshape(slabs, rows, CP, WIDE)
    own, to_below, to_above = lower(offsets, bases, psi, gconv_rows, w)
    from_below = lax.ppermute(to_above, "lat", upward)
    from_above = lax.ppermute(to_below, "lat", downward)
    gdisco = weight_grad(basis, gconv)
    grad, first_sums = input_grad(x, gconv_rows, own, from_below, from_above, small[0], width)
    sums = jnp.sum(jnp.concatenate([first_sums, second_sums]), axis=-1)
    valid = jnp.array([CIN, CIN, C, C], jnp.int32)[:, None]
    sums = jnp.where(jnp.arange(CP, dtype=jnp.int32)[None, :] < valid, sums, 0.0)
    sums = jnp.pad(sums, ((0, 0), (0, 8 * LANES - CP))).reshape(4, 8, LANES)
    packed = pack(gdisco, gup, gdn, sums, dates * lats, lines, held)
    summed = scatter(packed.reshape(dates, lats, held, LANES))

    def by_pixel(values):
        values = values.reshape(slabs, rows, CP, WIDE)[:, :, :C, :width]
        return jnp.swapaxes(values.reshape(samples, steps, rows, C, width), 3, 4)

    return by_pixel(output), by_pixel(grad), summed[:lines].reshape(-1)


def solution(mesh):
    field = P("date", None, "lat", None, None)
    flat = P(("date", "lat"))
    return jax.shard_map(
        local,
        mesh=mesh,
        in_specs=(field, field, field, flat, P(), P("date"), P("lat", None), P(), P()),
        out_specs=(field, field, flat),
        check_vma=False,
    )
```

```python
import functools
import math

import jax
import jax.numpy as jnp
from jax import lax
from jax.experimental import pallas as pl
from jax.experimental.pallas import tpu as pltpu
from jax.sharding import PartitionSpec as P

C = 641
HID = 1282
BASIS = 4
SUPPORT = 12
REACH = 2
CIN = 649
BF16, F32 = jnp.bfloat16, jnp.float32
MESH = pl.DeviceIdType.MESH
LANES = 128
STEP = 16
CP = 656
HP = 1296
WIDE = 768
HL = 1408
UNROLL = 8
VMEM = 60 << 20


OFF_G1=BASIS*CIN*C+C; OFF_S1=OFF_G1+CIN; OFF_G2=OFF_S1+CIN; OFF_S2=OFF_G2+C; OFF_UP=OFF_S2+C; OFF_DN=OFF_UP+(C+1)*HID;
SMALL=((OFF_G1,CIN),(OFF_S1,CIN),(OFF_G2,C),(OFF_S2,C))
MATS=((0,C,BASIS*CIN+1,128,3),(OFF_UP,HID,C+1,64,2),(OFF_DN,C,HID+1,128,2))
F_ROWS=29952
def lane_ids(): return lax.broadcasted_iota(jnp.int32,(8,LANES),1)
def place(base,cols,period,b):
    start=base+cols*b
    return start//LANES, start%LANES
def unpack_kernel(nrow,pad, g_ref, w_ref,wt_ref,up_ref,upt_ref,dn_ref,dnt_ref,small_ref,flat,chunks):
    def fill(s,_):
        flat[pl.ds(nrow*s,pad),:]=g_ref[s].astype(F32); return 0
    lax.fori_loop(0,g_ref.shape[0],fill,0)
    lane=lane_ids()
    def split(base,cols,period,groups):
        J=-(-cols//LANES); pitch=period+8; height=pitch*8*groups+8; last=cols-(J-1)*LANES
        def body(b,_):
            row,s=place(base,cols,period,b)
            back=(LANES-s)%LANES
            for g in range(groups):
                rolled=[pltpu.roll(flat[pl.ds(row+641*8*g+j,8,stride=641),:],back,axis=1) for j in range(J+1)]
                for j in range(J):
                    val=jnp.where(lane<LANES-s,rolled[j],rolled[j+1])
                    if j==J-1: val=jnp.where(lane<last,val,0.0)
                    chunks[pl.ds(j*height+8*g*pitch+b,8,stride=pitch),:]=val
            return 0
        lax.fori_loop(0,period,body,0,unroll=8)
        def border(a,_):
            for j in range(J): chunks[pl.ds(j*height+a*pitch-8,8),:]=chunks[pl.ds(j*height+a*pitch,8),:]
            return 0
        lax.fori_loop(1,8*groups,border,0)
        return J,height,period
    def convert(dst,dst_row,src_row,rows,pad_rows,J,height,period):
        full=rows//16
        def piece(j,r): return chunks[pl.ds(j*height+r//period*(period+8)+r%period,8),:]
        def pair(j,r): return jnp.concatenate([piece(j,r),piece(j,r+8)],axis=0)
        def body(m,_):
            for j in range(J):
                dst[pl.ds(pl.multiple_of(dst_row+16*m,16),16),j*LANES:(j+1)*LANES]=pair(j,src_row+16*m).astype(BF16)
            return 0
        lax.fori_loop(0,full,body,0,unroll=4)
        keep=lax.broadcasted_iota(jnp.int32,(16,LANES),0)<rows-16*full
        for m in range(full,pad_rows//16):
            for j in range(J):
                v=jnp.where(keep,pair(j,src_row+16*m),0.0) if m==full else jnp.zeros((16,LANES),F32)
                dst[dst_row+16*m:dst_row+16*m+16,j*LANES:(j+1)*LANES]=v.astype(BF16)
    J,h,p=split(*MATS[0][:2],*MATS[0][3:])
    for k in range(BASIS):
        convert(w_ref,k*CP,k*CIN,CIN+(k==BASIS-1),CP,J,h,p)
    J,h,p=split(*MATS[1][:2],*MATS[1][3:])
    convert(up_ref,0,0,C+1,CP,J,h,p)
    J,h,p=split(*MATS[2][:2],*MATS[2][3:])
    convert(dn_ref,0,0,HID+1,HP,J,h,p)
    wt_ref[...]=w_ref[:,:CP].T
    upt_ref[...]=up_ref[:,:HP].T
    dnt_ref[...]=dn_ref[:,:CP].T
    for i,(off,n) in enumerate(SMALL):
        row,s=divmod(off,LANES)
        r=pltpu.roll(flat[row:row+8,:],(LANES-s)%LANES,axis=1)
        v=jnp.where(lane<LANES-s,r,pltpu.roll(r,7,axis=0))
        sub=lax.broadcasted_iota(jnp.int32,(8,LANES),0)
        v=jnp.where(sub*LANES+lane<n,v,0.0)
        t=v.T
        for j in range(6):
            rows=min(LANES,CP-j*LANES)
            small_ref[i,j*LANES:j*LANES+rows,:]=jnp.broadcast_to(t[:rows,j:j+1],(rows,LANES))
def unpack(gathered,nrow):
    n,pad,_=gathered.shape
    return pl.pallas_call(functools.partial(unpack_kernel,nrow,pad),
        out_shape=(jax.ShapeDtypeStruct((BASIS*CP,WIDE),BF16),jax.ShapeDtypeStruct((CP,BASIS*CP),BF16),
            jax.ShapeDtypeStruct((CP,HL),BF16),jax.ShapeDtypeStruct((HP,CP),BF16),
            jax.ShapeDtypeStruct((HP,WIDE),BF16),jax.ShapeDtypeStruct((CP,HP),BF16),jax.ShapeDtypeStruct((4,CP,LANES),F32)),
        scratch_shapes=[pltpu.VMEM((F_ROWS,LANES),F32),pltpu.VMEM((6*(136*24+8),LANES),F32)],
        compiler_params=pltpu.CompilerParams(vmem_limit_bytes=VMEM),name="unpack")(gathered)
def pack_kernel(nrow,pad,gd_ref,gu_ref,gn_ref,sm_ref,out_ref,flat,chunks):
    lane=lane_ids(); sub=lax.broadcasted_iota(jnp.int32,(8,LANES),0)
    def gather(src,src_row,dst_row,rows,J,height,last,period):
        full=rows//8
        def cols(m,j):
            v=src[pl.ds(pl.multiple_of(src_row+8*m,8),8),j*LANES:(j+1)*LANES]
            return jnp.where(lane<last,v,0.0) if j==J-1 else v
        def body(m,_):
            r=dst_row+8*m; at=r//period*(period+8)+r%period
            for j in range(J):
                v=cols(m,j)
                chunks[pl.ds(j*height+at+8,8),:]=v
                chunks[pl.ds(j*height+at,8),:]=v
            return 0
        lax.fori_loop(0,full,body,0,unroll=4)
        if rows%8:
            r=dst_row+8*full; at=r//period*(period+8)+r%period
            for j in range(J):
                v=jnp.where(sub<rows-8*full,cols(full,j),0.0)
                chunks[pl.ds(j*height+at+8,8),:]=v
                chunks[pl.ds(j*height+at,8),:]=v
    def clear(J,height,row,period):
        row=row//period*(period+8)+row%period
        count=(height-row)//8
        def body(m,_):
            for j in range(J): chunks[pl.ds(j*height+row+8*m,8),:]=jnp.zeros((8,LANES),F32)
            return 0
        lax.fori_loop(0,count,body,0)
    def merge(base,cols,period,groups):
        J=-(-cols//LANES); pitch=period+8; height=pitch*8*groups+8
        def body(b,tails,rows=J):
            row,s=place(base,cols,period,b)
            new=[]
            for g in range(groups):
                x=[pltpu.roll(chunks[pl.ds(j*height+8*g*pitch+b,8,stride=pitch),:],s,axis=1) for j in range(J)]
                first=lane>=s
                for j in range(J):
                    v=jnp.where(first,x[j],tails[g] if j==0 else x[j-1])
                    if j<rows: flat[pl.ds(row+641*8*g+j,8,stride=641),:]=v
                new.append(jnp.where(s==LANES-1,jnp.where(first,0.0,x[J-1]),v))
            return tuple(new)
        row0=base//LANES
        init=[jnp.zeros((8,LANES),F32)]*groups
        if base%LANES:
            init[0]=jnp.where(sub==0,flat[row0:row0+8,:],0.0)
        tails=lax.fori_loop(0,period-8,body,tuple(init),unroll=8)
        for b in range(period-8,period):
            tails=body(b,tails,J-1 if base%LANES and b==period-1 else J)
        if base%LANES:
            for g in range(groups):
                at=pl.ds(row0+641*(8*g+1),8,stride=641)
                flat[at,:]=flat[at,:]+tails[g]
    h=136*24+8
    for k in range(BASIS): gather(gd_ref,k*CP,k*CIN,CIN+(k==BASIS-1),6,h,1,128)
    clear(6,h,2600,128)
    merge(0,C,128,3)
    h=72*16+8
    gather(gu_ref,0,0,C+1,11,h,2,64)
    clear(11,h,648,64)
    merge(OFF_UP,HID,64,2)
    h=136*16+8
    gather(gn_ref,0,0,HID+1,6,h,1,128)
    clear(6,h,1288,128)
    merge(OFF_DN,C,128,2)
    for i,(off,n) in enumerate(SMALL):
        row,s=divmod(off,LANES)
        r=pltpu.roll(sm_ref[i],s,axis=1)
        prev=pltpu.roll(r,1,axis=0)
        v=jnp.where(lane>=s,r,jnp.where(sub==0,0.0,prev))
        flat[row:row+8,:]=flat[row:row+8,:]+v
    def store(s,_):
        out_ref[s]=flat[pl.ds(nrow*s,pad),:].astype(BF16); return 0
    lax.fori_loop(0,out_ref.shape[0],store,0)
def pack(gd,gu,gn,sm,n,nrow,pad):
    return pl.pallas_call(functools.partial(pack_kernel,nrow,pad),
        out_shape=jax.ShapeDtypeStruct((n,pad,LANES),BF16),
        scratch_shapes=[pltpu.VMEM((F_ROWS,LANES),F32),pltpu.VMEM((6*(136*24+8),LANES),F32)],
        compiler_params=pltpu.CompilerParams(vmem_limit_bytes=VMEM),name="pack")(gd,gu,gn,sm)


def tiled(column):
    return jnp.concatenate([column] * (WIDE // LANES), axis=1)


def lane_of(rows, start=0):
    return lax.broadcasted_iota(jnp.int32, (rows, LANES), 1) + start


def wrapped(chunk, width):
    head, first, last = chunk[:, : WIDE - LANES], chunk[:, :LANES], chunk[:, WIDE - LANES :]
    edge = width - (WIDE - LANES)
    lane = lane_of(chunk.shape[0])
    beyond = jnp.where(
        lane < LANES - REACH, pltpu.roll(first, edge, axis=1), pltpu.roll(last, LANES - edge, axis=1)
    )
    return jnp.concatenate([head, jnp.where(lane < edge, last, beyond)], axis=1)


def cut(chunk, width):
    head, last = chunk[:, : WIDE - LANES], chunk[:, WIDE - LANES :]
    keep = lane_of(chunk.shape[0], WIDE - LANES) < width
    return jnp.concatenate([head, jnp.where(keep, last, 0.0)], axis=1)


def rows_below(count):
    return lax.broadcasted_iota(jnp.int32, (STEP, WIDE), 0) < count


def halves(chunk):
    return chunk[:8] + chunk[8:]


def column_sums(read, channels, count):
    whole = channels // STEP

    def body(m, sums):
        return tuple(a + halves(v) for a, v in zip(sums, read(m)))

    sums = lax.fori_loop(
        0, whole, body, tuple(jnp.zeros((8, WIDE), F32) for _ in range(count)), unroll=UNROLL
    )
    keep = rows_below(channels - whole * STEP)
    sums = [a + halves(jnp.where(keep, v, 0.0)) for a, v in zip(sums, read(whole))]
    return [jnp.sum(a, axis=0, keepdims=True) for a in sums]


def norm_stats(read, channels):
    (total,) = column_sums(lambda m: (read(m),), channels, 1)
    mean = total * (1.0 / channels)

    def squares(m):
        centered = read(m) - mean
        return (centered * centered,)

    (total,) = column_sums(squares, channels, 1)
    return mean, lax.rsqrt(total * (1.0 / channels) + 1e-05)


def each_chunk(body, unroll=None):
    def step(m, _):
        body(m, pl.ds(pl.multiple_of(m * STEP, STEP), STEP))
        return 0

    lax.fori_loop(0, CP // STEP, step, 0, unroll=unroll)


def lift_kernel(rows, lat, width, offsets, bases, psi, lo, own, hi, gain, shift, out, moved, table):
    first_row = lax.axis_index("lat") * rows
    for k in range(BASIS):
        table[SUPPORT + k] = 0
    for p in range(SUPPORT):
        k = bases[p]
        used = table[SUPPORT + k]
        table[k * 3 + used] = p
        table[SUPPORT + k] = used + 1
    for m in range(rows + 2):
        source = lo if m == 0 else hi if m == rows + 1 else own.at[:, m - 1]

        def read(c):
            return source[0, pl.ds(pl.multiple_of(c * STEP, STEP), STEP), :].astype(F32)

        mean, scale = norm_stats(read, CIN)

        def shifts(c, at):
            values = (source[0, at, :].astype(F32) - mean) * scale
            values = values * tiled(gain[at, :]) + tiled(shift[at, :])
            values = wrapped(values, width).astype(BF16)
            for d in range(-REACH, REACH + 1):
                moved[m, d + REACH, at, :] = pltpu.roll(values, -d % WIDE, axis=1) if d else values

        each_chunk(shifts, 4)
    for r in range(rows):
        for k in range(BASIS):
            parts = []
            for q in range(3):
                p = table[k * 3 + q]
                row = first_row + r + offsets[p, 0]
                inside = jnp.logical_and(row >= 0, row < lat)
                weight = jnp.where(inside, psi[first_row + r, p], 0.0)
                parts.append((weight, r + 1 + offsets[p, 0], offsets[p, 1] + REACH))

            def combine(c, at):
                total = None
                for weight, row, d in parts:
                    term = weight * moved[row, d, at, :].astype(F32)
                    total = term if total is None else total + term
                to = pl.ds(pl.multiple_of(k * CP + c * STEP, STEP), STEP)
                out[0, r, to, :] = cut(total, width).astype(BF16)

            each_chunk(combine, 4)
        last = slice(BASIS * CP - STEP, BASIS * CP)
        bias_row = CIN - (CP - STEP)
        sub = lax.broadcasted_iota(jnp.int32, (STEP, WIDE), 0)
        lane = lax.broadcasted_iota(jnp.int32, (STEP, WIDE), 1)
        ones = jnp.where(lane < width, 1.0, 0.0)
        out[0, r, last, :] = jnp.where(sub == bias_row, ones, out[0, r, last, :].astype(F32)).astype(BF16)


def lift(offsets, bases, psi, lo, own, hi, gain, shift, lat, width):
    slabs, rows = own.shape[:2]
    smem = pl.BlockSpec(memory_space=pltpu.SMEM)
    halo = pl.BlockSpec((1, CP, WIDE), lambda s: (s, 0, 0))
    column = pl.BlockSpec((CP, LANES), lambda s: (0, 0))
    return pl.pallas_call(
        functools.partial(lift_kernel, rows, lat, width),
        grid=(slabs,),
        in_specs=[
            smem,
            smem,
            smem,
            halo,
            pl.BlockSpec((1, rows, CP, WIDE), lambda s: (s, 0, 0, 0)),
            halo,
            column,
            column,
        ],
        out_specs=pl.BlockSpec((1, rows, BASIS * CP, WIDE), lambda s: (s, 0, 0, 0)),
        out_shape=jax.ShapeDtypeStruct((slabs, rows, BASIS * CP, WIDE), BF16),
        scratch_shapes=[
            pltpu.VMEM((rows + 2, 2 * REACH + 1, CP, WIDE), BF16),
            pltpu.SMEM((SUPPORT + BASIS,), jnp.int32),
        ],
        compiler_params=pltpu.CompilerParams(vmem_limit_bytes=VMEM),
        name="lift",
    )(offsets, bases, psi, lo, own, hi, gain, shift)


GELU_A = math.sqrt(2.0 / math.pi)
GELU_B = 0.044715


def block_kernel(
    width, basis, x, cot, mask, wt, upt, up, dnt, dn, gain, shift,
    out, gconv, gup, gdn, sums,
    res, second, pre, act, slope, gb, gpre, gsec,
):
    start = pl.program_id(0) == 0

    @pl.when(start)
    def _():
        gup[...] = jnp.zeros_like(gup)
        gdn[...] = jnp.zeros_like(gdn)
        sums[...] = jnp.zeros_like(sums)

    def dot(a, b):
        return jnp.dot(a, b, preferred_element_type=F32)

    res[...] = dot(wt[...], basis[0])

    def add_input(c, at):
        values = x[0, at, :].astype(F32)
        keep = lax.broadcasted_iota(jnp.int32, (STEP, WIDE), 0) + c * STEP < C
        res[at, :] = res[at, :] + jnp.where(keep, values, 0.0)
        gb[at, :] = (cot[0, at, :].astype(F32) * mask[0]).astype(BF16)

    each_chunk(add_input, 8)

    def read(c):
        return res[pl.ds(pl.multiple_of(c * STEP, STEP), STEP), :]

    mean, scale = norm_stats(read, C)

    def normalize(c, at):
        values = (res[at, :] - mean) * scale * tiled(gain[at, :]) + tiled(shift[at, :])
        row = lax.broadcasted_iota(jnp.int32, (STEP, WIDE), 0) + c * STEP
        second[at, :] = jnp.where(row == C, 1.0, values).astype(BF16)

    each_chunk(normalize, 8)
    pre[...] = dot(upt[...], second[...])

    def gelu(c, _):
        at = pl.ds(pl.multiple_of(c * STEP, STEP), STEP)
        v = pre[at, :]
        square = v * v
        bend = jnp.tanh(GELU_A * v * (1.0 + GELU_B * square))
        half = 0.5 * (1.0 + bend)
        row = lax.broadcasted_iota(jnp.int32, (STEP, WIDE), 0) + c * STEP
        act[at, :] = jnp.where(row == HID, 1.0, v * half).astype(BF16)
        rise = GELU_A * (1.0 + 3.0 * GELU_B * square)
        slope[at, :] = half + 0.5 * v * (1.0 - bend * bend) * rise
        return 0

    lax.fori_loop(0, HP // STEP, gelu, 0, unroll=8)
    pre[:CP, :] = dot(dnt[...], act[...])

    def finish(c, at):
        out[0, at, :] = (res[at, :] + pre[at, :]).astype(BF16)

    each_chunk(finish, 8)
    pre[...] = dot(dn[:, :CP], gb[...])

    def back(c, _):
        at = pl.ds(pl.multiple_of(c * STEP, STEP), STEP)
        gpre[at, :] = (pre[at, :] * slope[at, :]).astype(BF16)
        return 0

    lax.fori_loop(0, HP // STEP, back, 0, unroll=8)
    gsec[...] = dot(up[:, :HP], gpre[...])

    def means(c):
        at = pl.ds(pl.multiple_of(c * STEP, STEP), STEP)
        g = gsec[at, :] * tiled(gain[at, :])
        return g, g * ((res[at, :] - mean) * scale)

    flat, along = [v * (1.0 / C) for v in column_sums(means, C, 2)]

    def backward(c, at):
        dm = gsec[at, :]
        xhat = (res[at, :] - mean) * scale
        g = dm * tiled(gain[at, :])
        value = gb[at, :].astype(F32) + scale * (g - flat - xhat * along)
        row = lax.broadcasted_iota(jnp.int32, (STEP, WIDE), 0) + c * STEP
        value = jnp.where(row < C, value, 0.0)
        gconv[0, at, :] = wrapped(value, width).astype(BF16)
        along_lanes(sums.at[0], at, dm * xhat)
        along_lanes(sums.at[1], at, dm)

    each_chunk(backward, 8)

    def outer(a, b):
        return lax.dot_general(a, b, (((1,), (1,)), ((), ())), preferred_element_type=F32)

    gdn[:, :CP] += outer(act[...], gb[...])
    gup[:, :HP] += outer(second[...], gpre[...])


def along_lanes(ref, at, values):
    total = values[:, :LANES]
    for j in range(1, WIDE // LANES):
        total = total + values[:, j * LANES : (j + 1) * LANES]
    ref[at, :] = ref[at, :] + total


def block(basis, x, cot, mask, wt, upt, up, dnt, dn, gain, shift, width):
    count = x.shape[0]

    def per_row(height):
        return pl.BlockSpec((1, height, WIDE), lambda i: (i, 0, 0))

    def whole(a):
        return pl.BlockSpec(a.shape, lambda i: (0,) * len(a.shape), pipeline_mode=pl.Buffered(1))

    outs = (
        jax.ShapeDtypeStruct((count, CP, WIDE), BF16),
        jax.ShapeDtypeStruct((count, CP, WIDE), BF16),
        jax.ShapeDtypeStruct((CP, HL), F32),
        jax.ShapeDtypeStruct((HP, WIDE), F32),
        jax.ShapeDtypeStruct((2, CP, LANES), F32),
    )
    weights = (wt, upt, up, dnt, dn, gain, shift)
    return pl.pallas_call(
        functools.partial(block_kernel, width),
        grid=(count,),
        in_specs=[per_row(BASIS * CP), per_row(CP), per_row(CP), per_row(1)] + [whole(a) for a in weights],
        out_specs=[per_row(CP), per_row(CP)] + [whole(a) for a in outs[2:]],
        out_shape=outs,
        scratch_shapes=[
            pltpu.VMEM((CP, WIDE), F32),
            pltpu.VMEM((CP, WIDE), BF16),
            pltpu.VMEM((HP, WIDE), F32),
            pltpu.VMEM((HP, WIDE), BF16),
            pltpu.VMEM((HP, WIDE), F32),
            pltpu.VMEM((CP, WIDE), BF16),
            pltpu.VMEM((HP, WIDE), BF16),
            pltpu.VMEM((CP, WIDE), F32),
        ],
        compiler_params=pltpu.CompilerParams(vmem_limit_bytes=VMEM),
        name="block",
    )(basis, x, cot, mask, *weights)


def outer_kernel(basis, gconv, out):
    i = pl.program_id(0)
    term = lax.dot_general(basis[0], gconv[0], (((1,), (1,)), ((), ())), preferred_element_type=F32)

    @pl.when(i == 0)
    def _():
        out[:, :CP] = term

    @pl.when(i > 0)
    def _():
        out[:, :CP] += term


def weight_grad(basis, gconv):
    count = basis.shape[0]
    return pl.pallas_call(
        outer_kernel,
        grid=(count,),
        in_specs=[
            pl.BlockSpec((1, BASIS * CP, WIDE), lambda i: (i, 0, 0)),
            pl.BlockSpec((1, CP, WIDE), lambda i: (i, 0, 0)),
        ],
        out_specs=pl.BlockSpec((BASIS * CP, WIDE), lambda i: (0, 0)),
        out_shape=jax.ShapeDtypeStruct((BASIS * CP, WIDE), F32),
        compiler_params=pltpu.CompilerParams(vmem_limit_bytes=VMEM),
        name="weight_grad",
    )(basis, gconv)


def lower_kernel(rows, offsets, bases, psi, gconv, w, own, lo, hi, lifted, place, coef):
    first_row = lax.axis_index("lat") * rows
    span = 2 * REACH + 1
    for n in range(3 * span):
        place[n] = 0
        for r in range(rows):
            coef[r, n] = 0.0
    for p in range(SUPPORT):
        n = (offsets[p, 0] + 1) * span + offsets[p, 1] + REACH
        place[n] = bases[p]
        for r in range(rows):
            coef[r, n] = psi[first_row + r, p]
    for r in range(rows):
        lifted[r] = jnp.dot(w[:, :CP], gconv[0, r], preferred_element_type=F32).astype(BF16)
    for target in range(-1, rows + 1):
        terms = []
        for d in range(-REACH, REACH + 1):
            for o in (-1, 0, 1):
                r = target - o
                if 0 <= r < rows:
                    n = (o + 1) * span + d + REACH
                    terms.append((d, r, coef[r, n], place[n] * CP))

        def gather(c, at):
            total = None
            for d in range(-REACH, REACH + 1):
                part = None
                for e, r, weight, base in terms:
                    if e == d:
                        source = pl.ds(pl.multiple_of(base + c * STEP, STEP), STEP)
                        term = weight * lifted[r, source, :].astype(F32)
                        part = term if part is None else part + term
                if d:
                    part = pltpu.roll(part.astype(BF16), d % WIDE, axis=1).astype(F32)
                total = part if total is None else total + part
            if target < 0:
                lo[0, at, :] = total.astype(BF16)
            elif target == rows:
                hi[0, at, :] = total.astype(BF16)
            else:
                own[0, target, at, :] = total

        each_chunk(gather, 8)


def lower(offsets, bases, psi, gconv, w):
    slabs, rows = gconv.shape[:2]
    smem = pl.BlockSpec(memory_space=pltpu.SMEM)
    halo = pl.BlockSpec((1, CP, WIDE), lambda s: (s, 0, 0))
    per_slab = pl.BlockSpec((1, rows, CP, WIDE), lambda s: (s, 0, 0, 0))
    edge = jax.ShapeDtypeStruct((slabs, CP, WIDE), BF16)
    return pl.pallas_call(
        functools.partial(lower_kernel, rows),
        grid=(slabs,),
        in_specs=[
            smem,
            smem,
            smem,
            per_slab,
            pl.BlockSpec(w.shape, lambda s: (0, 0), pipeline_mode=pl.Buffered(1)),
        ],
        out_specs=[per_slab, halo, halo],
        out_shape=(jax.ShapeDtypeStruct((slabs, rows, CP, WIDE), F32), edge, edge),
        scratch_shapes=[
            pltpu.VMEM((rows, BASIS * CP, WIDE), BF16),
            pltpu.SMEM((3 * (2 * REACH + 1),), jnp.int32),
            pltpu.SMEM((rows, 3 * (2 * REACH + 1)), F32),
        ],
        compiler_params=pltpu.CompilerParams(vmem_limit_bytes=VMEM),
        name="lower",
    )(offsets, bases, psi, gconv, w)


def input_kernel(rows, width, x, gconv, own, lo, hi, gain, out, sums, total):
    r = pl.program_id(1)

    @pl.when(jnp.logical_and(pl.program_id(0) == 0, r == 0))
    def _():
        sums[...] = jnp.zeros_like(sums)

    from_below = jnp.where(r == 0, 1.0, 0.0)
    from_above = jnp.where(r == rows - 1, 1.0, 0.0)

    def read(c):
        return x[0, 0, pl.ds(pl.multiple_of(c * STEP, STEP), STEP), :].astype(F32)

    mean, scale = norm_stats(read, CIN)

    def join(c, at):
        halo = lo[0, at, :].astype(F32) * from_below + hi[0, at, :].astype(F32) * from_above
        total[at, :] = own[0, 0, at, :] + halo

    each_chunk(join, 4)

    def means(c):
        at = pl.ds(pl.multiple_of(c * STEP, STEP), STEP)
        g = total[at, :] * tiled(gain[at, :])
        return g, g * ((read(c) - mean) * scale)

    flat, along = [v * (1.0 / CIN) for v in column_sums(means, CIN, 2)]

    def backward(c, at):
        dm = cut(total[at, :], width)
        xhat = (read(c) - mean) * scale
        g = dm * tiled(gain[at, :])
        value = scale * (g - flat - xhat * along) + gconv[0, 0, at, :].astype(F32)
        out[0, 0, at, :] = value.astype(BF16)
        along_lanes(sums.at[0], at, dm * xhat)
        along_lanes(sums.at[1], at, dm)

    each_chunk(backward, 8)


def input_grad(x, gconv, own, lo, hi, gain, width):
    slabs, rows = x.shape[:2]
    per_row = pl.BlockSpec((1, 1, CP, WIDE), lambda s, r: (s, r, 0, 0))
    halo = pl.BlockSpec((1, CP, WIDE), lambda s, r: (s, 0, 0))
    return pl.pallas_call(
        functools.partial(input_kernel, rows, width),
        grid=(slabs, rows),
        in_specs=[per_row, per_row, per_row, halo, halo, pl.BlockSpec((CP, LANES), lambda s, r: (0, 0))],
        out_specs=[per_row, pl.BlockSpec((2, CP, LANES), lambda s, r: (0, 0, 0))],
        out_shape=(
            jax.ShapeDtypeStruct((slabs, rows, CP, WIDE), BF16),
            jax.ShapeDtypeStruct((2, CP, LANES), F32),
        ),
        scratch_shapes=[pltpu.VMEM((CP, WIDE), F32)],
        compiler_params=pltpu.CompilerParams(vmem_limit_bytes=VMEM),
        name="input_grad",
    )(x, gconv, own, lo, hi, gain)


def flip(value, bit):
    return value + (1 - 2 * ((value // (1 << bit)) % 2)) * (1 << bit)


def flipped(value, mask):
    bit = 0
    while mask >> bit:
        if mask >> bit & 1:
            value = flip(value, bit)
        bit += 1
    return value


def span(bits):
    masks = [0]
    for b in bits:
        masks = masks + [m | 1 << b for m in masks]
    return masks


def orders(dates):
    bits = list(range(1, dates.bit_length() - 1))
    return bits + [0], bits[::-1] + [0]


def pieces(rows):
    cut = rows // (2 * STEP) * STEP
    return pl.ds(0, cut), pl.ds(cut, rows - cut)


def greet(dates, lats, d, l):
    barrier = pltpu.get_barrier_semaphore()
    count = 0
    for o in range(1, lats):
        pl.semaphore_signal(barrier, inc=1, device_id=(d, lax.rem(l + o, lats)), device_id_type=MESH)
        count += 1
    for b in range(dates.bit_length() - 1):
        pl.semaphore_signal(barrier, inc=1, device_id=(flip(d, b), l), device_id_type=MESH)
        count += 1
    pl.semaphore_wait(barrier, count)


def gather_kernel(dates, lats, src, out, local_sem, z_send, z_recv, send, recv):
    d, l = lax.axis_index("date"), lax.axis_index("lat")
    steps = dates.bit_length() - 1
    parts = pieces(src.shape[0])
    greet(dates, lats, d, l)
    own = pltpu.make_async_copy(src, out.at[d, l], local_sem)
    own.start()
    sent, arriving, flights = [], {}, {}

    def along(o):
        copy = pltpu.make_async_remote_copy(
            src_ref=src,
            dst_ref=out.at[d, l],
            send_sem=z_send.at[o - 1],
            recv_sem=z_recv.at[o - 1],
            device_id=(d, lax.rem(l + o, lats)),
            device_id_type=MESH,
        )
        copy.start()
        sent.append(copy)
        arriving[o] = copy

    def cross(o, p, i, n):
        order = orders(dates)[p]
        block = out.at[flipped(d, span(order[:i])[n]), lax.rem(l - o + lats, lats), parts[p]]
        slot = (1 << i) - 1 + n
        copy = pltpu.make_async_remote_copy(
            src_ref=src.at[parts[p]] if o == 0 and n == 0 else block,
            dst_ref=block,
            send_sem=send.at[o, p, slot],
            recv_sem=recv.at[o, p, slot],
            device_id=(flip(d, order[i]), l),
            device_id_type=MESH,
        )
        copy.start()
        sent.append(copy)
        flights[o, p, i, n] = copy

    for wave in range(lats + steps):
        if wave < lats:
            if wave:
                arriving[wave].wait_recv()
            if wave + 1 < lats:
                along(wave + 1)
            for i in range(steps):
                for p in range(2):
                    cross(wave, p, i, 0)
        for i in range(steps)[::-1]:
            o = wave - 1 - i
            if 0 <= o < lats:
                for n in range(1 << i):
                    for p in range(2):
                        flights[o, p, i, n].wait_recv()
                        for later in range(i + 1, steps):
                            cross(o, p, later, n + (1 << i))
    own.wait()
    for copy in sent:
        copy.wait_send()


def gather(shard, dates, lats):
    slots = dates - 1
    return pl.pallas_call(
        functools.partial(gather_kernel, dates, lats),
        in_specs=[pl.BlockSpec(memory_space=pl.ANY)],
        out_specs=pl.BlockSpec(memory_space=pl.ANY),
        out_shape=jax.ShapeDtypeStruct((dates, lats) + shard.shape, shard.dtype),
        scratch_shapes=[
            pltpu.SemaphoreType.DMA(()),
            pltpu.SemaphoreType.DMA((lats - 1,)),
            pltpu.SemaphoreType.DMA((lats - 1,)),
            pltpu.SemaphoreType.DMA((lats, 2, slots)),
            pltpu.SemaphoreType.DMA((lats, 2, slots)),
        ],
        compiler_params=pltpu.CompilerParams(collective_id=0, has_side_effects=True),
        name="gather_params",
    )(shard)


def scatter_kernel(dates, lats, src, out, sums, others, z_send, z_recv, send, recv):
    d, l = lax.axis_index("date"), lax.axis_index("lat")
    steps = dates.bit_length() - 1
    paths = [order[::-1] for order in orders(dates)]
    parts = pieces(src.shape[2])
    greet(dates, lats, d, l)
    sent, flights, z = [], {}, {}

    def left(p, i):
        return span(paths[p][i + 1 :][::-1])[::-1]

    def slot_of(i, n):
        return sum(1 << (steps - 1 - e) for e in range(i)) + n

    def held(o, p, i, mask):
        if i == 0:
            return src.at[flipped(d, mask), lax.rem(l + o, lats), parts[p]]
        return sums.at[o, slot_of(i - 1, left(p, i - 1).index(mask)), parts[p]]

    def cross(o, p, i, n):
        bit = paths[p][i]
        slot = slot_of(i, n)
        copy = pltpu.make_async_remote_copy(
            src_ref=held(o, p, i, left(p, i)[n] | 1 << bit),
            dst_ref=sums.at[o, slot, parts[p]],
            send_sem=send.at[o, p, slot],
            recv_sem=recv.at[o, p, slot],
            device_id=(flip(d, bit), l),
            device_id_type=MESH,
        )
        copy.start()
        sent.append(copy)
        flights[o, p, i, n] = copy

    def add(o, p, i, n):
        flights[o, p, i, n].wait_recv()
        have = held(o, p, i, left(p, i)[n])
        got = sums.at[o, slot_of(i, n), parts[p]]
        got[...] = (have[...].astype(F32) + got[...].astype(F32)).astype(BF16)
        if i + 1 < steps:
            if n < len(left(p, i + 1)):
                cross(o, p, i + 1, n)
        elif o:
            copy = pltpu.make_async_remote_copy(
                src_ref=got,
                dst_ref=others.at[o - 1, parts[p]],
                send_sem=z_send.at[o - 1, p],
                recv_sem=z_recv.at[o - 1, p],
                device_id=(d, lax.rem(l + o, lats)),
                device_id_type=MESH,
            )
            copy.start()
            sent.append(copy)
            z[o, p] = copy

    turns = list(range(1, lats)) + [0]
    for o in turns:
        for n in range(len(left(0, 0))):
            for p in range(2):
                cross(o, p, 0, n)
    for wave in range(lats + steps - 1):
        for i in range(steps):
            if 0 <= wave - i < lats:
                for n in range(len(left(0, i))):
                    for p in range(2):
                        add(turns[wave - i], p, i, n)
    for p in range(2):
        total = sums[0, slot_of(steps - 1, 0), parts[p]].astype(F32)
        for o in range(1, lats):
            z[o, p].wait_recv()
            total = total + others[o - 1, parts[p]].astype(F32)
        out[parts[p]] = total
    for copy in sent:
        copy.wait_send()


def scatter(packed):
    dates, lats, rows, lanes = packed.shape
    slots = dates - 1
    return pl.pallas_call(
        functools.partial(scatter_kernel, dates, lats),
        in_specs=[pl.BlockSpec(memory_space=pltpu.VMEM)],
        out_specs=pl.BlockSpec(memory_space=pltpu.VMEM),
        out_shape=jax.ShapeDtypeStruct((rows, lanes), F32),
        scratch_shapes=[
            pltpu.VMEM((lats, slots, rows, lanes), BF16),
            pltpu.VMEM((lats - 1, rows, lanes), BF16),
            pltpu.SemaphoreType.DMA((lats - 1, 2)),
            pltpu.SemaphoreType.DMA((lats - 1, 2)),
            pltpu.SemaphoreType.DMA((lats, 2, slots)),
            pltpu.SemaphoreType.DMA((lats, 2, slots)),
        ],
        compiler_params=pltpu.CompilerParams(
            collective_id=1, has_side_effects=True, vmem_limit_bytes=VMEM
        ),
        name="scatter_grads",
    )(packed)


def local(inputs, noise, cotangent, params, psi, step_counts, pixel_mask, offsets, bases):
    samples, steps, rows, width, _ = inputs.shape
    slabs = samples * steps
    dates, lats = lax.axis_size("date"), lax.axis_size("lat")
    lat = rows * lats

    def by_channel(values):
        return jnp.swapaxes(values, 3, 4).reshape(slabs, rows, -1, width)

    def padded(values):
        return jnp.pad(values, ((0, 0), (0, 0), (0, CP - values.shape[2]), (0, WIDE - width)))

    upward = [(i, i + 1) for i in range(lats - 1)]
    downward = [(i + 1, i) for i in range(lats - 1)]
    x = padded(jnp.concatenate([by_channel(inputs), by_channel(noise)], axis=2))
    below = lax.ppermute(x[:, rows - 1], "lat", upward)
    above = lax.ppermute(x[:, 0], "lat", downward)
    lines = params.shape[0] // LANES
    held = -(-lines // STEP) * STEP
    shard = jnp.pad(params.reshape(lines, LANES), ((0, held - lines), (0, 0)))
    gathered = gather(shard, dates, lats).reshape(dates * lats, held, LANES)
    w, wt, up, upt, dn, dnt, small = unpack(gathered, lines)
    cot = padded(by_channel(cotangent)).reshape(slabs * rows, CP, WIDE)
    active = jnp.arange(steps, dtype=jnp.int32)[None, :] < step_counts[:, None]
    mask = active.reshape(slabs, 1, 1) * pixel_mask[None]
    mask = jnp.pad(mask.astype(F32), ((0, 0), (0, 0), (0, WIDE - width)))
    basis = lift(offsets, bases, psi, below, x, above, small[0], small[1], lat, width)
    basis = basis.reshape(slabs * rows, BASIS * CP, WIDE)
    output, gconv, gup, gdn, second_sums = block(
        basis, x.reshape(slabs * rows, CP, WIDE), cot, mask.reshape(slabs * rows, 1, WIDE),
        wt, upt, up, dnt, dn, small[2], small[3], width,
    )
    gconv_rows = gconv.reshape(slabs, rows, CP, WIDE)
    own, to_below, to_above = lower(offsets, bases, psi, gconv_rows, w)
    from_below = lax.ppermute(to_above, "lat", upward)
    from_above = lax.ppermute(to_below, "lat", downward)
    gdisco = weight_grad(basis, gconv)
    grad, first_sums = input_grad(x, gconv_rows, own, from_below, from_above, small[0], width)
    sums = jnp.sum(jnp.concatenate([first_sums, second_sums]), axis=-1)
    valid = jnp.array([CIN, CIN, C, C], jnp.int32)[:, None]
    sums = jnp.where(jnp.arange(CP, dtype=jnp.int32)[None, :] < valid, sums, 0.0)
    sums = jnp.pad(sums, ((0, 0), (0, 8 * LANES - CP))).reshape(4, 8, LANES)
    packed = pack(gdisco, gup, gdn, sums, dates * lats, lines, held)
    summed = scatter(packed.reshape(dates, lats, held, LANES))

    def by_pixel(values):
        values = values.reshape(slabs, rows, CP, WIDE)[:, :, :C, :width]
        return jnp.swapaxes(values.reshape(samples, steps, rows, C, width), 3, 4)

    return by_pixel(output), by_pixel(grad), summed[:lines].reshape(-1)


def solution(mesh):
    field = P("date", None, "lat", None, None)
    flat = P(("date", "lat"))
    return jax.shard_map(
        local,
        mesh=mesh,
        in_specs=(field, field, field, flat, P(), P("date"), P("lat", None), P(), P()),
        out_specs=(field, field, flat),
        check_vma=False,
    )
```

```python
import functools
import math

import jax
import jax.numpy as jnp
from jax import lax
from jax.experimental import pallas as pl
from jax.experimental.pallas import tpu as pltpu
from jax.sharding import PartitionSpec as P

C = 641
HID = 1282
BASIS = 4
SUPPORT = 12
REACH = 2
CIN = 649
BF16, F32 = jnp.bfloat16, jnp.float32
MESH = pl.DeviceIdType.MESH
LANES = 128
STEP = 16
CP = 656
HP = 1296
WIDE = 768
HL = 1408
UNROLL = 8
VMEM = 60 << 20


OFF_G1=BASIS*CIN*C+C; OFF_S1=OFF_G1+CIN; OFF_G2=OFF_S1+CIN; OFF_S2=OFF_G2+C; OFF_UP=OFF_S2+C; OFF_DN=OFF_UP+(C+1)*HID;
SMALL=((OFF_G1,CIN),(OFF_S1,CIN),(OFF_G2,C),(OFF_S2,C))
MATS=((0,C,BASIS*CIN+1,128,3),(OFF_UP,HID,C+1,64,2),(OFF_DN,C,HID+1,128,2))
F_ROWS=29952
def lane_ids(): return lax.broadcasted_iota(jnp.int32,(8,LANES),1)
def place(base,cols,period,b):
    start=base+cols*b
    return start//LANES, start%LANES
def unpack_kernel(nrow,pad, g_ref, w_ref,wt_ref,up_ref,upt_ref,dn_ref,dnt_ref,flat,chunks):
    def fill(s,_):
        flat[pl.ds(nrow*s,pad),:]=g_ref[s].astype(F32); return 0
    lax.fori_loop(0,g_ref.shape[0],fill,0)
    lane=lane_ids()
    def split(base,cols,period,groups):
        J=-(-cols//LANES); pitch=period+8; height=pitch*8*groups+8; last=cols-(J-1)*LANES
        def body(b,_):
            row,s=place(base,cols,period,b)
            back=(LANES-s)%LANES
            for g in range(groups):
                rolled=[pltpu.roll(flat[pl.ds(row+641*8*g+j,8,stride=641),:],back,axis=1) for j in range(J+1)]
                for j in range(J):
                    val=jnp.where(lane<LANES-s,rolled[j],rolled[j+1])
                    if j==J-1: val=jnp.where(lane<last,val,0.0)
                    chunks[pl.ds(j*height+8*g*pitch+b,8,stride=pitch),:]=val
            return 0
        lax.fori_loop(0,period,body,0,unroll=8)
        def border(a,_):
            for j in range(J): chunks[pl.ds(j*height+a*pitch-8,8),:]=chunks[pl.ds(j*height+a*pitch,8),:]
            return 0
        lax.fori_loop(1,8*groups,border,0)
        return J,height,period
    def convert(dst,dst_row,src_row,rows,pad_rows,J,height,period):
        full=rows//16
        def piece(j,r): return chunks[pl.ds(j*height+r//period*(period+8)+r%period,8),:]
        def pair(j,r): return jnp.concatenate([piece(j,r),piece(j,r+8)],axis=0)
        def body(m,_):
            for j in range(J):
                dst[pl.ds(pl.multiple_of(dst_row+16*m,16),16),j*LANES:(j+1)*LANES]=pair(j,src_row+16*m).astype(BF16)
            return 0
        lax.fori_loop(0,full,body,0,unroll=4)
        keep=lax.broadcasted_iota(jnp.int32,(16,LANES),0)<rows-16*full
        for m in range(full,pad_rows//16):
            for j in range(J):
                v=jnp.where(keep,pair(j,src_row+16*m),0.0) if m==full else jnp.zeros((16,LANES),F32)
                dst[dst_row+16*m:dst_row+16*m+16,j*LANES:(j+1)*LANES]=v.astype(BF16)
    J,h,p=split(*MATS[0][:2],*MATS[0][3:])
    for k in range(BASIS):
        convert(w_ref,k*CP,k*CIN,CIN+(k==BASIS-1),CP,J,h,p)
    J,h,p=split(*MATS[1][:2],*MATS[1][3:])
    convert(up_ref,0,0,C+1,CP,J,h,p)
    J,h,p=split(*MATS[2][:2],*MATS[2][3:])
    convert(dn_ref,0,0,HID+1,HP,J,h,p)
    wt_ref[...]=w_ref[:,:CP].T
    upt_ref[...]=up_ref[:,:HP].T
    dnt_ref[...]=dn_ref[:,:CP].T
def unpack(gathered,nrow):
    n,pad,_=gathered.shape
    return pl.pallas_call(functools.partial(unpack_kernel,nrow,pad),
        out_shape=(jax.ShapeDtypeStruct((BASIS*CP,WIDE),BF16),jax.ShapeDtypeStruct((CP,BASIS*CP),BF16),
            jax.ShapeDtypeStruct((CP,HL),BF16),jax.ShapeDtypeStruct((HP,CP),BF16),
            jax.ShapeDtypeStruct((HP,WIDE),BF16),jax.ShapeDtypeStruct((CP,HP),BF16)),
        scratch_shapes=[pltpu.VMEM((F_ROWS,LANES),F32),pltpu.VMEM((6*(136*24+8),LANES),F32)],
        compiler_params=pltpu.CompilerParams(vmem_limit_bytes=VMEM),name="unpack")(gathered)
def pack_kernel(nrow,pad,gd_ref,gu_ref,gn_ref,out_ref,flat,chunks):
    lane=lane_ids(); sub=lax.broadcasted_iota(jnp.int32,(8,LANES),0)
    def gather(src,src_row,dst_row,rows,J,height,last,period):
        full=rows//8
        def cols(m,j):
            v=src[pl.ds(pl.multiple_of(src_row+8*m,8),8),j*LANES:(j+1)*LANES]
            return jnp.where(lane<last,v,0.0) if j==J-1 else v
        def body(m,_):
            r=dst_row+8*m; at=r//period*(period+8)+r%period
            for j in range(J):
                v=cols(m,j)
                chunks[pl.ds(j*height+at+8,8),:]=v
                chunks[pl.ds(j*height+at,8),:]=v
            return 0
        lax.fori_loop(0,full,body,0,unroll=4)
        if rows%8:
            r=dst_row+8*full; at=r//period*(period+8)+r%period
            for j in range(J):
                v=jnp.where(sub<rows-8*full,cols(full,j),0.0)
                chunks[pl.ds(j*height+at+8,8),:]=v
                chunks[pl.ds(j*height+at,8),:]=v
    def clear(J,height,row,period):
        row=row//period*(period+8)+row%period
        count=(height-row)//8
        def body(m,_):
            for j in range(J): chunks[pl.ds(j*height+row+8*m,8),:]=jnp.zeros((8,LANES),F32)
            return 0
        lax.fori_loop(0,count,body,0)
    def merge(base,cols,period,groups):
        J=-(-cols//LANES); pitch=period+8; height=pitch*8*groups+8
        def body(b,tails,rows=J):
            row,s=place(base,cols,period,b)
            new=[]
            for g in range(groups):
                x=[pltpu.roll(chunks[pl.ds(j*height+8*g*pitch+b,8,stride=pitch),:],s,axis=1) for j in range(J)]
                first=lane>=s
                for j in range(J):
                    v=jnp.where(first,x[j],tails[g] if j==0 else x[j-1])
                    if j<rows: flat[pl.ds(row+641*8*g+j,8,stride=641),:]=v
                new.append(jnp.where(s==LANES-1,jnp.where(first,0.0,x[J-1]),v))
            return tuple(new)
        row0=base//LANES
        init=[jnp.zeros((8,LANES),F32)]*groups
        if base%LANES:
            init[0]=jnp.where(sub==0,flat[row0:row0+8,:],0.0)
        tails=lax.fori_loop(0,period-8,body,tuple(init),unroll=8)
        for b in range(period-8,period):
            tails=body(b,tails,J-1 if base%LANES and b==period-1 else J)
        if base%LANES:
            for g in range(groups):
                at=pl.ds(row0+641*(8*g+1),8,stride=641)
                flat[at,:]=flat[at,:]+tails[g]
    h=136*24+8
    for k in range(BASIS): gather(gd_ref,k*CP,k*CIN,CIN+(k==BASIS-1),6,h,1,128)
    clear(6,h,2600,128)
    merge(0,C,128,3)
    h=72*16+8
    gather(gu_ref,0,0,C+1,11,h,2,64)
    clear(11,h,648,64)
    merge(OFF_UP,HID,64,2)
    h=136*16+8
    gather(gn_ref,0,0,HID+1,6,h,1,128)
    clear(6,h,1288,128)
    merge(OFF_DN,C,128,2)
    def store(s,_):
        out_ref[s]=flat[pl.ds(nrow*s,pad),:].astype(BF16); return 0
    lax.fori_loop(0,out_ref.shape[0],store,0)
def pack(gd,gu,gn,n,nrow,pad):
    return pl.pallas_call(functools.partial(pack_kernel,nrow,pad),
        out_shape=jax.ShapeDtypeStruct((n,pad,LANES),BF16),
        scratch_shapes=[pltpu.VMEM((F_ROWS,LANES),F32),pltpu.VMEM((6*(136*24+8),LANES),F32)],
        compiler_params=pltpu.CompilerParams(vmem_limit_bytes=VMEM),name="pack")(gd,gu,gn)


def tiled(column):
    return jnp.concatenate([column] * (WIDE // LANES), axis=1)


def lane_of(rows, start=0):
    return lax.broadcasted_iota(jnp.int32, (rows, LANES), 1) + start


def wrapped(chunk, width):
    head, first, last = chunk[:, : WIDE - LANES], chunk[:, :LANES], chunk[:, WIDE - LANES :]
    edge = width - (WIDE - LANES)
    lane = lane_of(chunk.shape[0])
    beyond = jnp.where(
        lane < LANES - REACH, pltpu.roll(first, edge, axis=1), pltpu.roll(last, LANES - edge, axis=1)
    )
    return jnp.concatenate([head, jnp.where(lane < edge, last, beyond)], axis=1)


def cut(chunk, width):
    head, last = chunk[:, : WIDE - LANES], chunk[:, WIDE - LANES :]
    keep = lane_of(chunk.shape[0], WIDE - LANES) < width
    return jnp.concatenate([head, jnp.where(keep, last, 0.0)], axis=1)


def rows_below(count):
    return lax.broadcasted_iota(jnp.int32, (STEP, WIDE), 0) < count


def halves(chunk):
    return chunk[:8] + chunk[8:]


def column_sums(read, channels, count):
    whole = channels // STEP

    def body(m, sums):
        return tuple(a + halves(v) for a, v in zip(sums, read(m)))

    sums = lax.fori_loop(
        0, whole, body, tuple(jnp.zeros((8, WIDE), F32) for _ in range(count)), unroll=UNROLL
    )
    keep = rows_below(channels - whole * STEP)
    sums = [a + halves(jnp.where(keep, v, 0.0)) for a, v in zip(sums, read(whole))]
    return [jnp.sum(a, axis=0, keepdims=True) for a in sums]


def norm_stats(read, channels):
    (total,) = column_sums(lambda m: (read(m),), channels, 1)
    mean = total * (1.0 / channels)

    def squares(m):
        centered = read(m) - mean
        return (centered * centered,)

    (total,) = column_sums(squares, channels, 1)
    return mean, lax.rsqrt(total * (1.0 / channels) + 1e-05)


def each_chunk(body, unroll=None):
    def step(m, _):
        body(m, pl.ds(pl.multiple_of(m * STEP, STEP), STEP))
        return 0

    lax.fori_loop(0, CP // STEP, step, 0, unroll=unroll)


def spread(source, gain, shift, width, moved):
    def read(c):
        return source[pl.ds(pl.multiple_of(c * STEP, STEP), STEP), :].astype(F32)

    mean, scale = norm_stats(read, CIN)

    def shifts(c, at):
        values = (read(c) - mean) * scale * tiled(gain[at, :]) + tiled(shift[at, :])
        values = wrapped(values, width).astype(BF16)
        for d in range(-REACH, REACH + 1):
            moved[d + REACH, at, :] = pltpu.roll(values, -d % WIDE, axis=1) if d else values

    each_chunk(shifts, 4)


def lift_kernel(
    rows, slab, lat, width, offsets, bases, psi, lo, hi, own, gain, shift, *refs
):
    out, moved, table, sems = refs[-4:]
    first_row = lax.axis_index("lat") * rows
    copies = [
        pltpu.make_async_copy(own.at[slab, r], moved.at[r + 1], sems.at[r]) for r in range(rows)
    ]
    for copy in copies:
        copy.start()
    for k in range(BASIS):
        table[SUPPORT + k] = 0
    for p in range(SUPPORT):
        k = bases[p]
        used = table[SUPPORT + k]
        table[k * 3 + used] = p
        table[SUPPORT + k] = used + 1
    for source, m in ((lo, 0), (hi, rows + 1)):
        spread(source.at[0], gain, shift, width, moved.at[m])
    for copy in copies:
        copy.wait()
    for r in range(rows):
        for k in range(BASIS):
            parts = []
            for q in range(3):
                p = table[k * 3 + q]
                row = first_row + r + offsets[p, 0]
                inside = jnp.logical_and(row >= 0, row < lat)
                weight = jnp.where(inside, psi[first_row + r, p], 0.0)
                parts.append((weight, r + 1 + offsets[p, 0], offsets[p, 1] + REACH))

            def combine(c, at):
                total = None
                for weight, row, d in parts:
                    term = weight * moved[row, d, at, :].astype(F32)
                    total = term if total is None else total + term
                to = pl.ds(pl.multiple_of(k * CP + c * STEP, STEP), STEP)
                out[0, r, to, :] = cut(total, width).astype(BF16)

            each_chunk(combine, 4)
        last = slice(BASIS * CP - STEP, BASIS * CP)
        bias_row = CIN - (CP - STEP)
        sub = lax.broadcasted_iota(jnp.int32, (STEP, WIDE), 0)
        lane = lax.broadcasted_iota(jnp.int32, (STEP, WIDE), 1)
        ones = jnp.where(lane < width, 1.0, 0.0)
        out[0, r, last, :] = jnp.where(sub == bias_row, ones, out[0, r, last, :].astype(F32)).astype(BF16)


def lift(offsets, bases, psi, lo, hi, own, gain, shift, before, slab, lat, width):
    slabs, rows = own.shape[:2]
    smem = pl.BlockSpec(memory_space=pltpu.SMEM)
    anywhere = pl.BlockSpec(memory_space=pl.ANY)
    halo = pl.BlockSpec((1, CP, WIDE), lambda s: (0, 0, 0))
    column = pl.BlockSpec((CP, LANES), lambda s: (0, 0))
    return pl.pallas_call(
        functools.partial(lift_kernel, rows, slab, lat, width),
        grid=(1,),
        in_specs=[smem, smem, smem, halo, halo, anywhere, column, column] + [anywhere] * len(before),
        out_specs=pl.BlockSpec((1, rows, BASIS * CP, WIDE), lambda s: (slab, 0, 0, 0)),
        out_shape=jax.ShapeDtypeStruct((slabs, rows, BASIS * CP, WIDE), BF16),
        scratch_shapes=[
            pltpu.VMEM((rows + 2, 2 * REACH + 1, CP, WIDE), BF16),
            pltpu.SMEM((SUPPORT + BASIS,), jnp.int32),
            pltpu.SemaphoreType.DMA((rows,)),
        ],
        input_output_aliases={8: 0} if before else {},
        compiler_params=pltpu.CompilerParams(vmem_limit_bytes=VMEM),
        cost_estimate=pl.CostEstimate(flops=40 << 20, bytes_accessed=40 << 20, transcendentals=0),
        name="lift",
    )(offsets, bases, psi, lo, hi, own, gain, shift, *before)


GELU_A = math.sqrt(2.0 / math.pi)
GELU_B = 0.044715


def block_kernel(
    width, basis, x, cot, mask, wt, upt, up, dnt, dn, gain, shift,
    out, gconv, gup, gdn, sums,
    res, second, pre, act, slope, gb, gpre, gsec,
):
    start = pl.program_id(0) == 0

    @pl.when(start)
    def _():
        gup[...] = jnp.zeros_like(gup)
        gdn[...] = jnp.zeros_like(gdn)
        sums[...] = jnp.zeros_like(sums)

    def dot(a, b):
        return jnp.dot(a, b, preferred_element_type=F32)

    res[...] = dot(wt[...], basis[0])

    def add_input(c, at):
        values = x[0, at, :].astype(F32)
        keep = lax.broadcasted_iota(jnp.int32, (STEP, WIDE), 0) + c * STEP < C
        res[at, :] = res[at, :] + jnp.where(keep, values, 0.0)
        gb[at, :] = (cot[0, at, :].astype(F32) * mask[0]).astype(BF16)

    each_chunk(add_input, 8)

    def read(c):
        return res[pl.ds(pl.multiple_of(c * STEP, STEP), STEP), :]

    mean, scale = norm_stats(read, C)

    def normalize(c, at):
        values = (res[at, :] - mean) * scale * tiled(gain[at, :]) + tiled(shift[at, :])
        row = lax.broadcasted_iota(jnp.int32, (STEP, WIDE), 0) + c * STEP
        second[at, :] = jnp.where(row == C, 1.0, values).astype(BF16)

    each_chunk(normalize, 8)
    pre[...] = dot(upt[...], second[...])

    def gelu(c, _):
        at = pl.ds(pl.multiple_of(c * STEP, STEP), STEP)
        v = pre[at, :]
        square = v * v
        bend = jnp.tanh(GELU_A * v * (1.0 + GELU_B * square))
        half = 0.5 * (1.0 + bend)
        row = lax.broadcasted_iota(jnp.int32, (STEP, WIDE), 0) + c * STEP
        act[at, :] = jnp.where(row == HID, 1.0, v * half).astype(BF16)
        rise = GELU_A * (1.0 + 3.0 * GELU_B * square)
        slope[at, :] = half + 0.5 * v * (1.0 - bend * bend) * rise
        return 0

    lax.fori_loop(0, HP // STEP, gelu, 0, unroll=8)
    pre[:CP, :] = dot(dnt[...], act[...])

    def finish(c, at):
        out[0, at, :] = (res[at, :] + pre[at, :]).astype(BF16)

    each_chunk(finish, 8)
    pre[...] = dot(dn[:, :CP], gb[...])

    def back(c, _):
        at = pl.ds(pl.multiple_of(c * STEP, STEP), STEP)
        gpre[at, :] = (pre[at, :] * slope[at, :]).astype(BF16)
        return 0

    lax.fori_loop(0, HP // STEP, back, 0, unroll=8)
    gsec[...] = dot(up[:, :HP], gpre[...])

    def means(c):
        at = pl.ds(pl.multiple_of(c * STEP, STEP), STEP)
        g = gsec[at, :] * tiled(gain[at, :])
        return g, g * ((res[at, :] - mean) * scale)

    flat, along = [v * (1.0 / C) for v in column_sums(means, C, 2)]

    def backward(c, at):
        dm = gsec[at, :]
        xhat = (res[at, :] - mean) * scale
        g = dm * tiled(gain[at, :])
        value = gb[at, :].astype(F32) + scale * (g - flat - xhat * along)
        row = lax.broadcasted_iota(jnp.int32, (STEP, WIDE), 0) + c * STEP
        value = jnp.where(row < C, value, 0.0)
        gconv[0, at, :] = wrapped(value, width).astype(BF16)
        along_lanes(sums.at[0], at, dm * xhat)
        along_lanes(sums.at[1], at, dm)

    each_chunk(backward, 8)

    def outer(a, b):
        return lax.dot_general(a, b, (((1,), (1,)), ((), ())), preferred_element_type=F32)

    gdn[:, :CP] += outer(act[...], gb[...])
    gup[:, :HP] += outer(second[...], gpre[...])


def along_lanes(ref, at, values):
    total = values[:, :LANES]
    for j in range(1, WIDE // LANES):
        total = total + values[:, j * LANES : (j + 1) * LANES]
    ref[at, :] = ref[at, :] + total


def block(basis, x, cot, mask, wt, upt, up, dnt, dn, gain, shift, width):
    count = x.shape[0]

    def per_row(height):
        return pl.BlockSpec((1, height, WIDE), lambda i: (i, 0, 0))

    def whole(a):
        return pl.BlockSpec(a.shape, lambda i: (0,) * len(a.shape), pipeline_mode=pl.Buffered(1))

    outs = (
        jax.ShapeDtypeStruct((count, CP, WIDE), BF16),
        jax.ShapeDtypeStruct((count, CP, WIDE), BF16),
        jax.ShapeDtypeStruct((CP, HL), F32),
        jax.ShapeDtypeStruct((HP, WIDE), F32),
        jax.ShapeDtypeStruct((2, CP, LANES), F32),
    )
    weights = (wt, upt, up, dnt, dn, gain, shift)
    return pl.pallas_call(
        functools.partial(block_kernel, width),
        grid=(count,),
        in_specs=[per_row(BASIS * CP), per_row(CP), per_row(CP), per_row(1)] + [whole(a) for a in weights],
        out_specs=[per_row(CP), per_row(CP)] + [whole(a) for a in outs[2:]],
        out_shape=outs,
        scratch_shapes=[
            pltpu.VMEM((CP, WIDE), F32),
            pltpu.VMEM((CP, WIDE), BF16),
            pltpu.VMEM((HP, WIDE), F32),
            pltpu.VMEM((HP, WIDE), BF16),
            pltpu.VMEM((HP, WIDE), F32),
            pltpu.VMEM((CP, WIDE), BF16),
            pltpu.VMEM((HP, WIDE), BF16),
            pltpu.VMEM((CP, WIDE), F32),
        ],
        compiler_params=pltpu.CompilerParams(vmem_limit_bytes=VMEM),
        name="block",
    )(basis, x, cot, mask, *weights)


def outer_kernel(basis, gconv, out):
    i = pl.program_id(0)
    term = lax.dot_general(basis[0], gconv[0], (((1,), (1,)), ((), ())), preferred_element_type=F32)

    @pl.when(i == 0)
    def _():
        out[:, :CP] = term

    @pl.when(i > 0)
    def _():
        out[:, :CP] += term


def weight_grad(basis, gconv):
    count = basis.shape[0]
    return pl.pallas_call(
        outer_kernel,
        grid=(count,),
        in_specs=[
            pl.BlockSpec((1, BASIS * CP, WIDE), lambda i: (i, 0, 0)),
            pl.BlockSpec((1, CP, WIDE), lambda i: (i, 0, 0)),
        ],
        out_specs=pl.BlockSpec((BASIS * CP, WIDE), lambda i: (0, 0)),
        out_shape=jax.ShapeDtypeStruct((BASIS * CP, WIDE), F32),
        compiler_params=pltpu.CompilerParams(vmem_limit_bytes=VMEM),
        name="weight_grad",
    )(basis, gconv)


def lower_kernel(rows, offsets, bases, psi, gconv, w, own, lo, hi, lifted, place, coef):
    first_row = lax.axis_index("lat") * rows
    span = 2 * REACH + 1
    for n in range(3 * span):
        place[n] = 0
        for r in range(rows):
            coef[r, n] = 0.0
    for p in range(SUPPORT):
        n = (offsets[p, 0] + 1) * span + offsets[p, 1] + REACH
        place[n] = bases[p]
        for r in range(rows):
            coef[r, n] = psi[first_row + r, p]
    for r in range(rows):
        lifted[r] = jnp.dot(w[:, :CP], gconv[0, r], preferred_element_type=F32).astype(BF16)
    for target in range(-1, rows + 1):
        terms = []
        for d in range(-REACH, REACH + 1):
            for o in (-1, 0, 1):
                r = target - o
                if 0 <= r < rows:
                    n = (o + 1) * span + d + REACH
                    terms.append((d, r, coef[r, n], place[n] * CP))

        def gather(c, at):
            total = None
            for d in range(-REACH, REACH + 1):
                part = None
                for e, r, weight, base in terms:
                    if e == d:
                        source = pl.ds(pl.multiple_of(base + c * STEP, STEP), STEP)
                        term = weight * lifted[r, source, :].astype(F32)
                        part = term if part is None else part + term
                if d:
                    part = pltpu.roll(part.astype(BF16), d % WIDE, axis=1).astype(F32)
                total = part if total is None else total + part
            if target < 0:
                lo[0, at, :] = total.astype(BF16)
            elif target == rows:
                hi[0, at, :] = total.astype(BF16)
            else:
                own[0, target, at, :] = total

        each_chunk(gather, 8)


def lower(offsets, bases, psi, gconv, w):
    slabs, rows = gconv.shape[:2]
    smem = pl.BlockSpec(memory_space=pltpu.SMEM)
    halo = pl.BlockSpec((1, CP, WIDE), lambda s: (s, 0, 0))
    per_slab = pl.BlockSpec((1, rows, CP, WIDE), lambda s: (s, 0, 0, 0))
    edge = jax.ShapeDtypeStruct((slabs, CP, WIDE), BF16)
    return pl.pallas_call(
        functools.partial(lower_kernel, rows),
        grid=(slabs,),
        in_specs=[
            smem,
            smem,
            smem,
            per_slab,
            pl.BlockSpec(w.shape, lambda s: (0, 0), pipeline_mode=pl.Buffered(1)),
        ],
        out_specs=[per_slab, halo, halo],
        out_shape=(jax.ShapeDtypeStruct((slabs, rows, CP, WIDE), F32), edge, edge),
        scratch_shapes=[
            pltpu.VMEM((rows, BASIS * CP, WIDE), BF16),
            pltpu.SMEM((3 * (2 * REACH + 1),), jnp.int32),
            pltpu.SMEM((rows, 3 * (2 * REACH + 1)), F32),
        ],
        compiler_params=pltpu.CompilerParams(vmem_limit_bytes=VMEM),
        name="lower",
    )(offsets, bases, psi, gconv, w)


def input_kernel(rows, width, x, gconv, own, lo, hi, gain, out, sums, total):
    r = pl.program_id(1)

    @pl.when(jnp.logical_and(pl.program_id(0) == 0, r == 0))
    def _():
        sums[...] = jnp.zeros_like(sums)

    from_below = jnp.where(r == 0, 1.0, 0.0)
    from_above = jnp.where(r == rows - 1, 1.0, 0.0)

    def read(c):
        return x[0, 0, pl.ds(pl.multiple_of(c * STEP, STEP), STEP), :].astype(F32)

    mean, scale = norm_stats(read, CIN)

    def join(c, at):
        halo = lo[0, at, :].astype(F32) * from_below + hi[0, at, :].astype(F32) * from_above
        total[at, :] = own[0, 0, at, :] + halo

    each_chunk(join, 4)

    def means(c):
        at = pl.ds(pl.multiple_of(c * STEP, STEP), STEP)
        g = total[at, :] * tiled(gain[at, :])
        return g, g * ((read(c) - mean) * scale)

    flat, along = [v * (1.0 / CIN) for v in column_sums(means, CIN, 2)]

    def backward(c, at):
        dm = cut(total[at, :], width)
        xhat = (read(c) - mean) * scale
        g = dm * tiled(gain[at, :])
        value = scale * (g - flat - xhat * along) + gconv[0, 0, at, :].astype(F32)
        out[0, 0, at, :] = value.astype(BF16)
        along_lanes(sums.at[0], at, dm * xhat)
        along_lanes(sums.at[1], at, dm)

    each_chunk(backward, 8)


def input_grad(x, gconv, own, lo, hi, gain, width):
    slabs, rows = x.shape[:2]
    per_row = pl.BlockSpec((1, 1, CP, WIDE), lambda s, r: (s, r, 0, 0))
    halo = pl.BlockSpec((1, CP, WIDE), lambda s, r: (s, 0, 0))
    return pl.pallas_call(
        functools.partial(input_kernel, rows, width),
        grid=(slabs, rows),
        in_specs=[per_row, per_row, per_row, halo, halo, pl.BlockSpec((CP, LANES), lambda s, r: (0, 0))],
        out_specs=[per_row, pl.BlockSpec((2, CP, LANES), lambda s, r: (0, 0, 0))],
        out_shape=(
            jax.ShapeDtypeStruct((slabs, rows, CP, WIDE), BF16),
            jax.ShapeDtypeStruct((2, CP, LANES), F32),
        ),
        scratch_shapes=[pltpu.VMEM((CP, WIDE), F32)],
        compiler_params=pltpu.CompilerParams(vmem_limit_bytes=VMEM),
        name="input_grad",
    )(x, gconv, own, lo, hi, gain)


def flip(value, bit):
    return value + (1 - 2 * ((value // (1 << bit)) % 2)) * (1 << bit)


def flipped(value, mask):
    bit = 0
    while mask >> bit:
        if mask >> bit & 1:
            value = flip(value, bit)
        bit += 1
    return value


def span(bits):
    masks = [0]
    for b in bits:
        masks = masks + [m | 1 << b for m in masks]
    return masks


def orders(dates):
    bits = list(range(1, dates.bit_length() - 1))
    return bits + [0], bits[::-1] + [0]


def pieces(rows):
    cut = rows // (2 * STEP) * STEP
    return pl.ds(0, cut), pl.ds(cut, rows - cut)


def greet(dates, lats, d, l):
    barrier = pltpu.get_barrier_semaphore()
    count = 0
    for o in range(1, lats):
        pl.semaphore_signal(barrier, inc=1, device_id=(d, lax.rem(l + o, lats)), device_id_type=MESH)
        count += 1
    for b in range(dates.bit_length() - 1):
        pl.semaphore_signal(barrier, inc=1, device_id=(flip(d, b), l), device_id_type=MESH)
        count += 1
    pl.semaphore_wait(barrier, count)


def norms_kernel(dates, lats, owner, first, src, out, landed, local_sem, send, recv):
    d, l = lax.axis_index("date"), lax.axis_index("lat")
    mine = jnp.logical_and(d == owner[0], l == owner[1])
    barrier = pltpu.get_barrier_semaphore()
    others = [(a, b) for a in range(dates) for b in range(lats) if (a, b) != owner]

    def copy_to(n):
        return pltpu.make_async_remote_copy(
            src_ref=src,
            dst_ref=landed,
            send_sem=send.at[n],
            recv_sem=recv,
            device_id=others[n],
            device_id_type=MESH,
        )

    @pl.when(mine)
    def _():
        pl.semaphore_wait(barrier, len(others))
        copies = [copy_to(n) for n in range(len(others))]
        for copy in copies:
            copy.start()
        own = pltpu.make_async_copy(src, landed, local_sem)
        own.start()
        own.wait()
        for copy in copies:
            copy.wait_send()

    @pl.when(jnp.logical_not(mine))
    def _():
        pl.semaphore_signal(barrier, inc=1, device_id=owner, device_id_type=MESH)
        copy_to(0).wait_recv()

    lane = lane_ids()
    sub = lax.broadcasted_iota(jnp.int32, (8, LANES), 0)
    lines = landed[...].astype(F32)
    for i, (off, n) in enumerate(SMALL):
        row, s = divmod(off - first * LANES, LANES)
        r = pltpu.roll(lines[row : row + 8], (LANES - s) % LANES, axis=1)
        v = jnp.where(lane < LANES - s, r, pltpu.roll(r, 7, axis=0))
        t = jnp.where(sub * LANES + lane < n, v, 0.0).T
        for j in range(6):
            rows = min(LANES, CP - j * LANES)
            out[i, j * LANES : j * LANES + rows, :] = jnp.broadcast_to(t[:rows, j : j + 1], (rows, LANES))


def norms(shard, lines, dates, lats):
    start, end = OFF_G1 // LANES, (OFF_UP - 1) // LANES + 3
    owner = start // lines
    row = (start - owner * lines) // STEP * STEP
    count = -(-(end - owner * lines - row) // STEP) * STEP
    assert row + count <= shard.shape[0]
    return pl.pallas_call(
        functools.partial(norms_kernel, dates, lats, divmod(owner, lats), owner * lines + row),
        in_specs=[pl.BlockSpec(memory_space=pltpu.VMEM)],
        out_specs=pl.BlockSpec(memory_space=pltpu.VMEM),
        out_shape=jax.ShapeDtypeStruct((4, CP, LANES), F32),
        scratch_shapes=[
            pltpu.VMEM((count, LANES), BF16),
            pltpu.SemaphoreType.DMA(()),
            pltpu.SemaphoreType.DMA((dates * lats - 1,)),
            pltpu.SemaphoreType.DMA(()),
        ],
        compiler_params=pltpu.CompilerParams(
            collective_id=0, has_side_effects=True, vmem_limit_bytes=VMEM
        ),
        name="norms",
    )(lax.slice_in_dim(shard, row, row + count, axis=0))


def gather_kernel(
    dates, lats, width, src, x, gain, shift, out, moved, local_sem, z_send, z_recv, send, recv, buffers, buffer_sems
):
    d, l = lax.axis_index("date"), lax.axis_index("lat")
    steps = dates.bit_length() - 1
    parts = pieces(src.shape[0])
    greet(dates, lats, d, l)
    own = pltpu.make_async_copy(src, out.at[d, l], local_sem)
    own.start()
    sent, arriving, flights = [], {}, {}

    def along(o):
        copy = pltpu.make_async_remote_copy(
            src_ref=src,
            dst_ref=out.at[d, l],
            send_sem=z_send.at[o - 1],
            recv_sem=z_recv.at[o - 1],
            device_id=(d, lax.rem(l + o, lats)),
            device_id_type=MESH,
        )
        copy.start()
        sent.append(copy)
        arriving[o] = copy

    def cross(o, p, i, n):
        order = orders(dates)[p]
        block = out.at[flipped(d, span(order[:i])[n]), lax.rem(l - o + lats, lats), parts[p]]
        slot = (1 << i) - 1 + n
        copy = pltpu.make_async_remote_copy(
            src_ref=src.at[parts[p]] if o == 0 and n == 0 else block,
            dst_ref=block,
            send_sem=send.at[o, p, slot],
            recv_sem=recv.at[o, p, slot],
            device_id=(flip(d, order[i]), l),
            device_id_type=MESH,
        )
        copy.start()
        sent.append(copy)
        flights[o, p, i, n] = copy

    rows = [(s, r) for s in range(x.shape[0]) for r in range(x.shape[1])]
    saves = []

    def spread_rows():
        for n, (s, r) in enumerate(rows):
            if n >= 2:
                saves[n - 2].wait()
            spread(x.at[s, r], gain, shift, width, buffers.at[n % 2])
            save = pltpu.make_async_copy(buffers.at[n % 2], moved.at[s, r], buffer_sems.at[n % 2])
            save.start()
            saves.append(save)
            yield

    aside = spread_rows()
    for wave in range(lats + steps):
        if wave < lats:
            if wave:
                arriving[wave].wait_recv()
            if wave + 1 < lats:
                along(wave + 1)
            for i in range(steps):
                for p in range(2):
                    cross(wave, p, i, 0)
        next(aside, None)
        for i in range(steps)[::-1]:
            o = wave - 1 - i
            if 0 <= o < lats:
                for n in range(1 << i):
                    for p in range(2):
                        flights[o, p, i, n].wait_recv()
                        for later in range(i + 1, steps):
                            cross(o, p, later, n + (1 << i))
    for _ in aside:
        pass
    for save in saves[-2:]:
        save.wait()
    own.wait()
    for copy in sent:
        copy.wait_send()


def gather(shard, x, gain, shift, dates, lats, width):
    slots = dates - 1
    moved = x.shape[:2] + (2 * REACH + 1,) + x.shape[2:]
    anywhere = pl.BlockSpec(memory_space=pl.ANY)
    return pl.pallas_call(
        functools.partial(gather_kernel, dates, lats, width),
        in_specs=[anywhere] + [pl.BlockSpec(memory_space=pltpu.VMEM)] * 3,
        out_specs=[anywhere, anywhere],
        out_shape=(
            jax.ShapeDtypeStruct((dates, lats) + shard.shape, shard.dtype),
            jax.ShapeDtypeStruct(moved, BF16),
        ),
        scratch_shapes=[
            pltpu.SemaphoreType.DMA(()),
            pltpu.SemaphoreType.DMA((lats - 1,)),
            pltpu.SemaphoreType.DMA((lats - 1,)),
            pltpu.SemaphoreType.DMA((lats, 2, slots)),
            pltpu.SemaphoreType.DMA((lats, 2, slots)),
            pltpu.VMEM((2,) + moved[2:], BF16),
            pltpu.SemaphoreType.DMA((2,)),
        ],
        compiler_params=pltpu.CompilerParams(
            collective_id=2, has_side_effects=True, vmem_limit_bytes=VMEM
        ),
        name="gather_params",
    )(shard, x, gain, shift)


def scatter_kernel(dates, lats, src, out, sums, others, z_send, z_recv, send, recv):
    d, l = lax.axis_index("date"), lax.axis_index("lat")
    steps = dates.bit_length() - 1
    paths = [order[::-1] for order in orders(dates)]
    parts = pieces(src.shape[2])
    greet(dates, lats, d, l)
    sent, flights, z = [], {}, {}

    def left(p, i):
        return span(paths[p][i + 1 :][::-1])[::-1]

    def slot_of(i, n):
        return sum(1 << (steps - 1 - e) for e in range(i)) + n

    def held(o, p, i, mask):
        if i == 0:
            return src.at[flipped(d, mask), lax.rem(l + o, lats), parts[p]]
        return sums.at[o, slot_of(i - 1, left(p, i - 1).index(mask)), parts[p]]

    def cross(o, p, i, n):
        bit = paths[p][i]
        slot = slot_of(i, n)
        copy = pltpu.make_async_remote_copy(
            src_ref=held(o, p, i, left(p, i)[n] | 1 << bit),
            dst_ref=sums.at[o, slot, parts[p]],
            send_sem=send.at[o, p, slot],
            recv_sem=recv.at[o, p, slot],
            device_id=(flip(d, bit), l),
            device_id_type=MESH,
        )
        copy.start()
        sent.append(copy)
        flights[o, p, i, n] = copy

    def add(o, p, i, n):
        flights[o, p, i, n].wait_recv()
        have = held(o, p, i, left(p, i)[n])
        got = sums.at[o, slot_of(i, n), parts[p]]
        got[...] = (have[...].astype(F32) + got[...].astype(F32)).astype(BF16)
        if i + 1 < steps:
            if n < len(left(p, i + 1)):
                cross(o, p, i + 1, n)
        elif o:
            copy = pltpu.make_async_remote_copy(
                src_ref=got,
                dst_ref=others.at[o - 1, parts[p]],
                send_sem=z_send.at[o - 1, p],
                recv_sem=z_recv.at[o - 1, p],
                device_id=(d, lax.rem(l + o, lats)),
                device_id_type=MESH,
            )
            copy.start()
            sent.append(copy)
            z[o, p] = copy

    turns = list(range(1, lats)) + [0]
    for o in turns:
        for n in range(len(left(0, 0))):
            for p in range(2):
                cross(o, p, 0, n)
    for wave in range(lats + steps - 1):
        for i in range(steps):
            if 0 <= wave - i < lats:
                for n in range(len(left(0, i))):
                    for p in range(2):
                        add(turns[wave - i], p, i, n)
    for p in range(2):
        total = sums[0, slot_of(steps - 1, 0), parts[p]].astype(F32)
        for o in range(1, lats):
            z[o, p].wait_recv()
            total = total + others[o - 1, parts[p]].astype(F32)
        out[parts[p]] = total
    for copy in sent:
        copy.wait_send()


def scatter(packed):
    dates, lats, rows, lanes = packed.shape
    slots = dates - 1
    return pl.pallas_call(
        functools.partial(scatter_kernel, dates, lats),
        in_specs=[pl.BlockSpec(memory_space=pltpu.VMEM)],
        out_specs=pl.BlockSpec(memory_space=pltpu.VMEM),
        out_shape=jax.ShapeDtypeStruct((rows, lanes), F32),
        scratch_shapes=[
            pltpu.VMEM((lats, slots, rows, lanes), BF16),
            pltpu.VMEM((lats - 1, rows, lanes), BF16),
            pltpu.SemaphoreType.DMA((lats - 1, 2)),
            pltpu.SemaphoreType.DMA((lats - 1, 2)),
            pltpu.SemaphoreType.DMA((lats, 2, slots)),
            pltpu.SemaphoreType.DMA((lats, 2, slots)),
        ],
        compiler_params=pltpu.CompilerParams(
            collective_id=1, has_side_effects=True, vmem_limit_bytes=VMEM
        ),
        name="scatter_grads",
    )(packed)


def add_vectors(packed, vectors, lines):
    first, lead = divmod(OFF_G1, LANES)
    count = -(-(lead + vectors.shape[0]) // LANES)
    extra = jnp.pad(vectors, (lead, count * LANES - lead - vectors.shape[0])).reshape(count, LANES)
    done = 0
    while done < count:
        shard, row = divmod(first + done, lines)
        amount = min(count - done, lines - row)
        old = lax.slice(packed, (shard, row, 0), (shard + 1, row + amount, LANES))
        packed = lax.dynamic_update_slice(packed, old + extra[None, done : done + amount], (shard, row, 0))
        done += amount
    return packed


def local(inputs, noise, cotangent, params, psi, step_counts, pixel_mask, offsets, bases):
    samples, steps, rows, width, _ = inputs.shape
    slabs = samples * steps
    dates, lats = lax.axis_size("date"), lax.axis_size("lat")
    lat = rows * lats

    def by_channel(values):
        return jnp.swapaxes(values, 3, 4).reshape(slabs, rows, -1, width)

    def padded(values):
        return jnp.pad(values, ((0, 0), (0, 0), (0, CP - values.shape[2]), (0, WIDE - width)))

    upward = [(i, i + 1) for i in range(lats - 1)]
    downward = [(i + 1, i) for i in range(lats - 1)]
    lines = params.shape[0] // LANES
    held = -(-lines // STEP) * STEP
    shard = jnp.pad(params.reshape(lines, LANES), ((0, held - lines), (0, 0)))
    small = norms(shard, lines, dates, lats)
    shard, inputs, small = lax.optimization_barrier((shard, inputs, small))
    x = padded(jnp.concatenate([by_channel(inputs), by_channel(noise)], axis=2))
    edges = [(x[s, rows - 1 :], x[s, :1]) for s in range(slabs)]
    gathered, moved = gather(shard, x, small[0], small[1], dates, lats, width)
    gathered = gathered.reshape(dates * lats, held, LANES)
    cot = padded(by_channel(cotangent)).reshape(slabs * rows, CP, WIDE)
    active = jnp.arange(steps, dtype=jnp.int32)[None, :] < step_counts[:, None]
    mask = active.reshape(slabs, 1, 1) * pixel_mask[None]
    mask = jnp.pad(mask.astype(F32), ((0, 0), (0, 0), (0, WIDE - width)))
    matrices = unpack(gathered, lines)
    halos, done = [], gathered
    for s in range(slabs):
        top, bottom, done = lax.optimization_barrier((*edges[s], done))
        halos.append((lax.ppermute(top, "lat", upward), lax.ppermute(bottom, "lat", downward)))
        done = halos[-1], matrices
    matrices = done[1]
    basis = ()
    for s in range(slabs):
        basis = (lift(offsets, bases, psi, *halos[s], moved, small[0], small[1], basis, s, lat, width),)
    basis = basis[0]
    w, wt, up, upt, dn, dnt = matrices
    basis = basis.reshape(slabs * rows, BASIS * CP, WIDE)
    output, gconv, gup, gdn, second_sums = block(
        basis, x.reshape(slabs * rows, CP, WIDE), cot, mask.reshape(slabs * rows, 1, WIDE),
        wt, upt, up, dnt, dn, small[2], small[3], width,
    )
    gconv_rows = gconv.reshape(slabs, rows, CP, WIDE)
    own, to_below, to_above = lower(offsets, bases, psi, gconv_rows, w)
    from_below = lax.ppermute(to_above, "lat", upward)
    from_above = lax.ppermute(to_below, "lat", downward)
    gdisco = weight_grad(basis, gconv)
    packed = pack(gdisco, gup, gdn, dates * lats, lines, held)
    grad, first_sums = input_grad(x, gconv_rows, own, from_below, from_above, small[0], width)
    sums = jnp.sum(jnp.concatenate([first_sums, second_sums]), axis=-1)
    vectors = jnp.concatenate([sums[0, :CIN], sums[1, :CIN], sums[2, :C], sums[3, :C]])
    packed = add_vectors(packed, vectors.astype(BF16), lines)
    summed = scatter(packed.reshape(dates, lats, held, LANES))

    def by_pixel(values):
        values = values.reshape(slabs, rows, CP, WIDE)[:, :, :C, :width]
        return jnp.swapaxes(values.reshape(samples, steps, rows, C, width), 3, 4)

    return by_pixel(output), by_pixel(grad), summed[:lines].reshape(-1)


def solution(mesh):
    field = P("date", None, "lat", None, None)
    flat = P(("date", "lat"))
    return jax.shard_map(
        local,
        mesh=mesh,
        in_specs=(field, field, field, flat, P(), P("date"), P("lat", None), P(), P()),
        out_specs=(field, field, flat),
        check_vma=False,
    )
```

```python
import functools
import math

import jax
import jax.numpy as jnp
from jax import lax
from jax.experimental import pallas as pl
from jax.experimental.pallas import tpu as pltpu
from jax.sharding import PartitionSpec as P

C = 641
HID = 1282
BASIS = 4
SUPPORT = 12
REACH = 2
CIN = 649
BF16, F32 = jnp.bfloat16, jnp.float32
MESH = pl.DeviceIdType.MESH
LANES = 128
STEP = 16
CP = 656
HP = 1296
WIDE = 768
HL = 1408
UNROLL = 8
VMEM = 60 << 20


OFF_G1=BASIS*CIN*C+C; OFF_S1=OFF_G1+CIN; OFF_G2=OFF_S1+CIN; OFF_S2=OFF_G2+C; OFF_UP=OFF_S2+C; OFF_DN=OFF_UP+(C+1)*HID;
SMALL=((OFF_G1,CIN),(OFF_S1,CIN),(OFF_G2,C),(OFF_S2,C))
MATS=((0,C,BASIS*CIN+1,128,3),(OFF_UP,HID,C+1,64,2),(OFF_DN,C,HID+1,128,2))
F_ROWS=29952
def lane_ids(): return lax.broadcasted_iota(jnp.int32,(8,LANES),1)
def place(base,cols,period,b):
    start=base+cols*b
    return start//LANES, start%LANES
def unpack_kernel(nrow,pad, g_ref, w_ref,wt_ref,up_ref,upt_ref,dn_ref,dnt_ref,flat,chunks):
    def fill(s,_):
        flat[pl.ds(nrow*s,pad),:]=g_ref[s].astype(F32); return 0
    lax.fori_loop(0,g_ref.shape[0],fill,0)
    lane=lane_ids()
    def split(base,cols,period,groups):
        J=-(-cols//LANES); pitch=period+8; height=pitch*8*groups+8; last=cols-(J-1)*LANES
        def body(b,_):
            row,s=place(base,cols,period,b)
            back=(LANES-s)%LANES
            for g in range(groups):
                rolled=[pltpu.roll(flat[pl.ds(row+641*8*g+j,8,stride=641),:],back,axis=1) for j in range(J+1)]
                for j in range(J):
                    val=jnp.where(lane<LANES-s,rolled[j],rolled[j+1])
                    if j==J-1: val=jnp.where(lane<last,val,0.0)
                    chunks[pl.ds(j*height+8*g*pitch+b,8,stride=pitch),:]=val
            return 0
        lax.fori_loop(0,period,body,0,unroll=8)
        def border(a,_):
            for j in range(J): chunks[pl.ds(j*height+a*pitch-8,8),:]=chunks[pl.ds(j*height+a*pitch,8),:]
            return 0
        lax.fori_loop(1,8*groups,border,0)
        return J,height,period
    def convert(dst,dst_row,src_row,rows,pad_rows,J,height,period):
        full=rows//16
        def piece(j,r): return chunks[pl.ds(j*height+r//period*(period+8)+r%period,8),:]
        def pair(j,r): return jnp.concatenate([piece(j,r),piece(j,r+8)],axis=0)
        def body(m,_):
            for j in range(J):
                dst[pl.ds(pl.multiple_of(dst_row+16*m,16),16),j*LANES:(j+1)*LANES]=pair(j,src_row+16*m).astype(BF16)
            return 0
        lax.fori_loop(0,full,body,0,unroll=4)
        keep=lax.broadcasted_iota(jnp.int32,(16,LANES),0)<rows-16*full
        for m in range(full,pad_rows//16):
            for j in range(J):
                v=jnp.where(keep,pair(j,src_row+16*m),0.0) if m==full else jnp.zeros((16,LANES),F32)
                dst[dst_row+16*m:dst_row+16*m+16,j*LANES:(j+1)*LANES]=v.astype(BF16)
    J,h,p=split(*MATS[0][:2],*MATS[0][3:])
    for k in range(BASIS):
        convert(w_ref,k*CP,k*CIN,CIN+(k==BASIS-1),CP,J,h,p)
    J,h,p=split(*MATS[1][:2],*MATS[1][3:])
    convert(up_ref,0,0,C+1,CP,J,h,p)
    J,h,p=split(*MATS[2][:2],*MATS[2][3:])
    convert(dn_ref,0,0,HID+1,HP,J,h,p)
    wt_ref[...]=w_ref[:,:CP].T
    upt_ref[...]=up_ref[:,:HP].T
    dnt_ref[...]=dn_ref[:,:CP].T
def unpack(gathered,nrow):
    n,pad,_=gathered.shape
    return pl.pallas_call(functools.partial(unpack_kernel,nrow,pad),
        out_shape=(jax.ShapeDtypeStruct((BASIS*CP,WIDE),BF16),jax.ShapeDtypeStruct((CP,BASIS*CP),BF16),
            jax.ShapeDtypeStruct((CP,HL),BF16),jax.ShapeDtypeStruct((HP,CP),BF16),
            jax.ShapeDtypeStruct((HP,WIDE),BF16),jax.ShapeDtypeStruct((CP,HP),BF16)),
        scratch_shapes=[pltpu.VMEM((F_ROWS,LANES),F32),pltpu.VMEM((6*(136*24+8),LANES),F32)],
        compiler_params=pltpu.CompilerParams(vmem_limit_bytes=VMEM),name="unpack")(gathered)
def pack_kernel(nrow,pad,gd_ref,gu_ref,gn_ref,out_ref,flat,chunks):
    lane=lane_ids(); sub=lax.broadcasted_iota(jnp.int32,(8,LANES),0)
    def gather(src,src_row,dst_row,rows,J,height,last,period):
        full=rows//8
        def cols(m,j):
            v=src[pl.ds(pl.multiple_of(src_row+8*m,8),8),j*LANES:(j+1)*LANES]
            return jnp.where(lane<last,v,0.0) if j==J-1 else v
        def body(m,_):
            r=dst_row+8*m; at=r//period*(period+8)+r%period
            for j in range(J):
                v=cols(m,j)
                chunks[pl.ds(j*height+at+8,8),:]=v
                chunks[pl.ds(j*height+at,8),:]=v
            return 0
        lax.fori_loop(0,full,body,0,unroll=4)
        if rows%8:
            r=dst_row+8*full; at=r//period*(period+8)+r%period
            for j in range(J):
                v=jnp.where(sub<rows-8*full,cols(full,j),0.0)
                chunks[pl.ds(j*height+at+8,8),:]=v
                chunks[pl.ds(j*height+at,8),:]=v
    def clear(J,height,row,period):
        row=row//period*(period+8)+row%period
        count=(height-row)//8
        def body(m,_):
            for j in range(J): chunks[pl.ds(j*height+row+8*m,8),:]=jnp.zeros((8,LANES),F32)
            return 0
        lax.fori_loop(0,count,body,0)
    def merge(base,cols,period,groups):
        J=-(-cols//LANES); pitch=period+8; height=pitch*8*groups+8
        def body(b,tails,rows=J):
            row,s=place(base,cols,period,b)
            new=[]
            for g in range(groups):
                x=[pltpu.roll(chunks[pl.ds(j*height+8*g*pitch+b,8,stride=pitch),:],s,axis=1) for j in range(J)]
                first=lane>=s
                for j in range(J):
                    v=jnp.where(first,x[j],tails[g] if j==0 else x[j-1])
                    if j<rows: flat[pl.ds(row+641*8*g+j,8,stride=641),:]=v
                new.append(jnp.where(s==LANES-1,jnp.where(first,0.0,x[J-1]),v))
            return tuple(new)
        row0=base//LANES
        init=[jnp.zeros((8,LANES),F32)]*groups
        if base%LANES:
            init[0]=jnp.where(sub==0,flat[row0:row0+8,:],0.0)
        tails=lax.fori_loop(0,period-8,body,tuple(init),unroll=8)
        for b in range(period-8,period):
            tails=body(b,tails,J-1 if base%LANES and b==period-1 else J)
        if base%LANES:
            for g in range(groups):
                at=pl.ds(row0+641*(8*g+1),8,stride=641)
                flat[at,:]=flat[at,:]+tails[g]
    h=136*24+8
    for k in range(BASIS): gather(gd_ref,k*CP,k*CIN,CIN+(k==BASIS-1),6,h,1,128)
    clear(6,h,2600,128)
    merge(0,C,128,3)
    h=72*16+8
    gather(gu_ref,0,0,C+1,11,h,2,64)
    clear(11,h,648,64)
    merge(OFF_UP,HID,64,2)
    h=136*16+8
    gather(gn_ref,0,0,HID+1,6,h,1,128)
    clear(6,h,1288,128)
    merge(OFF_DN,C,128,2)
    def store(s,_):
        out_ref[s]=flat[pl.ds(nrow*s,pad),:].astype(BF16); return 0
    lax.fori_loop(0,out_ref.shape[0],store,0)
def pack(gd,gu,gn,n,nrow,pad):
    return pl.pallas_call(functools.partial(pack_kernel,nrow,pad),
        out_shape=jax.ShapeDtypeStruct((n,pad,LANES),BF16),
        scratch_shapes=[pltpu.VMEM((F_ROWS,LANES),F32),pltpu.VMEM((6*(136*24+8),LANES),F32)],
        compiler_params=pltpu.CompilerParams(vmem_limit_bytes=VMEM),name="pack")(gd,gu,gn)


def tiled(column):
    return jnp.concatenate([column] * (WIDE // LANES), axis=1)


def lane_of(rows, start=0):
    return lax.broadcasted_iota(jnp.int32, (rows, LANES), 1) + start


def wrapped(chunk, width):
    head, first, last = chunk[:, : WIDE - LANES], chunk[:, :LANES], chunk[:, WIDE - LANES :]
    edge = width - (WIDE - LANES)
    lane = lane_of(chunk.shape[0])
    beyond = jnp.where(
        lane < LANES - REACH, pltpu.roll(first, edge, axis=1), pltpu.roll(last, LANES - edge, axis=1)
    )
    return jnp.concatenate([head, jnp.where(lane < edge, last, beyond)], axis=1)


def cut(chunk, width):
    head, last = chunk[:, : WIDE - LANES], chunk[:, WIDE - LANES :]
    keep = lane_of(chunk.shape[0], WIDE - LANES) < width
    return jnp.concatenate([head, jnp.where(keep, last, 0.0)], axis=1)


def rows_below(count):
    return lax.broadcasted_iota(jnp.int32, (STEP, WIDE), 0) < count


def halves(chunk):
    return chunk[:8] + chunk[8:]


def column_sums(read, channels, count):
    whole = channels // STEP

    def body(m, sums):
        return tuple(a + halves(v) for a, v in zip(sums, read(m)))

    sums = lax.fori_loop(
        0, whole, body, tuple(jnp.zeros((8, WIDE), F32) for _ in range(count)), unroll=UNROLL
    )
    keep = rows_below(channels - whole * STEP)
    sums = [a + halves(jnp.where(keep, v, 0.0)) for a, v in zip(sums, read(whole))]
    return [jnp.sum(a, axis=0, keepdims=True) for a in sums]


def norm_stats(read, channels):
    (total,) = column_sums(lambda m: (read(m),), channels, 1)
    mean = total * (1.0 / channels)

    def squares(m):
        centered = read(m) - mean
        return (centered * centered,)

    (total,) = column_sums(squares, channels, 1)
    return mean, lax.rsqrt(total * (1.0 / channels) + 1e-05)


def each_chunk(body, unroll=None):
    def step(m, _):
        body(m, pl.ds(pl.multiple_of(m * STEP, STEP), STEP))
        return 0

    lax.fori_loop(0, CP // STEP, step, 0, unroll=unroll)


def spread(source, gain, shift, width, moved):
    def read(c):
        return source[pl.ds(pl.multiple_of(c * STEP, STEP), STEP), :].astype(F32)

    mean, scale = norm_stats(read, CIN)

    def shifts(c, at):
        values = (read(c) - mean) * scale * tiled(gain[at, :]) + tiled(shift[at, :])
        values = wrapped(values, width).astype(BF16)
        for d in range(-REACH, REACH + 1):
            moved[d + REACH, at, :] = pltpu.roll(values, -d % WIDE, axis=1) if d else values

    each_chunk(shifts, 4)


def lift_kernel(
    rows, slab, lat, width, offsets, bases, psi, lo, hi, own, gain, shift, *refs
):
    out, moved, table, sems = refs[-4:]
    first_row = lax.axis_index("lat") * rows
    copies = [
        pltpu.make_async_copy(own.at[slab, r], moved.at[r + 1], sems.at[r]) for r in range(rows)
    ]
    for copy in copies:
        copy.start()
    for k in range(BASIS):
        table[SUPPORT + k] = 0
    for p in range(SUPPORT):
        k = bases[p]
        used = table[SUPPORT + k]
        table[k * 3 + used] = p
        table[SUPPORT + k] = used + 1
    for source, m in ((lo, 0), (hi, rows + 1)):
        spread(source.at[0], gain, shift, width, moved.at[m])
    for copy in copies:
        copy.wait()
    for r in range(rows):
        for k in range(BASIS):
            parts = []
            for q in range(3):
                p = table[k * 3 + q]
                row = first_row + r + offsets[p, 0]
                inside = jnp.logical_and(row >= 0, row < lat)
                weight = jnp.where(inside, psi[first_row + r, p], 0.0)
                parts.append((weight, r + 1 + offsets[p, 0], offsets[p, 1] + REACH))

            def combine(c, at):
                total = None
                for weight, row, d in parts:
                    term = weight * moved[row, d, at, :].astype(F32)
                    total = term if total is None else total + term
                to = pl.ds(pl.multiple_of(k * CP + c * STEP, STEP), STEP)
                out[0, r, to, :] = cut(total, width).astype(BF16)

            each_chunk(combine, 4)
        last = slice(BASIS * CP - STEP, BASIS * CP)
        bias_row = CIN - (CP - STEP)
        sub = lax.broadcasted_iota(jnp.int32, (STEP, WIDE), 0)
        lane = lax.broadcasted_iota(jnp.int32, (STEP, WIDE), 1)
        ones = jnp.where(lane < width, 1.0, 0.0)
        out[0, r, last, :] = jnp.where(sub == bias_row, ones, out[0, r, last, :].astype(F32)).astype(BF16)


def lift(offsets, bases, psi, lo, hi, own, gain, shift, before, slab, lat, width):
    slabs, rows = own.shape[:2]
    smem = pl.BlockSpec(memory_space=pltpu.SMEM)
    anywhere = pl.BlockSpec(memory_space=pl.ANY)
    halo = pl.BlockSpec((1, CP, WIDE), lambda s: (0, 0, 0))
    column = pl.BlockSpec((CP, LANES), lambda s: (0, 0))
    return pl.pallas_call(
        functools.partial(lift_kernel, rows, slab, lat, width),
        grid=(1,),
        in_specs=[smem, smem, smem, halo, halo, anywhere, column, column] + [anywhere] * len(before),
        out_specs=pl.BlockSpec((1, rows, BASIS * CP, WIDE), lambda s: (slab, 0, 0, 0)),
        out_shape=jax.ShapeDtypeStruct((slabs, rows, BASIS * CP, WIDE), BF16),
        scratch_shapes=[
            pltpu.VMEM((rows + 2, 2 * REACH + 1, CP, WIDE), BF16),
            pltpu.SMEM((SUPPORT + BASIS,), jnp.int32),
            pltpu.SemaphoreType.DMA((rows,)),
        ],
        input_output_aliases={8: 0} if before else {},
        compiler_params=pltpu.CompilerParams(vmem_limit_bytes=VMEM),
        cost_estimate=pl.CostEstimate(flops=40 << 20, bytes_accessed=40 << 20, transcendentals=0),
        name="lift",
    )(offsets, bases, psi, lo, hi, own, gain, shift, *before)


GELU_A = math.sqrt(2.0 / math.pi)
GELU_B = 0.044715


TILE = 256


def weave(*lists):
    order = []
    for which, steps in enumerate(lists):
        for n, step in enumerate(steps):
            order.append(((n + 0.5) / len(steps), which, n, step))
    for _, _, _, step in sorted(order, key=lambda entry: entry[:3]):
        step()


class Job:
    def __init__(self, buffers, weights, totals, mask):
        self.basis, self.x, self.cot, self.out, self.gconv = buffers[:5]
        self.res, self.second, self.pre, self.act, self.mid, self.gact, self.gb, self.gpre = buffers[5:]
        self.wt, self.upt, self.up, self.dnt, self.dn, self.gain, self.shift = weights
        self.gup, self.gdn, self.sums = totals
        self.mask = mask

    @staticmethod
    def at(c):
        return slice(c * STEP, (c + 1) * STEP)

    @staticmethod
    def wide(column):
        return jnp.concatenate([column] * (TILE // LANES), axis=1)

    @staticmethod
    def only(c, values, channels, other=0.0):
        if (c + 1) * STEP <= channels:
            return values
        row = lax.broadcasted_iota(jnp.int32, (STEP, TILE), 0)
        return jnp.where(row < channels - c * STEP, values, other)

    def product(self, out, left, right, count):
        rows = left.shape[0]
        size = -(-rows // (count * STEP)) * STEP

        def step(start):
            at = slice(start, min(start + size, rows))
            values = left[at, : right.shape[0]]
            out[at, :] = jnp.dot(values, right[...], preferred_element_type=F32)

        return [functools.partial(step, start) for start in range(0, rows, size)]

    def outer(self, out, left, right, count):
        rows = left.shape[0]
        size = -(-rows // (count * STEP)) * STEP

        def step(start):
            at = slice(start, min(start + size, rows))
            term = lax.dot_general(
                left[at, :], right[...], (((1,), (1,)), ((), ())), preferred_element_type=F32
            )
            out[at, : right.shape[0]] += term

        return [functools.partial(step, start) for start in range(0, rows, size)]

    def m1(self):
        return self.product(self.res, self.wt, self.basis, 4)

    def v1(self):
        state = {"sum": jnp.zeros((8, TILE), F32), "square": jnp.zeros((8, TILE), F32)}
        mask = self.mask()

        def add(c):
            at = self.at(c)
            value = self.res[at, :] + self.only(c, self.x[at, :].astype(F32), C)
            self.res[at, :] = value
            self.gb[at, :] = (self.cot[at, :].astype(F32) * mask).astype(BF16)
            state["sum"] = state["sum"] + halves(self.only(c, value, C))

        def mean():
            self.mean = jnp.sum(state["sum"], axis=0, keepdims=True) * (1.0 / C)

        def square(c):
            value = self.res[self.at(c), :] - self.mean
            state["square"] = state["square"] + halves(self.only(c, value * value, C))

        def scale():
            total = jnp.sum(state["square"], axis=0, keepdims=True)
            self.scale = lax.rsqrt(total * (1.0 / C) + 1e-05)

        def normalize(c):
            at = self.at(c)
            value = (self.res[at, :] - self.mean) * self.scale
            value = value * self.wide(self.gain[at, :]) + self.wide(self.shift[at, :])
            row = lax.broadcasted_iota(jnp.int32, (STEP, TILE), 0)
            if c == C // STEP:
                value = jnp.where(row == C % STEP, 1.0, value)
            self.second[at, :] = value.astype(BF16)

        chunks = range(CP // STEP)
        steps = [functools.partial(add, c) for c in chunks] + [mean]
        steps += [functools.partial(square, c) for c in chunks] + [scale]
        return steps + [functools.partial(normalize, c) for c in chunks]

    def m2(self):
        return self.product(self.pre, self.upt, self.second, 9)

    def v2(self):
        def gelu(c):
            at = self.at(c)
            v = self.pre[at, :]
            square = v * v
            bend = jnp.tanh(GELU_A * v * (1.0 + GELU_B * square))
            half = 0.5 * (1.0 + bend)
            value = v * half
            if c == HID // STEP:
                row = lax.broadcasted_iota(jnp.int32, (STEP, TILE), 0)
                value = jnp.where(row == HID % STEP, 1.0, value)
            self.act[at, :] = value.astype(BF16)
            rise = GELU_A * (1.0 + 3.0 * GELU_B * square)
            self.pre[at, :] = half + 0.5 * v * (1.0 - bend * bend) * rise

        return [functools.partial(gelu, c) for c in range(HP // STEP)]

    def m3(self):
        back = self.product(self.gact, self.dn, self.gb, 9)
        return self.product(self.mid, self.dnt, self.act, 4) + back

    def v3(self):
        def finish(c):
            at = self.at(c)
            self.out[at, :] = (self.res[at, :] + self.mid[at, :]).astype(BF16)

        def back(c):
            at = self.at(c)
            self.gpre[at, :] = (self.gact[at, :] * self.pre[at, :]).astype(BF16)

        steps = [functools.partial(finish, c) for c in range(CP // STEP)]
        return steps + [functools.partial(back, c) for c in range(HP // STEP)]

    def m4(self):
        return self.product(self.mid, self.up, self.gpre, 4)

    def v4(self):
        state = {"flat": jnp.zeros((8, TILE), F32), "along": jnp.zeros((8, TILE), F32)}

        def terms(c):
            at = self.at(c)
            dm = self.mid[at, :]
            xhat = (self.res[at, :] - self.mean) * self.scale
            return dm, xhat, dm * self.wide(self.gain[at, :])

        def means(c):
            _, xhat, g = terms(c)
            g = self.only(c, g, C)
            state["flat"] = state["flat"] + halves(g)
            state["along"] = state["along"] + halves(g * xhat)

        def join():
            for name in state:
                state[name] = jnp.sum(state[name], axis=0, keepdims=True) * (1.0 / C)

        def backward(c):
            at = self.at(c)
            dm, xhat, g = terms(c)
            value = g - state["flat"] - xhat * state["along"]
            value = self.gb[at, :].astype(F32) + self.scale * value
            self.gconv[at, :] = self.only(c, value, C).astype(BF16)
            for n, term in enumerate((dm * xhat, dm)):
                self.sums[n, at, :] += term[:, :LANES] + term[:, LANES:]

        chunks = range(CP // STEP)
        steps = [functools.partial(means, c) for c in chunks] + [join]
        return steps + [functools.partial(backward, c) for c in chunks]

    def m5(self):
        first = self.outer(self.gdn, self.act, self.gb, 3)
        return first + self.outer(self.gup, self.second, self.gpre, 2)


def block_kernel(
    basis, x, cot, mask, wt, upt, up, dnt, dn, gain, shift, out, gconv, gup, gdn, sums, *scratch
):
    count = basis.shape[0]
    tiles = WIDE // TILE
    in_sems, out_sems = scratch[-2:]
    per_job = (len(scratch) - 2) // 2
    sets = [scratch[:per_job], scratch[per_job : 2 * per_job]]
    for total in (gup, gdn, sums):
        total[...] = jnp.zeros_like(total)

    def place(i, j):
        return i // tiles * 2 + j, pl.ds(pl.multiple_of(i % tiles * TILE, TILE), TILE)

    def arrive(i, j):
        row, lanes = place(i, j)
        return [
            pltpu.make_async_copy(source.at[row, :, lanes], sets[j][n], in_sems.at[j, n])
            for n, source in enumerate((basis, x, cot))
        ]

    def leave(i, j):
        row, lanes = place(i, j)
        return [
            pltpu.make_async_copy(sets[j][3 + n], target.at[row, :, lanes], out_sems.at[j, n])
            for n, target in enumerate((out, gconv))
        ]

    last = count // 2 * tiles - 1
    for j in range(2):
        for copy in arrive(0, j):
            copy.start()

    def pair(i, _):
        def row_mask(j):
            row, lanes = place(i, j)
            return lambda: mask[row, :, lanes]

        weights, totals = (wt, upt, up, dnt, dn, gain, shift), (gup, gdn, sums)
        a, b = (Job(sets[j], weights, totals, row_mask(j)) for j in range(2))
        after = jnp.minimum(i + 1, last)
        coming = [arrive(after, j) for j in range(2)]
        leaving = [leave(i, j) for j in range(2)]
        for j in range(2):
            for copy in arrive(i, j):
                copy.wait()
        weave(a.m1())
        coming[0][0].start()
        weave(a.v1(), b.m1())
        coming[1][0].start()
        for n in (1, 2):
            coming[0][n].start()
        weave(a.m2(), b.v1())
        for n in (1, 2):
            coming[1][n].start()
        weave(a.v2(), b.m2())
        weave(a.m3(), b.v2())
        weave(a.v3(), b.m3())
        leaving[0][0].start()
        weave(a.m4(), b.v3())
        leaving[1][0].start()
        weave(a.v4(), b.m4())
        leaving[0][1].start()
        weave(a.m5(), b.v4())
        leaving[1][1].start()
        weave(b.m5())
        for copies in leaving:
            for copy in copies:
                copy.wait()
        return 0

    lax.fori_loop(0, last + 1, pair, 0)
    for j in range(2):
        for copy in arrive(last, j):
            copy.wait()


def block(basis, x, cot, mask, wt, upt, up, dnt, dn, gain, shift):
    count = x.shape[0]
    anywhere = pl.BlockSpec(memory_space=pl.ANY)
    held = pl.BlockSpec(memory_space=pltpu.VMEM)
    low, high = pltpu.VMEM((CP, TILE), BF16), pltpu.VMEM((CP, TILE), F32)
    hidden_low, hidden_high = pltpu.VMEM((HP, TILE), BF16), pltpu.VMEM((HP, TILE), F32)
    per_job = [pltpu.VMEM((BASIS * CP, TILE), BF16), low, low, low, low]
    per_job += [high, low, hidden_high, hidden_low, high, hidden_high, low, hidden_low]
    return pl.pallas_call(
        block_kernel,
        in_specs=[anywhere] * 3 + [held] * 8,
        out_specs=[anywhere] * 2 + [held] * 3,
        out_shape=(
            jax.ShapeDtypeStruct((count, CP, WIDE), BF16),
            jax.ShapeDtypeStruct((count, CP, WIDE), BF16),
            jax.ShapeDtypeStruct((CP, HL), F32),
            jax.ShapeDtypeStruct((HP, WIDE), F32),
            jax.ShapeDtypeStruct((2, CP, LANES), F32),
        ),
        scratch_shapes=per_job * 2 + [pltpu.SemaphoreType.DMA((2, 3)), pltpu.SemaphoreType.DMA((2, 2))],
        compiler_params=pltpu.CompilerParams(vmem_limit_bytes=VMEM),
        name="block",
    )(basis, x, cot, mask, wt, upt, up, dnt, dn, gain, shift)


def along_lanes(ref, at, values):
    total = values[:, :LANES]
    for j in range(1, WIDE // LANES):
        total = total + values[:, j * LANES : (j + 1) * LANES]
    ref[at, :] = ref[at, :] + total


def outer_kernel(basis, gconv, out):
    i = pl.program_id(0)
    term = lax.dot_general(basis[0], gconv[0], (((1,), (1,)), ((), ())), preferred_element_type=F32)

    @pl.when(i == 0)
    def _():
        out[:, :CP] = term

    @pl.when(i > 0)
    def _():
        out[:, :CP] += term


def weight_grad(basis, gconv):
    count = basis.shape[0]
    return pl.pallas_call(
        outer_kernel,
        grid=(count,),
        in_specs=[
            pl.BlockSpec((1, BASIS * CP, WIDE), lambda i: (i, 0, 0)),
            pl.BlockSpec((1, CP, WIDE), lambda i: (i, 0, 0)),
        ],
        out_specs=pl.BlockSpec((BASIS * CP, WIDE), lambda i: (0, 0)),
        out_shape=jax.ShapeDtypeStruct((BASIS * CP, WIDE), F32),
        compiler_params=pltpu.CompilerParams(vmem_limit_bytes=VMEM),
        name="weight_grad",
    )(basis, gconv)


GROUP = 11 * STEP
GROUP_STEP = 10 * STEP


def lower_kernel(rows, width, offsets, bases, psi, gconv, w, own, lo, hi, *scratch):
    place, coef, in_sems, w_sems, out_sems = scratch[-5:]
    per_slab = (len(scratch) - 5) // 2
    sets = [scratch[:per_slab], scratch[per_slab : 2 * per_slab]]
    first_row = lax.axis_index("lat") * rows
    span = 2 * REACH + 1
    groups = 1 + (CP - GROUP) // GROUP_STEP
    for n in range(3 * span):
        place[n] = 0
        for r in range(rows):
            coef[r, n] = 0.0
    for p in range(SUPPORT):
        n = (offsets[p, 0] + 1) * span + offsets[p, 1] + REACH
        place[n] = bases[p]
        for r in range(rows):
            coef[r, n] = psi[first_row + r, p]

    def channels(g):
        return pl.ds(pl.multiple_of(g * GROUP_STEP, STEP), GROUP)

    def weights(j, g):
        return pltpu.make_async_copy(w.at[:, channels(g), :], sets[j][1], w_sems.at[j])

    def products(j):
        ring, part, lifted = sets[j][:3]

        def step(r, k):
            values = jnp.dot(part[k, :, :CP], ring[r], preferred_element_type=F32)
            lifted[r, k] = values.astype(BF16)

        return [functools.partial(step, r, k) for r in range(rows) for k in range(BASIS)]

    def gathers(j):
        lifted, inner, below, above = sets[j][2:]

        def step(c, target):
            at = slice(c * STEP, (c + 1) * STEP)
            total = None
            for d in range(-REACH, REACH + 1):
                part = None
                for o in (-1, 0, 1):
                    r = target - o
                    if 0 <= r < rows:
                        n = (o + 1) * span + d + REACH
                        term = coef[r, n] * lifted[r, place[n], at, :].astype(F32)
                        part = term if part is None else part + term
                if d:
                    part = pltpu.roll(part.astype(BF16), d % WIDE, axis=1).astype(F32)
                total = part if total is None else total + part
            if target < 0:
                below[at, :] = total.astype(BF16)
            elif target == rows:
                above[at, :] = total.astype(BF16)
            else:
                inner[target, at, :] = total

        return [functools.partial(step, c, t) for c in range(GROUP // STEP) for t in range(-1, rows + 1)]

    def pair_of_slabs(both, _):
        def leaving(j, g):
            slab = both * 2 + j
            targets = (own.at[slab, :, channels(g), :], lo.at[slab, channels(g), :], hi.at[slab, channels(g), :])
            return [
                pltpu.make_async_copy(sets[j][3 + n], target, out_sems.at[j, n])
                for n, target in enumerate(targets)
            ]

        rings = [pltpu.make_async_copy(gconv.at[both * 2 + j], sets[j][0], in_sems.at[j]) for j in range(2)]
        for j in range(2):
            rings[j].start()
            weights(j, 0).start()
        for j in range(2):
            rings[j].wait()
            ring = sets[j][0]
            edge = width - (WIDE - LANES)
            lane = lane_of(CP)
            for r in range(rows):
                first, last = ring[r, :, :LANES].astype(F32), ring[r, :, WIDE - LANES :].astype(F32)
                beyond = jnp.where(
                    lane < LANES - REACH,
                    pltpu.roll(first, edge, axis=1),
                    pltpu.roll(last, LANES - edge, axis=1),
                )
                ring[r, :, WIDE - LANES :] = jnp.where(lane < edge, last, beyond).astype(BF16)
        weights(0, 0).wait()
        weave(products(0))
        weights(0, min(1, groups - 1)).start()

        def group(g, _):
            after, later = jnp.minimum(g + 1, groups - 1), jnp.minimum(g + 2, groups - 1)
            def free(j):
                @pl.when(g > 0)
                def _():
                    for copy in leaving(j, jnp.maximum(g - 1, 0)):
                        copy.wait()

            weights(1, g).wait()
            free(0)
            weave(products(1), gathers(0))
            weights(1, after).start()
            for copy in leaving(0, g):
                copy.start()
            weights(0, after).wait()
            free(1)
            weave(products(0), gathers(1))
            weights(0, later).start()
            for copy in leaving(1, g):
                copy.start()
            return 0

        lax.fori_loop(0, groups, group, 0)
        for j in range(2):
            weights(j, groups - 1).wait()
            for copy in leaving(j, groups - 1):
                copy.wait()
        return 0

    lax.fori_loop(0, gconv.shape[0] // 2, pair_of_slabs, 0)


def lower(offsets, bases, psi, gconv, w, width):
    slabs, rows = gconv.shape[:2]
    smem = pl.BlockSpec(memory_space=pltpu.SMEM)
    anywhere = pl.BlockSpec(memory_space=pl.ANY)
    edge = jax.ShapeDtypeStruct((slabs, CP, WIDE), BF16)
    per_slab = [
        pltpu.VMEM((rows, CP, WIDE), BF16),
        pltpu.VMEM((BASIS, GROUP, WIDE), BF16),
        pltpu.VMEM((rows, BASIS, GROUP, WIDE), BF16),
        pltpu.VMEM((rows, GROUP, WIDE), F32),
        pltpu.VMEM((GROUP, WIDE), BF16),
        pltpu.VMEM((GROUP, WIDE), BF16),
    ]
    return pl.pallas_call(
        functools.partial(lower_kernel, rows, width),
        in_specs=[smem, smem, smem, anywhere, anywhere],
        out_specs=[anywhere] * 3,
        out_shape=(jax.ShapeDtypeStruct((slabs, rows, CP, WIDE), F32), edge, edge),
        scratch_shapes=per_slab * 2
        + [
            pltpu.SMEM((3 * (2 * REACH + 1),), jnp.int32),
            pltpu.SMEM((rows, 3 * (2 * REACH + 1)), F32),
            pltpu.SemaphoreType.DMA((2,)),
            pltpu.SemaphoreType.DMA((2,)),
            pltpu.SemaphoreType.DMA((2, 3)),
        ],
        compiler_params=pltpu.CompilerParams(vmem_limit_bytes=VMEM),
        name="lower",
    )(offsets, bases, psi, gconv, w.reshape(BASIS, CP, WIDE))


def input_kernel(rows, width, x, gconv, own, lo, hi, gain, out, sums, total):
    r = pl.program_id(1)

    @pl.when(jnp.logical_and(pl.program_id(0) == 0, r == 0))
    def _():
        sums[...] = jnp.zeros_like(sums)

    from_below = jnp.where(r == 0, 1.0, 0.0)
    from_above = jnp.where(r == rows - 1, 1.0, 0.0)

    def read(c):
        return x[0, 0, pl.ds(pl.multiple_of(c * STEP, STEP), STEP), :].astype(F32)

    mean, scale = norm_stats(read, CIN)

    def join(c, at):
        halo = lo[0, at, :].astype(F32) * from_below + hi[0, at, :].astype(F32) * from_above
        total[at, :] = own[0, 0, at, :] + halo

    each_chunk(join, 4)

    def means(c):
        at = pl.ds(pl.multiple_of(c * STEP, STEP), STEP)
        g = total[at, :] * tiled(gain[at, :])
        return g, g * ((read(c) - mean) * scale)

    flat, along = [v * (1.0 / CIN) for v in column_sums(means, CIN, 2)]

    def backward(c, at):
        dm = cut(total[at, :], width)
        xhat = (read(c) - mean) * scale
        g = dm * tiled(gain[at, :])
        value = scale * (g - flat - xhat * along) + gconv[0, 0, at, :].astype(F32)
        out[0, 0, at, :] = value.astype(BF16)
        along_lanes(sums.at[0], at, dm * xhat)
        along_lanes(sums.at[1], at, dm)

    each_chunk(backward, 8)


def input_grad(x, gconv, own, lo, hi, gain, width):
    slabs, rows = x.shape[:2]
    per_row = pl.BlockSpec((1, 1, CP, WIDE), lambda s, r: (s, r, 0, 0))
    halo = pl.BlockSpec((1, CP, WIDE), lambda s, r: (s, 0, 0))
    return pl.pallas_call(
        functools.partial(input_kernel, rows, width),
        grid=(slabs, rows),
        in_specs=[per_row, per_row, per_row, halo, halo, pl.BlockSpec((CP, LANES), lambda s, r: (0, 0))],
        out_specs=[per_row, pl.BlockSpec((2, CP, LANES), lambda s, r: (0, 0, 0))],
        out_shape=(
            jax.ShapeDtypeStruct((slabs, rows, CP, WIDE), BF16),
            jax.ShapeDtypeStruct((2, CP, LANES), F32),
        ),
        scratch_shapes=[pltpu.VMEM((CP, WIDE), F32)],
        compiler_params=pltpu.CompilerParams(vmem_limit_bytes=VMEM),
        name="input_grad",
    )(x, gconv, own, lo, hi, gain)


def flip(value, bit):
    return value + (1 - 2 * ((value // (1 << bit)) % 2)) * (1 << bit)


def flipped(value, mask):
    bit = 0
    while mask >> bit:
        if mask >> bit & 1:
            value = flip(value, bit)
        bit += 1
    return value


def span(bits):
    masks = [0]
    for b in bits:
        masks = masks + [m | 1 << b for m in masks]
    return masks


def orders(dates):
    bits = list(range(1, dates.bit_length() - 1))
    return bits + [0], bits[::-1] + [0]


def pieces(rows):
    cut = rows // (2 * STEP) * STEP
    return pl.ds(0, cut), pl.ds(cut, rows - cut)


def greet(dates, lats, d, l):
    barrier = pltpu.get_barrier_semaphore()
    count = 0
    for o in range(1, lats):
        pl.semaphore_signal(barrier, inc=1, device_id=(d, lax.rem(l + o, lats)), device_id_type=MESH)
        count += 1
    for b in range(dates.bit_length() - 1):
        pl.semaphore_signal(barrier, inc=1, device_id=(flip(d, b), l), device_id_type=MESH)
        count += 1
    pl.semaphore_wait(barrier, count)


def norms_kernel(dates, lats, owner, first, src, out, landed, local_sem, send, recv):
    d, l = lax.axis_index("date"), lax.axis_index("lat")
    mine = jnp.logical_and(d == owner[0], l == owner[1])
    barrier = pltpu.get_barrier_semaphore()
    others = [(a, b) for a in range(dates) for b in range(lats) if (a, b) != owner]

    def copy_to(n):
        return pltpu.make_async_remote_copy(
            src_ref=src,
            dst_ref=landed,
            send_sem=send.at[n],
            recv_sem=recv,
            device_id=others[n],
            device_id_type=MESH,
        )

    @pl.when(mine)
    def _():
        pl.semaphore_wait(barrier, len(others))
        copies = [copy_to(n) for n in range(len(others))]
        for copy in copies:
            copy.start()
        own = pltpu.make_async_copy(src, landed, local_sem)
        own.start()
        own.wait()
        for copy in copies:
            copy.wait_send()

    @pl.when(jnp.logical_not(mine))
    def _():
        pl.semaphore_signal(barrier, inc=1, device_id=owner, device_id_type=MESH)
        copy_to(0).wait_recv()

    lane = lane_ids()
    sub = lax.broadcasted_iota(jnp.int32, (8, LANES), 0)
    lines = landed[...].astype(F32)
    for i, (off, n) in enumerate(SMALL):
        row, s = divmod(off - first * LANES, LANES)
        r = pltpu.roll(lines[row : row + 8], (LANES - s) % LANES, axis=1)
        v = jnp.where(lane < LANES - s, r, pltpu.roll(r, 7, axis=0))
        t = jnp.where(sub * LANES + lane < n, v, 0.0).T
        for j in range(6):
            rows = min(LANES, CP - j * LANES)
            out[i, j * LANES : j * LANES + rows, :] = jnp.broadcast_to(t[:rows, j : j + 1], (rows, LANES))


def norms(shard, lines, dates, lats):
    start, end = OFF_G1 // LANES, (OFF_UP - 1) // LANES + 3
    owner = start // lines
    row = (start - owner * lines) // STEP * STEP
    count = -(-(end - owner * lines - row) // STEP) * STEP
    assert row + count <= shard.shape[0]
    return pl.pallas_call(
        functools.partial(norms_kernel, dates, lats, divmod(owner, lats), owner * lines + row),
        in_specs=[pl.BlockSpec(memory_space=pltpu.VMEM)],
        out_specs=pl.BlockSpec(memory_space=pltpu.VMEM),
        out_shape=jax.ShapeDtypeStruct((4, CP, LANES), F32),
        scratch_shapes=[
            pltpu.VMEM((count, LANES), BF16),
            pltpu.SemaphoreType.DMA(()),
            pltpu.SemaphoreType.DMA((dates * lats - 1,)),
            pltpu.SemaphoreType.DMA(()),
        ],
        compiler_params=pltpu.CompilerParams(
            collective_id=0, has_side_effects=True, vmem_limit_bytes=VMEM
        ),
        name="norms",
    )(lax.slice_in_dim(shard, row, row + count, axis=0))


def gather_kernel(
    dates, lats, width, src, x, gain, shift, out, moved, local_sem, z_send, z_recv, send, recv, buffers, buffer_sems
):
    d, l = lax.axis_index("date"), lax.axis_index("lat")
    steps = dates.bit_length() - 1
    parts = pieces(src.shape[0])
    greet(dates, lats, d, l)
    own = pltpu.make_async_copy(src, out.at[d, l], local_sem)
    own.start()
    sent, arriving, flights = [], {}, {}

    def along(o):
        copy = pltpu.make_async_remote_copy(
            src_ref=src,
            dst_ref=out.at[d, l],
            send_sem=z_send.at[o - 1],
            recv_sem=z_recv.at[o - 1],
            device_id=(d, lax.rem(l + o, lats)),
            device_id_type=MESH,
        )
        copy.start()
        sent.append(copy)
        arriving[o] = copy

    def cross(o, p, i, n):
        order = orders(dates)[p]
        block = out.at[flipped(d, span(order[:i])[n]), lax.rem(l - o + lats, lats), parts[p]]
        slot = (1 << i) - 1 + n
        copy = pltpu.make_async_remote_copy(
            src_ref=src.at[parts[p]] if o == 0 and n == 0 else block,
            dst_ref=block,
            send_sem=send.at[o, p, slot],
            recv_sem=recv.at[o, p, slot],
            device_id=(flip(d, order[i]), l),
            device_id_type=MESH,
        )
        copy.start()
        sent.append(copy)
        flights[o, p, i, n] = copy

    rows = [(s, r) for s in range(x.shape[0]) for r in range(x.shape[1])]
    saves = []

    def spread_rows():
        for n, (s, r) in enumerate(rows):
            if n >= 2:
                saves[n - 2].wait()
            spread(x.at[s, r], gain, shift, width, buffers.at[n % 2])
            save = pltpu.make_async_copy(buffers.at[n % 2], moved.at[s, r], buffer_sems.at[n % 2])
            save.start()
            saves.append(save)
            yield

    aside = spread_rows()
    for wave in range(lats + steps):
        if wave < lats:
            if wave:
                arriving[wave].wait_recv()
            if wave + 1 < lats:
                along(wave + 1)
            for i in range(steps):
                for p in range(2):
                    cross(wave, p, i, 0)
        next(aside, None)
        for i in range(steps)[::-1]:
            o = wave - 1 - i
            if 0 <= o < lats:
                for n in range(1 << i):
                    for p in range(2):
                        flights[o, p, i, n].wait_recv()
                        for later in range(i + 1, steps):
                            cross(o, p, later, n + (1 << i))
    for _ in aside:
        pass
    for save in saves[-2:]:
        save.wait()
    own.wait()
    for copy in sent:
        copy.wait_send()


def gather(shard, x, gain, shift, dates, lats, width):
    slots = dates - 1
    moved = x.shape[:2] + (2 * REACH + 1,) + x.shape[2:]
    anywhere = pl.BlockSpec(memory_space=pl.ANY)
    return pl.pallas_call(
        functools.partial(gather_kernel, dates, lats, width),
        in_specs=[anywhere] + [pl.BlockSpec(memory_space=pltpu.VMEM)] * 3,
        out_specs=[anywhere, anywhere],
        out_shape=(
            jax.ShapeDtypeStruct((dates, lats) + shard.shape, shard.dtype),
            jax.ShapeDtypeStruct(moved, BF16),
        ),
        scratch_shapes=[
            pltpu.SemaphoreType.DMA(()),
            pltpu.SemaphoreType.DMA((lats - 1,)),
            pltpu.SemaphoreType.DMA((lats - 1,)),
            pltpu.SemaphoreType.DMA((lats, 2, slots)),
            pltpu.SemaphoreType.DMA((lats, 2, slots)),
            pltpu.VMEM((2,) + moved[2:], BF16),
            pltpu.SemaphoreType.DMA((2,)),
        ],
        compiler_params=pltpu.CompilerParams(
            collective_id=2, has_side_effects=True, vmem_limit_bytes=VMEM
        ),
        name="gather_params",
    )(shard, x, gain, shift)


def scatter_kernel(dates, lats, src, out, sums, others, z_send, z_recv, send, recv):
    d, l = lax.axis_index("date"), lax.axis_index("lat")
    steps = dates.bit_length() - 1
    paths = [order[::-1] for order in orders(dates)]
    parts = pieces(src.shape[2])
    greet(dates, lats, d, l)
    sent, flights, z = [], {}, {}

    def left(p, i):
        return span(paths[p][i + 1 :][::-1])[::-1]

    def slot_of(i, n):
        return sum(1 << (steps - 1 - e) for e in range(i)) + n

    def held(o, p, i, mask):
        if i == 0:
            return src.at[flipped(d, mask), lax.rem(l + o, lats), parts[p]]
        return sums.at[o, slot_of(i - 1, left(p, i - 1).index(mask)), parts[p]]

    def cross(o, p, i, n):
        bit = paths[p][i]
        slot = slot_of(i, n)
        copy = pltpu.make_async_remote_copy(
            src_ref=held(o, p, i, left(p, i)[n] | 1 << bit),
            dst_ref=sums.at[o, slot, parts[p]],
            send_sem=send.at[o, p, slot],
            recv_sem=recv.at[o, p, slot],
            device_id=(flip(d, bit), l),
            device_id_type=MESH,
        )
        copy.start()
        sent.append(copy)
        flights[o, p, i, n] = copy

    def add(o, p, i, n):
        flights[o, p, i, n].wait_recv()
        have = held(o, p, i, left(p, i)[n])
        got = sums.at[o, slot_of(i, n), parts[p]]
        got[...] = (have[...].astype(F32) + got[...].astype(F32)).astype(BF16)
        if i + 1 < steps:
            if n < len(left(p, i + 1)):
                cross(o, p, i + 1, n)
        elif o:
            copy = pltpu.make_async_remote_copy(
                src_ref=got,
                dst_ref=others.at[o - 1, parts[p]],
                send_sem=z_send.at[o - 1, p],
                recv_sem=z_recv.at[o - 1, p],
                device_id=(d, lax.rem(l + o, lats)),
                device_id_type=MESH,
            )
            copy.start()
            sent.append(copy)
            z[o, p] = copy

    turns = list(range(1, lats)) + [0]
    for o in turns:
        for n in range(len(left(0, 0))):
            for p in range(2):
                cross(o, p, 0, n)
    for wave in range(lats + steps - 1):
        for i in range(steps):
            if 0 <= wave - i < lats:
                for n in range(len(left(0, i))):
                    for p in range(2):
                        add(turns[wave - i], p, i, n)
    for p in range(2):
        total = sums[0, slot_of(steps - 1, 0), parts[p]].astype(F32)
        for o in range(1, lats):
            z[o, p].wait_recv()
            total = total + others[o - 1, parts[p]].astype(F32)
        out[parts[p]] = total
    for copy in sent:
        copy.wait_send()


def scatter(packed):
    dates, lats, rows, lanes = packed.shape
    slots = dates - 1
    return pl.pallas_call(
        functools.partial(scatter_kernel, dates, lats),
        in_specs=[pl.BlockSpec(memory_space=pltpu.VMEM)],
        out_specs=pl.BlockSpec(memory_space=pltpu.VMEM),
        out_shape=jax.ShapeDtypeStruct((rows, lanes), F32),
        scratch_shapes=[
            pltpu.VMEM((lats, slots, rows, lanes), BF16),
            pltpu.VMEM((lats - 1, rows, lanes), BF16),
            pltpu.SemaphoreType.DMA((lats - 1, 2)),
            pltpu.SemaphoreType.DMA((lats - 1, 2)),
            pltpu.SemaphoreType.DMA((lats, 2, slots)),
            pltpu.SemaphoreType.DMA((lats, 2, slots)),
        ],
        compiler_params=pltpu.CompilerParams(
            collective_id=1, has_side_effects=True, vmem_limit_bytes=VMEM
        ),
        name="scatter_grads",
    )(packed)


def add_vectors(packed, vectors, lines):
    first, lead = divmod(OFF_G1, LANES)
    count = -(-(lead + vectors.shape[0]) // LANES)
    extra = jnp.pad(vectors, (lead, count * LANES - lead - vectors.shape[0])).reshape(count, LANES)
    done = 0
    while done < count:
        shard, row = divmod(first + done, lines)
        amount = min(count - done, lines - row)
        old = lax.slice(packed, (shard, row, 0), (shard + 1, row + amount, LANES))
        packed = lax.dynamic_update_slice(packed, old + extra[None, done : done + amount], (shard, row, 0))
        done += amount
    return packed


def local(inputs, noise, cotangent, params, psi, step_counts, pixel_mask, offsets, bases):
    samples, steps, rows, width, _ = inputs.shape
    slabs = samples * steps
    dates, lats = lax.axis_size("date"), lax.axis_size("lat")
    lat = rows * lats

    def by_channel(values):
        return jnp.swapaxes(values, 3, 4).reshape(slabs, rows, -1, width)

    def padded(values):
        return jnp.pad(values, ((0, 0), (0, 0), (0, CP - values.shape[2]), (0, WIDE - width)))

    upward = [(i, i + 1) for i in range(lats - 1)]
    downward = [(i + 1, i) for i in range(lats - 1)]
    lines = params.shape[0] // LANES
    held = -(-lines // STEP) * STEP
    shard = jnp.pad(params.reshape(lines, LANES), ((0, held - lines), (0, 0)))
    small = norms(shard, lines, dates, lats)
    shard, inputs, small = lax.optimization_barrier((shard, inputs, small))
    x = padded(jnp.concatenate([by_channel(inputs), by_channel(noise)], axis=2))
    edges = [(x[s, rows - 1 :], x[s, :1]) for s in range(slabs)]
    gathered, moved = gather(shard, x, small[0], small[1], dates, lats, width)
    gathered = gathered.reshape(dates * lats, held, LANES)
    cot = padded(by_channel(cotangent)).reshape(slabs * rows, CP, WIDE)
    active = jnp.arange(steps, dtype=jnp.int32)[None, :] < step_counts[:, None]
    mask = active.reshape(slabs, 1, 1) * pixel_mask[None]
    mask = jnp.pad(mask.astype(F32), ((0, 0), (0, 0), (0, WIDE - width)))
    matrices = unpack(gathered, lines)
    halos, done = [], gathered
    for s in range(slabs):
        top, bottom, done = lax.optimization_barrier((*edges[s], done))
        halos.append((lax.ppermute(top, "lat", upward), lax.ppermute(bottom, "lat", downward)))
        done = halos[-1], matrices
    matrices = done[1]
    basis = ()
    for s in range(slabs):
        basis = (lift(offsets, bases, psi, *halos[s], moved, small[0], small[1], basis, s, lat, width),)
    basis = basis[0]
    w, wt, up, upt, dn, dnt = matrices
    basis = basis.reshape(slabs * rows, BASIS * CP, WIDE)
    output, gconv, gup, gdn, second_sums = block(
        basis, x.reshape(slabs * rows, CP, WIDE), cot, mask.reshape(slabs * rows, 1, WIDE),
        wt, upt, up, dnt, dn, small[2], small[3],
    )
    gconv_rows = gconv.reshape(slabs, rows, CP, WIDE)
    own, to_below, to_above = lower(offsets, bases, psi, gconv_rows, w, width)
    from_below = lax.ppermute(to_above, "lat", upward)
    from_above = lax.ppermute(to_below, "lat", downward)
    gdisco = weight_grad(basis, gconv)
    packed = pack(gdisco, gup, gdn, dates * lats, lines, held)
    grad, first_sums = input_grad(x, gconv_rows, own, from_below, from_above, small[0], width)
    sums = jnp.sum(jnp.concatenate([first_sums, second_sums]), axis=-1)
    vectors = jnp.concatenate([sums[0, :CIN], sums[1, :CIN], sums[2, :C], sums[3, :C]])
    packed = add_vectors(packed, vectors.astype(BF16), lines)
    summed = scatter(packed.reshape(dates, lats, held, LANES))

    def by_pixel(values):
        values = values.reshape(slabs, rows, CP, WIDE)[:, :, :C, :width]
        return jnp.swapaxes(values.reshape(samples, steps, rows, C, width), 3, 4)

    return by_pixel(output), by_pixel(grad), summed[:lines].reshape(-1)


def solution(mesh):
    field = P("date", None, "lat", None, None)
    flat = P(("date", "lat"))
    return jax.shard_map(
        local,
        mesh=mesh,
        in_specs=(field, field, field, flat, P(), P("date"), P("lat", None), P(), P()),
        out_specs=(field, field, flat),
        check_vma=False,
    )
```

```python
import functools
import math

import jax
import jax.numpy as jnp
from jax import lax
from jax.experimental import pallas as pl
from jax.experimental.pallas import tpu as pltpu
from jax.sharding import PartitionSpec as P

C = 641
HID = 1282
BASIS = 4
SUPPORT = 12
REACH = 2
CIN = 649
BF16, F32 = jnp.bfloat16, jnp.float32
MESH = pl.DeviceIdType.MESH
LANES = 128
STEP = 16
CP = 656
HP = 1296
WIDE = 768
HL = 1408
UNROLL = 8
ASIDE = 2
VMEM = 60 << 20


OFF_G1=BASIS*CIN*C+C; OFF_S1=OFF_G1+CIN; OFF_G2=OFF_S1+CIN; OFF_S2=OFF_G2+C; OFF_UP=OFF_S2+C; OFF_DN=OFF_UP+(C+1)*HID;
SMALL=((OFF_G1,CIN),(OFF_S1,CIN),(OFF_G2,C),(OFF_S2,C))
MATS=((0,C,BASIS*CIN+1,128,3),(OFF_UP,HID,C+1,64,2),(OFF_DN,C,HID+1,128,2))
F_ROWS=29952
def lane_ids(): return lax.broadcasted_iota(jnp.int32,(8,LANES),1)
def place(base,cols,period,b):
    start=base+cols*b
    return start//LANES, start%LANES
def rolled(values, amount):
    out = []
    for n in range(0, len(values), 2):
        pieces = values[n : n + 2]
        if len(pieces) == 2:
            both = jnp.concatenate(pieces, axis=0).astype(BF16)
            both = pltpu.roll(both, amount, axis=1).astype(F32)
            out += [both[:8], both[8:]]
        else:
            out.append(pltpu.roll(pieces[0].astype(BF16).astype(F32), amount, axis=1))
    return out


def flatten(lists):
    return [value for values in lists for value in values]


def unflat(values, width):
    return [values[n : n + width] for n in range(0, len(values), width)]


def unpack_kernel(nrow,pad, g_ref, w_ref,wt_ref,up_ref,upt_ref,dn_ref,dnt_ref,flat,chunks):
    def fill(s,_):
        flat[pl.ds(nrow*s,pad),:]=g_ref[s].astype(F32); return 0
    lax.fori_loop(0,g_ref.shape[0],fill,0)
    lane=lane_ids()
    def split(base,cols,period,groups):
        J=-(-cols//LANES); pitch=period+8; height=pitch*8*groups+8; last=cols-(J-1)*LANES
        def body(b,_):
            row,s=place(base,cols,period,b)
            back=(LANES-s)%LANES
            found=[[flat[pl.ds(row+641*8*g+j,8,stride=641),:] for g in range(groups)] for j in range(J+1)]
            found=unflat(rolled(flatten(found),back),groups)
            for g in range(groups):
                for j in range(J):
                    val=jnp.where(lane<LANES-s,found[j][g],found[j+1][g])
                    if j==J-1: val=jnp.where(lane<last,val,0.0)
                    chunks[pl.ds(j*height+8*g*pitch+b,8,stride=pitch),:]=val
            return 0
        lax.fori_loop(0,period,body,0,unroll=8)
        def border(a,_):
            for j in range(J): chunks[pl.ds(j*height+a*pitch-8,8),:]=chunks[pl.ds(j*height+a*pitch,8),:]
            return 0
        lax.fori_loop(1,8*groups,border,0)
        return J,height,period
    def convert(dst,dst_row,src_row,rows,pad_rows,J,height,period):
        full=rows//16
        def piece(j,r): return chunks[pl.ds(j*height+r//period*(period+8)+r%period,8),:]
        def pair(j,r): return jnp.concatenate([piece(j,r),piece(j,r+8)],axis=0)
        def body(m,_):
            for j in range(J):
                dst[pl.ds(pl.multiple_of(dst_row+16*m,16),16),j*LANES:(j+1)*LANES]=pair(j,src_row+16*m).astype(BF16)
            return 0
        lax.fori_loop(0,full,body,0,unroll=4)
        keep=lax.broadcasted_iota(jnp.int32,(16,LANES),0)<rows-16*full
        for m in range(full,pad_rows//16):
            for j in range(J):
                v=jnp.where(keep,pair(j,src_row+16*m),0.0) if m==full else jnp.zeros((16,LANES),F32)
                dst[dst_row+16*m:dst_row+16*m+16,j*LANES:(j+1)*LANES]=v.astype(BF16)
    J,h,p=split(*MATS[0][:2],*MATS[0][3:])
    for k in range(BASIS):
        convert(w_ref,k*CP,k*CIN,CIN+(k==BASIS-1),CP,J,h,p)
    J,h,p=split(*MATS[1][:2],*MATS[1][3:])
    convert(up_ref,0,0,C+1,CP,J,h,p)
    J,h,p=split(*MATS[2][:2],*MATS[2][3:])
    convert(dn_ref,0,0,HID+1,HP,J,h,p)
    wt_ref[...]=w_ref[:,:CP].T
    upt_ref[...]=up_ref[:,:HP].T
    dnt_ref[...]=dn_ref[:,:CP].T
def unpack(gathered,nrow):
    n,pad,_=gathered.shape
    return pl.pallas_call(functools.partial(unpack_kernel,nrow,pad),
        out_shape=(jax.ShapeDtypeStruct((BASIS*CP,WIDE),BF16),jax.ShapeDtypeStruct((CP,BASIS*CP),BF16),
            jax.ShapeDtypeStruct((CP,HL),BF16),jax.ShapeDtypeStruct((HP,CP),BF16),
            jax.ShapeDtypeStruct((HP,WIDE),BF16),jax.ShapeDtypeStruct((CP,HP),BF16)),
        scratch_shapes=[pltpu.VMEM((F_ROWS,LANES),F32),pltpu.VMEM((6*(136*24+8),LANES),F32)],
        compiler_params=pltpu.CompilerParams(vmem_limit_bytes=VMEM),name="unpack")(gathered)
def pack_kernel(nrow,pad,gd_ref,gu_ref,gn_ref,out_ref,flat,chunks):
    lane=lane_ids(); sub=lax.broadcasted_iota(jnp.int32,(8,LANES),0)
    def gather(src,src_row,dst_row,rows,J,height,last,period):
        full=rows//8
        def cols(m,j):
            v=src[pl.ds(pl.multiple_of(src_row+8*m,8),8),j*LANES:(j+1)*LANES]
            return jnp.where(lane<last,v,0.0) if j==J-1 else v
        def body(m,_):
            r=dst_row+8*m; at=r//period*(period+8)+r%period
            for j in range(J):
                v=cols(m,j)
                chunks[pl.ds(j*height+at+8,8),:]=v
                chunks[pl.ds(j*height+at,8),:]=v
            return 0
        lax.fori_loop(0,full,body,0,unroll=4)
        if rows%8:
            r=dst_row+8*full; at=r//period*(period+8)+r%period
            for j in range(J):
                v=jnp.where(sub<rows-8*full,cols(full,j),0.0)
                chunks[pl.ds(j*height+at+8,8),:]=v
                chunks[pl.ds(j*height+at,8),:]=v
    def clear(J,height,row,period):
        row=row//period*(period+8)+row%period
        count=(height-row)//8
        def body(m,_):
            for j in range(J): chunks[pl.ds(j*height+row+8*m,8),:]=jnp.zeros((8,LANES),F32)
            return 0
        lax.fori_loop(0,count,body,0)
    def merge(base,cols,period,groups):
        J=-(-cols//LANES); pitch=period+8; height=pitch*8*groups+8
        def body(b,tails,rows=J):
            row,s=place(base,cols,period,b)
            new=[]
            found=[chunks[pl.ds(j*height+8*g*pitch+b,8,stride=pitch),:] for g in range(groups) for j in range(J)]
            found=unflat(rolled(found,s),J)
            for g in range(groups):
                x=found[g]
                first=lane>=s
                for j in range(J):
                    v=jnp.where(first,x[j],tails[g] if j==0 else x[j-1])
                    if j<rows: flat[pl.ds(row+641*8*g+j,8,stride=641),:]=v
                new.append(jnp.where(s==LANES-1,jnp.where(first,0.0,x[J-1]),v))
            return tuple(new)
        row0=base//LANES
        init=[jnp.zeros((8,LANES),F32)]*groups
        if base%LANES:
            init[0]=jnp.where(sub==0,flat[row0:row0+8,:],0.0)
        tails=lax.fori_loop(0,period-8,body,tuple(init),unroll=8)
        for b in range(period-8,period):
            tails=body(b,tails,J-1 if base%LANES and b==period-1 else J)
        if base%LANES:
            for g in range(groups):
                at=pl.ds(row0+641*(8*g+1),8,stride=641)
                flat[at,:]=flat[at,:]+tails[g]
    h=136*24+8
    for k in range(BASIS): gather(gd_ref,k*CP,k*CIN,CIN+(k==BASIS-1),6,h,1,128)
    clear(6,h,2600,128)
    merge(0,C,128,3)
    h=72*16+8
    gather(gu_ref,0,0,C+1,11,h,2,64)
    clear(11,h,648,64)
    merge(OFF_UP,HID,64,2)
    h=136*16+8
    gather(gn_ref,0,0,HID+1,6,h,1,128)
    clear(6,h,1288,128)
    merge(OFF_DN,C,128,2)
    def store(s,_):
        out_ref[s]=flat[pl.ds(nrow*s,pad),:].astype(BF16); return 0
    lax.fori_loop(0,out_ref.shape[0],store,0)
def pack(gd,gu,gn,n,nrow,pad):
    return pl.pallas_call(functools.partial(pack_kernel,nrow,pad),
        out_shape=jax.ShapeDtypeStruct((n,pad,LANES),BF16),
        scratch_shapes=[pltpu.VMEM((F_ROWS,LANES),F32),pltpu.VMEM((6*(136*24+8),LANES),F32)],
        compiler_params=pltpu.CompilerParams(vmem_limit_bytes=VMEM),name="pack")(gd,gu,gn)


def tiled(column):
    return jnp.concatenate([column] * (WIDE // LANES), axis=1)


def lane_of(rows, start=0):
    return lax.broadcasted_iota(jnp.int32, (rows, LANES), 1) + start


def wrapped(chunk, width):
    head, first, last = chunk[:, : WIDE - LANES], chunk[:, :LANES], chunk[:, WIDE - LANES :]
    edge = width - (WIDE - LANES)
    lane = lane_of(chunk.shape[0])
    beyond = jnp.where(
        lane < LANES - REACH, pltpu.roll(first, edge, axis=1), pltpu.roll(last, LANES - edge, axis=1)
    )
    return jnp.concatenate([head, jnp.where(lane < edge, last, beyond)], axis=1)


def cut(chunk, width):
    head, last = chunk[:, : WIDE - LANES], chunk[:, WIDE - LANES :]
    keep = lane_of(chunk.shape[0], WIDE - LANES) < width
    return jnp.concatenate([head, jnp.where(keep, last, 0.0)], axis=1)


def rows_below(count):
    return lax.broadcasted_iota(jnp.int32, (STEP, WIDE), 0) < count


def halves(chunk):
    return chunk[:8] + chunk[8:]


def column_sums(read, channels, count):
    whole = channels // STEP

    def body(m, sums):
        return tuple(a + halves(v) for a, v in zip(sums, read(m)))

    sums = lax.fori_loop(
        0, whole, body, tuple(jnp.zeros((8, WIDE), F32) for _ in range(count)), unroll=UNROLL
    )
    keep = rows_below(channels - whole * STEP)
    sums = [a + halves(jnp.where(keep, v, 0.0)) for a, v in zip(sums, read(whole))]
    return [jnp.sum(a, axis=0, keepdims=True) for a in sums]


def norm_stats(read, channels):
    (total,) = column_sums(lambda m: (read(m),), channels, 1)
    mean = total * (1.0 / channels)

    def squares(m):
        centered = read(m) - mean
        return (centered * centered,)

    (total,) = column_sums(squares, channels, 1)
    return mean, lax.rsqrt(total * (1.0 / channels) + 1e-05)


def each_chunk(body, unroll=None):
    def step(m, _):
        body(m, pl.ds(pl.multiple_of(m * STEP, STEP), STEP))
        return 0

    lax.fori_loop(0, CP // STEP, step, 0, unroll=unroll)


def spread(source, gain, shift, width, moved):
    def read(c):
        return source[pl.ds(pl.multiple_of(c * STEP, STEP), STEP), :].astype(F32)

    mean, scale = norm_stats(read, CIN)

    def shifts(c, at):
        values = (read(c) - mean) * scale * tiled(gain[at, :]) + tiled(shift[at, :])
        values = wrapped(values, width).astype(BF16)
        for d in range(-REACH, REACH + 1):
            moved[d + REACH, at, :] = pltpu.roll(values, -d % WIDE, axis=1) if d else values

    each_chunk(shifts, 4)


def lift_kernel(
    rows, slab, lat, width, offsets, bases, psi, lo, hi, own, gain, shift, *refs
):
    out, moved, table, sems = refs[-4:]
    first_row = lax.axis_index("lat") * rows
    copies = [
        pltpu.make_async_copy(own.at[slab, r], moved.at[r + 1], sems.at[r]) for r in range(rows)
    ]
    for copy in copies:
        copy.start()
    for k in range(BASIS):
        table[SUPPORT + k] = 0
    for p in range(SUPPORT):
        k = bases[p]
        used = table[SUPPORT + k]
        table[k * 3 + used] = p
        table[SUPPORT + k] = used + 1
    for source, m in ((lo, 0), (hi, rows + 1)):
        spread(source.at[0], gain, shift, width, moved.at[m])
    for copy in copies:
        copy.wait()
    for r in range(rows):
        for k in range(BASIS):
            parts = []
            for q in range(3):
                p = table[k * 3 + q]
                row = first_row + r + offsets[p, 0]
                inside = jnp.logical_and(row >= 0, row < lat)
                weight = jnp.where(inside, psi[first_row + r, p], 0.0)
                parts.append((weight, r + 1 + offsets[p, 0], offsets[p, 1] + REACH))

            def combine(c, at):
                total = None
                for weight, row, d in parts:
                    term = weight * moved[row, d, at, :].astype(F32)
                    total = term if total is None else total + term
                to = pl.ds(pl.multiple_of(k * CP + c * STEP, STEP), STEP)
                out[0, r, to, :] = cut(total, width).astype(BF16)

            each_chunk(combine, 4)
        last = slice(BASIS * CP - STEP, BASIS * CP)
        bias_row = CIN - (CP - STEP)
        sub = lax.broadcasted_iota(jnp.int32, (STEP, WIDE), 0)
        lane = lax.broadcasted_iota(jnp.int32, (STEP, WIDE), 1)
        ones = jnp.where(lane < width, 1.0, 0.0)
        out[0, r, last, :] = jnp.where(sub == bias_row, ones, out[0, r, last, :].astype(F32)).astype(BF16)


def lift(offsets, bases, psi, lo, hi, own, gain, shift, before, slab, lat, width):
    slabs, rows = own.shape[:2]
    smem = pl.BlockSpec(memory_space=pltpu.SMEM)
    anywhere = pl.BlockSpec(memory_space=pl.ANY)
    halo = pl.BlockSpec((1, CP, WIDE), lambda s: (0, 0, 0))
    column = pl.BlockSpec((CP, LANES), lambda s: (0, 0))
    return pl.pallas_call(
        functools.partial(lift_kernel, rows, slab, lat, width),
        grid=(1,),
        in_specs=[smem, smem, smem, halo, halo, anywhere, column, column] + [anywhere] * len(before),
        out_specs=pl.BlockSpec((1, rows, BASIS * CP, WIDE), lambda s: (slab, 0, 0, 0)),
        out_shape=jax.ShapeDtypeStruct((slabs, rows, BASIS * CP, WIDE), BF16),
        scratch_shapes=[
            pltpu.VMEM((rows + 2, 2 * REACH + 1, CP, WIDE), BF16),
            pltpu.SMEM((SUPPORT + BASIS,), jnp.int32),
            pltpu.SemaphoreType.DMA((rows,)),
        ],
        input_output_aliases={8: 0} if before else {},
        compiler_params=pltpu.CompilerParams(vmem_limit_bytes=VMEM),
        cost_estimate=pl.CostEstimate(flops=40 << 20, bytes_accessed=40 << 20, transcendentals=0),
        name="lift",
    )(offsets, bases, psi, lo, hi, own, gain, shift, *before)


GELU_A = math.sqrt(2.0 / math.pi)
GELU_B = 0.044715


TILE = 256


def weave(*lists):
    order = []
    for which, steps in enumerate(lists):
        for n, step in enumerate(steps):
            order.append(((n + 0.5) / len(steps), which, n, step))
    for _, _, _, step in sorted(order, key=lambda entry: entry[:3]):
        step()


class Job:
    def __init__(self, buffers, weights, totals, mask):
        self.basis, self.x, self.cot, self.out, self.gconv = buffers[:5]
        self.res, self.second, self.pre, self.act, self.mid, self.gact, self.gb, self.gpre = buffers[5:]
        self.wt, self.upt, self.up, self.dnt, self.dn, self.gain, self.shift = weights
        self.gup, self.gdn, self.sums = totals
        self.mask = mask

    @staticmethod
    def at(c):
        return slice(c * STEP, (c + 1) * STEP)

    @staticmethod
    def wide(column):
        return jnp.concatenate([column] * (TILE // LANES), axis=1)

    @staticmethod
    def only(c, values, channels, other=0.0):
        if (c + 1) * STEP <= channels:
            return values
        row = lax.broadcasted_iota(jnp.int32, (STEP, TILE), 0)
        return jnp.where(row < channels - c * STEP, values, other)

    def product(self, out, left, right, count):
        rows = left.shape[0]
        size = -(-rows // (count * STEP)) * STEP

        def step(start):
            at = slice(start, min(start + size, rows))
            values = left[at, : right.shape[0]]
            out[at, :] = jnp.dot(values, right[...], preferred_element_type=F32)

        return [functools.partial(step, start) for start in range(0, rows, size)]

    def outer(self, out, left, right, count):
        rows = left.shape[0]
        size = -(-rows // (count * STEP)) * STEP

        def step(start):
            at = slice(start, min(start + size, rows))
            term = lax.dot_general(
                left[at, :], right[...], (((1,), (1,)), ((), ())), preferred_element_type=F32
            )
            out[at, : right.shape[0]] += term

        return [functools.partial(step, start) for start in range(0, rows, size)]

    def m1(self):
        return self.product(self.res, self.wt, self.basis, 4)

    def v1(self):
        state = {"sum": jnp.zeros((8, TILE), F32), "square": jnp.zeros((8, TILE), F32)}
        mask = self.mask()

        def add(c):
            at = self.at(c)
            value = self.res[at, :] + self.only(c, self.x[at, :].astype(F32), C)
            self.res[at, :] = value
            self.gb[at, :] = (self.cot[at, :].astype(F32) * mask).astype(BF16)
            state["sum"] = state["sum"] + halves(self.only(c, value, C))

        def mean():
            self.mean = jnp.sum(state["sum"], axis=0, keepdims=True) * (1.0 / C)

        def square(c):
            value = self.res[self.at(c), :] - self.mean
            state["square"] = state["square"] + halves(self.only(c, value * value, C))

        def scale():
            total = jnp.sum(state["square"], axis=0, keepdims=True)
            self.scale = lax.rsqrt(total * (1.0 / C) + 1e-05)

        def normalize(c):
            at = self.at(c)
            value = (self.res[at, :] - self.mean) * self.scale
            value = value * self.wide(self.gain[at, :]) + self.wide(self.shift[at, :])
            row = lax.broadcasted_iota(jnp.int32, (STEP, TILE), 0)
            if c == C // STEP:
                value = jnp.where(row == C % STEP, 1.0, value)
            self.second[at, :] = value.astype(BF16)

        chunks = range(CP // STEP)
        steps = [functools.partial(add, c) for c in chunks] + [mean]
        steps += [functools.partial(square, c) for c in chunks] + [scale]
        return steps + [functools.partial(normalize, c) for c in chunks]

    def m2(self):
        return self.product(self.pre, self.upt, self.second, 9)

    def v2(self):
        def gelu(c):
            at = self.at(c)
            v = self.pre[at, :]
            square = v * v
            bend = jnp.tanh(GELU_A * v * (1.0 + GELU_B * square))
            half = 0.5 * (1.0 + bend)
            value = v * half
            if c == HID // STEP:
                row = lax.broadcasted_iota(jnp.int32, (STEP, TILE), 0)
                value = jnp.where(row == HID % STEP, 1.0, value)
            self.act[at, :] = value.astype(BF16)
            rise = GELU_A * (1.0 + 3.0 * GELU_B * square)
            self.pre[at, :] = half + 0.5 * v * (1.0 - bend * bend) * rise

        return [functools.partial(gelu, c) for c in range(HP // STEP)]

    def m3(self):
        back = self.product(self.gact, self.dn, self.gb, 9)
        return self.product(self.mid, self.dnt, self.act, 4) + back

    def v3(self):
        def finish(c):
            at = self.at(c)
            self.out[at, :] = (self.res[at, :] + self.mid[at, :]).astype(BF16)

        def back(c):
            at = self.at(c)
            self.gpre[at, :] = (self.gact[at, :] * self.pre[at, :]).astype(BF16)

        steps = [functools.partial(finish, c) for c in range(CP // STEP)]
        return steps + [functools.partial(back, c) for c in range(HP // STEP)]

    def m4(self):
        return self.product(self.mid, self.up, self.gpre, 4)

    def v4(self):
        state = {"flat": jnp.zeros((8, TILE), F32), "along": jnp.zeros((8, TILE), F32)}

        def terms(c):
            at = self.at(c)
            dm = self.mid[at, :]
            xhat = (self.res[at, :] - self.mean) * self.scale
            return dm, xhat, dm * self.wide(self.gain[at, :])

        def means(c):
            _, xhat, g = terms(c)
            g = self.only(c, g, C)
            state["flat"] = state["flat"] + halves(g)
            state["along"] = state["along"] + halves(g * xhat)

        def join():
            for name in state:
                state[name] = jnp.sum(state[name], axis=0, keepdims=True) * (1.0 / C)

        def backward(c):
            at = self.at(c)
            dm, xhat, g = terms(c)
            value = g - state["flat"] - xhat * state["along"]
            value = self.gb[at, :].astype(F32) + self.scale * value
            self.gconv[at, :] = self.only(c, value, C).astype(BF16)
            for n, term in enumerate((dm * xhat, dm)):
                self.sums[n, at, :] += term[:, :LANES] + term[:, LANES:]

        chunks = range(CP // STEP)
        steps = [functools.partial(means, c) for c in chunks] + [join]
        return steps + [functools.partial(backward, c) for c in chunks]

    def m5(self):
        first = self.outer(self.gdn, self.act, self.gb, 3)
        return first + self.outer(self.gup, self.second, self.gpre, 2)


def block_kernel(
    basis, x, cot, mask, wt, upt, up, dnt, dn, gain, shift, out, gconv, gup, gdn, sums, *scratch
):
    count = basis.shape[0]
    tiles = WIDE // TILE
    in_sems, out_sems = scratch[-2:]
    per_job = (len(scratch) - 2) // 2
    sets = [scratch[:per_job], scratch[per_job : 2 * per_job]]
    for total in (gup, gdn, sums):
        total[...] = jnp.zeros_like(total)

    def place(i, j):
        return i // tiles * 2 + j, pl.ds(pl.multiple_of(i % tiles * TILE, TILE), TILE)

    def arrive(i, j):
        row, lanes = place(i, j)
        return [
            pltpu.make_async_copy(source.at[row, :, lanes], sets[j][n], in_sems.at[j, n])
            for n, source in enumerate((basis, x, cot))
        ]

    def leave(i, j):
        row, lanes = place(i, j)
        return [
            pltpu.make_async_copy(sets[j][3 + n], target.at[row, :, lanes], out_sems.at[j, n])
            for n, target in enumerate((out, gconv))
        ]

    last = count // 2 * tiles - 1
    for j in range(2):
        for copy in arrive(0, j):
            copy.start()

    def pair(i, _):
        def row_mask(j):
            row, lanes = place(i, j)
            return lambda: mask[row, :, lanes]

        weights, totals = (wt, upt, up, dnt, dn, gain, shift), (gup, gdn, sums)
        a, b = (Job(sets[j], weights, totals, row_mask(j)) for j in range(2))
        after = jnp.minimum(i + 1, last)
        coming = [arrive(after, j) for j in range(2)]
        leaving = [leave(i, j) for j in range(2)]
        for j in range(2):
            for copy in arrive(i, j):
                copy.wait()
        weave(a.m1())
        coming[0][0].start()
        weave(a.v1(), b.m1())
        coming[1][0].start()
        for n in (1, 2):
            coming[0][n].start()
        weave(a.m2(), b.v1())
        for n in (1, 2):
            coming[1][n].start()
        weave(a.v2(), b.m2())
        weave(a.m3(), b.v2())
        weave(a.v3(), b.m3())
        leaving[0][0].start()
        weave(a.m4(), b.v3())
        leaving[1][0].start()
        weave(a.v4(), b.m4())
        leaving[0][1].start()
        weave(a.m5(), b.v4())
        leaving[1][1].start()
        weave(b.m5())
        for copies in leaving:
            for copy in copies:
                copy.wait()
        return 0

    lax.fori_loop(0, last + 1, pair, 0)
    for j in range(2):
        for copy in arrive(last, j):
            copy.wait()


def block(basis, x, cot, mask, wt, upt, up, dnt, dn, gain, shift):
    count = x.shape[0]
    anywhere = pl.BlockSpec(memory_space=pl.ANY)
    held = pl.BlockSpec(memory_space=pltpu.VMEM)
    low, high = pltpu.VMEM((CP, TILE), BF16), pltpu.VMEM((CP, TILE), F32)
    hidden_low, hidden_high = pltpu.VMEM((HP, TILE), BF16), pltpu.VMEM((HP, TILE), F32)
    per_job = [pltpu.VMEM((BASIS * CP, TILE), BF16), low, low, low, low]
    per_job += [high, low, hidden_high, hidden_low, high, hidden_high, low, hidden_low]
    return pl.pallas_call(
        block_kernel,
        in_specs=[anywhere] * 3 + [held] * 8,
        out_specs=[anywhere] * 2 + [held] * 3,
        out_shape=(
            jax.ShapeDtypeStruct((count, CP, WIDE), BF16),
            jax.ShapeDtypeStruct((count, CP, WIDE), BF16),
            jax.ShapeDtypeStruct((CP, HL), F32),
            jax.ShapeDtypeStruct((HP, WIDE), F32),
            jax.ShapeDtypeStruct((2, CP, LANES), F32),
        ),
        scratch_shapes=per_job * 2 + [pltpu.SemaphoreType.DMA((2, 3)), pltpu.SemaphoreType.DMA((2, 2))],
        compiler_params=pltpu.CompilerParams(vmem_limit_bytes=VMEM),
        name="block",
    )(basis, x, cot, mask, wt, upt, up, dnt, dn, gain, shift)


def along_lanes(ref, at, values):
    total = values[:, :LANES]
    for j in range(1, WIDE // LANES):
        total = total + values[:, j * LANES : (j + 1) * LANES]
    ref[at, :] = ref[at, :] + total


def outer_kernel(basis, gconv, out):
    i = pl.program_id(0)
    term = lax.dot_general(basis[0], gconv[0], (((1,), (1,)), ((), ())), preferred_element_type=F32)

    @pl.when(i == 0)
    def _():
        out[:, :CP] = term

    @pl.when(i > 0)
    def _():
        out[:, :CP] += term


def weight_grad(basis, gconv):
    count = basis.shape[0]
    return pl.pallas_call(
        outer_kernel,
        grid=(count,),
        in_specs=[
            pl.BlockSpec((1, BASIS * CP, WIDE), lambda i: (i, 0, 0)),
            pl.BlockSpec((1, CP, WIDE), lambda i: (i, 0, 0)),
        ],
        out_specs=pl.BlockSpec((BASIS * CP, WIDE), lambda i: (0, 0)),
        out_shape=jax.ShapeDtypeStruct((BASIS * CP, WIDE), F32),
        compiler_params=pltpu.CompilerParams(vmem_limit_bytes=VMEM),
        name="weight_grad",
    )(basis, gconv)


GROUP = 11 * STEP
GROUP_STEP = 10 * STEP


def lower_kernel(rows, width, offsets, bases, psi, gconv, w, own, lo, hi, *scratch):
    place, coef, in_sems, w_sems, out_sems = scratch[-5:]
    per_slab = (len(scratch) - 5) // 2
    sets = [scratch[:per_slab], scratch[per_slab : 2 * per_slab]]
    first_row = lax.axis_index("lat") * rows
    span = 2 * REACH + 1
    groups = 1 + (CP - GROUP) // GROUP_STEP
    for n in range(3 * span):
        place[n] = 0
        for r in range(rows):
            coef[r, n] = 0.0
    for p in range(SUPPORT):
        n = (offsets[p, 0] + 1) * span + offsets[p, 1] + REACH
        place[n] = bases[p]
        for r in range(rows):
            coef[r, n] = psi[first_row + r, p]

    def channels(g):
        return pl.ds(pl.multiple_of(g * GROUP_STEP, STEP), GROUP)

    def weights(j, g):
        return pltpu.make_async_copy(w.at[:, channels(g), :], sets[j][1], w_sems.at[j])

    def products(j):
        ring, part, lifted = sets[j][:3]

        def step(r, k):
            values = jnp.dot(part[k, :, :CP], ring[r], preferred_element_type=F32)
            lifted[r, k] = values.astype(BF16)

        return [functools.partial(step, r, k) for r in range(rows) for k in range(BASIS)]

    def gathers(j):
        lifted, inner, below, above = sets[j][2:]

        def step(c, target):
            at = slice(c * STEP, (c + 1) * STEP)
            total = None
            for d in range(-REACH, REACH + 1):
                part = None
                for o in (-1, 0, 1):
                    r = target - o
                    if 0 <= r < rows:
                        n = (o + 1) * span + d + REACH
                        term = coef[r, n] * lifted[r, place[n], at, :].astype(F32)
                        part = term if part is None else part + term
                if d:
                    part = pltpu.roll(part.astype(BF16), d % WIDE, axis=1).astype(F32)
                total = part if total is None else total + part
            if target < 0:
                below[at, :] = total.astype(BF16)
            elif target == rows:
                above[at, :] = total.astype(BF16)
            else:
                inner[target, at, :] = total

        return [functools.partial(step, c, t) for c in range(GROUP // STEP) for t in range(-1, rows + 1)]

    def pair_of_slabs(both, _):
        def leaving(j, g):
            slab = both * 2 + j
            targets = (own.at[slab, :, channels(g), :], lo.at[slab, channels(g), :], hi.at[slab, channels(g), :])
            return [
                pltpu.make_async_copy(sets[j][3 + n], target, out_sems.at[j, n])
                for n, target in enumerate(targets)
            ]

        rings = [pltpu.make_async_copy(gconv.at[both * 2 + j], sets[j][0], in_sems.at[j]) for j in range(2)]
        for j in range(2):
            rings[j].start()
            weights(j, 0).start()
        for j in range(2):
            rings[j].wait()
            ring = sets[j][0]
            edge = width - (WIDE - LANES)
            lane = lane_of(CP)
            for r in range(rows):
                first, last = ring[r, :, :LANES].astype(F32), ring[r, :, WIDE - LANES :].astype(F32)
                beyond = jnp.where(
                    lane < LANES - REACH,
                    pltpu.roll(first, edge, axis=1),
                    pltpu.roll(last, LANES - edge, axis=1),
                )
                ring[r, :, WIDE - LANES :] = jnp.where(lane < edge, last, beyond).astype(BF16)
        weights(0, 0).wait()
        weave(products(0))
        weights(0, min(1, groups - 1)).start()

        def group(g, _):
            after, later = jnp.minimum(g + 1, groups - 1), jnp.minimum(g + 2, groups - 1)
            def free(j):
                @pl.when(g > 0)
                def _():
                    for copy in leaving(j, jnp.maximum(g - 1, 0)):
                        copy.wait()

            weights(1, g).wait()
            free(0)
            weave(products(1), gathers(0))
            weights(1, after).start()
            for copy in leaving(0, g):
                copy.start()
            weights(0, after).wait()
            free(1)
            weave(products(0), gathers(1))
            weights(0, later).start()
            for copy in leaving(1, g):
                copy.start()
            return 0

        lax.fori_loop(0, groups, group, 0)
        for j in range(2):
            weights(j, groups - 1).wait()
            for copy in leaving(j, groups - 1):
                copy.wait()
        return 0

    lax.fori_loop(0, gconv.shape[0] // 2, pair_of_slabs, 0)


def lower(offsets, bases, psi, gconv, w, width):
    slabs, rows = gconv.shape[:2]
    smem = pl.BlockSpec(memory_space=pltpu.SMEM)
    anywhere = pl.BlockSpec(memory_space=pl.ANY)
    edge = jax.ShapeDtypeStruct((slabs, CP, WIDE), BF16)
    per_slab = [
        pltpu.VMEM((rows, CP, WIDE), BF16),
        pltpu.VMEM((BASIS, GROUP, WIDE), BF16),
        pltpu.VMEM((rows, BASIS, GROUP, WIDE), BF16),
        pltpu.VMEM((rows, GROUP, WIDE), F32),
        pltpu.VMEM((GROUP, WIDE), BF16),
        pltpu.VMEM((GROUP, WIDE), BF16),
    ]
    return pl.pallas_call(
        functools.partial(lower_kernel, rows, width),
        in_specs=[smem, smem, smem, anywhere, anywhere],
        out_specs=[anywhere] * 3,
        out_shape=(jax.ShapeDtypeStruct((slabs, rows, CP, WIDE), F32), edge, edge),
        scratch_shapes=per_slab * 2
        + [
            pltpu.SMEM((3 * (2 * REACH + 1),), jnp.int32),
            pltpu.SMEM((rows, 3 * (2 * REACH + 1)), F32),
            pltpu.SemaphoreType.DMA((2,)),
            pltpu.SemaphoreType.DMA((2,)),
            pltpu.SemaphoreType.DMA((2, 3)),
        ],
        compiler_params=pltpu.CompilerParams(vmem_limit_bytes=VMEM),
        name="lower",
    )(offsets, bases, psi, gconv, w.reshape(BASIS, CP, WIDE))


def input_rows(width, x, gconv, own, lo, hi, gain, grad, sums, buffers, in_sems, out_sems):
    rows = x.shape[1]
    places = [(s, r) for s in range(x.shape[0]) for r in range(rows)]
    saves = []

    def loads(n):
        s, r = places[n]
        sources = [x.at[s, r], gconv.at[s, r], own.at[s, r]]
        sources += [lo.at[s]] if r == 0 else []
        sources += [hi.at[s]] if r == rows - 1 else []
        slots = [0, 1, 2] + ([3] if r == 0 else []) + ([4] if r == rows - 1 else [])
        return [
            pltpu.make_async_copy(source, buffers[n % 2][slot], in_sems.at[n % 2, slot])
            for source, slot in zip(sources, slots)
        ]

    flying = loads(0)
    for copy in flying:
        copy.start()
    sums[...] = jnp.zeros_like(sums)
    for n, (s, r) in enumerate(places):
        for copy in flying:
            copy.wait()
        if n + 1 < len(places):
            flying = loads(n + 1)
            for copy in flying:
                copy.start()
        here, conv, total, below, above, result = buffers[n % 2]

        def read(c):
            return here[pl.ds(pl.multiple_of(c * STEP, STEP), STEP), :].astype(F32)

        mean, scale = norm_stats(read, CIN)
        yield

        if r == 0 or r == rows - 1:

            def join(c, at):
                value = total[at, :]
                if r == 0:
                    value = value + below[at, :].astype(F32)
                if r == rows - 1:
                    value = value + above[at, :].astype(F32)
                total[at, :] = value

            each_chunk(join, 8)
            yield

        def means(c):
            at = pl.ds(pl.multiple_of(c * STEP, STEP), STEP)
            g = total[at, :] * tiled(gain[at, :])
            return g, g * ((read(c) - mean) * scale)

        flat, along = [v * (1.0 / CIN) for v in column_sums(means, CIN, 2)]
        yield
        if n >= 2:
            saves[n - 2].wait()

        def backward(c, at):
            dm = cut(total[at, :], width)
            xhat = (read(c) - mean) * scale
            g = dm * tiled(gain[at, :])
            value = scale * (g - flat - xhat * along) + conv[at, :].astype(F32)
            result[at, :] = value.astype(BF16)
            along_lanes(sums.at[0], at, dm * xhat)
            along_lanes(sums.at[1], at, dm)

        each_chunk(backward, 8)
        save = pltpu.make_async_copy(result, grad.at[s, r], out_sems.at[n % 2])
        save.start()
        saves.append(save)
        yield
    for save in saves[-2:]:
        save.wait()


def flip(value, bit):
    return value + (1 - 2 * ((value // (1 << bit)) % 2)) * (1 << bit)


def flipped(value, mask):
    bit = 0
    while mask >> bit:
        if mask >> bit & 1:
            value = flip(value, bit)
        bit += 1
    return value


def span(bits):
    masks = [0]
    for b in bits:
        masks = masks + [m | 1 << b for m in masks]
    return masks


def orders(dates):
    bits = list(range(1, dates.bit_length() - 1))
    return bits + [0], bits[::-1] + [0]


def pieces(rows):
    cut = rows // (2 * STEP) * STEP
    return pl.ds(0, cut), pl.ds(cut, rows - cut)


def greet(dates, lats, d, l, owner):
    barrier = pltpu.get_barrier_semaphore()
    bits = range(dates.bit_length() - 1)
    peers = [(d, lax.rem(l + o, lats)) for o in range(1, lats)] + [(flip(d, b), l) for b in bits]
    for peer in peers:
        pl.semaphore_signal(barrier, inc=1, device_id=peer, device_id_type=MESH)
    next_to = [(owner[0], b) for b in range(lats) if b != owner[1]] + [(flip(owner[0], b), owner[1]) for b in bits]
    away = [(a, b) for a in range(dates) for b in range(lats) if (a, b) not in next_to + [owner]]
    mine = jnp.logical_and(d == owner[0], l == owner[1])
    near = functools.reduce(jnp.logical_or, [jnp.logical_and(d == a, l == b) for a, b in next_to])
    far = jnp.logical_not(jnp.logical_or(mine, near))

    @pl.when(mine)
    def _():
        for peer in away:
            pl.semaphore_signal(barrier, inc=1, device_id=peer, device_id_type=MESH)
        pl.semaphore_wait(barrier, len(peers) + len(away))

    @pl.when(near)
    def _():
        pl.semaphore_wait(barrier, len(peers))

    @pl.when(far)
    def _():
        pl.semaphore_signal(barrier, inc=1, device_id=owner, device_id_type=MESH)
        pl.semaphore_wait(barrier, len(peers) + 1)


def read_norms(landed, first, out):
    lane = lane_ids()
    sub = lax.broadcasted_iota(jnp.int32, (8, LANES), 0)
    lines = landed[...].astype(F32)
    for i, (off, n) in enumerate(SMALL):
        row, s = divmod(off - first * LANES, LANES)
        r = pltpu.roll(lines[row : row + 8], (LANES - s) % LANES, axis=1)
        v = jnp.where(lane < LANES - s, r, pltpu.roll(r, 7, axis=0))
        t = jnp.where(sub * LANES + lane < n, v, 0.0).T
        for j in range(6):
            rows = min(LANES, CP - j * LANES)
            out[i, j * LANES : j * LANES + rows, :] = jnp.broadcast_to(t[:rows, j : j + 1], (rows, LANES))


def norm_home(lines, lats):
    start, end = OFF_G1 // LANES, (OFF_UP - 1) // LANES + 3
    owner = start // lines
    row = (start - owner * lines) // STEP * STEP
    count = -(-(end - owner * lines - row) // STEP) * STEP
    assert row + count <= -(-lines // STEP) * STEP
    return divmod(owner, lats), owner * lines + row, row, count


def gather_kernel(
    dates, lats, lines, width, src, x, out, moved, small, local_sem, z_send, z_recv, send, recv,
    buffers, buffer_sems, landed, norm_sem, norm_send, norm_recv,
):
    d, l = lax.axis_index("date"), lax.axis_index("lat")
    steps = dates.bit_length() - 1
    parts = pieces(src.shape[0])
    owner, first, row, count = norm_home(lines, lats)
    mine = jnp.logical_and(d == owner[0], l == owner[1])
    others = [(a, b) for a in range(dates) for b in range(lats) if (a, b) != owner]
    window = src.at[pl.ds(row, count)]

    greet(dates, lats, d, l, owner)

    def norms_to(n):
        return pltpu.make_async_remote_copy(
            src_ref=window,
            dst_ref=landed,
            send_sem=norm_send.at[n],
            recv_sem=norm_recv,
            device_id=others[n],
            device_id_type=MESH,
        )

    @pl.when(mine)
    def _():
        for n in range(len(others)):
            norms_to(n).start()
        pltpu.make_async_copy(window, landed, norm_sem).start()

    own = pltpu.make_async_copy(src, out.at[d, l], local_sem)
    own.start()
    sent, arriving, flights = [], {}, {}

    def along(o):
        copy = pltpu.make_async_remote_copy(
            src_ref=src,
            dst_ref=out.at[d, l],
            send_sem=z_send.at[o - 1],
            recv_sem=z_recv.at[o - 1],
            device_id=(d, lax.rem(l + o, lats)),
            device_id_type=MESH,
        )
        copy.start()
        sent.append(copy)
        arriving[o] = copy

    def cross(o, p, i, n):
        order = orders(dates)[p]
        block = out.at[flipped(d, span(order[:i])[n]), lax.rem(l - o + lats, lats), parts[p]]
        slot = (1 << i) - 1 + n
        copy = pltpu.make_async_remote_copy(
            src_ref=src.at[parts[p]] if o == 0 and n == 0 else block,
            dst_ref=block,
            send_sem=send.at[o, p, slot],
            recv_sem=recv.at[o, p, slot],
            device_id=(flip(d, order[i]), l),
            device_id_type=MESH,
        )
        copy.start()
        sent.append(copy)
        flights[o, p, i, n] = copy

    rows = [(s, r) for s in range(x.shape[0]) for r in range(x.shape[1])]
    saves = []

    def spread_rows():
        @pl.when(mine)
        def _():
            pltpu.make_async_copy(window, landed, norm_sem).wait()

        @pl.when(jnp.logical_not(mine))
        def _():
            norms_to(0).wait_recv()

        read_norms(landed, first, small)
        for n, (s, r) in enumerate(rows):
            if n >= 2:
                saves[n - 2].wait()
            spread(x.at[s, r], small.at[0], small.at[1], width, buffers.at[n % 2])
            save = pltpu.make_async_copy(buffers.at[n % 2], moved.at[s, r], buffer_sems.at[n % 2])
            save.start()
            saves.append(save)
            yield

    aside = spread_rows()
    for wave in range(lats + steps):
        if wave < lats:
            if wave:
                arriving[wave].wait_recv()
            if wave + 1 < lats:
                along(wave + 1)
            for i in range(steps):
                for p in range(2):
                    cross(wave, p, i, 0)
        next(aside, None)
        for i in range(steps)[::-1]:
            o = wave - 1 - i
            if 0 <= o < lats:
                for n in range(1 << i):
                    for p in range(2):
                        flights[o, p, i, n].wait_recv()
                        for later in range(i + 1, steps):
                            cross(o, p, later, n + (1 << i))
    for _ in aside:
        pass
    for save in saves[-2:]:
        save.wait()
    own.wait()
    for copy in sent:
        copy.wait_send()

    @pl.when(mine)
    def _():
        for n in range(len(others)):
            norms_to(n).wait_send()


def gather(shard, x, lines, dates, lats, width):
    slots = dates - 1
    moved = x.shape[:2] + (2 * REACH + 1,) + x.shape[2:]
    anywhere = pl.BlockSpec(memory_space=pl.ANY)
    return pl.pallas_call(
        functools.partial(gather_kernel, dates, lats, lines, width),
        in_specs=[anywhere, pl.BlockSpec(memory_space=pltpu.VMEM)],
        out_specs=[anywhere, anywhere, pl.BlockSpec(memory_space=pltpu.VMEM)],
        out_shape=(
            jax.ShapeDtypeStruct((dates, lats) + shard.shape, shard.dtype),
            jax.ShapeDtypeStruct(moved, BF16),
            jax.ShapeDtypeStruct((4, CP, LANES), F32),
        ),
        scratch_shapes=[
            pltpu.SemaphoreType.DMA(()),
            pltpu.SemaphoreType.DMA((lats - 1,)),
            pltpu.SemaphoreType.DMA((lats - 1,)),
            pltpu.SemaphoreType.DMA((lats, 2, slots)),
            pltpu.SemaphoreType.DMA((lats, 2, slots)),
            pltpu.VMEM((2,) + moved[2:], BF16),
            pltpu.SemaphoreType.DMA((2,)),
            pltpu.VMEM((norm_home(lines, lats)[3], LANES), BF16),
            pltpu.SemaphoreType.DMA(()),
            pltpu.SemaphoreType.DMA((dates * lats - 1,)),
            pltpu.SemaphoreType.DMA(()),
        ],
        compiler_params=pltpu.CompilerParams(
            collective_id=2, has_side_effects=True, vmem_limit_bytes=VMEM
        ),
        name="gather_params",
    )(shard, x)


def vector_rows(sums, tiny, first):
    lane = lane_ids()
    sub = lax.broadcasted_iota(jnp.int32, (8, LANES), 0)
    tiny[...] = jnp.zeros_like(tiny)
    for n, (off, channels) in enumerate(SMALL):
        lines = []
        for j in range(6):
            height = min(LANES, CP - j * LANES)
            block = sums[n // 2][n % 2, j * LANES : j * LANES + height, :]
            if height < LANES:
                block = jnp.concatenate([block, jnp.zeros((LANES - height, LANES), F32)], axis=0)
            lines.append(jnp.sum(block.T, axis=0, keepdims=True))
        lines = jnp.concatenate(lines + [jnp.zeros((2, LANES), F32)], axis=0)
        lines = jnp.where(sub * LANES + lane < channels, lines, 0.0)
        row, s = divmod(off - first * LANES, LANES)
        r = pltpu.roll(lines, s, axis=1)
        moved = jnp.where(lane >= s, r, jnp.where(sub == 0, 0.0, pltpu.roll(r, 1, axis=0)))
        tiny[row : row + 8, :] = tiny[row : row + 8, :] + moved


def vector_home(lines, lats):
    start, end = OFF_G1 // LANES, (OFF_UP - 1) // LANES + 1
    owner = start // lines
    row = (start - owner * lines) // 8 * 8
    count = -(-(end + 8 - owner * lines - row) // 8) * 8
    assert end <= (owner + 1) * lines
    return divmod(owner, lats), owner * lines + row, row, count


def scatter_kernel(
    dates, lats, lines, width, src, x, gconv, own, lo, hi, gain, second_sums, out, grad,
    sums, others, z_send, z_recv, send, recv, first_sums, tiny, landed, tiny_send, tiny_recv,
    in_sems, out_sems, *row_buffers
):
    d, l = lax.axis_index("date"), lax.axis_index("lat")
    steps = dates.bit_length() - 1
    paths = [order[::-1] for order in orders(dates)]
    parts = pieces(src.shape[2])
    owner, first, row, count = vector_home(lines, lats)
    mine = jnp.logical_and(d == owner[0], l == owner[1])
    senders = [(a, b) for a in range(dates) for b in range(lats) if (a, b) != owner]

    greet(dates, lats, d, l, owner)
    sent, flights, z = [], {}, {}
    half = len(row_buffers) // 2
    aside = input_rows(
        width, x, gconv, own, lo, hi, gain, grad, first_sums,
        [row_buffers[:half], row_buffers[half:]], in_sems, out_sems,
    )

    def left(p, i):
        return span(paths[p][i + 1 :][::-1])[::-1]

    def slot_of(i, n):
        return sum(1 << (steps - 1 - e) for e in range(i)) + n

    def held(o, p, i, mask):
        if i == 0:
            return src.at[flipped(d, mask), lax.rem(l + o, lats), parts[p]]
        return sums.at[o, slot_of(i - 1, left(p, i - 1).index(mask)), parts[p]]

    def cross(o, p, i, n):
        bit = paths[p][i]
        slot = slot_of(i, n)
        copy = pltpu.make_async_remote_copy(
            src_ref=held(o, p, i, left(p, i)[n] | 1 << bit),
            dst_ref=sums.at[o, slot, parts[p]],
            send_sem=send.at[o, p, slot],
            recv_sem=recv.at[o, p, slot],
            device_id=(flip(d, bit), l),
            device_id_type=MESH,
        )
        copy.start()
        sent.append(copy)
        flights[o, p, i, n] = copy

    def add(o, p, i, n):
        flights[o, p, i, n].wait_recv()
        have = held(o, p, i, left(p, i)[n])
        got = sums.at[o, slot_of(i, n), parts[p]]
        got[...] = (have[...].astype(F32) + got[...].astype(F32)).astype(BF16)
        if i + 1 < steps:
            if n < len(left(p, i + 1)):
                cross(o, p, i + 1, n)
        elif o:
            copy = pltpu.make_async_remote_copy(
                src_ref=got,
                dst_ref=others.at[o - 1, parts[p]],
                send_sem=z_send.at[o - 1, p],
                recv_sem=z_recv.at[o - 1, p],
                device_id=(d, lax.rem(l + o, lats)),
                device_id_type=MESH,
            )
            copy.start()
            sent.append(copy)
            z[o, p] = copy

    turns = list(range(1, lats)) + [0]
    for o in turns:
        for n in range(len(left(0, 0))):
            for p in range(2):
                cross(o, p, 0, n)
    for wave in range(lats + steps - 1):
        for i in range(steps):
            if 0 <= wave - i < lats:
                if i:
                    for _ in range(ASIDE):
                        next(aside, None)
                for n in range(len(left(0, i))):
                    for p in range(2):
                        add(turns[wave - i], p, i, n)
    for _ in aside:
        pass
    vector_rows((first_sums, second_sums), tiny, first)

    def to_owner(n):
        return pltpu.make_async_remote_copy(
            src_ref=tiny,
            dst_ref=landed.at[n],
            send_sem=tiny_send,
            recv_sem=tiny_recv.at[n],
            device_id=owner,
            device_id_type=MESH,
        )

    @pl.when(jnp.logical_not(mine))
    def _():
        to_owner(d * lats + l).start()

    for p in range(2):
        total = sums[0, slot_of(steps - 1, 0), parts[p]].astype(F32)
        for o in range(1, lats):
            z[o, p].wait_recv()
            total = total + others[o - 1, parts[p]].astype(F32)
        out[parts[p]] = total

    @pl.when(mine)
    def _():
        total = tiny[...]
        for a, b in senders:
            to_owner(a * lats + b).wait_recv()
            total = total + landed[a * lats + b]
        out[row : row + count, :] = out[row : row + count, :] + total

    @pl.when(jnp.logical_not(mine))
    def _():
        to_owner(d * lats + l).wait_send()

    for copy in sent:
        copy.wait_send()


def scatter(packed, lines, x, gconv, own, lo, hi, gain, second_sums, width):
    dates, lats, rows, lanes = packed.shape
    slots = dates - 1
    tiny = (vector_home(lines, lats)[3], LANES)
    anywhere, held = pl.BlockSpec(memory_space=pl.ANY), pl.BlockSpec(memory_space=pltpu.VMEM)
    low = pltpu.VMEM((CP, WIDE), BF16)
    row_buffers = [low, low, pltpu.VMEM((CP, WIDE), F32), low, low, low]
    return pl.pallas_call(
        functools.partial(scatter_kernel, dates, lats, lines, width),
        in_specs=[held] + [anywhere] * 5 + [held] * 2,
        out_specs=[held, anywhere],
        out_shape=(jax.ShapeDtypeStruct((rows, lanes), F32), jax.ShapeDtypeStruct(x.shape, BF16)),
        scratch_shapes=[
            pltpu.VMEM((lats, slots, rows, lanes), BF16),
            pltpu.VMEM((lats - 1, rows, lanes), BF16),
            pltpu.SemaphoreType.DMA((lats - 1, 2)),
            pltpu.SemaphoreType.DMA((lats - 1, 2)),
            pltpu.SemaphoreType.DMA((lats, 2, slots)),
            pltpu.SemaphoreType.DMA((lats, 2, slots)),
            pltpu.VMEM((2, CP, LANES), F32),
            pltpu.VMEM(tiny, F32),
            pltpu.VMEM((dates * lats,) + tiny, F32),
            pltpu.SemaphoreType.DMA(()),
            pltpu.SemaphoreType.DMA((dates * lats,)),
            pltpu.SemaphoreType.DMA((2, 5)),
            pltpu.SemaphoreType.DMA((2,)),
        ]
        + row_buffers * 2,
        compiler_params=pltpu.CompilerParams(
            collective_id=1, has_side_effects=True, vmem_limit_bytes=VMEM
        ),
        name="scatter_grads",
    )(packed, x, gconv, own, lo, hi, gain, second_sums)


def local(inputs, noise, cotangent, params, psi, step_counts, pixel_mask, offsets, bases):
    samples, steps, rows, width, _ = inputs.shape
    slabs = samples * steps
    dates, lats = lax.axis_size("date"), lax.axis_size("lat")
    lat = rows * lats

    def by_channel(values):
        return jnp.swapaxes(values, 3, 4).reshape(slabs, rows, -1, width)

    def padded(values):
        return jnp.pad(values, ((0, 0), (0, 0), (0, CP - values.shape[2]), (0, WIDE - width)))

    upward = [(i, i + 1) for i in range(lats - 1)]
    downward = [(i + 1, i) for i in range(lats - 1)]
    lines = params.shape[0] // LANES
    held = -(-lines // STEP) * STEP
    shard = jnp.pad(params.reshape(lines, LANES), ((0, held - lines), (0, 0)))
    x = padded(jnp.concatenate([by_channel(inputs), by_channel(noise)], axis=2))
    edges = [(x[s, rows - 1 :], x[s, :1]) for s in range(slabs)]
    gathered, moved, small = gather(shard, x, lines, dates, lats, width)
    gathered = gathered.reshape(dates * lats, held, LANES)
    cot = padded(by_channel(cotangent)).reshape(slabs * rows, CP, WIDE)
    active = jnp.arange(steps, dtype=jnp.int32)[None, :] < step_counts[:, None]
    mask = active.reshape(slabs, 1, 1) * pixel_mask[None]
    mask = jnp.pad(mask.astype(F32), ((0, 0), (0, 0), (0, WIDE - width)))
    matrices = unpack(gathered, lines)
    halos, done = [], gathered
    for s in range(slabs):
        top, bottom, done = lax.optimization_barrier((*edges[s], done))
        halos.append((lax.ppermute(top, "lat", upward), lax.ppermute(bottom, "lat", downward)))
        done = halos[-1], matrices
    matrices = done[1]
    basis = ()
    for s in range(slabs):
        basis = (lift(offsets, bases, psi, *halos[s], moved, small[0], small[1], basis, s, lat, width),)
    basis = basis[0]
    w, wt, up, upt, dn, dnt = matrices
    basis = basis.reshape(slabs * rows, BASIS * CP, WIDE)
    output, gconv, gup, gdn, second_sums = block(
        basis, x.reshape(slabs * rows, CP, WIDE), cot, mask.reshape(slabs * rows, 1, WIDE),
        wt, upt, up, dnt, dn, small[2], small[3],
    )
    gconv_rows = gconv.reshape(slabs, rows, CP, WIDE)
    own, to_below, to_above = lower(offsets, bases, psi, gconv_rows, w, width)
    from_below = lax.ppermute(to_above, "lat", upward)
    from_above = lax.ppermute(to_below, "lat", downward)
    gdisco = weight_grad(basis, gconv)
    packed = pack(gdisco, gup, gdn, dates * lats, lines, held)
    summed, grad = scatter(
        packed.reshape(dates, lats, held, LANES), lines,
        x, gconv_rows, own, from_below, from_above, small[0], second_sums, width,
    )

    def by_pixel(values):
        values = values.reshape(slabs, rows, CP, WIDE)[:, :, :C, :width]
        return jnp.swapaxes(values.reshape(samples, steps, rows, C, width), 3, 4)

    return by_pixel(output), by_pixel(grad), summed[:lines].reshape(-1)


def solution(mesh):
    field = P("date", None, "lat", None, None)
    flat = P(("date", "lat"))
    return jax.shard_map(
        local,
        mesh=mesh,
        in_specs=(field, field, field, flat, P(), P("date"), P("lat", None), P(), P()),
        out_specs=(field, field, flat),
        check_vma=False,
    )
```

```python
import functools
import math

import jax
import jax.numpy as jnp
from jax import lax
from jax.experimental import pallas as pl
from jax.experimental.pallas import tpu as pltpu
from jax.sharding import PartitionSpec as P

C = 641
HID = 1282
BASIS = 4
SUPPORT = 12
REACH = 2
CIN = 649
BF16, F32 = jnp.bfloat16, jnp.float32
MESH = pl.DeviceIdType.MESH
LANES = 128
STEP = 16
CP = 656
HP = 1296
WIDE = 768
HL = 1408
UNROLL = 8
ASIDE = 2
VMEM = 60 << 20


OFF_G1=BASIS*CIN*C+C; OFF_S1=OFF_G1+CIN; OFF_G2=OFF_S1+CIN; OFF_S2=OFF_G2+C; OFF_UP=OFF_S2+C; OFF_DN=OFF_UP+(C+1)*HID;
SMALL=((OFF_G1,CIN),(OFF_S1,CIN),(OFF_G2,C),(OFF_S2,C))
MATS=((0,C,BASIS*CIN+1,128,3),(OFF_UP,HID,C+1,64,2),(OFF_DN,C,HID+1,128,2))
F_ROWS=29952
def lane_ids(): return lax.broadcasted_iota(jnp.int32,(8,LANES),1)
def place(base,cols,period,b):
    start=base+cols*b
    return start//LANES, start%LANES
def rolled(values, amount):
    out = []
    for n in range(0, len(values), 2):
        pieces = values[n : n + 2]
        if len(pieces) == 2:
            both = jnp.concatenate(pieces, axis=0).astype(BF16)
            both = pltpu.roll(both, amount, axis=1).astype(F32)
            out += [both[:8], both[8:]]
        else:
            out.append(pltpu.roll(pieces[0].astype(BF16).astype(F32), amount, axis=1))
    return out


def flatten(lists):
    return [value for values in lists for value in values]


def unflat(values, width):
    return [values[n : n + width] for n in range(0, len(values), width)]


def unpack_kernel(nrow,pad, g_ref, w_ref,wt_ref,up_ref,upt_ref,dn_ref,dnt_ref,flat,chunks):
    def fill(s,_):
        flat[pl.ds(nrow*s,pad),:]=g_ref[s].astype(F32); return 0
    lax.fori_loop(0,g_ref.shape[0],fill,0)
    lane=lane_ids()
    def split(base,cols,period,groups):
        J=-(-cols//LANES); pitch=period+8; height=pitch*8*groups+8; last=cols-(J-1)*LANES
        def body(b,_):
            row,s=place(base,cols,period,b)
            back=(LANES-s)%LANES
            found=[[flat[pl.ds(row+641*8*g+j,8,stride=641),:] for g in range(groups)] for j in range(J+1)]
            found=unflat(rolled(flatten(found),back),groups)
            for g in range(groups):
                for j in range(J):
                    val=jnp.where(lane<LANES-s,found[j][g],found[j+1][g])
                    if j==J-1: val=jnp.where(lane<last,val,0.0)
                    chunks[pl.ds(j*height+8*g*pitch+b,8,stride=pitch),:]=val
            return 0
        lax.fori_loop(0,period,body,0,unroll=8)
        def border(a,_):
            for j in range(J): chunks[pl.ds(j*height+a*pitch-8,8),:]=chunks[pl.ds(j*height+a*pitch,8),:]
            return 0
        lax.fori_loop(1,8*groups,border,0)
        return J,height,period
    def convert(dst,dst_row,src_row,rows,pad_rows,J,height,period):
        full=rows//16
        def piece(j,r): return chunks[pl.ds(j*height+r//period*(period+8)+r%period,8),:]
        def pair(j,r): return jnp.concatenate([piece(j,r),piece(j,r+8)],axis=0)
        def body(m,_):
            for j in range(J):
                dst[pl.ds(pl.multiple_of(dst_row+16*m,16),16),j*LANES:(j+1)*LANES]=pair(j,src_row+16*m).astype(BF16)
            return 0
        lax.fori_loop(0,full,body,0,unroll=4)
        keep=lax.broadcasted_iota(jnp.int32,(16,LANES),0)<rows-16*full
        for m in range(full,pad_rows//16):
            for j in range(J):
                v=jnp.where(keep,pair(j,src_row+16*m),0.0) if m==full else jnp.zeros((16,LANES),F32)
                dst[dst_row+16*m:dst_row+16*m+16,j*LANES:(j+1)*LANES]=v.astype(BF16)
    J,h,p=split(*MATS[0][:2],*MATS[0][3:])
    for k in range(BASIS):
        convert(w_ref,k*CP,k*CIN,CIN+(k==BASIS-1),CP,J,h,p)
    J,h,p=split(*MATS[1][:2],*MATS[1][3:])
    convert(up_ref,0,0,C+1,CP,J,h,p)
    J,h,p=split(*MATS[2][:2],*MATS[2][3:])
    convert(dn_ref,0,0,HID+1,HP,J,h,p)
    wt_ref[...]=w_ref[:,:CP].T
    upt_ref[...]=up_ref[:,:HP].T
    dnt_ref[...]=dn_ref[:,:CP].T
def unpack(gathered,nrow):
    n,pad,_=gathered.shape
    return pl.pallas_call(functools.partial(unpack_kernel,nrow,pad),
        out_shape=(jax.ShapeDtypeStruct((BASIS*CP,WIDE),BF16),jax.ShapeDtypeStruct((CP,BASIS*CP),BF16),
            jax.ShapeDtypeStruct((CP,HL),BF16),jax.ShapeDtypeStruct((HP,CP),BF16),
            jax.ShapeDtypeStruct((HP,WIDE),BF16),jax.ShapeDtypeStruct((CP,HP),BF16)),
        scratch_shapes=[pltpu.VMEM((F_ROWS,LANES),F32),pltpu.VMEM((6*(136*24+8),LANES),F32)],
        compiler_params=pltpu.CompilerParams(vmem_limit_bytes=VMEM),name="unpack")(gathered)
def chunk_gather(src, chunks, src_row, dst_row, rows, J, height, last, period):
    lane, sub = lane_ids(), lax.broadcasted_iota(jnp.int32, (8, LANES), 0)

    def step(m):
        at = dst_row + 8 * m
        at = at // period * (period + 8) + at % period
        for j in range(J):
            v = src[pl.ds(src_row + 8 * m, 8), j * LANES : (j + 1) * LANES]
            if j == J - 1:
                v = jnp.where(lane < last, v, 0.0)
            if isinstance(m, int) and 8 * m + 8 > rows:
                v = jnp.where(sub < rows - 8 * m, v, 0.0)
            chunks[pl.ds(j * height + at + 8, 8), :] = v
            chunks[pl.ds(j * height + at, 8), :] = v

    return step


def chunk_clear(chunks, J, height, row, period):
    row = row // period * (period + 8) + row % period

    def body(m, _):
        for j in range(J):
            chunks[pl.ds(j * height + row + 8 * m, 8), :] = jnp.zeros((8, LANES), F32)
        return 0

    lax.fori_loop(0, (height - row) // 8, body, 0)


def line_merge(flat, flat0, chunks, base, cols, period, groups):
    lane, sub = lane_ids(), lax.broadcasted_iota(jnp.int32, (8, LANES), 0)
    J, pitch = -(-cols // LANES), period + 8
    height = pitch * 8 * groups + 8
    row0 = base // LANES - flat0

    def step(b, tails, last=False):
        row, s = place(base, cols, period, b)
        row = row - flat0
        found = [
            chunks[pl.ds(j * height + 8 * g * pitch + b, 8, stride=pitch), :]
            for g in range(groups)
            for j in range(J)
        ]
        found = unflat(rolled(found, s), J)
        new = []
        keep = lane >= s
        for g in range(groups):
            x = found[g]
            for j in range(J):
                v = jnp.where(keep, x[j], tails[g] if j == 0 else x[j - 1])
                if not (last and j == J - 1):
                    flat[pl.ds(row + 641 * 8 * g + j, 8, stride=641), :] = v
            new.append(jnp.where(s == LANES - 1, jnp.where(keep, 0.0, x[J - 1]), v))
        return tuple(new)

    def first():
        init = [jnp.zeros((8, LANES), F32)] * groups
        if base == OFF_DN:
            init[0] = jnp.where(sub == 0, flat[row0 : row0 + 8, :], 0.0)
        return tuple(init)

    def finish(tails):
        if base % LANES:
            for g in range(groups):
                at = pl.ds(row0 + 641 * (8 * g + 1), 8, stride=641)
                flat[at, :] = flat[at, :] + tails[g]

    return step, first, finish


FFN_ROW = OFF_UP // LANES // 8 * 8
FFN_ROWS = OFF_DN // LANES + 641 * 16 + 40 - FFN_ROW
DISCO_ROWS = 641 * 24 + 16


def grads_kernel(nrow, basis, gconv, gup, gdn, out, *refs):
    low, conv, gd, flat, ffn, chunks, gu, gn, stage, in_sems, ffn_sems, out_sems = refs
    count = basis.shape[0]
    shards, pad = out.shape[:2]

    def loads(i):
        return [
            pltpu.make_async_copy(basis.at[i], low.at[i % 2], in_sems.at[i % 2, 0]),
            pltpu.make_async_copy(gconv.at[i], conv.at[i % 2], in_sems.at[i % 2, 1]),
        ]

    weights = [pltpu.make_async_copy(a, b, ffn_sems.at[n]) for n, (a, b) in enumerate(((gup, gu), (gdn, gn)))]
    flying = {}
    for i in range(min(2, count)):
        flying[i] = loads(i)
        for copy in flying[i]:
            copy.start()
        weights[i].start()

    def outer(i, n):
        if n == 0:
            for copy in flying[i]:
                copy.wait()
        at = slice(n * CP, (n + 1) * CP)
        term = lax.dot_general(
            low[i % 2, at, :], conv[i % 2], (((1,), (1,)), ((), ())), preferred_element_type=F32
        )
        if i:
            gd[at, :CP] += term
        else:
            gd[at, :CP] = term
        if n == BASIS - 1 and i + 2 < count:
            flying[i + 2] = loads(i + 2)
            for copy in flying[i + 2]:
                copy.start()

    def lay(n, src, rows, J, height, last, base, cols, period, groups):
        state = {}
        copy = chunk_gather(src, chunks, 0, 0, rows, J, height, last, period)
        step, first, finish = line_merge(ffn, FFN_ROW, chunks, base, cols, period, groups)
        pieces = -(-rows // 8)

        def begin():
            weights[n].wait()

        def gather(start):
            for m in range(start, min(start + 4, pieces)):
                copy(m)

        def ready():
            chunk_clear(chunks, J, height, 8 * pieces, period)
            state["tails"] = first()

        def merge(b):
            state["tails"] = step(b, state["tails"], last=base % LANES and b == period - 1)

        def done():
            finish(state["tails"])

        steps = [begin] + [functools.partial(gather, m) for m in range(0, pieces, 4)] + [ready]
        return steps + [functools.partial(merge, b) for b in range(period)] + [done]

    products = [functools.partial(outer, i, n) for i in range(count) for n in range(BASIS)]
    for n in range(2):
        if n >= count:
            weights[n].start()
    up_steps = lay(0, gu, C + 1, 11, 72 * 16 + 8, 2, OFF_UP, HID, 64, 2)
    down_steps = lay(1, gn, HID + 1, 6, 136 * 16 + 8, 1, OFF_DN, C, 128, 2)
    weave(products, up_steps + down_steps)

    height = 136 * 24 + 8
    for k in range(BASIS):
        rows = CIN + (k == BASIS - 1)
        copy = chunk_gather(gd, chunks, k * CP, k * CIN, rows, 6, height, 1, 128)

        def body(m, _):
            copy(m)
            return 0

        lax.fori_loop(0, rows // 8, body, 0, unroll=4)
        copy(rows // 8)
    chunk_clear(chunks, 6, height, 2600, 128)
    step, first, _ = line_merge(flat, 0, chunks, 0, C, 128, 3)
    lax.fori_loop(0, 128, step, first(), unroll=8)
    seam = OFF_UP // LANES
    for shard in range(shards):
        if nrow * shard < seam < nrow * shard + pad:
            amount = nrow * shard + pad - seam
            flat[seam : seam + amount, :] = ffn[seam - FFN_ROW : seam - FFN_ROW + amount, :]
    slots = stage.shape[0]

    def save(shard, slot):
        return pltpu.make_async_copy(stage.at[slot], out.at[shard], out_sems.at[slot])

    for shard in range(shards):
        slot = shard % slots
        if shard >= slots:
            save(shard - slots, slot).wait()
        source, start = (flat, nrow * shard) if nrow * shard < seam else (ffn, nrow * shard - FFN_ROW)
        stage[slot] = source[start : start + pad, :].astype(BF16)
        save(shard, slot).start()
    for shard in range(max(shards - slots, 0), shards):
        save(shard, shard % slots).wait()


def grads(basis, gconv, gup, gdn, n, nrow, pad):
    anywhere = pl.BlockSpec(memory_space=pl.ANY)
    return pl.pallas_call(
        functools.partial(grads_kernel, nrow),
        in_specs=[anywhere] * 4,
        out_specs=anywhere,
        out_shape=jax.ShapeDtypeStruct((n, pad, LANES), BF16),
        scratch_shapes=[
            pltpu.VMEM((2, BASIS * CP, WIDE), BF16),
            pltpu.VMEM((2, CP, WIDE), BF16),
            pltpu.VMEM((BASIS * CP, WIDE), F32),
            pltpu.VMEM((DISCO_ROWS, LANES), F32),
            pltpu.VMEM((FFN_ROWS, LANES), F32),
            pltpu.VMEM((6 * (136 * 24 + 8), LANES), F32),
            pltpu.VMEM(gup.shape, F32),
            pltpu.VMEM(gdn.shape, F32),
            pltpu.VMEM((4, pad, LANES), BF16),
            pltpu.SemaphoreType.DMA((2, 2)),
            pltpu.SemaphoreType.DMA((2,)),
            pltpu.SemaphoreType.DMA((4,)),
        ],
        compiler_params=pltpu.CompilerParams(vmem_limit_bytes=VMEM),
        name="grads",
    )(basis, gconv, gup, gdn)


def tiled(column):
    return jnp.concatenate([column] * (WIDE // LANES), axis=1)


def lane_of(rows, start=0):
    return lax.broadcasted_iota(jnp.int32, (rows, LANES), 1) + start


def wrapped(chunk, width):
    head, first, last = chunk[:, : WIDE - LANES], chunk[:, :LANES], chunk[:, WIDE - LANES :]
    edge = width - (WIDE - LANES)
    lane = lane_of(chunk.shape[0])
    beyond = jnp.where(
        lane < LANES - REACH, pltpu.roll(first, edge, axis=1), pltpu.roll(last, LANES - edge, axis=1)
    )
    return jnp.concatenate([head, jnp.where(lane < edge, last, beyond)], axis=1)


def cut(chunk, width):
    head, last = chunk[:, : WIDE - LANES], chunk[:, WIDE - LANES :]
    keep = lane_of(chunk.shape[0], WIDE - LANES) < width
    return jnp.concatenate([head, jnp.where(keep, last, 0.0)], axis=1)


def rows_below(count):
    return lax.broadcasted_iota(jnp.int32, (STEP, WIDE), 0) < count


def halves(chunk):
    return chunk[:8] + chunk[8:]


def column_sums(read, channels, count):
    whole = channels // STEP

    def body(m, sums):
        return tuple(a + halves(v) for a, v in zip(sums, read(m)))

    sums = lax.fori_loop(
        0, whole, body, tuple(jnp.zeros((8, WIDE), F32) for _ in range(count)), unroll=UNROLL
    )
    keep = rows_below(channels - whole * STEP)
    sums = [a + halves(jnp.where(keep, v, 0.0)) for a, v in zip(sums, read(whole))]
    return [jnp.sum(a, axis=0, keepdims=True) for a in sums]


def norm_stats(read, channels):
    (total,) = column_sums(lambda m: (read(m),), channels, 1)
    mean = total * (1.0 / channels)

    def squares(m):
        centered = read(m) - mean
        return (centered * centered,)

    (total,) = column_sums(squares, channels, 1)
    return mean, lax.rsqrt(total * (1.0 / channels) + 1e-05)


def each_chunk(body, unroll=None):
    def step(m, _):
        body(m, pl.ds(pl.multiple_of(m * STEP, STEP), STEP))
        return 0

    lax.fori_loop(0, CP // STEP, step, 0, unroll=unroll)


def spread(source, gain, shift, width, moved):
    def read(c):
        return source[pl.ds(pl.multiple_of(c * STEP, STEP), STEP), :].astype(F32)

    mean, scale = norm_stats(read, CIN)

    def shifts(c, at):
        values = (read(c) - mean) * scale * tiled(gain[at, :]) + tiled(shift[at, :])
        values = wrapped(values, width).astype(BF16)
        for d in range(-REACH, REACH + 1):
            moved[d + REACH, at, :] = pltpu.roll(values, -d % WIDE, axis=1) if d else values

    each_chunk(shifts, 4)


def lift_kernel(
    rows, slab, lat, width, offsets, bases, psi, lo, hi, own, gain, shift, *refs
):
    out, moved, table, sems = refs[-4:]
    first_row = lax.axis_index("lat") * rows
    copies = [
        pltpu.make_async_copy(own.at[slab, r], moved.at[r + 1], sems.at[r]) for r in range(rows)
    ]
    for copy in copies:
        copy.start()
    for k in range(BASIS):
        table[SUPPORT + k] = 0
    for p in range(SUPPORT):
        k = bases[p]
        used = table[SUPPORT + k]
        table[k * 3 + used] = p
        table[SUPPORT + k] = used + 1
    for source, m in ((lo, 0), (hi, rows + 1)):
        spread(source.at[0], gain, shift, width, moved.at[m])
    for copy in copies:
        copy.wait()
    for r in range(rows):
        for k in range(BASIS):
            parts = []
            for q in range(3):
                p = table[k * 3 + q]
                row = first_row + r + offsets[p, 0]
                inside = jnp.logical_and(row >= 0, row < lat)
                weight = jnp.where(inside, psi[first_row + r, p], 0.0)
                parts.append((weight, r + 1 + offsets[p, 0], offsets[p, 1] + REACH))

            def combine(c, at):
                total = None
                for weight, row, d in parts:
                    term = weight * moved[row, d, at, :].astype(F32)
                    total = term if total is None else total + term
                to = pl.ds(pl.multiple_of(k * CP + c * STEP, STEP), STEP)
                out[0, r, to, :] = cut(total, width).astype(BF16)

            each_chunk(combine, 4)
        last = slice(BASIS * CP - STEP, BASIS * CP)
        bias_row = CIN - (CP - STEP)
        sub = lax.broadcasted_iota(jnp.int32, (STEP, WIDE), 0)
        lane = lax.broadcasted_iota(jnp.int32, (STEP, WIDE), 1)
        ones = jnp.where(lane < width, 1.0, 0.0)
        out[0, r, last, :] = jnp.where(sub == bias_row, ones, out[0, r, last, :].astype(F32)).astype(BF16)


def lift(offsets, bases, psi, lo, hi, own, gain, shift, before, slab, lat, width):
    slabs, rows = own.shape[:2]
    smem = pl.BlockSpec(memory_space=pltpu.SMEM)
    anywhere = pl.BlockSpec(memory_space=pl.ANY)
    halo = pl.BlockSpec((1, CP, WIDE), lambda s: (0, 0, 0))
    column = pl.BlockSpec((CP, LANES), lambda s: (0, 0))
    return pl.pallas_call(
        functools.partial(lift_kernel, rows, slab, lat, width),
        grid=(1,),
        in_specs=[smem, smem, smem, halo, halo, anywhere, column, column] + [anywhere] * len(before),
        out_specs=pl.BlockSpec((1, rows, BASIS * CP, WIDE), lambda s: (slab, 0, 0, 0)),
        out_shape=jax.ShapeDtypeStruct((slabs, rows, BASIS * CP, WIDE), BF16),
        scratch_shapes=[
            pltpu.VMEM((rows + 2, 2 * REACH + 1, CP, WIDE), BF16),
            pltpu.SMEM((SUPPORT + BASIS,), jnp.int32),
            pltpu.SemaphoreType.DMA((rows,)),
        ],
        input_output_aliases={8: 0} if before else {},
        compiler_params=pltpu.CompilerParams(vmem_limit_bytes=VMEM),
        cost_estimate=pl.CostEstimate(flops=40 << 20, bytes_accessed=40 << 20, transcendentals=0),
        name="lift",
    )(offsets, bases, psi, lo, hi, own, gain, shift, *before)


GELU_A = math.sqrt(2.0 / math.pi)
GELU_B = 0.044715


TILE = 256


def weave(*lists):
    order = []
    for which, steps in enumerate(lists):
        for n, step in enumerate(steps):
            order.append(((n + 0.5) / len(steps), which, n, step))
    for _, _, _, step in sorted(order, key=lambda entry: entry[:3]):
        step()


class Job:
    def __init__(self, buffers, weights, totals, mask):
        self.basis, self.x, self.cot, self.out, self.gconv = buffers[:5]
        self.res, self.second, self.pre, self.act, self.mid, self.gact, self.gb, self.gpre = buffers[5:]
        self.wt, self.upt, self.up, self.dnt, self.dn, self.gain, self.shift = weights
        self.gup, self.gdn, self.sums = totals
        self.mask = mask

    @staticmethod
    def at(c):
        return slice(c * STEP, (c + 1) * STEP)

    @staticmethod
    def wide(column):
        return jnp.concatenate([column] * (TILE // LANES), axis=1)

    @staticmethod
    def only(c, values, channels, other=0.0):
        if (c + 1) * STEP <= channels:
            return values
        row = lax.broadcasted_iota(jnp.int32, (STEP, TILE), 0)
        return jnp.where(row < channels - c * STEP, values, other)

    def product(self, out, left, right, count):
        rows = left.shape[0]
        size = -(-rows // (count * STEP)) * STEP

        def step(start):
            at = slice(start, min(start + size, rows))
            values = left[at, : right.shape[0]]
            out[at, :] = jnp.dot(values, right[...], preferred_element_type=F32)

        return [functools.partial(step, start) for start in range(0, rows, size)]

    def outer(self, out, left, right, count):
        rows = left.shape[0]
        size = -(-rows // (count * STEP)) * STEP

        def step(start):
            at = slice(start, min(start + size, rows))
            term = lax.dot_general(
                left[at, :], right[...], (((1,), (1,)), ((), ())), preferred_element_type=F32
            )
            out[at, : right.shape[0]] += term

        return [functools.partial(step, start) for start in range(0, rows, size)]

    def m1(self):
        return self.product(self.res, self.wt, self.basis, 4)

    def v1(self):
        state = {"sum": jnp.zeros((8, TILE), F32), "square": jnp.zeros((8, TILE), F32)}
        mask = self.mask()

        def add(c):
            at = self.at(c)
            value = self.res[at, :] + self.only(c, self.x[at, :].astype(F32), C)
            self.res[at, :] = value
            self.gb[at, :] = (self.cot[at, :].astype(F32) * mask).astype(BF16)
            state["sum"] = state["sum"] + halves(self.only(c, value, C))

        def mean():
            self.mean = jnp.sum(state["sum"], axis=0, keepdims=True) * (1.0 / C)

        def square(c):
            value = self.res[self.at(c), :] - self.mean
            state["square"] = state["square"] + halves(self.only(c, value * value, C))

        def scale():
            total = jnp.sum(state["square"], axis=0, keepdims=True)
            self.scale = lax.rsqrt(total * (1.0 / C) + 1e-05)

        def normalize(c):
            at = self.at(c)
            value = (self.res[at, :] - self.mean) * self.scale
            value = value * self.wide(self.gain[at, :]) + self.wide(self.shift[at, :])
            row = lax.broadcasted_iota(jnp.int32, (STEP, TILE), 0)
            if c == C // STEP:
                value = jnp.where(row == C % STEP, 1.0, value)
            self.second[at, :] = value.astype(BF16)

        chunks = range(CP // STEP)
        steps = [functools.partial(add, c) for c in chunks] + [mean]
        steps += [functools.partial(square, c) for c in chunks] + [scale]
        return steps + [functools.partial(normalize, c) for c in chunks]

    def m2(self):
        return self.product(self.pre, self.upt, self.second, 9)

    def v2(self):
        def gelu(c):
            at = self.at(c)
            v = self.pre[at, :]
            square = v * v
            bend = jnp.tanh(GELU_A * v * (1.0 + GELU_B * square))
            half = 0.5 * (1.0 + bend)
            value = v * half
            if c == HID // STEP:
                row = lax.broadcasted_iota(jnp.int32, (STEP, TILE), 0)
                value = jnp.where(row == HID % STEP, 1.0, value)
            self.act[at, :] = value.astype(BF16)
            rise = GELU_A * (1.0 + 3.0 * GELU_B * square)
            self.pre[at, :] = half + 0.5 * v * (1.0 - bend * bend) * rise

        return [functools.partial(gelu, c) for c in range(HP // STEP)]

    def m3(self):
        back = self.product(self.gact, self.dn, self.gb, 9)
        return self.product(self.mid, self.dnt, self.act, 4) + back

    def v3(self):
        def finish(c):
            at = self.at(c)
            self.out[at, :] = (self.res[at, :] + self.mid[at, :]).astype(BF16)

        def back(c):
            at = self.at(c)
            self.gpre[at, :] = (self.gact[at, :] * self.pre[at, :]).astype(BF16)

        steps = [functools.partial(finish, c) for c in range(CP // STEP)]
        return steps + [functools.partial(back, c) for c in range(HP // STEP)]

    def m4(self):
        return self.product(self.mid, self.up, self.gpre, 4)

    def v4(self):
        state = {"flat": jnp.zeros((8, TILE), F32), "along": jnp.zeros((8, TILE), F32)}

        def terms(c):
            at = self.at(c)
            dm = self.mid[at, :]
            xhat = (self.res[at, :] - self.mean) * self.scale
            return dm, xhat, dm * self.wide(self.gain[at, :])

        def means(c):
            _, xhat, g = terms(c)
            g = self.only(c, g, C)
            state["flat"] = state["flat"] + halves(g)
            state["along"] = state["along"] + halves(g * xhat)

        def join():
            for name in state:
                state[name] = jnp.sum(state[name], axis=0, keepdims=True) * (1.0 / C)

        def backward(c):
            at = self.at(c)
            dm, xhat, g = terms(c)
            value = g - state["flat"] - xhat * state["along"]
            value = self.gb[at, :].astype(F32) + self.scale * value
            self.gconv[at, :] = self.only(c, value, C).astype(BF16)
            for n, term in enumerate((dm * xhat, dm)):
                self.sums[n, at, :] += term[:, :LANES] + term[:, LANES:]

        chunks = range(CP // STEP)
        steps = [functools.partial(means, c) for c in chunks] + [join]
        return steps + [functools.partial(backward, c) for c in chunks]

    def m5(self):
        first = self.outer(self.gdn, self.act, self.gb, 3)
        return first + self.outer(self.gup, self.second, self.gpre, 2)


def block_kernel(
    basis, x, cot, mask, wt, upt, up, dnt, dn, gain, shift, out, gconv, gup, gdn, sums, *scratch
):
    count = basis.shape[0]
    tiles = WIDE // TILE
    in_sems, out_sems = scratch[-2:]
    per_job = (len(scratch) - 2) // 2
    sets = [scratch[:per_job], scratch[per_job : 2 * per_job]]
    for total in (gup, gdn, sums):
        total[...] = jnp.zeros_like(total)

    def place(i, j):
        return i // tiles * 2 + j, pl.ds(pl.multiple_of(i % tiles * TILE, TILE), TILE)

    def arrive(i, j):
        row, lanes = place(i, j)
        return [
            pltpu.make_async_copy(source.at[row, :, lanes], sets[j][n], in_sems.at[j, n])
            for n, source in enumerate((basis, x, cot))
        ]

    def leave(i, j):
        row, lanes = place(i, j)
        return [
            pltpu.make_async_copy(sets[j][3 + n], target.at[row, :, lanes], out_sems.at[j, n])
            for n, target in enumerate((out, gconv))
        ]

    last = count // 2 * tiles - 1
    for j in range(2):
        for copy in arrive(0, j):
            copy.start()

    def pair(i, _):
        def row_mask(j):
            row, lanes = place(i, j)
            return lambda: mask[row, :, lanes]

        weights, totals = (wt, upt, up, dnt, dn, gain, shift), (gup, gdn, sums)
        a, b = (Job(sets[j], weights, totals, row_mask(j)) for j in range(2))
        after = jnp.minimum(i + 1, last)
        coming = [arrive(after, j) for j in range(2)]
        leaving = [leave(i, j) for j in range(2)]
        for j in range(2):
            for copy in arrive(i, j):
                copy.wait()
        weave(a.m1())
        coming[0][0].start()
        weave(a.v1(), b.m1())
        coming[1][0].start()
        for n in (1, 2):
            coming[0][n].start()
        weave(a.m2(), b.v1())
        for n in (1, 2):
            coming[1][n].start()
        weave(a.v2(), b.m2())
        weave(a.m3(), b.v2())
        weave(a.v3(), b.m3())
        leaving[0][0].start()
        weave(a.m4(), b.v3())
        leaving[1][0].start()
        weave(a.v4(), b.m4())
        leaving[0][1].start()
        weave(a.m5(), b.v4())
        leaving[1][1].start()
        weave(b.m5())
        for copies in leaving:
            for copy in copies:
                copy.wait()
        return 0

    lax.fori_loop(0, last + 1, pair, 0)
    for j in range(2):
        for copy in arrive(last, j):
            copy.wait()


def block(basis, x, cot, mask, wt, upt, up, dnt, dn, gain, shift):
    count = x.shape[0]
    anywhere = pl.BlockSpec(memory_space=pl.ANY)
    held = pl.BlockSpec(memory_space=pltpu.VMEM)
    low, high = pltpu.VMEM((CP, TILE), BF16), pltpu.VMEM((CP, TILE), F32)
    hidden_low, hidden_high = pltpu.VMEM((HP, TILE), BF16), pltpu.VMEM((HP, TILE), F32)
    per_job = [pltpu.VMEM((BASIS * CP, TILE), BF16), low, low, low, low]
    per_job += [high, low, hidden_high, hidden_low, high, hidden_high, low, hidden_low]
    return pl.pallas_call(
        block_kernel,
        in_specs=[anywhere] * 3 + [held] * 8,
        out_specs=[anywhere] * 2 + [held] * 3,
        out_shape=(
            jax.ShapeDtypeStruct((count, CP, WIDE), BF16),
            jax.ShapeDtypeStruct((count, CP, WIDE), BF16),
            jax.ShapeDtypeStruct((CP, HL), F32),
            jax.ShapeDtypeStruct((HP, WIDE), F32),
            jax.ShapeDtypeStruct((2, CP, LANES), F32),
        ),
        scratch_shapes=per_job * 2 + [pltpu.SemaphoreType.DMA((2, 3)), pltpu.SemaphoreType.DMA((2, 2))],
        compiler_params=pltpu.CompilerParams(vmem_limit_bytes=VMEM),
        name="block",
    )(basis, x, cot, mask, wt, upt, up, dnt, dn, gain, shift)


def along_lanes(ref, at, values):
    total = values[:, :LANES]
    for j in range(1, WIDE // LANES):
        total = total + values[:, j * LANES : (j + 1) * LANES]
    ref[at, :] = ref[at, :] + total


GROUP = 11 * STEP
GROUP_STEP = 10 * STEP


def lower_kernel(rows, width, offsets, bases, psi, gconv, w, own, lo, hi, *scratch):
    place, coef, in_sems, w_sems, out_sems = scratch[-5:]
    per_slab = (len(scratch) - 5) // 2
    sets = [scratch[:per_slab], scratch[per_slab : 2 * per_slab]]
    first_row = lax.axis_index("lat") * rows
    span = 2 * REACH + 1
    groups = 1 + (CP - GROUP) // GROUP_STEP
    for n in range(3 * span):
        place[n] = 0
        for r in range(rows):
            coef[r, n] = 0.0
    for p in range(SUPPORT):
        n = (offsets[p, 0] + 1) * span + offsets[p, 1] + REACH
        place[n] = bases[p]
        for r in range(rows):
            coef[r, n] = psi[first_row + r, p]

    def channels(g):
        return pl.ds(pl.multiple_of(g * GROUP_STEP, STEP), GROUP)

    def weights(j, g):
        return pltpu.make_async_copy(w.at[:, channels(g), :], sets[j][1], w_sems.at[j])

    def products(j):
        ring, part, lifted = sets[j][:3]

        def step(r, k):
            values = jnp.dot(part[k, :, :CP], ring[r], preferred_element_type=F32)
            lifted[r, k] = values.astype(BF16)

        return [functools.partial(step, r, k) for r in range(rows) for k in range(BASIS)]

    def gathers(j):
        lifted, inner, below, above = sets[j][2:]

        def step(c, target):
            at = slice(c * STEP, (c + 1) * STEP)
            total = None
            for d in range(-REACH, REACH + 1):
                part = None
                for o in (-1, 0, 1):
                    r = target - o
                    if 0 <= r < rows:
                        n = (o + 1) * span + d + REACH
                        term = coef[r, n] * lifted[r, place[n], at, :].astype(F32)
                        part = term if part is None else part + term
                if d:
                    part = pltpu.roll(part.astype(BF16), d % WIDE, axis=1).astype(F32)
                total = part if total is None else total + part
            if target < 0:
                below[at, :] = total.astype(BF16)
            elif target == rows:
                above[at, :] = total.astype(BF16)
            else:
                inner[target, at, :] = total

        return [functools.partial(step, c, t) for c in range(GROUP // STEP) for t in range(-1, rows + 1)]

    def pair_of_slabs(both, _):
        def leaving(j, g):
            slab = both * 2 + j
            targets = (own.at[slab, :, channels(g), :], lo.at[slab, channels(g), :], hi.at[slab, channels(g), :])
            return [
                pltpu.make_async_copy(sets[j][3 + n], target, out_sems.at[j, n])
                for n, target in enumerate(targets)
            ]

        rings = [pltpu.make_async_copy(gconv.at[both * 2 + j], sets[j][0], in_sems.at[j]) for j in range(2)]
        for j in range(2):
            rings[j].start()
            weights(j, 0).start()
        for j in range(2):
            rings[j].wait()
            ring = sets[j][0]
            edge = width - (WIDE - LANES)
            lane = lane_of(CP)
            for r in range(rows):
                first, last = ring[r, :, :LANES].astype(F32), ring[r, :, WIDE - LANES :].astype(F32)
                beyond = jnp.where(
                    lane < LANES - REACH,
                    pltpu.roll(first, edge, axis=1),
                    pltpu.roll(last, LANES - edge, axis=1),
                )
                ring[r, :, WIDE - LANES :] = jnp.where(lane < edge, last, beyond).astype(BF16)
        weights(0, 0).wait()
        weave(products(0))
        weights(0, min(1, groups - 1)).start()

        def group(g, _):
            after, later = jnp.minimum(g + 1, groups - 1), jnp.minimum(g + 2, groups - 1)
            def free(j):
                @pl.when(g > 0)
                def _():
                    for copy in leaving(j, jnp.maximum(g - 1, 0)):
                        copy.wait()

            weights(1, g).wait()
            free(0)
            weave(products(1), gathers(0))
            weights(1, after).start()
            for copy in leaving(0, g):
                copy.start()
            weights(0, after).wait()
            free(1)
            weave(products(0), gathers(1))
            weights(0, later).start()
            for copy in leaving(1, g):
                copy.start()
            return 0

        lax.fori_loop(0, groups, group, 0)
        for j in range(2):
            weights(j, groups - 1).wait()
            for copy in leaving(j, groups - 1):
                copy.wait()
        return 0

    lax.fori_loop(0, gconv.shape[0] // 2, pair_of_slabs, 0)


def lower(offsets, bases, psi, gconv, w, width):
    slabs, rows = gconv.shape[:2]
    smem = pl.BlockSpec(memory_space=pltpu.SMEM)
    anywhere = pl.BlockSpec(memory_space=pl.ANY)
    edge = jax.ShapeDtypeStruct((slabs, CP, WIDE), BF16)
    per_slab = [
        pltpu.VMEM((rows, CP, WIDE), BF16),
        pltpu.VMEM((BASIS, GROUP, WIDE), BF16),
        pltpu.VMEM((rows, BASIS, GROUP, WIDE), BF16),
        pltpu.VMEM((rows, GROUP, WIDE), F32),
        pltpu.VMEM((GROUP, WIDE), BF16),
        pltpu.VMEM((GROUP, WIDE), BF16),
    ]
    return pl.pallas_call(
        functools.partial(lower_kernel, rows, width),
        in_specs=[smem, smem, smem, anywhere, anywhere],
        out_specs=[anywhere] * 3,
        out_shape=(jax.ShapeDtypeStruct((slabs, rows, CP, WIDE), F32), edge, edge),
        scratch_shapes=per_slab * 2
        + [
            pltpu.SMEM((3 * (2 * REACH + 1),), jnp.int32),
            pltpu.SMEM((rows, 3 * (2 * REACH + 1)), F32),
            pltpu.SemaphoreType.DMA((2,)),
            pltpu.SemaphoreType.DMA((2,)),
            pltpu.SemaphoreType.DMA((2, 3)),
        ],
        compiler_params=pltpu.CompilerParams(vmem_limit_bytes=VMEM),
        name="lower",
    )(offsets, bases, psi, gconv, w.reshape(BASIS, CP, WIDE))


def input_rows(width, x, gconv, own, lo, hi, gain, grad, sums, buffers, in_sems, out_sems, arrived):
    rows = x.shape[1]
    places = [(s, r) for s in range(x.shape[0]) for r in range(rows)]
    saves = []

    def loads(n):
        s, r = places[n]
        sources = [x.at[s, r], gconv.at[s, r], own.at[s, r]]
        sources += [lo.at[0]] if r == 0 and s == 0 else []
        sources += [hi.at[0]] if r == rows - 1 and s == 0 else []
        slots = [0, 1, 2] + ([3] if r == 0 else []) + ([4] if r == rows - 1 else [])
        return [
            pltpu.make_async_copy(source, buffers[n % 2][slot], in_sems.at[n % 2, slot])
            for source, slot in zip(sources, slots)
        ]

    flying = loads(0)
    for copy in flying:
        copy.start()
    sums[...] = jnp.zeros_like(sums)
    for n, (s, r) in enumerate(places):
        for copy in flying:
            copy.wait()
        if n + 1 < len(places):
            flying = loads(n + 1)
            for copy in flying:
                copy.start()
        here, conv, total, below, above, result = buffers[n % 2]
        if s:
            below = arrived(s, 0) if r == 0 else None
            above = arrived(s, 1) if r == rows - 1 else None

        def read(c):
            return here[pl.ds(pl.multiple_of(c * STEP, STEP), STEP), :].astype(F32)

        mean, scale = norm_stats(read, CIN)
        yield

        if r == 0 or r == rows - 1:

            def join(c, at):
                value = total[at, :]
                if r == 0:
                    value = value + below[at, :].astype(F32)
                if r == rows - 1:
                    value = value + above[at, :].astype(F32)
                total[at, :] = value

            each_chunk(join, 8)
            yield

        def means(c):
            at = pl.ds(pl.multiple_of(c * STEP, STEP), STEP)
            g = total[at, :] * tiled(gain[at, :])
            return g, g * ((read(c) - mean) * scale)

        flat, along = [v * (1.0 / CIN) for v in column_sums(means, CIN, 2)]
        yield
        if n >= 2:
            saves[n - 2].wait()

        def backward(c, at):
            dm = cut(total[at, :], width)
            xhat = (read(c) - mean) * scale
            g = dm * tiled(gain[at, :])
            value = scale * (g - flat - xhat * along) + conv[at, :].astype(F32)
            result[at, :] = value.astype(BF16)
            along_lanes(sums.at[0], at, dm * xhat)
            along_lanes(sums.at[1], at, dm)

        each_chunk(backward, 8)
        save = pltpu.make_async_copy(result, grad.at[s, r], out_sems.at[n % 2])
        save.start()
        saves.append(save)
        yield
    for save in saves[-2:]:
        save.wait()


def flip(value, bit):
    return value + (1 - 2 * ((value // (1 << bit)) % 2)) * (1 << bit)


def flipped(value, mask):
    bit = 0
    while mask >> bit:
        if mask >> bit & 1:
            value = flip(value, bit)
        bit += 1
    return value


def span(bits):
    masks = [0]
    for b in bits:
        masks = masks + [m | 1 << b for m in masks]
    return masks


def orders(dates):
    bits = list(range(1, dates.bit_length() - 1))
    return bits + [0], bits[::-1] + [0]


def pieces(rows):
    cut = rows // (2 * STEP) * STEP
    return pl.ds(0, cut), pl.ds(cut, rows - cut)


def greet(dates, lats, d, l, owner):
    barrier = pltpu.get_barrier_semaphore()
    bits = range(dates.bit_length() - 1)
    peers = [(d, lax.rem(l + o, lats)) for o in range(1, lats)] + [(flip(d, b), l) for b in bits]
    for peer in peers:
        pl.semaphore_signal(barrier, inc=1, device_id=peer, device_id_type=MESH)
    next_to = [(owner[0], b) for b in range(lats) if b != owner[1]] + [(flip(owner[0], b), owner[1]) for b in bits]
    away = [(a, b) for a in range(dates) for b in range(lats) if (a, b) not in next_to + [owner]]
    mine = jnp.logical_and(d == owner[0], l == owner[1])
    near = functools.reduce(jnp.logical_or, [jnp.logical_and(d == a, l == b) for a, b in next_to])
    far = jnp.logical_not(jnp.logical_or(mine, near))

    @pl.when(mine)
    def _():
        for peer in away:
            pl.semaphore_signal(barrier, inc=1, device_id=peer, device_id_type=MESH)
        pl.semaphore_wait(barrier, len(peers) + len(away))

    @pl.when(near)
    def _():
        pl.semaphore_wait(barrier, len(peers))

    @pl.when(far)
    def _():
        pl.semaphore_signal(barrier, inc=1, device_id=owner, device_id_type=MESH)
        pl.semaphore_wait(barrier, len(peers) + 1)


def read_norms(landed, first, out):
    lane = lane_ids()
    sub = lax.broadcasted_iota(jnp.int32, (8, LANES), 0)
    lines = landed[...].astype(F32)
    for i, (off, n) in enumerate(SMALL):
        row, s = divmod(off - first * LANES, LANES)
        r = pltpu.roll(lines[row : row + 8], (LANES - s) % LANES, axis=1)
        v = jnp.where(lane < LANES - s, r, pltpu.roll(r, 7, axis=0))
        t = jnp.where(sub * LANES + lane < n, v, 0.0).T
        for j in range(6):
            rows = min(LANES, CP - j * LANES)
            out[i, j * LANES : j * LANES + rows, :] = jnp.broadcast_to(t[:rows, j : j + 1], (rows, LANES))


def norm_home(lines, lats):
    start, end = OFF_G1 // LANES, (OFF_UP - 1) // LANES + 3
    owner = start // lines
    row = (start - owner * lines) // STEP * STEP
    count = -(-(end - owner * lines - row) // STEP) * STEP
    assert row + count <= -(-lines // STEP) * STEP
    return divmod(owner, lats), owner * lines + row, row, count


def gather_kernel(
    dates, lats, lines, width, src, x, out, moved, small, local_sem, z_send, z_recv, send, recv,
    buffers, buffer_sems, landed, norm_sem, norm_send, norm_recv,
):
    d, l = lax.axis_index("date"), lax.axis_index("lat")
    steps = dates.bit_length() - 1
    parts = pieces(src.shape[0])
    owner, first, row, count = norm_home(lines, lats)
    mine = jnp.logical_and(d == owner[0], l == owner[1])
    others = [(a, b) for a in range(dates) for b in range(lats) if (a, b) != owner]
    window = src.at[pl.ds(row, count)]

    greet(dates, lats, d, l, owner)

    def norms_to(n):
        return pltpu.make_async_remote_copy(
            src_ref=window,
            dst_ref=landed,
            send_sem=norm_send.at[n],
            recv_sem=norm_recv,
            device_id=others[n],
            device_id_type=MESH,
        )

    @pl.when(mine)
    def _():
        for n in range(len(others)):
            norms_to(n).start()
        pltpu.make_async_copy(window, landed, norm_sem).start()

    own = pltpu.make_async_copy(src, out.at[d, l], local_sem)
    own.start()
    sent, arriving, flights = [], {}, {}

    def along(o):
        copy = pltpu.make_async_remote_copy(
            src_ref=src,
            dst_ref=out.at[d, l],
            send_sem=z_send.at[o - 1],
            recv_sem=z_recv.at[o - 1],
            device_id=(d, lax.rem(l + o, lats)),
            device_id_type=MESH,
        )
        copy.start()
        sent.append(copy)
        arriving[o] = copy

    def cross(o, p, i, n):
        order = orders(dates)[p]
        block = out.at[flipped(d, span(order[:i])[n]), lax.rem(l - o + lats, lats), parts[p]]
        slot = (1 << i) - 1 + n
        copy = pltpu.make_async_remote_copy(
            src_ref=src.at[parts[p]] if o == 0 and n == 0 else block,
            dst_ref=block,
            send_sem=send.at[o, p, slot],
            recv_sem=recv.at[o, p, slot],
            device_id=(flip(d, order[i]), l),
            device_id_type=MESH,
        )
        copy.start()
        sent.append(copy)
        flights[o, p, i, n] = copy

    rows = [(s, r) for s in range(x.shape[0]) for r in range(x.shape[1])]
    saves = []

    def spread_rows():
        @pl.when(mine)
        def _():
            pltpu.make_async_copy(window, landed, norm_sem).wait()

        @pl.when(jnp.logical_not(mine))
        def _():
            norms_to(0).wait_recv()

        read_norms(landed, first, small)
        for n, (s, r) in enumerate(rows):
            if n >= 2:
                saves[n - 2].wait()
            spread(x.at[s, r], small.at[0], small.at[1], width, buffers.at[n % 2])
            save = pltpu.make_async_copy(buffers.at[n % 2], moved.at[s, r], buffer_sems.at[n % 2])
            save.start()
            saves.append(save)
            yield

    aside = spread_rows()
    for wave in range(lats + steps):
        if wave < lats:
            if wave:
                arriving[wave].wait_recv()
            if wave + 1 < lats:
                along(wave + 1)
            for i in range(steps):
                for p in range(2):
                    cross(wave, p, i, 0)
        next(aside, None)
        for i in range(steps)[::-1]:
            o = wave - 1 - i
            if 0 <= o < lats:
                for n in range(1 << i):
                    for p in range(2):
                        flights[o, p, i, n].wait_recv()
                        for later in range(i + 1, steps):
                            cross(o, p, later, n + (1 << i))
    for _ in aside:
        pass
    for save in saves[-2:]:
        save.wait()
    own.wait()
    for copy in sent:
        copy.wait_send()

    @pl.when(mine)
    def _():
        for n in range(len(others)):
            norms_to(n).wait_send()


def gather(shard, x, lines, dates, lats, width):
    slots = dates - 1
    moved = x.shape[:2] + (2 * REACH + 1,) + x.shape[2:]
    anywhere = pl.BlockSpec(memory_space=pl.ANY)
    return pl.pallas_call(
        functools.partial(gather_kernel, dates, lats, lines, width),
        in_specs=[anywhere, pl.BlockSpec(memory_space=pltpu.VMEM)],
        out_specs=[anywhere, anywhere, pl.BlockSpec(memory_space=pltpu.VMEM)],
        out_shape=(
            jax.ShapeDtypeStruct((dates, lats) + shard.shape, shard.dtype),
            jax.ShapeDtypeStruct(moved, BF16),
            jax.ShapeDtypeStruct((4, CP, LANES), F32),
        ),
        scratch_shapes=[
            pltpu.SemaphoreType.DMA(()),
            pltpu.SemaphoreType.DMA((lats - 1,)),
            pltpu.SemaphoreType.DMA((lats - 1,)),
            pltpu.SemaphoreType.DMA((lats, 2, slots)),
            pltpu.SemaphoreType.DMA((lats, 2, slots)),
            pltpu.VMEM((2,) + moved[2:], BF16),
            pltpu.SemaphoreType.DMA((2,)),
            pltpu.VMEM((norm_home(lines, lats)[3], LANES), BF16),
            pltpu.SemaphoreType.DMA(()),
            pltpu.SemaphoreType.DMA((dates * lats - 1,)),
            pltpu.SemaphoreType.DMA(()),
        ],
        compiler_params=pltpu.CompilerParams(
            collective_id=2, has_side_effects=True, vmem_limit_bytes=VMEM
        ),
        name="gather_params",
    )(shard, x)


def vector_rows(sums, tiny, first):
    lane = lane_ids()
    sub = lax.broadcasted_iota(jnp.int32, (8, LANES), 0)
    tiny[...] = jnp.zeros_like(tiny)
    for n, (off, channels) in enumerate(SMALL):
        lines = []
        for j in range(6):
            height = min(LANES, CP - j * LANES)
            block = sums[n // 2][n % 2, j * LANES : j * LANES + height, :]
            if height < LANES:
                block = jnp.concatenate([block, jnp.zeros((LANES - height, LANES), F32)], axis=0)
            lines.append(jnp.sum(block.T, axis=0, keepdims=True))
        lines = jnp.concatenate(lines + [jnp.zeros((2, LANES), F32)], axis=0)
        lines = jnp.where(sub * LANES + lane < channels, lines, 0.0)
        row, s = divmod(off - first * LANES, LANES)
        r = pltpu.roll(lines, s, axis=1)
        moved = jnp.where(lane >= s, r, jnp.where(sub == 0, 0.0, pltpu.roll(r, 1, axis=0)))
        tiny[row : row + 8, :] = tiny[row : row + 8, :] + moved


def vector_home(lines, lats):
    start, end = OFF_G1 // LANES, (OFF_UP - 1) // LANES + 1
    owner = start // lines
    row = (start - owner * lines) // 8 * 8
    count = -(-(end + 8 - owner * lines - row) // 8) * 8
    assert end <= (owner + 1) * lines
    return divmod(owner, lats), owner * lines + row, row, count


def scatter_kernel(
    dates, lats, lines, width, src, x, gconv, own, lo, hi, to_below, to_above, gain, second_sums, out, grad,
    sums, others, z_send, z_recv, send, recv, first_sums, tiny, landed, tiny_send, tiny_recv,
    in_sems, out_sems, halo, halo_send, halo_recv, *row_buffers
):
    d, l = lax.axis_index("date"), lax.axis_index("lat")
    steps = dates.bit_length() - 1
    paths = [order[::-1] for order in orders(dates)]
    parts = pieces(src.shape[2])
    owner, first, row, count = vector_home(lines, lats)
    mine = jnp.logical_and(d == owner[0], l == owner[1])
    senders = [(a, b) for a in range(dates) for b in range(lats) if (a, b) != owner]

    greet(dates, lats, d, l, owner)
    sent, flights, z = [], {}, {}
    half = len(row_buffers) // 2
    gets = [l > 0, l < lats - 1]

    def halo_copy(slab, way):
        return pltpu.make_async_remote_copy(
            src_ref=(to_below if way else to_above).at[slab],
            dst_ref=halo.at[slab - 1, way],
            send_sem=halo_send.at[slab - 1, way],
            recv_sem=halo_recv.at[slab - 1, way],
            device_id=(d, lax.rem(l + (lats - 1 if way else 1), lats)),
            device_id_type=MESH,
        )

    def arrived(slab, way):
        @pl.when(gets[way])
        def _():
            halo_copy(slab, way).wait_recv()

        @pl.when(jnp.logical_not(gets[way]))
        def _():
            halo[slab - 1, way] = jnp.zeros_like(halo[slab - 1, way])

        return halo.at[slab - 1, way]

    aside = input_rows(
        width, x, gconv, own, lo, hi, gain, grad, first_sums,
        [row_buffers[:half], row_buffers[half:]], in_sems, out_sems, arrived,
    )

    def left(p, i):
        return span(paths[p][i + 1 :][::-1])[::-1]

    def slot_of(i, n):
        return sum(1 << (steps - 1 - e) for e in range(i)) + n

    def held(o, p, i, mask):
        if i == 0:
            return src.at[flipped(d, mask), lax.rem(l + o, lats), parts[p]]
        return sums.at[o, slot_of(i - 1, left(p, i - 1).index(mask)), parts[p]]

    def cross(o, p, i, n):
        bit = paths[p][i]
        slot = slot_of(i, n)
        copy = pltpu.make_async_remote_copy(
            src_ref=held(o, p, i, left(p, i)[n] | 1 << bit),
            dst_ref=sums.at[o, slot, parts[p]],
            send_sem=send.at[o, p, slot],
            recv_sem=recv.at[o, p, slot],
            device_id=(flip(d, bit), l),
            device_id_type=MESH,
        )
        copy.start()
        sent.append(copy)
        flights[o, p, i, n] = copy

    def add(o, p, i, n):
        flights[o, p, i, n].wait_recv()
        have = held(o, p, i, left(p, i)[n])
        got = sums.at[o, slot_of(i, n), parts[p]]
        got[...] = (have[...].astype(F32) + got[...].astype(F32)).astype(BF16)
        if i + 1 < steps:
            if n < len(left(p, i + 1)):
                cross(o, p, i + 1, n)
        elif o:
            copy = pltpu.make_async_remote_copy(
                src_ref=got,
                dst_ref=others.at[o - 1, parts[p]],
                send_sem=z_send.at[o - 1, p],
                recv_sem=z_recv.at[o - 1, p],
                device_id=(d, lax.rem(l + o, lats)),
                device_id_type=MESH,
            )
            copy.start()
            sent.append(copy)
            z[o, p] = copy

    turns = list(range(1, lats)) + [0]
    for o in turns:
        for n in range(len(left(0, 0))):
            for p in range(2):
                cross(o, p, 0, n)
    for slab in range(1, x.shape[0]):
        for way in range(2):

            @pl.when(gets[1 - way])
            def _():
                halo_copy(slab, way).start()

    for wave in range(lats + steps - 1):
        for i in range(steps):
            if 0 <= wave - i < lats:
                if i:
                    for _ in range(ASIDE):
                        next(aside, None)
                for n in range(len(left(0, i))):
                    for p in range(2):
                        add(turns[wave - i], p, i, n)
    for _ in aside:
        pass
    vector_rows((first_sums, second_sums), tiny, first)

    def to_owner(n):
        return pltpu.make_async_remote_copy(
            src_ref=tiny,
            dst_ref=landed.at[n],
            send_sem=tiny_send,
            recv_sem=tiny_recv.at[n],
            device_id=owner,
            device_id_type=MESH,
        )

    @pl.when(jnp.logical_not(mine))
    def _():
        to_owner(d * lats + l).start()

    for p in range(2):
        total = sums[0, slot_of(steps - 1, 0), parts[p]].astype(F32)
        for o in range(1, lats):
            z[o, p].wait_recv()
            total = total + others[o - 1, parts[p]].astype(F32)
        out[parts[p]] = total

    @pl.when(mine)
    def _():
        total = tiny[...]
        for a, b in senders:
            to_owner(a * lats + b).wait_recv()
            total = total + landed[a * lats + b]
        out[row : row + count, :] = out[row : row + count, :] + total

    @pl.when(jnp.logical_not(mine))
    def _():
        to_owner(d * lats + l).wait_send()

    for copy in sent:
        copy.wait_send()
    for slab in range(1, x.shape[0]):
        for way in range(2):

            @pl.when(gets[1 - way])
            def _():
                halo_copy(slab, way).wait_send()


def scatter(packed, lines, x, gconv, own, lo, hi, to_below, to_above, gain, second_sums, width):
    dates, lats, rows, lanes = packed.shape
    slots = dates - 1
    tiny = (vector_home(lines, lats)[3], LANES)
    anywhere, held = pl.BlockSpec(memory_space=pl.ANY), pl.BlockSpec(memory_space=pltpu.VMEM)
    low = pltpu.VMEM((CP, WIDE), BF16)
    row_buffers = [low, low, pltpu.VMEM((CP, WIDE), F32), low, low, low]
    return pl.pallas_call(
        functools.partial(scatter_kernel, dates, lats, lines, width),
        in_specs=[held] + [anywhere] * 7 + [held] * 2,
        out_specs=[held, anywhere],
        out_shape=(jax.ShapeDtypeStruct((rows, lanes), F32), jax.ShapeDtypeStruct(x.shape, BF16)),
        scratch_shapes=[
            pltpu.VMEM((lats, slots, rows, lanes), BF16),
            pltpu.VMEM((lats - 1, rows, lanes), BF16),
            pltpu.SemaphoreType.DMA((lats - 1, 2)),
            pltpu.SemaphoreType.DMA((lats - 1, 2)),
            pltpu.SemaphoreType.DMA((lats, 2, slots)),
            pltpu.SemaphoreType.DMA((lats, 2, slots)),
            pltpu.VMEM((2, CP, LANES), F32),
            pltpu.VMEM(tiny, F32),
            pltpu.VMEM((dates * lats,) + tiny, F32),
            pltpu.SemaphoreType.DMA(()),
            pltpu.SemaphoreType.DMA((dates * lats,)),
            pltpu.SemaphoreType.DMA((2, 5)),
            pltpu.SemaphoreType.DMA((2,)),
            pltpu.VMEM((max(x.shape[0] - 1, 1), 2, CP, WIDE), BF16),
            pltpu.SemaphoreType.DMA((max(x.shape[0] - 1, 1), 2)),
            pltpu.SemaphoreType.DMA((max(x.shape[0] - 1, 1), 2)),
        ]
        + row_buffers * 2,
        compiler_params=pltpu.CompilerParams(
            collective_id=1, has_side_effects=True, vmem_limit_bytes=VMEM
        ),
        name="scatter_grads",
    )(packed, x, gconv, own, lo, hi, to_below, to_above, gain, second_sums)


def local(inputs, noise, cotangent, params, psi, step_counts, pixel_mask, offsets, bases):
    samples, steps, rows, width, _ = inputs.shape
    slabs = samples * steps
    dates, lats = lax.axis_size("date"), lax.axis_size("lat")
    lat = rows * lats

    def by_channel(values):
        return jnp.swapaxes(values, 3, 4).reshape(slabs, rows, -1, width)

    def padded(values):
        return jnp.pad(values, ((0, 0), (0, 0), (0, CP - values.shape[2]), (0, WIDE - width)))

    upward = [(i, i + 1) for i in range(lats - 1)]
    downward = [(i + 1, i) for i in range(lats - 1)]
    lines = params.shape[0] // LANES
    held = -(-lines // STEP) * STEP
    shard = jnp.pad(params.reshape(lines, LANES), ((0, held - lines), (0, 0)))
    x = padded(jnp.concatenate([by_channel(inputs), by_channel(noise)], axis=2))
    edges = [(x[s, rows - 1 :], x[s, :1]) for s in range(slabs)]
    gathered, moved, small = gather(shard, x, lines, dates, lats, width)
    gathered = gathered.reshape(dates * lats, held, LANES)
    cot = padded(by_channel(cotangent)).reshape(slabs * rows, CP, WIDE)
    active = jnp.arange(steps, dtype=jnp.int32)[None, :] < step_counts[:, None]
    mask = active.reshape(slabs, 1, 1) * pixel_mask[None]
    mask = jnp.pad(mask.astype(F32), ((0, 0), (0, 0), (0, WIDE - width)))
    matrices = unpack(gathered, lines)
    halos, done = [], gathered
    for s in range(slabs):
        top, bottom, done = lax.optimization_barrier((*edges[s], done))
        halos.append((lax.ppermute(top, "lat", upward), lax.ppermute(bottom, "lat", downward)))
        done = halos[-1], matrices
    matrices = done[1]
    basis = ()
    for s in range(slabs):
        basis = (lift(offsets, bases, psi, *halos[s], moved, small[0], small[1], basis, s, lat, width),)
    basis = basis[0]
    w, wt, up, upt, dn, dnt = matrices
    basis = basis.reshape(slabs * rows, BASIS * CP, WIDE)
    output, gconv, gup, gdn, second_sums = block(
        basis, x.reshape(slabs * rows, CP, WIDE), cot, mask.reshape(slabs * rows, 1, WIDE),
        wt, upt, up, dnt, dn, small[2], small[3],
    )
    gconv_rows = gconv.reshape(slabs, rows, CP, WIDE)
    own, to_below, to_above = lower(offsets, bases, psi, gconv_rows, w, width)
    from_below = lax.ppermute(to_above[:1], "lat", upward)
    from_above = lax.ppermute(to_below[:1], "lat", downward)
    packed = grads(basis, gconv, gup, gdn, dates * lats, lines, held)
    summed, grad = scatter(
        packed.reshape(dates, lats, held, LANES), lines,
        x, gconv_rows, own, from_below, from_above, to_below, to_above, small[0], second_sums, width,
    )

    def by_pixel(values):
        values = values.reshape(slabs, rows, CP, WIDE)[:, :, :C, :width]
        return jnp.swapaxes(values.reshape(samples, steps, rows, C, width), 3, 4)

    return by_pixel(output), by_pixel(grad), summed[:lines].reshape(-1)


def solution(mesh):
    field = P("date", None, "lat", None, None)
    flat = P(("date", "lat"))
    return jax.shard_map(
        local,
        mesh=mesh,
        in_specs=(field, field, field, flat, P(), P("date"), P("lat", None), P(), P()),
        out_specs=(field, field, flat),
        check_vma=False,
    )
```

```python
import functools
import math

import jax
import jax.numpy as jnp
from jax import lax
from jax.experimental import pallas as pl
from jax.experimental.pallas import tpu as pltpu
from jax.sharding import PartitionSpec as P

C = 641
HID = 1282
BASIS = 4
SUPPORT = 12
REACH = 2
CIN = 649
BF16, F32 = jnp.bfloat16, jnp.float32
MESH = pl.DeviceIdType.MESH
LANES = 128
STEP = 16
CP = 656
HP = 1296
WIDE = 768
HL = 1408
UNROLL = 8
ASIDE = 2
PARTS = 2
VMEM = 60 << 20


OFF_G1=BASIS*CIN*C+C; OFF_S1=OFF_G1+CIN; OFF_G2=OFF_S1+CIN; OFF_S2=OFF_G2+C; OFF_UP=OFF_S2+C; OFF_DN=OFF_UP+(C+1)*HID;
SMALL=((OFF_G1,CIN),(OFF_S1,CIN),(OFF_G2,C),(OFF_S2,C))
MATS=((0,C,BASIS*CIN+1,128,3),(OFF_UP,HID,C+1,64,2),(OFF_DN,C,HID+1,128,2))
F_ROWS=29952
def lane_ids(): return lax.broadcasted_iota(jnp.int32,(8,LANES),1)
def place(base,cols,period,b):
    start=base+cols*b
    return start//LANES, start%LANES
def rolled(values, amount):
    out = []
    for n in range(0, len(values), 2):
        pieces = values[n : n + 2]
        if len(pieces) == 2:
            both = jnp.concatenate(pieces, axis=0).astype(BF16)
            both = pltpu.roll(both, amount, axis=1).astype(F32)
            out += [both[:8], both[8:]]
        else:
            out.append(pltpu.roll(pieces[0].astype(BF16).astype(F32), amount, axis=1))
    return out


def flatten(lists):
    return [value for values in lists for value in values]


def unflat(values, width):
    return [values[n : n + width] for n in range(0, len(values), width)]


def unpack_kernel(nrow,pad,g_ref,w_out,wt_out,up_out,upt_out,dn_out,dnt_out,held,w_ref,wt_ref,up_ref,upt_ref,dn_ref,dnt_ref,flat,chunks,in_sems,out_sems):
    shards=held.shape[0]
    parts=[pl.ds(n*shards//4,(n+1)*shards//4-n*shards//4) for n in range(4)]
    loads=[pltpu.make_async_copy(g_ref.at[part],held.at[part],in_sems.at[n]) for n,part in enumerate(parts)]
    for copy in loads:
        copy.start()
    saves=[]
    def save(source,target):
        copy=pltpu.make_async_copy(source,target,out_sems.at[len(saves)])
        copy.start()
        saves.append(copy)
    def fill(s,_):
        flat[pl.ds(nrow*s,pad),:]=held[s].astype(F32); return 0
    for n,copy in enumerate(loads):
        copy.wait()
        lax.fori_loop(n*shards//4,(n+1)*shards//4,fill,0)
    lane=lane_ids()
    def split(base,cols,period,groups):
        J=-(-cols//LANES); pitch=period+8; height=pitch*8*groups+8; last=cols-(J-1)*LANES
        def body(b,_):
            row,s=place(base,cols,period,b)
            back=(LANES-s)%LANES
            found=[[flat[pl.ds(row+641*8*g+j,8,stride=641),:] for g in range(groups)] for j in range(J+1)]
            found=unflat(rolled(flatten(found),back),groups)
            for g in range(groups):
                for j in range(J):
                    val=jnp.where(lane<LANES-s,found[j][g],found[j+1][g])
                    if j==J-1: val=jnp.where(lane<last,val,0.0)
                    chunks[pl.ds(j*height+8*g*pitch+b,8,stride=pitch),:]=val
            return 0
        lax.fori_loop(0,period,body,0,unroll=8)
        def border(a,_):
            for j in range(J): chunks[pl.ds(j*height+a*pitch-8,8),:]=chunks[pl.ds(j*height+a*pitch,8),:]
            return 0
        lax.fori_loop(1,8*groups,border,0)
        return J,height,period
    def convert(dst,dst_row,src_row,rows,pad_rows,J,height,period):
        full=rows//16
        def piece(j,r): return chunks[pl.ds(j*height+r//period*(period+8)+r%period,8),:]
        def pair(j,r): return jnp.concatenate([piece(j,r),piece(j,r+8)],axis=0)
        def body(m,_):
            for j in range(J):
                dst[pl.ds(pl.multiple_of(dst_row+16*m,16),16),j*LANES:(j+1)*LANES]=pair(j,src_row+16*m).astype(BF16)
            return 0
        lax.fori_loop(0,full,body,0,unroll=4)
        keep=lax.broadcasted_iota(jnp.int32,(16,LANES),0)<rows-16*full
        for m in range(full,pad_rows//16):
            for j in range(J):
                v=jnp.where(keep,pair(j,src_row+16*m),0.0) if m==full else jnp.zeros((16,LANES),F32)
                dst[dst_row+16*m:dst_row+16*m+16,j*LANES:(j+1)*LANES]=v.astype(BF16)
    J,h,p=split(*MATS[0][:2],*MATS[0][3:])
    for k in range(BASIS):
        convert(w_ref,k*CP,k*CIN,CIN+(k==BASIS-1),CP,J,h,p)
    save(w_ref,w_out)
    wt_ref[...]=w_ref[:,:CP].T
    save(wt_ref,wt_out)
    J,h,p=split(*MATS[1][:2],*MATS[1][3:])
    convert(up_ref,0,0,C+1,CP,J,h,p)
    save(up_ref,up_out)
    upt_ref[...]=up_ref[:,:HP].T
    save(upt_ref,upt_out)
    J,h,p=split(*MATS[2][:2],*MATS[2][3:])
    convert(dn_ref,0,0,HID+1,HP,J,h,p)
    save(dn_ref,dn_out)
    dnt_ref[...]=dn_ref[:,:CP].T
    save(dnt_ref,dnt_out)
    for copy in saves:
        copy.wait()


def unpack(gathered,nrow):
    shapes=[(BASIS*CP,WIDE),(CP,BASIS*CP),(CP,HL),(HP,CP),(HP,WIDE),(CP,HP)]
    anywhere=pl.BlockSpec(memory_space=pl.ANY)
    return pl.pallas_call(functools.partial(unpack_kernel,nrow,gathered.shape[1]),
        in_specs=[anywhere],
        out_specs=[anywhere]*6,
        out_shape=tuple(jax.ShapeDtypeStruct(shape,BF16) for shape in shapes),
        scratch_shapes=[pltpu.VMEM(gathered.shape,BF16)]+[pltpu.VMEM(shape,BF16) for shape in shapes]
        +[pltpu.VMEM((F_ROWS,LANES),F32),pltpu.VMEM((6*(136*24+8),LANES),F32),pltpu.SemaphoreType.DMA((4,)),pltpu.SemaphoreType.DMA((6,))],
        compiler_params=pltpu.CompilerParams(vmem_limit_bytes=VMEM),name="unpack")(gathered)


def chunk_gather(src, chunks, src_row, dst_row, rows, J, height, last, period):
    lane, sub = lane_ids(), lax.broadcasted_iota(jnp.int32, (8, LANES), 0)

    def step(m):
        at = dst_row + 8 * m
        at = at // period * (period + 8) + at % period
        for j in range(J):
            v = src[pl.ds(src_row + 8 * m, 8), j * LANES : (j + 1) * LANES]
            if j == J - 1:
                v = jnp.where(lane < last, v, 0.0)
            if isinstance(m, int) and 8 * m + 8 > rows:
                v = jnp.where(sub < rows - 8 * m, v, 0.0)
            chunks[pl.ds(j * height + at + 8, 8), :] = v
            chunks[pl.ds(j * height + at, 8), :] = v

    return step


def chunk_clear(chunks, J, height, row, period):
    row = row // period * (period + 8) + row % period

    def body(m, _):
        for j in range(J):
            chunks[pl.ds(j * height + row + 8 * m, 8), :] = jnp.zeros((8, LANES), F32)
        return 0

    lax.fori_loop(0, (height - row) // 8, body, 0)


def line_merge(flat, flat0, chunks, base, cols, period, groups):
    lane, sub = lane_ids(), lax.broadcasted_iota(jnp.int32, (8, LANES), 0)
    J, pitch = -(-cols // LANES), period + 8
    height = pitch * 8 * groups + 8
    row0 = base // LANES - flat0

    def step(b, tails, last=False):
        row, s = place(base, cols, period, b)
        row = row - flat0
        found = [
            chunks[pl.ds(j * height + 8 * g * pitch + b, 8, stride=pitch), :]
            for g in range(groups)
            for j in range(J)
        ]
        found = unflat(rolled(found, s), J)
        new = []
        keep = lane >= s
        for g in range(groups):
            x = found[g]
            for j in range(J):
                v = jnp.where(keep, x[j], tails[g] if j == 0 else x[j - 1])
                if not (last and j == J - 1):
                    flat[pl.ds(row + 641 * 8 * g + j, 8, stride=641), :] = v
            new.append(jnp.where(s == LANES - 1, jnp.where(keep, 0.0, x[J - 1]), v))
        return tuple(new)

    def first():
        init = [jnp.zeros((8, LANES), F32)] * groups
        if base == OFF_DN:
            init[0] = jnp.where(sub == 0, flat[row0 : row0 + 8, :], 0.0)
        return tuple(init)

    def finish(tails):
        if base % LANES:
            for g in range(groups):
                at = pl.ds(row0 + 641 * (8 * g + 1), 8, stride=641)
                flat[at, :] = flat[at, :] + tails[g]

    return step, first, finish


FFN_ROW = OFF_UP // LANES // 8 * 8
FFN_ROWS = OFF_DN // LANES + 641 * 16 + 40 - FFN_ROW
DISCO_ROWS = 641 * 24 + 16


def grads_kernel(nrow, basis, gconv, gup, gdn, out, *refs):
    low, conv, gd, flat, ffn, chunks, gu, gn, stage, in_sems, ffn_sems, out_sems = refs
    count = basis.shape[0]
    shards, pad = out.shape[:2]

    def loads(i):
        return [
            pltpu.make_async_copy(basis.at[i], low.at[i % 2], in_sems.at[i % 2, 0]),
            pltpu.make_async_copy(gconv.at[i], conv.at[i % 2], in_sems.at[i % 2, 1]),
        ]

    weights = [pltpu.make_async_copy(a, b, ffn_sems.at[n]) for n, (a, b) in enumerate(((gup, gu), (gdn, gn)))]
    flying = {}
    for i in range(min(2, count)):
        flying[i] = loads(i)
        for copy in flying[i]:
            copy.start()
        weights[i].start()

    def outer(i, n):
        if n == 0:
            for copy in flying[i]:
                copy.wait()
        at = slice(n * CP, (n + 1) * CP)
        term = lax.dot_general(
            low[i % 2, at, :], conv[i % 2], (((1,), (1,)), ((), ())), preferred_element_type=F32
        )
        if i:
            gd[at, :CP] += term
        else:
            gd[at, :CP] = term
        if n == BASIS - 1 and i + 2 < count:
            flying[i + 2] = loads(i + 2)
            for copy in flying[i + 2]:
                copy.start()

    def lay(n, src, rows, J, height, last, base, cols, period, groups):
        state = {}
        copy = chunk_gather(src, chunks, 0, 0, rows, J, height, last, period)
        step, first, finish = line_merge(ffn, FFN_ROW, chunks, base, cols, period, groups)
        pieces = -(-rows // 8)

        def begin():
            weights[n].wait()

        def gather(start):
            for m in range(start, min(start + 4, pieces)):
                copy(m)

        def ready():
            chunk_clear(chunks, J, height, 8 * pieces, period)
            state["tails"] = first()

        def merge(b):
            state["tails"] = step(b, state["tails"], last=base % LANES and b == period - 1)

        def done():
            finish(state["tails"])

        steps = [begin] + [functools.partial(gather, m) for m in range(0, pieces, 4)] + [ready]
        return steps + [functools.partial(merge, b) for b in range(period)] + [done]

    products = [functools.partial(outer, i, n) for i in range(count) for n in range(BASIS)]
    for n in range(2):
        if n >= count:
            weights[n].start()
    up_steps = lay(0, gu, C + 1, 11, 72 * 16 + 8, 2, OFF_UP, HID, 64, 2)
    down_steps = lay(1, gn, HID + 1, 6, 136 * 16 + 8, 1, OFF_DN, C, 128, 2)
    weave(products, up_steps + down_steps)

    height = 136 * 24 + 8
    for k in range(BASIS):
        rows = CIN + (k == BASIS - 1)
        copy = chunk_gather(gd, chunks, k * CP, k * CIN, rows, 6, height, 1, 128)

        def body(m, _):
            copy(m)
            return 0

        lax.fori_loop(0, rows // 8, body, 0, unroll=4)
        copy(rows // 8)
    chunk_clear(chunks, 6, height, 2600, 128)
    step, first, _ = line_merge(flat, 0, chunks, 0, C, 128, 3)
    lax.fori_loop(0, 128, step, first(), unroll=8)
    seam = OFF_UP // LANES
    for shard in range(shards):
        if nrow * shard < seam < nrow * shard + pad:
            amount = nrow * shard + pad - seam
            flat[seam : seam + amount, :] = ffn[seam - FFN_ROW : seam - FFN_ROW + amount, :]
    slots = stage.shape[0]

    def save(shard, slot):
        return pltpu.make_async_copy(stage.at[slot], out.at[shard], out_sems.at[slot])

    for shard in range(shards):
        slot = shard % slots
        if shard >= slots:
            save(shard - slots, slot).wait()
        source, start = (flat, nrow * shard) if nrow * shard < seam else (ffn, nrow * shard - FFN_ROW)
        stage[slot] = source[start : start + pad, :].astype(BF16)
        save(shard, slot).start()
    for shard in range(max(shards - slots, 0), shards):
        save(shard, shard % slots).wait()


def grads(basis, gconv, gup, gdn, n, nrow, pad):
    anywhere = pl.BlockSpec(memory_space=pl.ANY)
    return pl.pallas_call(
        functools.partial(grads_kernel, nrow),
        in_specs=[anywhere] * 4,
        out_specs=anywhere,
        out_shape=jax.ShapeDtypeStruct((n, pad, LANES), BF16),
        scratch_shapes=[
            pltpu.VMEM((2, BASIS * CP, WIDE), BF16),
            pltpu.VMEM((2, CP, WIDE), BF16),
            pltpu.VMEM((BASIS * CP, WIDE), F32),
            pltpu.VMEM((DISCO_ROWS, LANES), F32),
            pltpu.VMEM((FFN_ROWS, LANES), F32),
            pltpu.VMEM((6 * (136 * 24 + 8), LANES), F32),
            pltpu.VMEM(gup.shape, F32),
            pltpu.VMEM(gdn.shape, F32),
            pltpu.VMEM((4, pad, LANES), BF16),
            pltpu.SemaphoreType.DMA((2, 2)),
            pltpu.SemaphoreType.DMA((2,)),
            pltpu.SemaphoreType.DMA((4,)),
        ],
        compiler_params=pltpu.CompilerParams(vmem_limit_bytes=VMEM),
        name="grads",
    )(basis, gconv, gup, gdn)


def tiled(column):
    return jnp.concatenate([column] * (WIDE // LANES), axis=1)


def lane_of(rows, start=0):
    return lax.broadcasted_iota(jnp.int32, (rows, LANES), 1) + start


def wrapped(chunk, width):
    head, first, last = chunk[:, : WIDE - LANES], chunk[:, :LANES], chunk[:, WIDE - LANES :]
    edge = width - (WIDE - LANES)
    lane = lane_of(chunk.shape[0])
    beyond = jnp.where(
        lane < LANES - REACH, pltpu.roll(first, edge, axis=1), pltpu.roll(last, LANES - edge, axis=1)
    )
    return jnp.concatenate([head, jnp.where(lane < edge, last, beyond)], axis=1)


def cut(chunk, width):
    head, last = chunk[:, : WIDE - LANES], chunk[:, WIDE - LANES :]
    keep = lane_of(chunk.shape[0], WIDE - LANES) < width
    return jnp.concatenate([head, jnp.where(keep, last, 0.0)], axis=1)


def rows_below(count):
    return lax.broadcasted_iota(jnp.int32, (STEP, WIDE), 0) < count


def halves(chunk):
    return chunk[:8] + chunk[8:]


def column_sums(read, channels, count):
    whole = channels // STEP

    def body(m, sums):
        return tuple(a + halves(v) for a, v in zip(sums, read(m)))

    sums = lax.fori_loop(
        0, whole, body, tuple(jnp.zeros((8, WIDE), F32) for _ in range(count)), unroll=UNROLL
    )
    keep = rows_below(channels - whole * STEP)
    sums = [a + halves(jnp.where(keep, v, 0.0)) for a, v in zip(sums, read(whole))]
    return [jnp.sum(a, axis=0, keepdims=True) for a in sums]


def norm_stats(read, channels):
    (total,) = column_sums(lambda m: (read(m),), channels, 1)
    mean = total * (1.0 / channels)

    def squares(m):
        centered = read(m) - mean
        return (centered * centered,)

    (total,) = column_sums(squares, channels, 1)
    return mean, lax.rsqrt(total * (1.0 / channels) + 1e-05)


def each_chunk(body, unroll=None):
    def step(m, _):
        body(m, pl.ds(pl.multiple_of(m * STEP, STEP), STEP))
        return 0

    lax.fori_loop(0, CP // STEP, step, 0, unroll=unroll)


def spread(source, gain, shift, width, moved):
    def read(c):
        return source[pl.ds(pl.multiple_of(c * STEP, STEP), STEP), :].astype(F32)

    mean, scale = norm_stats(read, CIN)
    yield

    def shifts(c, at):
        values = (read(c) - mean) * scale * tiled(gain[at, :]) + tiled(shift[at, :])
        values = wrapped(values, width).astype(BF16)
        for d in range(-REACH, REACH + 1):
            moved[d + REACH, at, :] = pltpu.roll(values, -d % WIDE, axis=1) if d else values

    def step(m, _):
        shifts(m, pl.ds(pl.multiple_of(m * STEP, STEP), STEP))
        return 0

    chunks = CP // STEP
    for n in range(PARTS):
        lax.fori_loop(n * chunks // PARTS, (n + 1) * chunks // PARTS, step, 0, unroll=4)
        yield


def points_of(bases):
    named = [bases[p] for p in range(SUPPORT)]
    ranks = []
    for p in range(SUPPORT):
        rank = jnp.int32(0)
        for before in range(p):
            rank = rank + jnp.where(named[before] == named[p], 1, 0)
        ranks.append(rank)
    picks = {}
    for k in range(BASIS):
        for q in range(3):
            pick = jnp.int32(0)
            for p in range(SUPPORT):
                pick = pick + jnp.where(jnp.logical_and(named[p] == k, ranks[p] == q), p, 0)
            picks[k, q] = pick
    return picks


def combine_row(r, first_row, lat, width, offsets, picks, psi, moved, out):
    for k in range(BASIS):
        parts = []
        for q in range(3):
            p = picks[k, q]
            row = first_row + r + offsets[p, 0]
            inside = jnp.logical_and(row >= 0, row < lat)
            weight = jnp.where(inside, psi[first_row + r, p], 0.0)
            parts.append((weight, r + 1 + offsets[p, 0], offsets[p, 1] + REACH))

        def combine(c, at):
            total = None
            for weight, row, d in parts:
                term = weight * moved[row, d, at, :].astype(F32)
                total = term if total is None else total + term
            to = pl.ds(pl.multiple_of(k * CP + c * STEP, STEP), STEP)
            out[to, :] = cut(total, width).astype(BF16)

        each_chunk(combine, 4)
    last = slice(BASIS * CP - STEP, BASIS * CP)
    bias_row = CIN - (CP - STEP)
    sub = lax.broadcasted_iota(jnp.int32, (STEP, WIDE), 0)
    lane = lax.broadcasted_iota(jnp.int32, (STEP, WIDE), 1)
    ones = jnp.where(lane < width, 1.0, 0.0)
    out[last, :] = jnp.where(sub == bias_row, ones, out[last, :].astype(F32)).astype(BF16)


def lift_kernel(rows, slab, lat, width, offsets, bases, psi, lo, hi, own, gain, shift, *refs):
    out, moved, built, sems, out_sems = refs[-5:]
    first_row = lax.axis_index("lat") * rows
    copies = [
        pltpu.make_async_copy(own.at[slab, r], moved.at[r + 1], sems.at[r]) for r in range(rows)
    ]
    for copy in copies:
        copy.start()
    picks = points_of(bases)
    for source, m in ((lo, 0), (hi, rows + 1)):
        for _ in spread(source.at[0], gain, shift, width, moved.at[m]):
            pass
    for copy in copies:
        copy.wait()
    saves = []
    for r in range(rows):
        combine_row(r, first_row, lat, width, offsets, picks, psi, moved, built.at[r])
        saves.append(pltpu.make_async_copy(built.at[r], out.at[slab, r], out_sems.at[r]))
        saves[r].start()
    for save in saves:
        save.wait()


def lift(offsets, bases, psi, lo, hi, own, gain, shift, before, slab, lat, width):
    slabs, rows = own.shape[:2]
    smem = pl.BlockSpec(memory_space=pltpu.SMEM)
    anywhere, held = pl.BlockSpec(memory_space=pl.ANY), pl.BlockSpec(memory_space=pltpu.VMEM)
    return pl.pallas_call(
        functools.partial(lift_kernel, rows, slab, lat, width),
        in_specs=[smem, smem, smem, held, held, anywhere, held, held] + [anywhere] * len(before),
        out_specs=anywhere,
        out_shape=jax.ShapeDtypeStruct((slabs, rows, BASIS * CP, WIDE), BF16),
        scratch_shapes=[
            pltpu.VMEM((rows + 2, 2 * REACH + 1, CP, WIDE), BF16),
            pltpu.VMEM((rows, BASIS * CP, WIDE), BF16),
            pltpu.SemaphoreType.DMA((rows,)),
            pltpu.SemaphoreType.DMA((rows,)),
        ],
        input_output_aliases={8: 0} if before else {},
        compiler_params=pltpu.CompilerParams(vmem_limit_bytes=VMEM),
        cost_estimate=pl.CostEstimate(flops=40 << 20, bytes_accessed=40 << 20, transcendentals=0),
        name="lift",
    )(offsets, bases, psi, lo, hi, own, gain, shift, *before)


GELU_A = math.sqrt(2.0 / math.pi)
GELU_B = 0.044715


TILE = 256


def weave(*lists):
    order = []
    for which, steps in enumerate(lists):
        for n, step in enumerate(steps):
            order.append(((n + 0.5) / len(steps), which, n, step))
    for _, _, _, step in sorted(order, key=lambda entry: entry[:3]):
        step()


class Job:
    def __init__(self, buffers, weights, totals, mask):
        self.basis, self.x, self.cot, self.out, self.gconv = buffers[:5]
        self.res, self.second, self.pre, self.act, self.mid, self.gact, self.gb, self.gpre = buffers[5:]
        self.wt, self.upt, self.up, self.dnt, self.dn, self.gain, self.shift = weights
        self.gup, self.gdn, self.sums = totals
        self.mask = mask

    @staticmethod
    def at(c):
        return slice(c * STEP, (c + 1) * STEP)

    @staticmethod
    def wide(column):
        return jnp.concatenate([column] * (TILE // LANES), axis=1)

    @staticmethod
    def only(c, values, channels, other=0.0):
        if (c + 1) * STEP <= channels:
            return values
        row = lax.broadcasted_iota(jnp.int32, (STEP, TILE), 0)
        return jnp.where(row < channels - c * STEP, values, other)

    def product(self, out, left, right, count):
        rows = left.shape[0]
        size = -(-rows // (count * STEP)) * STEP

        def step(start):
            at = slice(start, min(start + size, rows))
            values = left[at, : right.shape[0]]
            out[at, :] = jnp.dot(values, right[...], preferred_element_type=F32)

        return [functools.partial(step, start) for start in range(0, rows, size)]

    def outer(self, out, left, right, count):
        rows = left.shape[0]
        size = -(-rows // (count * STEP)) * STEP

        def step(start):
            at = slice(start, min(start + size, rows))
            term = lax.dot_general(
                left[at, :], right[...], (((1,), (1,)), ((), ())), preferred_element_type=F32
            )
            out[at, : right.shape[0]] += term

        return [functools.partial(step, start) for start in range(0, rows, size)]

    def m1(self):
        return self.product(self.res, self.wt, self.basis, 4)

    def v1(self):
        state = {"sum": jnp.zeros((8, TILE), F32), "square": jnp.zeros((8, TILE), F32)}
        mask = self.mask()

        def add(c):
            at = self.at(c)
            value = self.res[at, :] + self.only(c, self.x[at, :].astype(F32), C)
            self.res[at, :] = value
            self.gb[at, :] = (self.cot[at, :].astype(F32) * mask).astype(BF16)
            state["sum"] = state["sum"] + halves(self.only(c, value, C))

        def mean():
            self.mean = jnp.sum(state["sum"], axis=0, keepdims=True) * (1.0 / C)

        def square(c):
            value = self.res[self.at(c), :] - self.mean
            state["square"] = state["square"] + halves(self.only(c, value * value, C))

        def scale():
            total = jnp.sum(state["square"], axis=0, keepdims=True)
            self.scale = lax.rsqrt(total * (1.0 / C) + 1e-05)

        def normalize(c):
            at = self.at(c)
            value = (self.res[at, :] - self.mean) * self.scale
            value = value * self.wide(self.gain[at, :]) + self.wide(self.shift[at, :])
            row = lax.broadcasted_iota(jnp.int32, (STEP, TILE), 0)
            if c == C // STEP:
                value = jnp.where(row == C % STEP, 1.0, value)
            self.second[at, :] = value.astype(BF16)

        chunks = range(CP // STEP)
        steps = [functools.partial(add, c) for c in chunks] + [mean]
        steps += [functools.partial(square, c) for c in chunks] + [scale]
        return steps + [functools.partial(normalize, c) for c in chunks]

    def m2(self):
        return self.product(self.pre, self.upt, self.second, 9)

    def v2(self):
        def gelu(c):
            at = self.at(c)
            v = self.pre[at, :]
            square = v * v
            bend = jnp.tanh(GELU_A * v * (1.0 + GELU_B * square))
            half = 0.5 * (1.0 + bend)
            value = v * half
            if c == HID // STEP:
                row = lax.broadcasted_iota(jnp.int32, (STEP, TILE), 0)
                value = jnp.where(row == HID % STEP, 1.0, value)
            self.act[at, :] = value.astype(BF16)
            rise = GELU_A * (1.0 + 3.0 * GELU_B * square)
            self.pre[at, :] = half + 0.5 * v * (1.0 - bend * bend) * rise

        return [functools.partial(gelu, c) for c in range(HP // STEP)]

    def m3(self):
        back = self.product(self.gact, self.dn, self.gb, 9)
        return self.product(self.mid, self.dnt, self.act, 4) + back

    def v3(self):
        def finish(c):
            at = self.at(c)
            self.out[at, :] = (self.res[at, :] + self.mid[at, :]).astype(BF16)

        def back(c):
            at = self.at(c)
            self.gpre[at, :] = (self.gact[at, :] * self.pre[at, :]).astype(BF16)

        steps = [functools.partial(finish, c) for c in range(CP // STEP)]
        return steps + [functools.partial(back, c) for c in range(HP // STEP)]

    def m4(self):
        return self.product(self.mid, self.up, self.gpre, 4)

    def v4(self):
        state = {"flat": jnp.zeros((8, TILE), F32), "along": jnp.zeros((8, TILE), F32)}

        def terms(c):
            at = self.at(c)
            dm = self.mid[at, :]
            xhat = (self.res[at, :] - self.mean) * self.scale
            return dm, xhat, dm * self.wide(self.gain[at, :])

        def means(c):
            _, xhat, g = terms(c)
            g = self.only(c, g, C)
            state["flat"] = state["flat"] + halves(g)
            state["along"] = state["along"] + halves(g * xhat)

        def join():
            for name in state:
                state[name] = jnp.sum(state[name], axis=0, keepdims=True) * (1.0 / C)

        def backward(c):
            at = self.at(c)
            dm, xhat, g = terms(c)
            value = g - state["flat"] - xhat * state["along"]
            value = self.gb[at, :].astype(F32) + self.scale * value
            self.gconv[at, :] = self.only(c, value, C).astype(BF16)
            for n, term in enumerate((dm * xhat, dm)):
                self.sums[n, at, :] += term[:, :LANES] + term[:, LANES:]

        chunks = range(CP // STEP)
        steps = [functools.partial(means, c) for c in chunks] + [join]
        return steps + [functools.partial(backward, c) for c in chunks]

    def m5(self):
        first = self.outer(self.gdn, self.act, self.gb, 3)
        return first + self.outer(self.gup, self.second, self.gpre, 2)


def block_kernel(
    basis, x, cot, mask, wt, upt, up, dnt, dn, gain, shift, out, gconv, gup, gdn, sums, *scratch
):
    count = basis.shape[0]
    tiles = WIDE // TILE
    in_sems, out_sems = scratch[-2:]
    per_job = (len(scratch) - 2) // 2
    sets = [scratch[:per_job], scratch[per_job : 2 * per_job]]
    for total in (gup, gdn, sums):
        total[...] = jnp.zeros_like(total)

    def place(i, j):
        return i // tiles * 2 + j, pl.ds(pl.multiple_of(i % tiles * TILE, TILE), TILE)

    def arrive(i, j):
        row, lanes = place(i, j)
        return [
            pltpu.make_async_copy(source.at[row, :, lanes], sets[j][n], in_sems.at[j, n])
            for n, source in enumerate((basis, x, cot))
        ]

    def leave(i, j):
        row, lanes = place(i, j)
        return [
            pltpu.make_async_copy(sets[j][3 + n], target.at[row, :, lanes], out_sems.at[j, n])
            for n, target in enumerate((out, gconv))
        ]

    last = count // 2 * tiles - 1
    for j in range(2):
        for copy in arrive(0, j):
            copy.start()

    def pair(i, _):
        def row_mask(j):
            row, lanes = place(i, j)
            return lambda: mask[row, :, lanes]

        weights, totals = (wt, upt, up, dnt, dn, gain, shift), (gup, gdn, sums)
        a, b = (Job(sets[j], weights, totals, row_mask(j)) for j in range(2))
        after = jnp.minimum(i + 1, last)
        coming = [arrive(after, j) for j in range(2)]
        leaving = [leave(i, j) for j in range(2)]
        for j in range(2):
            for copy in arrive(i, j):
                copy.wait()
        weave(a.m1())
        coming[0][0].start()
        weave(a.v1(), b.m1())
        coming[1][0].start()
        for n in (1, 2):
            coming[0][n].start()
        weave(a.m2(), b.v1())
        for n in (1, 2):
            coming[1][n].start()
        weave(a.v2(), b.m2())
        weave(a.m3(), b.v2())
        weave(a.v3(), b.m3())
        leaving[0][0].start()
        weave(a.m4(), b.v3())
        leaving[1][0].start()
        weave(a.v4(), b.m4())
        leaving[0][1].start()
        weave(a.m5(), b.v4())
        leaving[1][1].start()
        weave(b.m5())
        for copies in leaving:
            for copy in copies:
                copy.wait()
        return 0

    lax.fori_loop(0, last + 1, pair, 0)
    for j in range(2):
        for copy in arrive(last, j):
            copy.wait()


def block(basis, x, cot, mask, wt, upt, up, dnt, dn, gain, shift):
    count = x.shape[0]
    anywhere = pl.BlockSpec(memory_space=pl.ANY)
    held = pl.BlockSpec(memory_space=pltpu.VMEM)
    low, high = pltpu.VMEM((CP, TILE), BF16), pltpu.VMEM((CP, TILE), F32)
    hidden_low, hidden_high = pltpu.VMEM((HP, TILE), BF16), pltpu.VMEM((HP, TILE), F32)
    per_job = [pltpu.VMEM((BASIS * CP, TILE), BF16), low, low, low, low]
    per_job += [high, low, hidden_high, hidden_low, high, hidden_high, low, hidden_low]
    return pl.pallas_call(
        block_kernel,
        in_specs=[anywhere] * 3 + [held] * 8,
        out_specs=[anywhere] * 2 + [held] * 3,
        out_shape=(
            jax.ShapeDtypeStruct((count, CP, WIDE), BF16),
            jax.ShapeDtypeStruct((count, CP, WIDE), BF16),
            jax.ShapeDtypeStruct((CP, HL), F32),
            jax.ShapeDtypeStruct((HP, WIDE), F32),
            jax.ShapeDtypeStruct((2, CP, LANES), F32),
        ),
        scratch_shapes=per_job * 2 + [pltpu.SemaphoreType.DMA((2, 3)), pltpu.SemaphoreType.DMA((2, 2))],
        compiler_params=pltpu.CompilerParams(vmem_limit_bytes=VMEM),
        name="block",
    )(basis, x, cot, mask, wt, upt, up, dnt, dn, gain, shift)


def along_lanes(ref, at, values):
    total = values[:, :LANES]
    for j in range(1, WIDE // LANES):
        total = total + values[:, j * LANES : (j + 1) * LANES]
    ref[at, :] = ref[at, :] + total


GROUP = 11 * STEP
GROUP_STEP = 10 * STEP


def lower_kernel(rows, width, offsets, bases, psi, gconv, w, own, lo0, hi0, lo1, hi1, *scratch):
    place, coef, in_sems, w_sems, out_sems = scratch[-5:]
    per_slab = (len(scratch) - 5) // 2
    sets = [scratch[:per_slab], scratch[per_slab : 2 * per_slab]]
    first_row = lax.axis_index("lat") * rows
    span = 2 * REACH + 1
    groups = 1 + (CP - GROUP) // GROUP_STEP
    for n in range(3 * span):
        place[n] = 0
        for r in range(rows):
            coef[r, n] = 0.0
    for p in range(SUPPORT):
        n = (offsets[p, 0] + 1) * span + offsets[p, 1] + REACH
        place[n] = bases[p]
        for r in range(rows):
            coef[r, n] = psi[first_row + r, p]

    def channels(g):
        return pl.ds(pl.multiple_of(g * GROUP_STEP, STEP), GROUP)

    def weights(j, g):
        return pltpu.make_async_copy(w.at[:, channels(g), :], sets[j][1], w_sems.at[j])

    def products(j):
        ring, part, lifted = sets[j][:3]

        def step(r, k):
            values = jnp.dot(part[k, :, :CP], ring[r], preferred_element_type=F32)
            lifted[r, k] = values.astype(BF16)

        return [functools.partial(step, r, k) for r in range(rows) for k in range(BASIS)]

    def gathers(j):
        lifted, inner, below, above = sets[j][2:]

        def step(c, target):
            at = slice(c * STEP, (c + 1) * STEP)
            total = None
            for d in range(-REACH, REACH + 1):
                part = None
                for o in (-1, 0, 1):
                    r = target - o
                    if 0 <= r < rows:
                        n = (o + 1) * span + d + REACH
                        term = coef[r, n] * lifted[r, place[n], at, :].astype(F32)
                        part = term if part is None else part + term
                if d:
                    part = pltpu.roll(part.astype(BF16), d % WIDE, axis=1).astype(F32)
                total = part if total is None else total + part
            if target < 0:
                below[at, :] = total.astype(BF16)
            elif target == rows:
                above[at, :] = total.astype(BF16)
            else:
                inner[target, at, :] = total

        return [functools.partial(step, c, t) for c in range(GROUP // STEP) for t in range(-1, rows + 1)]

    def pair_of_slabs(both, _):
        def leaving(j, g):
            slab = both * 2 + j
            lo, hi = ((lo0, hi0), (lo1, hi1))[j]
            targets = (own.at[slab, :, channels(g), :], lo.at[both, channels(g), :], hi.at[both, channels(g), :])
            return [
                pltpu.make_async_copy(sets[j][3 + n], target, out_sems.at[j, n])
                for n, target in enumerate(targets)
            ]

        rings = [pltpu.make_async_copy(gconv.at[both * 2 + j], sets[j][0], in_sems.at[j]) for j in range(2)]
        for j in range(2):
            rings[j].start()
            weights(j, 0).start()
        for j in range(2):
            rings[j].wait()
            ring = sets[j][0]
            edge = width - (WIDE - LANES)
            lane = lane_of(CP)
            for r in range(rows):
                first, last = ring[r, :, :LANES].astype(F32), ring[r, :, WIDE - LANES :].astype(F32)
                beyond = jnp.where(
                    lane < LANES - REACH,
                    pltpu.roll(first, edge, axis=1),
                    pltpu.roll(last, LANES - edge, axis=1),
                )
                ring[r, :, WIDE - LANES :] = jnp.where(lane < edge, last, beyond).astype(BF16)
        weights(0, 0).wait()
        weave(products(0))
        weights(0, min(1, groups - 1)).start()

        def group(g, _):
            after, later = jnp.minimum(g + 1, groups - 1), jnp.minimum(g + 2, groups - 1)
            def free(j):
                @pl.when(g > 0)
                def _():
                    for copy in leaving(j, jnp.maximum(g - 1, 0)):
                        copy.wait()

            weights(1, g).wait()
            free(0)
            weave(products(1), gathers(0))
            weights(1, after).start()
            for copy in leaving(0, g):
                copy.start()
            weights(0, after).wait()
            free(1)
            weave(products(0), gathers(1))
            weights(0, later).start()
            for copy in leaving(1, g):
                copy.start()
            return 0

        lax.fori_loop(0, groups, group, 0)
        for j in range(2):
            weights(j, groups - 1).wait()
            for copy in leaving(j, groups - 1):
                copy.wait()
        return 0

    lax.fori_loop(0, gconv.shape[0] // 2, pair_of_slabs, 0)


def lower(offsets, bases, psi, gconv, w, width):
    slabs, rows = gconv.shape[:2]
    smem = pl.BlockSpec(memory_space=pltpu.SMEM)
    anywhere = pl.BlockSpec(memory_space=pl.ANY)
    edge = jax.ShapeDtypeStruct((slabs // 2, CP, WIDE), BF16)
    per_slab = [
        pltpu.VMEM((rows, CP, WIDE), BF16),
        pltpu.VMEM((BASIS, GROUP, WIDE), BF16),
        pltpu.VMEM((rows, BASIS, GROUP, WIDE), BF16),
        pltpu.VMEM((rows, GROUP, WIDE), F32),
        pltpu.VMEM((GROUP, WIDE), BF16),
        pltpu.VMEM((GROUP, WIDE), BF16),
    ]
    return pl.pallas_call(
        functools.partial(lower_kernel, rows, width),
        in_specs=[smem, smem, smem, anywhere, anywhere],
        out_specs=[anywhere] * 5,
        out_shape=(jax.ShapeDtypeStruct((slabs, rows, CP, WIDE), F32),) + (edge,) * 4,
        scratch_shapes=per_slab * 2
        + [
            pltpu.SMEM((3 * (2 * REACH + 1),), jnp.int32),
            pltpu.SMEM((rows, 3 * (2 * REACH + 1)), F32),
            pltpu.SemaphoreType.DMA((2,)),
            pltpu.SemaphoreType.DMA((2,)),
            pltpu.SemaphoreType.DMA((2, 3)),
        ],
        compiler_params=pltpu.CompilerParams(vmem_limit_bytes=VMEM),
        name="lower",
    )(offsets, bases, psi, gconv, w.reshape(BASIS, CP, WIDE))


def input_rows(width, x, gconv, own, lo, hi, gain, grad, sums, buffers, in_sems, out_sems, arrived):
    rows = x.shape[1]
    places = [(s, r) for s in range(x.shape[0]) for r in range(rows)]
    saves = []

    def loads(n):
        s, r = places[n]
        sources = [x.at[s, r], gconv.at[s, r], own.at[s, r]]
        sources += [lo.at[s // 2]] if r == 0 and s % 2 == 0 else []
        sources += [hi.at[s // 2]] if r == rows - 1 and s % 2 == 0 else []
        slots = [0, 1, 2] + ([3] if r == 0 else []) + ([4] if r == rows - 1 else [])
        return [
            pltpu.make_async_copy(source, buffers[n % 2][slot], in_sems.at[n % 2, slot])
            for source, slot in zip(sources, slots)
        ]

    flying = loads(0)
    for copy in flying:
        copy.start()
    sums[...] = jnp.zeros_like(sums)
    for n, (s, r) in enumerate(places):
        for copy in flying:
            copy.wait()
        if n + 1 < len(places):
            flying = loads(n + 1)
            for copy in flying:
                copy.start()
        here, conv, total, below, above, result = buffers[n % 2]
        if s % 2:
            below = arrived(s, 0) if r == 0 else None
            above = arrived(s, 1) if r == rows - 1 else None

        def read(c):
            return here[pl.ds(pl.multiple_of(c * STEP, STEP), STEP), :].astype(F32)

        mean, scale = norm_stats(read, CIN)
        yield

        if r == 0 or r == rows - 1:

            def join(c, at):
                value = total[at, :]
                if r == 0:
                    value = value + below[at, :].astype(F32)
                if r == rows - 1:
                    value = value + above[at, :].astype(F32)
                total[at, :] = value

            each_chunk(join, 8)
            yield

        def means(c):
            at = pl.ds(pl.multiple_of(c * STEP, STEP), STEP)
            g = total[at, :] * tiled(gain[at, :])
            return g, g * ((read(c) - mean) * scale)

        flat, along = [v * (1.0 / CIN) for v in column_sums(means, CIN, 2)]
        yield
        if n >= 2:
            saves[n - 2].wait()

        def backward(c, at):
            dm = cut(total[at, :], width)
            xhat = (read(c) - mean) * scale
            g = dm * tiled(gain[at, :])
            value = scale * (g - flat - xhat * along) + conv[at, :].astype(F32)
            result[at, :] = value.astype(BF16)
            along_lanes(sums.at[0], at, dm * xhat)
            along_lanes(sums.at[1], at, dm)

        each_chunk(backward, 8)
        save = pltpu.make_async_copy(result, grad.at[s, r], out_sems.at[n % 2])
        save.start()
        saves.append(save)
        yield
    for save in saves[-2:]:
        save.wait()


def flip(value, bit):
    return value + (1 - 2 * ((value // (1 << bit)) % 2)) * (1 << bit)


def flipped(value, mask):
    bit = 0
    while mask >> bit:
        if mask >> bit & 1:
            value = flip(value, bit)
        bit += 1
    return value


def span(bits):
    masks = [0]
    for b in bits:
        masks = masks + [m | 1 << b for m in masks]
    return masks


def orders(dates):
    bits = list(range(1, dates.bit_length() - 1))
    return bits + [0], bits[::-1] + [0]


def pieces(rows):
    cut = rows // (2 * STEP) * STEP
    return pl.ds(0, cut), pl.ds(cut, rows - cut)


def greet(dates, lats, d, l, owner):
    barrier = pltpu.get_barrier_semaphore()
    bits = range(dates.bit_length() - 1)
    peers = [(d, lax.rem(l + o, lats)) for o in range(1, lats)] + [(flip(d, b), l) for b in bits]
    for peer in peers:
        pl.semaphore_signal(barrier, inc=1, device_id=peer, device_id_type=MESH)
    next_to = [(owner[0], b) for b in range(lats) if b != owner[1]] + [(flip(owner[0], b), owner[1]) for b in bits]
    away = [(a, b) for a in range(dates) for b in range(lats) if (a, b) not in next_to + [owner]]
    mine = jnp.logical_and(d == owner[0], l == owner[1])
    near = functools.reduce(jnp.logical_or, [jnp.logical_and(d == a, l == b) for a, b in next_to])
    far = jnp.logical_not(jnp.logical_or(mine, near))

    @pl.when(mine)
    def _():
        for peer in away:
            pl.semaphore_signal(barrier, inc=1, device_id=peer, device_id_type=MESH)
        pl.semaphore_wait(barrier, len(peers) + len(away))

    @pl.when(near)
    def _():
        pl.semaphore_wait(barrier, len(peers))

    @pl.when(far)
    def _():
        pl.semaphore_signal(barrier, inc=1, device_id=owner, device_id_type=MESH)
        pl.semaphore_wait(barrier, len(peers) + 1)


def read_norms(landed, first, out):
    lane = lane_ids()
    sub = lax.broadcasted_iota(jnp.int32, (8, LANES), 0)
    lines = landed[...].astype(F32)
    for i, (off, n) in enumerate(SMALL):
        row, s = divmod(off - first * LANES, LANES)
        r = pltpu.roll(lines[row : row + 8], (LANES - s) % LANES, axis=1)
        v = jnp.where(lane < LANES - s, r, pltpu.roll(r, 7, axis=0))
        t = jnp.where(sub * LANES + lane < n, v, 0.0).T
        for j in range(6):
            rows = min(LANES, CP - j * LANES)
            out[i, j * LANES : j * LANES + rows, :] = jnp.broadcast_to(t[:rows, j : j + 1], (rows, LANES))


def norm_home(lines, lats):
    start, end = OFF_G1 // LANES, (OFF_UP - 1) // LANES + 3
    owner = start // lines
    row = (start - owner * lines) // STEP * STEP
    count = -(-(end - owner * lines - row) // STEP) * STEP
    assert row + count <= -(-lines // STEP) * STEP
    return divmod(owner, lats), owner * lines + row, row, count


def gather_kernel(
    dates, lats, lines, width, src, x, out, moved, small, halo, local_sem, z_send, z_recv, send, recv,
    buffers, buffer_sems, landed, norm_sem, norm_send, norm_recv, halo_send, halo_recv,
):
    d, l = lax.axis_index("date"), lax.axis_index("lat")
    steps = dates.bit_length() - 1
    parts = pieces(src.shape[0])
    owner, first, row, count = norm_home(lines, lats)
    mine = jnp.logical_and(d == owner[0], l == owner[1])
    others = [(a, b) for a in range(dates) for b in range(lats) if (a, b) != owner]
    window = src.at[pl.ds(row, count)]

    greet(dates, lats, d, l, owner)

    def norms_to(n):
        return pltpu.make_async_remote_copy(
            src_ref=window,
            dst_ref=landed,
            send_sem=norm_send.at[n],
            recv_sem=norm_recv,
            device_id=others[n],
            device_id_type=MESH,
        )

    @pl.when(mine)
    def _():
        for n in range(len(others)):
            norms_to(n).start()
        pltpu.make_async_copy(window, landed, norm_sem).start()

    own = pltpu.make_async_copy(src, out.at[d, l], local_sem)
    own.start()
    sent, arriving, flights = [], {}, {}

    def along(o):
        copy = pltpu.make_async_remote_copy(
            src_ref=src,
            dst_ref=out.at[d, l],
            send_sem=z_send.at[o - 1],
            recv_sem=z_recv.at[o - 1],
            device_id=(d, lax.rem(l + o, lats)),
            device_id_type=MESH,
        )
        copy.start()
        sent.append(copy)
        arriving[o] = copy

    def cross(o, p, i, n):
        order = orders(dates)[p]
        block = out.at[flipped(d, span(order[:i])[n]), lax.rem(l - o + lats, lats), parts[p]]
        slot = (1 << i) - 1 + n
        copy = pltpu.make_async_remote_copy(
            src_ref=src.at[parts[p]] if o == 0 and n == 0 else block,
            dst_ref=block,
            send_sem=send.at[o, p, slot],
            recv_sem=recv.at[o, p, slot],
            device_id=(flip(d, order[i]), l),
            device_id_type=MESH,
        )
        copy.start()
        sent.append(copy)
        flights[o, p, i, n] = copy

    rows = [(s, r) for s in range(x.shape[0]) for r in range(x.shape[1])]
    saves = []

    def spread_rows():
        @pl.when(mine)
        def _():
            pltpu.make_async_copy(window, landed, norm_sem).wait()

        @pl.when(jnp.logical_not(mine))
        def _():
            norms_to(0).wait_recv()

        read_norms(landed, first, small)
        for n, (s, r) in enumerate(rows):
            if n >= 2:
                saves[n - 2].wait()
            yield from spread(x.at[s, r], small.at[0], small.at[1], width, buffers.at[n % 2])
            save = pltpu.make_async_copy(buffers.at[n % 2], moved.at[s, r], buffer_sems.at[n % 2])
            save.start()
            saves.append(save)
            yield

    def halo_copy(way):
        return pltpu.make_async_remote_copy(
            src_ref=x.at[0, 0 if way else x.shape[1] - 1],
            dst_ref=halo.at[way],
            send_sem=halo_send.at[way],
            recv_sem=halo_recv.at[way],
            device_id=(d, lax.rem(l + (lats - 1 if way else 1), lats)),
            device_id_type=MESH,
        )

    sends = [l < lats - 1, l > 0]
    aside = spread_rows()
    for wave in range(lats + steps):
        if wave < lats:
            if wave:
                arriving[wave].wait_recv()
            if wave == 0:
                for o in range(1, lats):
                    along(o)
            for i in range(steps):
                for p in range(2):
                    cross(wave, p, i, 0)
            if wave == 0:
                for way in range(2):

                    @pl.when(sends[way])
                    def _():
                        halo_copy(way).start()

        next(aside, None)
        for i in range(steps)[::-1]:
            o = wave - 1 - i
            if 0 <= o < lats:
                next(aside, None)
                for n in range(1 << i):
                    for p in range(2):
                        flights[o, p, i, n].wait_recv()
                        for later in range(i + 1, steps):
                            cross(o, p, later, n + (1 << i))
    for _ in aside:
        pass
    for save in saves[-2:]:
        save.wait()
    blank = buffers.at[0, 0]
    blank[...] = jnp.zeros_like(blank)
    for way in range(2):

        @pl.when(sends[1 - way])
        def _():
            halo_copy(way).wait_recv()

        @pl.when(jnp.logical_not(sends[1 - way]))
        def _():
            pltpu.sync_copy(blank, halo.at[way])

        @pl.when(sends[way])
        def _():
            halo_copy(way).wait_send()

    own.wait()
    for copy in sent:
        copy.wait_send()

    @pl.when(mine)
    def _():
        for n in range(len(others)):
            norms_to(n).wait_send()


def gather(shard, x, lines, dates, lats, width):
    slots = dates - 1
    moved = x.shape[:2] + (2 * REACH + 1,) + x.shape[2:]
    anywhere = pl.BlockSpec(memory_space=pl.ANY)
    return pl.pallas_call(
        functools.partial(gather_kernel, dates, lats, lines, width),
        in_specs=[anywhere, pl.BlockSpec(memory_space=pltpu.VMEM)],
        out_specs=[anywhere, anywhere, pl.BlockSpec(memory_space=pltpu.VMEM), anywhere],
        out_shape=(
            jax.ShapeDtypeStruct((dates, lats) + shard.shape, shard.dtype),
            jax.ShapeDtypeStruct(moved, BF16),
            jax.ShapeDtypeStruct((4, CP, LANES), F32),
            jax.ShapeDtypeStruct((2,) + x.shape[2:], BF16),
        ),
        scratch_shapes=[
            pltpu.SemaphoreType.DMA(()),
            pltpu.SemaphoreType.DMA((lats - 1,)),
            pltpu.SemaphoreType.DMA((lats - 1,)),
            pltpu.SemaphoreType.DMA((lats, 2, slots)),
            pltpu.SemaphoreType.DMA((lats, 2, slots)),
            pltpu.VMEM((2,) + moved[2:], BF16),
            pltpu.SemaphoreType.DMA((2,)),
            pltpu.VMEM((norm_home(lines, lats)[3], LANES), BF16),
            pltpu.SemaphoreType.DMA(()),
            pltpu.SemaphoreType.DMA((dates * lats - 1,)),
            pltpu.SemaphoreType.DMA(()),
            pltpu.SemaphoreType.DMA((2,)),
            pltpu.SemaphoreType.DMA((2,)),
        ],
        compiler_params=pltpu.CompilerParams(
            collective_id=2, has_side_effects=True, vmem_limit_bytes=VMEM
        ),
        name="gather_params",
    )(shard, x)


def vector_rows(sums, tiny, first):
    lane = lane_ids()
    sub = lax.broadcasted_iota(jnp.int32, (8, LANES), 0)
    tiny[...] = jnp.zeros_like(tiny)
    for n, (off, channels) in enumerate(SMALL):
        lines = []
        for j in range(6):
            height = min(LANES, CP - j * LANES)
            block = sums[n // 2][n % 2, j * LANES : j * LANES + height, :]
            if height < LANES:
                block = jnp.concatenate([block, jnp.zeros((LANES - height, LANES), F32)], axis=0)
            lines.append(jnp.sum(block.T, axis=0, keepdims=True))
        lines = jnp.concatenate(lines + [jnp.zeros((2, LANES), F32)], axis=0)
        lines = jnp.where(sub * LANES + lane < channels, lines, 0.0)
        row, s = divmod(off - first * LANES, LANES)
        r = pltpu.roll(lines, s, axis=1)
        moved = jnp.where(lane >= s, r, jnp.where(sub == 0, 0.0, pltpu.roll(r, 1, axis=0)))
        tiny[row : row + 8, :] = tiny[row : row + 8, :] + moved


def vector_home(lines, lats):
    start, end = OFF_G1 // LANES, (OFF_UP - 1) // LANES + 1
    owner = start // lines
    row = (start - owner * lines) // 8 * 8
    count = -(-(end + 8 - owner * lines - row) // 8) * 8
    assert end <= (owner + 1) * lines
    return divmod(owner, lats), owner * lines + row, row, count


def scatter_kernel(
    dates, lats, lines, width, src, x, gconv, own, lo, hi, to_below, to_above, gain, second_sums, out, grad,
    sums, others, z_send, z_recv, send, recv, first_sums, tiny, landed, tiny_send, tiny_recv,
    in_sems, out_sems, halo, halo_send, halo_recv, *row_buffers
):
    d, l = lax.axis_index("date"), lax.axis_index("lat")
    steps = dates.bit_length() - 1
    paths = [order[::-1] for order in orders(dates)]
    parts = pieces(src.shape[2])
    owner, first, row, count = vector_home(lines, lats)
    mine = jnp.logical_and(d == owner[0], l == owner[1])
    senders = [(a, b) for a in range(dates) for b in range(lats) if (a, b) != owner]

    greet(dates, lats, d, l, owner)
    sent, flights, z = [], {}, {}
    half = len(row_buffers) // 2
    gets = [l > 0, l < lats - 1]

    def halo_copy(slab, way):
        return pltpu.make_async_remote_copy(
            src_ref=(to_below if way else to_above).at[slab // 2],
            dst_ref=halo.at[slab // 2, way],
            send_sem=halo_send.at[slab // 2, way],
            recv_sem=halo_recv.at[slab // 2, way],
            device_id=(d, lax.rem(l + (lats - 1 if way else 1), lats)),
            device_id_type=MESH,
        )

    def arrived(slab, way):
        @pl.when(gets[way])
        def _():
            halo_copy(slab, way).wait_recv()

        @pl.when(jnp.logical_not(gets[way]))
        def _():
            halo[slab // 2, way] = jnp.zeros_like(halo[slab // 2, way])

        return halo.at[slab // 2, way]

    aside = input_rows(
        width, x, gconv, own, lo, hi, gain, grad, first_sums,
        [row_buffers[:half], row_buffers[half:]], in_sems, out_sems, arrived,
    )

    def left(p, i):
        return span(paths[p][i + 1 :][::-1])[::-1]

    def slot_of(i, n):
        return sum(1 << (steps - 1 - e) for e in range(i)) + n

    def held(o, p, i, mask):
        if i == 0:
            return src.at[flipped(d, mask), lax.rem(l + o, lats), parts[p]]
        return sums.at[o, slot_of(i - 1, left(p, i - 1).index(mask)), parts[p]]

    def cross(o, p, i, n):
        bit = paths[p][i]
        slot = slot_of(i, n)
        copy = pltpu.make_async_remote_copy(
            src_ref=held(o, p, i, left(p, i)[n] | 1 << bit),
            dst_ref=sums.at[o, slot, parts[p]],
            send_sem=send.at[o, p, slot],
            recv_sem=recv.at[o, p, slot],
            device_id=(flip(d, bit), l),
            device_id_type=MESH,
        )
        copy.start()
        sent.append(copy)
        flights[o, p, i, n] = copy

    def add(o, p, i, n):
        flights[o, p, i, n].wait_recv()
        have = held(o, p, i, left(p, i)[n])
        got = sums.at[o, slot_of(i, n), parts[p]]
        got[...] = (have[...].astype(F32) + got[...].astype(F32)).astype(BF16)
        if i + 1 < steps:
            if n < len(left(p, i + 1)):
                cross(o, p, i + 1, n)
        elif o:
            copy = pltpu.make_async_remote_copy(
                src_ref=got,
                dst_ref=others.at[o - 1, parts[p]],
                send_sem=z_send.at[o - 1, p],
                recv_sem=z_recv.at[o - 1, p],
                device_id=(d, lax.rem(l + o, lats)),
                device_id_type=MESH,
            )
            copy.start()
            sent.append(copy)
            z[o, p] = copy

    turns = list(range(1, lats)) + [0]
    for o in turns:
        for n in range(len(left(0, 0))):
            for p in range(2):
                cross(o, p, 0, n)
    for slab in range(1, x.shape[0], 2):
        for way in range(2):

            @pl.when(gets[1 - way])
            def _():
                halo_copy(slab, way).start()

    for wave in range(lats + steps - 1):
        for i in range(steps):
            if 0 <= wave - i < lats:
                if i:
                    for _ in range(ASIDE):
                        next(aside, None)
                for n in range(len(left(0, i))):
                    for p in range(2):
                        add(turns[wave - i], p, i, n)
    for _ in aside:
        pass
    vector_rows((first_sums, second_sums), tiny, first)

    def to_owner(n):
        return pltpu.make_async_remote_copy(
            src_ref=tiny,
            dst_ref=landed.at[n],
            send_sem=tiny_send,
            recv_sem=tiny_recv.at[n],
            device_id=owner,
            device_id_type=MESH,
        )

    @pl.when(jnp.logical_not(mine))
    def _():
        to_owner(d * lats + l).start()

    for p in range(2):
        total = sums[0, slot_of(steps - 1, 0), parts[p]].astype(F32)
        for o in range(1, lats):
            z[o, p].wait_recv()
            total = total + others[o - 1, parts[p]].astype(F32)
        amount = min(parts[p].start + parts[p].size, lines) - parts[p].start
        out[pl.ds(parts[p].start, amount)] = total[:amount]

    @pl.when(mine)
    def _():
        total = tiny[...]
        for a, b in senders:
            to_owner(a * lats + b).wait_recv()
            total = total + landed[a * lats + b]
        out[row : row + count, :] = out[row : row + count, :] + total

    @pl.when(jnp.logical_not(mine))
    def _():
        to_owner(d * lats + l).wait_send()

    for copy in sent:
        copy.wait_send()
    for slab in range(1, x.shape[0], 2):
        for way in range(2):

            @pl.when(gets[1 - way])
            def _():
                halo_copy(slab, way).wait_send()


def scatter(packed, lines, x, gconv, own, lo, hi, to_below, to_above, gain, second_sums, width):
    dates, lats, rows, lanes = packed.shape
    slots = dates - 1
    tiny = (vector_home(lines, lats)[3], LANES)
    anywhere, held = pl.BlockSpec(memory_space=pl.ANY), pl.BlockSpec(memory_space=pltpu.VMEM)
    low = pltpu.VMEM((CP, WIDE), BF16)
    row_buffers = [low, low, pltpu.VMEM((CP, WIDE), F32), low, low, low]
    return pl.pallas_call(
        functools.partial(scatter_kernel, dates, lats, lines, width),
        in_specs=[held] + [anywhere] * 7 + [held] * 2,
        out_specs=[held, anywhere],
        out_shape=(jax.ShapeDtypeStruct((lines, lanes), F32), jax.ShapeDtypeStruct(x.shape, BF16)),
        scratch_shapes=[
            pltpu.VMEM((lats, slots, rows, lanes), BF16),
            pltpu.VMEM((lats - 1, rows, lanes), BF16),
            pltpu.SemaphoreType.DMA((lats - 1, 2)),
            pltpu.SemaphoreType.DMA((lats - 1, 2)),
            pltpu.SemaphoreType.DMA((lats, 2, slots)),
            pltpu.SemaphoreType.DMA((lats, 2, slots)),
            pltpu.VMEM((2, CP, LANES), F32),
            pltpu.VMEM(tiny, F32),
            pltpu.VMEM((dates * lats,) + tiny, F32),
            pltpu.SemaphoreType.DMA(()),
            pltpu.SemaphoreType.DMA((dates * lats,)),
            pltpu.SemaphoreType.DMA((2, 5)),
            pltpu.SemaphoreType.DMA((2,)),
            pltpu.VMEM((x.shape[0] // 2, 2, CP, WIDE), BF16),
            pltpu.SemaphoreType.DMA((x.shape[0] // 2, 2)),
            pltpu.SemaphoreType.DMA((x.shape[0] // 2, 2)),
        ]
        + row_buffers * 2,
        compiler_params=pltpu.CompilerParams(
            collective_id=1, has_side_effects=True, vmem_limit_bytes=VMEM
        ),
        name="scatter_grads",
    )(packed, x, gconv, own, lo, hi, to_below, to_above, gain, second_sums)


def local(inputs, noise, cotangent, params, psi, step_counts, pixel_mask, offsets, bases):
    samples, steps, rows, width, _ = inputs.shape
    slabs = samples * steps
    dates, lats = lax.axis_size("date"), lax.axis_size("lat")
    lat = rows * lats

    def by_channel(values):
        return jnp.swapaxes(values, 3, 4).reshape(slabs, rows, -1, width)

    def padded(values):
        return jnp.pad(values, ((0, 0), (0, 0), (0, CP - values.shape[2]), (0, WIDE - width)))

    upward = [(i, i + 1) for i in range(lats - 1)]
    downward = [(i + 1, i) for i in range(lats - 1)]
    lines = params.shape[0] // LANES
    held = -(-lines // STEP) * STEP
    shard = jnp.pad(params.reshape(lines, LANES), ((0, held - lines), (0, 0)))
    x = padded(jnp.concatenate([by_channel(inputs), by_channel(noise)], axis=2))
    edges = [(x[s, rows - 1 :], x[s, :1]) for s in range(slabs)]
    gathered, moved, small, halo = gather(shard, x, lines, dates, lats, width)
    gathered = gathered.reshape(dates * lats, held, LANES)
    cot = padded(by_channel(cotangent)).reshape(slabs * rows, CP, WIDE)
    active = jnp.arange(steps, dtype=jnp.int32)[None, :] < step_counts[:, None]
    mask = active.reshape(slabs, 1, 1) * pixel_mask[None]
    mask = jnp.pad(mask.astype(F32), ((0, 0), (0, 0), (0, WIDE - width)))
    matrices = unpack(gathered, lines)
    halos, done = [(halo[:1], halo[1:])], halo
    for s in range(1, slabs):
        top, bottom, done = lax.optimization_barrier((*edges[s], done))
        halos.append((lax.ppermute(top, "lat", upward), lax.ppermute(bottom, "lat", downward)))
        done = halos[-1]
    basis = ()
    for s in range(slabs):
        basis = (lift(offsets, bases, psi, *halos[s], moved, small[0], small[1], basis, s, lat, width),)
    basis = basis[0]
    w, wt, up, upt, dn, dnt = matrices
    basis = basis.reshape(slabs * rows, BASIS * CP, WIDE)
    output, gconv, gup, gdn, second_sums = block(
        basis, x.reshape(slabs * rows, CP, WIDE), cot, mask.reshape(slabs * rows, 1, WIDE),
        wt, upt, up, dnt, dn, small[2], small[3],
    )
    gconv_rows = gconv.reshape(slabs, rows, CP, WIDE)
    own, below_even, above_even, to_below, to_above = lower(offsets, bases, psi, gconv_rows, w, width)
    from_below = lax.ppermute(above_even, "lat", upward)
    from_above = lax.ppermute(below_even, "lat", downward)
    packed = grads(basis, gconv, gup, gdn, dates * lats, lines, held)
    summed, grad = scatter(
        packed.reshape(dates, lats, held, LANES), lines,
        x, gconv_rows, own, from_below, from_above, to_below, to_above, small[0], second_sums, width,
    )

    def by_pixel(values):
        values = values.reshape(slabs, rows, CP, WIDE)[:, :, :C, :width]
        return jnp.swapaxes(values.reshape(samples, steps, rows, C, width), 3, 4)

    return by_pixel(output), by_pixel(grad), summed.reshape(-1)


def solution(mesh):
    field = P("date", None, "lat", None, None)
    flat = P(("date", "lat"))
    return jax.shard_map(
        local,
        mesh=mesh,
        in_specs=(field, field, field, flat, P(), P("date"), P("lat", None), P(), P()),
        out_specs=(field, field, flat),
        check_vma=False,
    )
```

```python
import functools
import math

import jax
import jax.numpy as jnp
from jax import lax
from jax.experimental import pallas as pl
from jax.experimental.pallas import tpu as pltpu
from jax.sharding import PartitionSpec as P

C = 641
HID = 1282
BASIS = 4
SUPPORT = 12
REACH = 2
CIN = 649
BF16, F32 = jnp.bfloat16, jnp.float32
MESH = pl.DeviceIdType.MESH
LANES = 128
STEP = 16
CP = 656
HP = 1296
WIDE = 768
HL = 1408
UNROLL = 8
ASIDE = 2
PARTS = 2
VMEM = 60 << 20


OFF_G1=BASIS*CIN*C+C; OFF_S1=OFF_G1+CIN; OFF_G2=OFF_S1+CIN; OFF_S2=OFF_G2+C; OFF_UP=OFF_S2+C; OFF_DN=OFF_UP+(C+1)*HID;
SMALL=((OFF_G1,CIN),(OFF_S1,CIN),(OFF_G2,C),(OFF_S2,C))
MATS=((0,C,BASIS*CIN+1,128,3),(OFF_UP,HID,C+1,64,2),(OFF_DN,C,HID+1,128,2))
F_ROWS=29952
def lane_ids(): return lax.broadcasted_iota(jnp.int32,(8,LANES),1)
def place(base,cols,period,b):
    start=base+cols*b
    return start//LANES, start%LANES
def rolled(values, amount):
    out = []
    for n in range(0, len(values), 2):
        pieces = values[n : n + 2]
        if len(pieces) == 2:
            both = jnp.concatenate(pieces, axis=0).astype(BF16)
            both = pltpu.roll(both, amount, axis=1).astype(F32)
            out += [both[:8], both[8:]]
        else:
            out.append(pltpu.roll(pieces[0].astype(BF16).astype(F32), amount, axis=1))
    return out


def flatten(lists):
    return [value for values in lists for value in values]


def unflat(values, width):
    return [values[n : n + width] for n in range(0, len(values), width)]


def unpack_kernel(nrow,pad,g_ref,w_out,wt_out,up_out,upt_out,dn_out,dnt_out,held,w_ref,wt_ref,up_ref,upt_ref,dn_ref,dnt_ref,flat,chunks,in_sems,out_sems):
    shards=held.shape[0]
    parts=[pl.ds(n*shards//4,(n+1)*shards//4-n*shards//4) for n in range(4)]
    loads=[pltpu.make_async_copy(g_ref.at[part],held.at[part],in_sems.at[n]) for n,part in enumerate(parts)]
    for copy in loads:
        copy.start()
    saves=[]
    def save(source,target):
        copy=pltpu.make_async_copy(source,target,out_sems.at[len(saves)])
        copy.start()
        saves.append(copy)
    def fill(s,_):
        flat[pl.ds(nrow*s,pad),:]=held[s].astype(F32); return 0
    for n,copy in enumerate(loads):
        copy.wait()
        lax.fori_loop(n*shards//4,(n+1)*shards//4,fill,0)
    lane=lane_ids()
    def split(base,cols,period,groups):
        J=-(-cols//LANES); pitch=period+8; height=pitch*8*groups+8; last=cols-(J-1)*LANES
        def body(b,_):
            row,s=place(base,cols,period,b)
            back=(LANES-s)%LANES
            found=[[flat[pl.ds(row+641*8*g+j,8,stride=641),:] for g in range(groups)] for j in range(J+1)]
            found=unflat(rolled(flatten(found),back),groups)
            for g in range(groups):
                for j in range(J):
                    val=jnp.where(lane<LANES-s,found[j][g],found[j+1][g])
                    if j==J-1: val=jnp.where(lane<last,val,0.0)
                    chunks[pl.ds(j*height+8*g*pitch+b,8,stride=pitch),:]=val
            return 0
        lax.fori_loop(0,period,body,0,unroll=8)
        def border(a,_):
            for j in range(J): chunks[pl.ds(j*height+a*pitch-8,8),:]=chunks[pl.ds(j*height+a*pitch,8),:]
            return 0
        lax.fori_loop(1,8*groups,border,0)
        return J,height,period
    def convert(dst,dst_row,src_row,rows,pad_rows,J,height,period):
        full=rows//16
        def piece(j,r): return chunks[pl.ds(j*height+r//period*(period+8)+r%period,8),:]
        def pair(j,r): return jnp.concatenate([piece(j,r),piece(j,r+8)],axis=0)
        def body(m,_):
            for j in range(J):
                dst[pl.ds(pl.multiple_of(dst_row+16*m,16),16),j*LANES:(j+1)*LANES]=pair(j,src_row+16*m).astype(BF16)
            return 0
        lax.fori_loop(0,full,body,0,unroll=4)
        keep=lax.broadcasted_iota(jnp.int32,(16,LANES),0)<rows-16*full
        for m in range(full,pad_rows//16):
            for j in range(J):
                v=jnp.where(keep,pair(j,src_row+16*m),0.0) if m==full else jnp.zeros((16,LANES),F32)
                dst[dst_row+16*m:dst_row+16*m+16,j*LANES:(j+1)*LANES]=v.astype(BF16)
    J,h,p=split(*MATS[0][:2],*MATS[0][3:])
    for k in range(BASIS):
        convert(w_ref,k*CP,k*CIN,CIN+(k==BASIS-1),CP,J,h,p)
    save(w_ref,w_out)
    wt_ref[...]=w_ref[:,:CP].T
    save(wt_ref,wt_out)
    J,h,p=split(*MATS[1][:2],*MATS[1][3:])
    convert(up_ref,0,0,C+1,CP,J,h,p)
    save(up_ref,up_out)
    upt_ref[...]=up_ref[:,:HP].T
    save(upt_ref,upt_out)
    J,h,p=split(*MATS[2][:2],*MATS[2][3:])
    convert(dn_ref,0,0,HID+1,HP,J,h,p)
    save(dn_ref,dn_out)
    dnt_ref[...]=dn_ref[:,:CP].T
    save(dnt_ref,dnt_out)
    for copy in saves:
        copy.wait()


def unpack(gathered,nrow):
    shapes=[(BASIS*CP,WIDE),(CP,BASIS*CP),(CP,HL),(HP,CP),(HP,WIDE),(CP,HP)]
    anywhere=pl.BlockSpec(memory_space=pl.ANY)
    return pl.pallas_call(functools.partial(unpack_kernel,nrow,gathered.shape[1]),
        in_specs=[anywhere],
        out_specs=[anywhere]*6,
        out_shape=tuple(jax.ShapeDtypeStruct(shape,BF16) for shape in shapes),
        scratch_shapes=[pltpu.VMEM(gathered.shape,BF16)]+[pltpu.VMEM(shape,BF16) for shape in shapes]
        +[pltpu.VMEM((F_ROWS,LANES),F32),pltpu.VMEM((6*(136*24+8),LANES),F32),pltpu.SemaphoreType.DMA((4,)),pltpu.SemaphoreType.DMA((6,))],
        compiler_params=pltpu.CompilerParams(vmem_limit_bytes=VMEM),name="unpack")(gathered)


def chunk_gather(src, chunks, src_row, dst_row, rows, J, height, last, period):
    lane, sub = lane_ids(), lax.broadcasted_iota(jnp.int32, (8, LANES), 0)

    def step(m):
        at = dst_row + 8 * m
        at = at // period * (period + 8) + at % period
        for j in range(J):
            v = src[pl.ds(src_row + 8 * m, 8), j * LANES : (j + 1) * LANES]
            if j == J - 1:
                v = jnp.where(lane < last, v, 0.0)
            if isinstance(m, int) and 8 * m + 8 > rows:
                v = jnp.where(sub < rows - 8 * m, v, 0.0)
            chunks[pl.ds(j * height + at + 8, 8), :] = v
            chunks[pl.ds(j * height + at, 8), :] = v

    return step


def chunk_clear(chunks, J, height, row, period):
    row = row // period * (period + 8) + row % period

    def body(m, _):
        for j in range(J):
            chunks[pl.ds(j * height + row + 8 * m, 8), :] = jnp.zeros((8, LANES), F32)
        return 0

    lax.fori_loop(0, (height - row) // 8, body, 0)


def line_merge(flat, flat0, chunks, base, cols, period, groups):
    lane, sub = lane_ids(), lax.broadcasted_iota(jnp.int32, (8, LANES), 0)
    J, pitch = -(-cols // LANES), period + 8
    height = pitch * 8 * groups + 8
    row0 = base // LANES - flat0

    def step(b, tails, last=False):
        row, s = place(base, cols, period, b)
        row = row - flat0
        found = [
            chunks[pl.ds(j * height + 8 * g * pitch + b, 8, stride=pitch), :]
            for g in range(groups)
            for j in range(J)
        ]
        found = unflat(rolled(found, s), J)
        new = []
        keep = lane >= s
        for g in range(groups):
            x = found[g]
            for j in range(J):
                v = jnp.where(keep, x[j], tails[g] if j == 0 else x[j - 1])
                if not (last and j == J - 1):
                    flat[pl.ds(row + 641 * 8 * g + j, 8, stride=641), :] = v
            new.append(jnp.where(s == LANES - 1, jnp.where(keep, 0.0, x[J - 1]), v))
        return tuple(new)

    def first():
        init = [jnp.zeros((8, LANES), F32)] * groups
        if base == OFF_DN:
            init[0] = jnp.where(sub == 0, flat[row0 : row0 + 8, :], 0.0)
        return tuple(init)

    def finish(tails):
        if base % LANES:
            for g in range(groups):
                at = pl.ds(row0 + 641 * (8 * g + 1), 8, stride=641)
                flat[at, :] = flat[at, :] + tails[g]

    return step, first, finish


FFN_ROW = OFF_UP // LANES // 8 * 8
FFN_ROWS = OFF_DN // LANES + 641 * 16 + 40 - FFN_ROW
DISCO_ROWS = 641 * 24 + 16


def grads_kernel(nrow, basis, gconv, gup, gdn, out, *refs):
    low, conv, gd, flat, ffn, chunks, gu, gn, stage, in_sems, ffn_sems, out_sems = refs
    count = basis.shape[0]
    shards, pad = out.shape[:2]

    def loads(i):
        return [
            pltpu.make_async_copy(basis.at[i], low.at[i % 2], in_sems.at[i % 2, 0]),
            pltpu.make_async_copy(gconv.at[i], conv.at[i % 2], in_sems.at[i % 2, 1]),
        ]

    weights = [pltpu.make_async_copy(a, b, ffn_sems.at[n]) for n, (a, b) in enumerate(((gup, gu), (gdn, gn)))]
    flying = {}
    for i in range(min(2, count)):
        flying[i] = loads(i)
        for copy in flying[i]:
            copy.start()
        weights[i].start()

    def outer(i, n):
        if n == 0:
            for copy in flying[i]:
                copy.wait()
        at = slice(n * CP, (n + 1) * CP)
        term = lax.dot_general(
            low[i % 2, at, :], conv[i % 2], (((1,), (1,)), ((), ())), preferred_element_type=F32
        )
        if i:
            gd[at, :CP] += term
        else:
            gd[at, :CP] = term
        if n == BASIS - 1 and i + 2 < count:
            flying[i + 2] = loads(i + 2)
            for copy in flying[i + 2]:
                copy.start()

    def lay(n, src, rows, J, height, last, base, cols, period, groups):
        state = {}
        copy = chunk_gather(src, chunks, 0, 0, rows, J, height, last, period)
        step, first, finish = line_merge(ffn, FFN_ROW, chunks, base, cols, period, groups)
        pieces = -(-rows // 8)

        def begin():
            weights[n].wait()

        def gather(start):
            for m in range(start, min(start + 4, pieces)):
                copy(m)

        def ready():
            chunk_clear(chunks, J, height, 8 * pieces, period)
            state["tails"] = first()

        def merge(b):
            state["tails"] = step(b, state["tails"], last=base % LANES and b == period - 1)

        def done():
            finish(state["tails"])

        steps = [begin] + [functools.partial(gather, m) for m in range(0, pieces, 4)] + [ready]
        return steps + [functools.partial(merge, b) for b in range(period)] + [done]

    products = [functools.partial(outer, i, n) for i in range(count) for n in range(BASIS)]
    for n in range(2):
        if n >= count:
            weights[n].start()
    up_steps = lay(0, gu, C + 1, 11, 72 * 16 + 8, 2, OFF_UP, HID, 64, 2)
    down_steps = lay(1, gn, HID + 1, 6, 136 * 16 + 8, 1, OFF_DN, C, 128, 2)
    weave(products, up_steps + down_steps)

    height = 136 * 24 + 8
    for k in range(BASIS):
        rows = CIN + (k == BASIS - 1)
        copy = chunk_gather(gd, chunks, k * CP, k * CIN, rows, 6, height, 1, 128)

        def body(m, _):
            copy(m)
            return 0

        lax.fori_loop(0, rows // 8, body, 0, unroll=4)
        copy(rows // 8)
    chunk_clear(chunks, 6, height, 2600, 128)
    step, first, _ = line_merge(flat, 0, chunks, 0, C, 128, 3)
    lax.fori_loop(0, 128, step, first(), unroll=8)
    seam = OFF_UP // LANES
    for shard in range(shards):
        if nrow * shard < seam < nrow * shard + pad:
            amount = nrow * shard + pad - seam
            flat[seam : seam + amount, :] = ffn[seam - FFN_ROW : seam - FFN_ROW + amount, :]
    slots = stage.shape[0]

    def save(shard, slot):
        return pltpu.make_async_copy(stage.at[slot], out.at[shard], out_sems.at[slot])

    for shard in range(shards):
        slot = shard % slots
        if shard >= slots:
            save(shard - slots, slot).wait()
        source, start = (flat, nrow * shard) if nrow * shard < seam else (ffn, nrow * shard - FFN_ROW)
        stage[slot] = source[start : start + pad, :].astype(BF16)
        save(shard, slot).start()
    for shard in range(max(shards - slots, 0), shards):
        save(shard, shard % slots).wait()


def grads(basis, gconv, gup, gdn, n, nrow, pad):
    anywhere = pl.BlockSpec(memory_space=pl.ANY)
    return pl.pallas_call(
        functools.partial(grads_kernel, nrow),
        in_specs=[anywhere] * 4,
        out_specs=anywhere,
        out_shape=jax.ShapeDtypeStruct((n, pad, LANES), BF16),
        scratch_shapes=[
            pltpu.VMEM((2, BASIS * CP, WIDE), BF16),
            pltpu.VMEM((2, CP, WIDE), BF16),
            pltpu.VMEM((BASIS * CP, WIDE), F32),
            pltpu.VMEM((DISCO_ROWS, LANES), F32),
            pltpu.VMEM((FFN_ROWS, LANES), F32),
            pltpu.VMEM((6 * (136 * 24 + 8), LANES), F32),
            pltpu.VMEM(gup.shape, F32),
            pltpu.VMEM(gdn.shape, F32),
            pltpu.VMEM((4, pad, LANES), BF16),
            pltpu.SemaphoreType.DMA((2, 2)),
            pltpu.SemaphoreType.DMA((2,)),
            pltpu.SemaphoreType.DMA((4,)),
        ],
        compiler_params=pltpu.CompilerParams(vmem_limit_bytes=VMEM),
        name="grads",
    )(basis, gconv, gup, gdn)


def tiled(column):
    return jnp.concatenate([column] * (WIDE // LANES), axis=1)


def lane_of(rows, start=0):
    return lax.broadcasted_iota(jnp.int32, (rows, LANES), 1) + start


def wrapped(chunk, width):
    head, first, last = chunk[:, : WIDE - LANES], chunk[:, :LANES], chunk[:, WIDE - LANES :]
    edge = width - (WIDE - LANES)
    lane = lane_of(chunk.shape[0])
    beyond = jnp.where(
        lane < LANES - REACH, pltpu.roll(first, edge, axis=1), pltpu.roll(last, LANES - edge, axis=1)
    )
    return jnp.concatenate([head, jnp.where(lane < edge, last, beyond)], axis=1)


def cut(chunk, width):
    head, last = chunk[:, : WIDE - LANES], chunk[:, WIDE - LANES :]
    keep = lane_of(chunk.shape[0], WIDE - LANES) < width
    return jnp.concatenate([head, jnp.where(keep, last, 0.0)], axis=1)


def rows_below(count):
    return lax.broadcasted_iota(jnp.int32, (STEP, WIDE), 0) < count


def halves(chunk):
    return chunk[:8] + chunk[8:]


def column_sums(read, channels, count):
    whole = channels // STEP

    def body(m, sums):
        return tuple(a + halves(v) for a, v in zip(sums, read(m)))

    sums = lax.fori_loop(
        0, whole, body, tuple(jnp.zeros((8, WIDE), F32) for _ in range(count)), unroll=UNROLL
    )
    keep = rows_below(channels - whole * STEP)
    sums = [a + halves(jnp.where(keep, v, 0.0)) for a, v in zip(sums, read(whole))]
    return [jnp.sum(a, axis=0, keepdims=True) for a in sums]


def norm_stats(read, channels):
    (total,) = column_sums(lambda m: (read(m),), channels, 1)
    mean = total * (1.0 / channels)

    def squares(m):
        centered = read(m) - mean
        return (centered * centered,)

    (total,) = column_sums(squares, channels, 1)
    return mean, lax.rsqrt(total * (1.0 / channels) + 1e-05)


def each_chunk(body, unroll=None):
    def step(m, _):
        body(m, pl.ds(pl.multiple_of(m * STEP, STEP), STEP))
        return 0

    lax.fori_loop(0, CP // STEP, step, 0, unroll=unroll)


def spread(source, gain, shift, width, moved):
    def read(c):
        return source[pl.ds(pl.multiple_of(c * STEP, STEP), STEP), :].astype(F32)

    mean, scale = norm_stats(read, CIN)
    yield

    def shifts(c, at):
        values = (read(c) - mean) * scale * tiled(gain[at, :]) + tiled(shift[at, :])
        values = wrapped(values, width).astype(BF16)
        for d in range(-REACH, REACH + 1):
            moved[d + REACH, at, :] = pltpu.roll(values, -d % WIDE, axis=1) if d else values

    def step(m, _):
        shifts(m, pl.ds(pl.multiple_of(m * STEP, STEP), STEP))
        return 0

    chunks = CP // STEP
    for n in range(PARTS):
        lax.fori_loop(n * chunks // PARTS, (n + 1) * chunks // PARTS, step, 0, unroll=4)
        yield


def points_of(bases):
    named = [bases[p] for p in range(SUPPORT)]
    ranks = []
    for p in range(SUPPORT):
        rank = jnp.int32(0)
        for before in range(p):
            rank = rank + jnp.where(named[before] == named[p], 1, 0)
        ranks.append(rank)
    picks = {}
    for k in range(BASIS):
        for q in range(3):
            pick = jnp.int32(0)
            for p in range(SUPPORT):
                pick = pick + jnp.where(jnp.logical_and(named[p] == k, ranks[p] == q), p, 0)
            picks[k, q] = pick
    return picks


def combine_row(r, first_row, lat, width, offsets, picks, psi, moved, out):
    for k in range(BASIS):
        parts = []
        for q in range(3):
            p = picks[k, q]
            row = first_row + r + offsets[p, 0]
            inside = jnp.logical_and(row >= 0, row < lat)
            weight = jnp.where(inside, psi[first_row + r, p], 0.0)
            parts.append((weight, r + 1 + offsets[p, 0], offsets[p, 1] + REACH))

        def combine(c, at):
            total = None
            for weight, row, d in parts:
                term = weight * moved[row, d, at, :].astype(F32)
                total = term if total is None else total + term
            to = pl.ds(pl.multiple_of(k * CP + c * STEP, STEP), STEP)
            out[to, :] = cut(total, width).astype(BF16)

        each_chunk(combine, 8)
    last = slice(BASIS * CP - STEP, BASIS * CP)
    bias_row = CIN - (CP - STEP)
    sub = lax.broadcasted_iota(jnp.int32, (STEP, WIDE), 0)
    lane = lax.broadcasted_iota(jnp.int32, (STEP, WIDE), 1)
    ones = jnp.where(lane < width, 1.0, 0.0)
    out[last, :] = jnp.where(sub == bias_row, ones, out[last, :].astype(F32)).astype(BF16)


def lift_kernel(rows, lat, width, offsets, bases, psi, own, small, *refs):
    out, moved, built, ends, sems, out_sems, end_sems = refs[-7:]
    halos = refs[:-7]
    slabs = out.shape[0]
    first_row = lax.axis_index("lat") * rows
    ways = [halos[0].at[0], halos[0].at[1]] + [halo.at[0] for halo in halos[1:]]
    sources = [pltpu.make_async_copy(way, ends.at[n], end_sems.at[n]) for n, way in enumerate(ways)]
    for copy in sources:
        copy.start()

    def inner(s):
        return [pltpu.make_async_copy(own.at[s, r], moved.at[r + 1], sems.at[r]) for r in range(rows)]

    picks = points_of(bases)
    saves = {}
    for s in range(slabs):
        for copy in inner(s):
            copy.start()
        for way, m in ((0, 0), (1, rows + 1)):
            sources[2 * s + way].wait()
            for _ in spread(ends.at[2 * s + way], small.at[0], small.at[1], width, moved.at[m]):
                pass
        for copy in inner(s):
            copy.wait()
        for r in range(rows):
            if s:
                saves[s - 1, r].wait()
            combine_row(r, first_row, lat, width, offsets, picks, psi, moved, built.at[r])
            saves[s, r] = pltpu.make_async_copy(built.at[r], out.at[s, r], out_sems.at[r])
            saves[s, r].start()
    for r in range(rows):
        saves[slabs - 1, r].wait()


def lift(offsets, bases, psi, halos, own, small, lat, width):
    slabs, rows = own.shape[:2]
    smem = pl.BlockSpec(memory_space=pltpu.SMEM)
    anywhere, held = pl.BlockSpec(memory_space=pl.ANY), pl.BlockSpec(memory_space=pltpu.VMEM)
    return pl.pallas_call(
        functools.partial(lift_kernel, rows, lat, width),
        in_specs=[smem, smem, smem, anywhere, held] + [anywhere] * len(halos),
        out_specs=anywhere,
        out_shape=jax.ShapeDtypeStruct((slabs, rows, BASIS * CP, WIDE), BF16),
        scratch_shapes=[
            pltpu.VMEM((rows + 2, 2 * REACH + 1, CP, WIDE), BF16),
            pltpu.VMEM((rows, BASIS * CP, WIDE), BF16),
            pltpu.VMEM((2 * slabs, CP, WIDE), BF16),
            pltpu.SemaphoreType.DMA((rows,)),
            pltpu.SemaphoreType.DMA((rows,)),
            pltpu.SemaphoreType.DMA((2 * slabs,)),
        ],
        compiler_params=pltpu.CompilerParams(vmem_limit_bytes=VMEM),
        cost_estimate=pl.CostEstimate(flops=40 << 20, bytes_accessed=40 << 20, transcendentals=0),
        name="lift",
    )(offsets, bases, psi, own, small, *halos)


GELU_A = math.sqrt(2.0 / math.pi)
GELU_B = 0.044715


TILE = 256


def weave(*lists):
    order = []
    for which, steps in enumerate(lists):
        for n, step in enumerate(steps):
            order.append(((n + 0.5) / len(steps), which, n, step))
    for _, _, _, step in sorted(order, key=lambda entry: entry[:3]):
        step()


class Job:
    def __init__(self, buffers, weights, totals, mask):
        self.basis, self.x, self.cot, self.out, self.gconv = buffers[:5]
        self.res, self.second, self.pre, self.act, self.mid, self.gact, self.gb, self.gpre = buffers[5:]
        self.wt, self.upt, self.up, self.dnt, self.dn, self.gain, self.shift = weights
        self.gup, self.gdn, self.sums = totals
        self.mask = mask

    @staticmethod
    def at(c):
        return slice(c * STEP, (c + 1) * STEP)

    @staticmethod
    def wide(column):
        return jnp.concatenate([column] * (TILE // LANES), axis=1)

    @staticmethod
    def only(c, values, channels, other=0.0):
        if (c + 1) * STEP <= channels:
            return values
        row = lax.broadcasted_iota(jnp.int32, (STEP, TILE), 0)
        return jnp.where(row < channels - c * STEP, values, other)

    def product(self, out, left, right, count):
        rows = left.shape[0]
        size = -(-rows // (count * STEP)) * STEP

        def step(start):
            at = slice(start, min(start + size, rows))
            values = left[at, : right.shape[0]]
            out[at, :] = jnp.dot(values, right[...], preferred_element_type=F32)

        return [functools.partial(step, start) for start in range(0, rows, size)]

    def outer(self, out, left, right, count):
        rows = left.shape[0]
        size = -(-rows // (count * STEP)) * STEP

        def step(start):
            at = slice(start, min(start + size, rows))
            term = lax.dot_general(
                left[at, :], right[...], (((1,), (1,)), ((), ())), preferred_element_type=F32
            )
            out[at, : right.shape[0]] += term

        return [functools.partial(step, start) for start in range(0, rows, size)]

    def m1(self):
        return self.product(self.res, self.wt, self.basis, 4)

    def v1(self):
        state = {"sum": jnp.zeros((8, TILE), F32), "square": jnp.zeros((8, TILE), F32)}
        mask = self.mask()

        def add(c):
            at = self.at(c)
            value = self.res[at, :] + self.only(c, self.x[at, :].astype(F32), C)
            self.res[at, :] = value
            self.gb[at, :] = (self.cot[at, :].astype(F32) * mask).astype(BF16)
            state["sum"] = state["sum"] + halves(self.only(c, value, C))

        def mean():
            self.mean = jnp.sum(state["sum"], axis=0, keepdims=True) * (1.0 / C)

        def square(c):
            value = self.res[self.at(c), :] - self.mean
            state["square"] = state["square"] + halves(self.only(c, value * value, C))

        def scale():
            total = jnp.sum(state["square"], axis=0, keepdims=True)
            self.scale = lax.rsqrt(total * (1.0 / C) + 1e-05)

        def normalize(c):
            at = self.at(c)
            value = (self.res[at, :] - self.mean) * self.scale
            value = value * self.wide(self.gain[at, :]) + self.wide(self.shift[at, :])
            row = lax.broadcasted_iota(jnp.int32, (STEP, TILE), 0)
            if c == C // STEP:
                value = jnp.where(row == C % STEP, 1.0, value)
            self.second[at, :] = value.astype(BF16)

        chunks = range(CP // STEP)
        steps = [functools.partial(add, c) for c in chunks] + [mean]
        steps += [functools.partial(square, c) for c in chunks] + [scale]
        return steps + [functools.partial(normalize, c) for c in chunks]

    def m2(self):
        return self.product(self.pre, self.upt, self.second, 9)

    def v2(self):
        def gelu(c):
            at = self.at(c)
            v = self.pre[at, :]
            square = v * v
            bend = jnp.tanh(GELU_A * v * (1.0 + GELU_B * square))
            half = 0.5 * (1.0 + bend)
            value = v * half
            if c == HID // STEP:
                row = lax.broadcasted_iota(jnp.int32, (STEP, TILE), 0)
                value = jnp.where(row == HID % STEP, 1.0, value)
            self.act[at, :] = value.astype(BF16)
            rise = GELU_A * (1.0 + 3.0 * GELU_B * square)
            self.pre[at, :] = half + 0.5 * v * (1.0 - bend * bend) * rise

        return [functools.partial(gelu, c) for c in range(HP // STEP)]

    def m3(self):
        back = self.product(self.gact, self.dn, self.gb, 9)
        return self.product(self.mid, self.dnt, self.act, 4) + back

    def v3(self):
        def finish(c):
            at = self.at(c)
            self.out[at, :] = (self.res[at, :] + self.mid[at, :]).astype(BF16)

        def back(c):
            at = self.at(c)
            self.gpre[at, :] = (self.gact[at, :] * self.pre[at, :]).astype(BF16)

        steps = [functools.partial(finish, c) for c in range(CP // STEP)]
        return steps + [functools.partial(back, c) for c in range(HP // STEP)]

    def m4(self):
        return self.product(self.mid, self.up, self.gpre, 4)

    def v4(self):
        state = {"flat": jnp.zeros((8, TILE), F32), "along": jnp.zeros((8, TILE), F32)}

        def terms(c):
            at = self.at(c)
            dm = self.mid[at, :]
            xhat = (self.res[at, :] - self.mean) * self.scale
            return dm, xhat, dm * self.wide(self.gain[at, :])

        def means(c):
            _, xhat, g = terms(c)
            g = self.only(c, g, C)
            state["flat"] = state["flat"] + halves(g)
            state["along"] = state["along"] + halves(g * xhat)

        def join():
            for name in state:
                state[name] = jnp.sum(state[name], axis=0, keepdims=True) * (1.0 / C)

        def backward(c):
            at = self.at(c)
            dm, xhat, g = terms(c)
            value = g - state["flat"] - xhat * state["along"]
            value = self.gb[at, :].astype(F32) + self.scale * value
            self.gconv[at, :] = self.only(c, value, C).astype(BF16)
            for n, term in enumerate((dm * xhat, dm)):
                self.sums[n, at, :] += term[:, :LANES] + term[:, LANES:]

        chunks = range(CP // STEP)
        steps = [functools.partial(means, c) for c in chunks] + [join]
        return steps + [functools.partial(backward, c) for c in chunks]

    def m5(self):
        first = self.outer(self.gdn, self.act, self.gb, 3)
        return first + self.outer(self.gup, self.second, self.gpre, 2)


def block_kernel(
    basis, x, cot, mask, wt, upt, up, dnt, dn, small, out, gconv, gup, gdn, sums, *scratch
):
    gain, shift = small.at[2], small.at[3]
    count = basis.shape[0]
    tiles = WIDE // TILE
    in_sems, out_sems = scratch[-2:]
    per_job = (len(scratch) - 2) // 2
    sets = [scratch[:per_job], scratch[per_job : 2 * per_job]]
    for total in (gup, gdn, sums):
        total[...] = jnp.zeros_like(total)

    def place(i, j):
        return i // tiles * 2 + j, pl.ds(pl.multiple_of(i % tiles * TILE, TILE), TILE)

    def arrive(i, j):
        row, lanes = place(i, j)
        return [
            pltpu.make_async_copy(source.at[row, :, lanes], sets[j][n], in_sems.at[j, n])
            for n, source in enumerate((basis, x, cot))
        ]

    def leave(i, j):
        row, lanes = place(i, j)
        return [
            pltpu.make_async_copy(sets[j][3 + n], target.at[row, :, lanes], out_sems.at[j, n])
            for n, target in enumerate((out, gconv))
        ]

    last = count // 2 * tiles - 1
    for j in range(2):
        for copy in arrive(0, j):
            copy.start()

    def pair(i, _):
        def row_mask(j):
            row, lanes = place(i, j)
            return lambda: mask[row, :, lanes]

        weights, totals = (wt, upt, up, dnt, dn, gain, shift), (gup, gdn, sums)
        a, b = (Job(sets[j], weights, totals, row_mask(j)) for j in range(2))
        after = jnp.minimum(i + 1, last)
        coming = [arrive(after, j) for j in range(2)]
        leaving = [leave(i, j) for j in range(2)]
        for j in range(2):
            for copy in arrive(i, j):
                copy.wait()
        weave(a.m1())
        coming[0][0].start()
        weave(a.v1(), b.m1())
        coming[1][0].start()
        for n in (1, 2):
            coming[0][n].start()
        weave(a.m2(), b.v1())
        for n in (1, 2):
            coming[1][n].start()
        weave(a.v2(), b.m2())
        weave(a.m3(), b.v2())
        weave(a.v3(), b.m3())
        leaving[0][0].start()
        weave(a.m4(), b.v3())
        leaving[1][0].start()
        weave(a.v4(), b.m4())
        leaving[0][1].start()
        weave(a.m5(), b.v4())
        leaving[1][1].start()
        weave(b.m5())
        for copies in leaving:
            for copy in copies:
                copy.wait()
        return 0

    lax.fori_loop(0, last + 1, pair, 0)
    for j in range(2):
        for copy in arrive(last, j):
            copy.wait()


def block(basis, x, cot, mask, wt, upt, up, dnt, dn, small):
    count = x.shape[0]
    anywhere = pl.BlockSpec(memory_space=pl.ANY)
    held = pl.BlockSpec(memory_space=pltpu.VMEM)
    low, high = pltpu.VMEM((CP, TILE), BF16), pltpu.VMEM((CP, TILE), F32)
    hidden_low, hidden_high = pltpu.VMEM((HP, TILE), BF16), pltpu.VMEM((HP, TILE), F32)
    per_job = [pltpu.VMEM((BASIS * CP, TILE), BF16), low, low, low, low]
    per_job += [high, low, hidden_high, hidden_low, high, hidden_high, low, hidden_low]
    return pl.pallas_call(
        block_kernel,
        in_specs=[anywhere] * 3 + [held] * 7,
        out_specs=[anywhere] * 2 + [held] * 3,
        out_shape=(
            jax.ShapeDtypeStruct((count, CP, WIDE), BF16),
            jax.ShapeDtypeStruct((count, CP, WIDE), BF16),
            jax.ShapeDtypeStruct((CP, HL), F32),
            jax.ShapeDtypeStruct((HP, WIDE), F32),
            jax.ShapeDtypeStruct((2, CP, LANES), F32),
        ),
        scratch_shapes=per_job * 2 + [pltpu.SemaphoreType.DMA((2, 3)), pltpu.SemaphoreType.DMA((2, 2))],
        compiler_params=pltpu.CompilerParams(vmem_limit_bytes=VMEM),
        name="block",
    )(basis, x, cot, mask, wt, upt, up, dnt, dn, small)


def along_lanes(ref, at, values):
    total = values[:, :LANES]
    for j in range(1, WIDE // LANES):
        total = total + values[:, j * LANES : (j + 1) * LANES]
    ref[at, :] = ref[at, :] + total


GROUP = 11 * STEP
GROUP_STEP = 10 * STEP


def lower_kernel(rows, width, offsets, bases, psi, gconv, w, own, lo0, hi0, lo1, hi1, *scratch):
    place, coef, in_sems, w_sems, out_sems = scratch[-5:]
    per_slab = (len(scratch) - 5) // 2
    sets = [scratch[:per_slab], scratch[per_slab : 2 * per_slab]]
    first_row = lax.axis_index("lat") * rows
    span = 2 * REACH + 1
    groups = 1 + (CP - GROUP) // GROUP_STEP
    for n in range(3 * span):
        place[n] = 0
        for r in range(rows):
            coef[r, n] = 0.0
    for p in range(SUPPORT):
        n = (offsets[p, 0] + 1) * span + offsets[p, 1] + REACH
        place[n] = bases[p]
        for r in range(rows):
            coef[r, n] = psi[first_row + r, p]

    def channels(g):
        return pl.ds(pl.multiple_of(g * GROUP_STEP, STEP), GROUP)

    def weights(j, g):
        return pltpu.make_async_copy(w.at[:, channels(g), :], sets[j][1], w_sems.at[j])

    def products(j):
        ring, part, lifted = sets[j][:3]

        def step(r, k):
            values = jnp.dot(part[k, :, :CP], ring[r], preferred_element_type=F32)
            lifted[r, k] = values.astype(BF16)

        return [functools.partial(step, r, k) for r in range(rows) for k in range(BASIS)]

    def gathers(j):
        lifted, inner, below, above = sets[j][2:]

        def step(c, target):
            at = slice(c * STEP, (c + 1) * STEP)
            total = None
            for d in range(-REACH, REACH + 1):
                part = None
                for o in (-1, 0, 1):
                    r = target - o
                    if 0 <= r < rows:
                        n = (o + 1) * span + d + REACH
                        term = coef[r, n] * lifted[r, place[n], at, :].astype(F32)
                        part = term if part is None else part + term
                if d:
                    part = pltpu.roll(part.astype(BF16), d % WIDE, axis=1).astype(F32)
                total = part if total is None else total + part
            if target < 0:
                below[at, :] = total.astype(BF16)
            elif target == rows:
                above[at, :] = total.astype(BF16)
            else:
                inner[target, at, :] = total

        return [functools.partial(step, c, t) for c in range(GROUP // STEP) for t in range(-1, rows + 1)]

    def pair_of_slabs(both, _):
        def leaving(j, g):
            slab = both * 2 + j
            lo, hi = ((lo0, hi0), (lo1, hi1))[j]
            targets = (own.at[slab, :, channels(g), :], lo.at[both, channels(g), :], hi.at[both, channels(g), :])
            return [
                pltpu.make_async_copy(sets[j][3 + n], target, out_sems.at[j, n])
                for n, target in enumerate(targets)
            ]

        rings = [pltpu.make_async_copy(gconv.at[both * 2 + j], sets[j][0], in_sems.at[j]) for j in range(2)]
        for j in range(2):
            rings[j].start()
            weights(j, 0).start()
        for j in range(2):
            rings[j].wait()
            ring = sets[j][0]
            edge = width - (WIDE - LANES)
            lane = lane_of(CP)
            for r in range(rows):
                first, last = ring[r, :, :LANES].astype(F32), ring[r, :, WIDE - LANES :].astype(F32)
                beyond = jnp.where(
                    lane < LANES - REACH,
                    pltpu.roll(first, edge, axis=1),
                    pltpu.roll(last, LANES - edge, axis=1),
                )
                ring[r, :, WIDE - LANES :] = jnp.where(lane < edge, last, beyond).astype(BF16)
        weights(0, 0).wait()
        weave(products(0))
        weights(0, min(1, groups - 1)).start()

        def group(g, _):
            after, later = jnp.minimum(g + 1, groups - 1), jnp.minimum(g + 2, groups - 1)
            def free(j):
                @pl.when(g > 0)
                def _():
                    for copy in leaving(j, jnp.maximum(g - 1, 0)):
                        copy.wait()

            weights(1, g).wait()
            free(0)
            weave(products(1), gathers(0))
            weights(1, after).start()
            for copy in leaving(0, g):
                copy.start()
            weights(0, after).wait()
            free(1)
            weave(products(0), gathers(1))
            weights(0, later).start()
            for copy in leaving(1, g):
                copy.start()
            return 0

        lax.fori_loop(0, groups, group, 0)
        for j in range(2):
            weights(j, groups - 1).wait()
            for copy in leaving(j, groups - 1):
                copy.wait()
        return 0

    lax.fori_loop(0, gconv.shape[0] // 2, pair_of_slabs, 0)


def lower(offsets, bases, psi, gconv, w, width):
    slabs, rows = gconv.shape[:2]
    smem = pl.BlockSpec(memory_space=pltpu.SMEM)
    anywhere = pl.BlockSpec(memory_space=pl.ANY)
    edge = jax.ShapeDtypeStruct((slabs // 2, CP, WIDE), BF16)
    per_slab = [
        pltpu.VMEM((rows, CP, WIDE), BF16),
        pltpu.VMEM((BASIS, GROUP, WIDE), BF16),
        pltpu.VMEM((rows, BASIS, GROUP, WIDE), BF16),
        pltpu.VMEM((rows, GROUP, WIDE), F32),
        pltpu.VMEM((GROUP, WIDE), BF16),
        pltpu.VMEM((GROUP, WIDE), BF16),
    ]
    return pl.pallas_call(
        functools.partial(lower_kernel, rows, width),
        in_specs=[smem, smem, smem, anywhere, anywhere],
        out_specs=[anywhere] * 5,
        out_shape=(jax.ShapeDtypeStruct((slabs, rows, CP, WIDE), F32),) + (edge,) * 4,
        scratch_shapes=per_slab * 2
        + [
            pltpu.SMEM((3 * (2 * REACH + 1),), jnp.int32),
            pltpu.SMEM((rows, 3 * (2 * REACH + 1)), F32),
            pltpu.SemaphoreType.DMA((2,)),
            pltpu.SemaphoreType.DMA((2,)),
            pltpu.SemaphoreType.DMA((2, 3)),
        ],
        compiler_params=pltpu.CompilerParams(vmem_limit_bytes=VMEM),
        name="lower",
    )(offsets, bases, psi, gconv, w.reshape(BASIS, CP, WIDE))


def input_rows(width, x, gconv, own, lo, hi, gain, grad, sums, buffers, in_sems, out_sems, arrived):
    rows = x.shape[1]
    places = [(s, r) for s in range(x.shape[0]) for r in range(rows)]
    saves = []

    def loads(n):
        s, r = places[n]
        sources = [x.at[s, r], gconv.at[s, r], own.at[s, r]]
        sources += [lo.at[s // 2]] if r == 0 and s % 2 == 0 else []
        sources += [hi.at[s // 2]] if r == rows - 1 and s % 2 == 0 else []
        slots = [0, 1, 2] + ([3] if r == 0 else []) + ([4] if r == rows - 1 else [])
        return [
            pltpu.make_async_copy(source, buffers[n % 2][slot], in_sems.at[n % 2, slot])
            for source, slot in zip(sources, slots)
        ]

    flying = loads(0)
    for copy in flying:
        copy.start()
    sums[...] = jnp.zeros_like(sums)
    for n, (s, r) in enumerate(places):
        for copy in flying:
            copy.wait()
        if n + 1 < len(places):
            flying = loads(n + 1)
            for copy in flying:
                copy.start()
        here, conv, total, below, above, result = buffers[n % 2]
        if s % 2:
            below = arrived(s, 0) if r == 0 else None
            above = arrived(s, 1) if r == rows - 1 else None

        def read(c):
            return here[pl.ds(pl.multiple_of(c * STEP, STEP), STEP), :].astype(F32)

        mean, scale = norm_stats(read, CIN)
        yield

        if r == 0 or r == rows - 1:

            def join(c, at):
                value = total[at, :]
                if r == 0:
                    value = value + below[at, :].astype(F32)
                if r == rows - 1:
                    value = value + above[at, :].astype(F32)
                total[at, :] = value

            each_chunk(join, 8)
            yield

        def means(c):
            at = pl.ds(pl.multiple_of(c * STEP, STEP), STEP)
            g = total[at, :] * tiled(gain[at, :])
            return g, g * ((read(c) - mean) * scale)

        flat, along = [v * (1.0 / CIN) for v in column_sums(means, CIN, 2)]
        yield
        if n >= 2:
            saves[n - 2].wait()

        def backward(c, at):
            dm = cut(total[at, :], width)
            xhat = (read(c) - mean) * scale
            g = dm * tiled(gain[at, :])
            value = scale * (g - flat - xhat * along) + conv[at, :].astype(F32)
            result[at, :] = value.astype(BF16)
            along_lanes(sums.at[0], at, dm * xhat)
            along_lanes(sums.at[1], at, dm)

        each_chunk(backward, 8)
        save = pltpu.make_async_copy(result, grad.at[s, r], out_sems.at[n % 2])
        save.start()
        saves.append(save)
        yield
    for save in saves[-2:]:
        save.wait()


def flip(value, bit):
    return value + (1 - 2 * ((value // (1 << bit)) % 2)) * (1 << bit)


def flipped(value, mask):
    bit = 0
    while mask >> bit:
        if mask >> bit & 1:
            value = flip(value, bit)
        bit += 1
    return value


def span(bits):
    masks = [0]
    for b in bits:
        masks = masks + [m | 1 << b for m in masks]
    return masks


def orders(dates):
    bits = list(range(1, dates.bit_length() - 1))
    return bits + [0], bits[::-1] + [0]


def pieces(rows):
    cut = rows // (2 * STEP) * STEP
    return pl.ds(0, cut), pl.ds(cut, rows - cut)


def greet(dates, lats, d, l, owner):
    barrier = pltpu.get_barrier_semaphore()
    bits = range(dates.bit_length() - 1)
    peers = [(d, lax.rem(l + o, lats)) for o in range(1, lats)] + [(flip(d, b), l) for b in bits]
    for peer in peers:
        pl.semaphore_signal(barrier, inc=1, device_id=peer, device_id_type=MESH)
    next_to = [(owner[0], b) for b in range(lats) if b != owner[1]] + [(flip(owner[0], b), owner[1]) for b in bits]
    away = [(a, b) for a in range(dates) for b in range(lats) if (a, b) not in next_to + [owner]]
    mine = jnp.logical_and(d == owner[0], l == owner[1])
    near = functools.reduce(jnp.logical_or, [jnp.logical_and(d == a, l == b) for a, b in next_to])
    far = jnp.logical_not(jnp.logical_or(mine, near))

    @pl.when(mine)
    def _():
        for peer in away:
            pl.semaphore_signal(barrier, inc=1, device_id=peer, device_id_type=MESH)
        pl.semaphore_wait(barrier, len(peers) + len(away))

    @pl.when(near)
    def _():
        pl.semaphore_wait(barrier, len(peers))

    @pl.when(far)
    def _():
        pl.semaphore_signal(barrier, inc=1, device_id=owner, device_id_type=MESH)
        pl.semaphore_wait(barrier, len(peers) + 1)


def read_norms(landed, first, out):
    lane = lane_ids()
    sub = lax.broadcasted_iota(jnp.int32, (8, LANES), 0)
    lines = landed[...].astype(F32)
    for i, (off, n) in enumerate(SMALL):
        row, s = divmod(off - first * LANES, LANES)
        r = pltpu.roll(lines[row : row + 8], (LANES - s) % LANES, axis=1)
        v = jnp.where(lane < LANES - s, r, pltpu.roll(r, 7, axis=0))
        t = jnp.where(sub * LANES + lane < n, v, 0.0).T
        for j in range(6):
            rows = min(LANES, CP - j * LANES)
            out[i, j * LANES : j * LANES + rows, :] = jnp.broadcast_to(t[:rows, j : j + 1], (rows, LANES))


def norm_home(lines, lats):
    start, end = OFF_G1 // LANES, (OFF_UP - 1) // LANES + 3
    owner = start // lines
    row = (start - owner * lines) // STEP * STEP
    count = -(-(end - owner * lines - row) // STEP) * STEP
    assert row + count <= -(-lines // STEP) * STEP
    return divmod(owner, lats), owner * lines + row, row, count


def gather_kernel(
    dates, lats, lines, width, src, x, out, moved, small, halo, local_sem, z_send, z_recv, send, recv,
    buffers, buffer_sems, landed, norm_sem, norm_send, norm_recv, halo_send, halo_recv, near, near_sem,
):
    d, l = lax.axis_index("date"), lax.axis_index("lat")
    steps = dates.bit_length() - 1
    parts = pieces(src.shape[0])
    owner, first, row, count = norm_home(lines, lats)
    mine = jnp.logical_and(d == owner[0], l == owner[1])
    others = [(a, b) for a in range(dates) for b in range(lats) if (a, b) != owner]
    window = src.at[pl.ds(row, count)]
    nearby = pltpu.make_async_copy(x, near, near_sem)
    nearby.start()

    greet(dates, lats, d, l, owner)

    def norms_to(n):
        return pltpu.make_async_remote_copy(
            src_ref=window,
            dst_ref=landed,
            send_sem=norm_send.at[n],
            recv_sem=norm_recv,
            device_id=others[n],
            device_id_type=MESH,
        )

    @pl.when(mine)
    def _():
        for n in range(len(others)):
            norms_to(n).start()
        pltpu.make_async_copy(window, landed, norm_sem).start()

    own = pltpu.make_async_copy(src, out.at[d, l], local_sem)
    own.start()
    sent, arriving, flights = [], {}, {}

    def along(o):
        copy = pltpu.make_async_remote_copy(
            src_ref=src,
            dst_ref=out.at[d, l],
            send_sem=z_send.at[o - 1],
            recv_sem=z_recv.at[o - 1],
            device_id=(d, lax.rem(l + o, lats)),
            device_id_type=MESH,
        )
        copy.start()
        sent.append(copy)
        arriving[o] = copy

    def cross(o, p, i, n):
        order = orders(dates)[p]
        block = out.at[flipped(d, span(order[:i])[n]), lax.rem(l - o + lats, lats), parts[p]]
        slot = (1 << i) - 1 + n
        copy = pltpu.make_async_remote_copy(
            src_ref=src.at[parts[p]] if o == 0 and n == 0 else block,
            dst_ref=block,
            send_sem=send.at[o, p, slot],
            recv_sem=recv.at[o, p, slot],
            device_id=(flip(d, order[i]), l),
            device_id_type=MESH,
        )
        copy.start()
        sent.append(copy)
        flights[o, p, i, n] = copy

    rows = [(s, r) for s in range(x.shape[0]) for r in range(x.shape[1])]
    saves = []

    def spread_rows():
        @pl.when(mine)
        def _():
            pltpu.make_async_copy(window, landed, norm_sem).wait()

        @pl.when(jnp.logical_not(mine))
        def _():
            norms_to(0).wait_recv()

        read_norms(landed, first, small)
        nearby.wait()
        for n, (s, r) in enumerate(rows):
            if n >= 2:
                saves[n - 2].wait()
            yield from spread(near.at[s, r], small.at[0], small.at[1], width, buffers.at[n % 2])
            save = pltpu.make_async_copy(buffers.at[n % 2], moved.at[s, r], buffer_sems.at[n % 2])
            save.start()
            saves.append(save)
            yield

    def halo_copy(way):
        return pltpu.make_async_remote_copy(
            src_ref=x.at[0, 0 if way else x.shape[1] - 1],
            dst_ref=halo.at[way],
            send_sem=halo_send.at[way],
            recv_sem=halo_recv.at[way],
            device_id=(d, lax.rem(l + (lats - 1 if way else 1), lats)),
            device_id_type=MESH,
        )

    sends = [l < lats - 1, l > 0]
    aside = spread_rows()
    for wave in range(lats + steps):
        if wave < lats:
            if wave:
                arriving[wave].wait_recv()
            if wave == 0:
                for o in range(1, lats):
                    along(o)
            for i in range(steps):
                for p in range(2):
                    cross(wave, p, i, 0)
            if wave == 0:
                for way in range(2):

                    @pl.when(sends[way])
                    def _():
                        halo_copy(way).start()

        next(aside, None)
        for i in range(steps)[::-1]:
            o = wave - 1 - i
            if 0 <= o < lats:
                next(aside, None)
                for n in range(1 << i):
                    for p in range(2):
                        flights[o, p, i, n].wait_recv()
                        for later in range(i + 1, steps):
                            cross(o, p, later, n + (1 << i))
    for _ in aside:
        pass
    for save in saves[-2:]:
        save.wait()
    blank = buffers.at[0, 0]
    blank[...] = jnp.zeros_like(blank)
    for way in range(2):

        @pl.when(sends[1 - way])
        def _():
            halo_copy(way).wait_recv()

        @pl.when(jnp.logical_not(sends[1 - way]))
        def _():
            pltpu.sync_copy(blank, halo.at[way])

        @pl.when(sends[way])
        def _():
            halo_copy(way).wait_send()

    own.wait()
    for copy in sent:
        copy.wait_send()

    @pl.when(mine)
    def _():
        for n in range(len(others)):
            norms_to(n).wait_send()


def gather(shard, x, lines, dates, lats, width):
    slots = dates - 1
    moved = x.shape[:2] + (2 * REACH + 1,) + x.shape[2:]
    anywhere = pl.BlockSpec(memory_space=pl.ANY)
    return pl.pallas_call(
        functools.partial(gather_kernel, dates, lats, lines, width),
        in_specs=[anywhere, anywhere],
        out_specs=[anywhere, anywhere, pl.BlockSpec(memory_space=pltpu.VMEM), anywhere],
        out_shape=(
            jax.ShapeDtypeStruct((dates, lats) + shard.shape, shard.dtype),
            jax.ShapeDtypeStruct(moved, BF16),
            jax.ShapeDtypeStruct((4, CP, LANES), F32),
            jax.ShapeDtypeStruct((2,) + x.shape[2:], BF16),
        ),
        scratch_shapes=[
            pltpu.SemaphoreType.DMA(()),
            pltpu.SemaphoreType.DMA((lats - 1,)),
            pltpu.SemaphoreType.DMA((lats - 1,)),
            pltpu.SemaphoreType.DMA((lats, 2, slots)),
            pltpu.SemaphoreType.DMA((lats, 2, slots)),
            pltpu.VMEM((2,) + moved[2:], BF16),
            pltpu.SemaphoreType.DMA((2,)),
            pltpu.VMEM((norm_home(lines, lats)[3], LANES), BF16),
            pltpu.SemaphoreType.DMA(()),
            pltpu.SemaphoreType.DMA((dates * lats - 1,)),
            pltpu.SemaphoreType.DMA(()),
            pltpu.SemaphoreType.DMA((2,)),
            pltpu.SemaphoreType.DMA((2,)),
            pltpu.VMEM(x.shape, BF16),
            pltpu.SemaphoreType.DMA(()),
        ],
        compiler_params=pltpu.CompilerParams(
            collective_id=2, has_side_effects=True, vmem_limit_bytes=VMEM
        ),
        name="gather_params",
    )(shard, x)


def vector_rows(sums, tiny, first):
    lane = lane_ids()
    sub = lax.broadcasted_iota(jnp.int32, (8, LANES), 0)
    tiny[...] = jnp.zeros_like(tiny)
    for n, (off, channels) in enumerate(SMALL):
        lines = []
        for j in range(6):
            height = min(LANES, CP - j * LANES)
            block = sums[n // 2][n % 2, j * LANES : j * LANES + height, :]
            if height < LANES:
                block = jnp.concatenate([block, jnp.zeros((LANES - height, LANES), F32)], axis=0)
            lines.append(jnp.sum(block.T, axis=0, keepdims=True))
        lines = jnp.concatenate(lines + [jnp.zeros((2, LANES), F32)], axis=0)
        lines = jnp.where(sub * LANES + lane < channels, lines, 0.0)
        row, s = divmod(off - first * LANES, LANES)
        r = pltpu.roll(lines, s, axis=1)
        moved = jnp.where(lane >= s, r, jnp.where(sub == 0, 0.0, pltpu.roll(r, 1, axis=0)))
        tiny[row : row + 8, :] = tiny[row : row + 8, :] + moved


def vector_home(lines, lats):
    start, end = OFF_G1 // LANES, (OFF_UP - 1) // LANES + 1
    owner = start // lines
    row = (start - owner * lines) // 8 * 8
    count = -(-(end + 8 - owner * lines - row) // 8) * 8
    assert end <= (owner + 1) * lines
    return divmod(owner, lats), owner * lines + row, row, count


def scatter_kernel(
    dates, lats, lines, width, src, x, gconv, own, lo, hi, to_below, to_above, small, second_sums, out, grad,
    sums, others, z_send, z_recv, send, recv, first_sums, tiny, landed, tiny_send, tiny_recv,
    in_sems, out_sems, halo, halo_send, halo_recv, near, near_sem, *row_buffers
):
    d, l = lax.axis_index("date"), lax.axis_index("lat")
    steps = dates.bit_length() - 1
    paths = [order[::-1] for order in orders(dates)]
    parts = pieces(src.shape[2])
    owner, first, row, count = vector_home(lines, lats)
    mine = jnp.logical_and(d == owner[0], l == owner[1])
    senders = [(a, b) for a in range(dates) for b in range(lats) if (a, b) != owner]

    nearby = pltpu.make_async_copy(src, near, near_sem)
    nearby.start()
    greet(dates, lats, d, l, owner)
    sent, flights, z = [], {}, {}
    half = len(row_buffers) // 2
    gets = [l > 0, l < lats - 1]

    def halo_copy(slab, way):
        return pltpu.make_async_remote_copy(
            src_ref=(to_below if way else to_above).at[slab // 2],
            dst_ref=halo.at[slab // 2, way],
            send_sem=halo_send.at[slab // 2, way],
            recv_sem=halo_recv.at[slab // 2, way],
            device_id=(d, lax.rem(l + (lats - 1 if way else 1), lats)),
            device_id_type=MESH,
        )

    def arrived(slab, way):
        @pl.when(gets[way])
        def _():
            halo_copy(slab, way).wait_recv()

        @pl.when(jnp.logical_not(gets[way]))
        def _():
            halo[slab // 2, way] = jnp.zeros_like(halo[slab // 2, way])

        return halo.at[slab // 2, way]

    aside = input_rows(
        width, x, gconv, own, lo, hi, small.at[0], grad, first_sums,
        [row_buffers[:half], row_buffers[half:]], in_sems, out_sems, arrived,
    )

    def left(p, i):
        return span(paths[p][i + 1 :][::-1])[::-1]

    def slot_of(i, n):
        return sum(1 << (steps - 1 - e) for e in range(i)) + n

    def held(o, p, i, mask):
        if i == 0:
            return near.at[flipped(d, mask), lax.rem(l + o, lats), parts[p]]
        return sums.at[o, slot_of(i - 1, left(p, i - 1).index(mask)), parts[p]]

    def first_block(o, p, mask):
        return src.at[flipped(d, mask), lax.rem(l + o, lats), parts[p]]

    def cross(o, p, i, n):
        bit = paths[p][i]
        slot = slot_of(i, n)
        copy = pltpu.make_async_remote_copy(
            src_ref=held(o, p, i, left(p, i)[n] | 1 << bit) if i else first_block(o, p, left(p, i)[n] | 1 << bit),
            dst_ref=sums.at[o, slot, parts[p]],
            send_sem=send.at[o, p, slot],
            recv_sem=recv.at[o, p, slot],
            device_id=(flip(d, bit), l),
            device_id_type=MESH,
        )
        copy.start()
        sent.append(copy)
        flights[o, p, i, n] = copy

    def add(o, p, i, n):
        flights[o, p, i, n].wait_recv()
        have = held(o, p, i, left(p, i)[n])
        got = sums.at[o, slot_of(i, n), parts[p]]
        got[...] = (have[...].astype(F32) + got[...].astype(F32)).astype(BF16)
        if i + 1 < steps:
            if n < len(left(p, i + 1)):
                cross(o, p, i + 1, n)
        elif o:
            copy = pltpu.make_async_remote_copy(
                src_ref=got,
                dst_ref=others.at[o - 1, parts[p]],
                send_sem=z_send.at[o - 1, p],
                recv_sem=z_recv.at[o - 1, p],
                device_id=(d, lax.rem(l + o, lats)),
                device_id_type=MESH,
            )
            copy.start()
            sent.append(copy)
            z[o, p] = copy

    turns = list(range(1, lats)) + [0]
    for o in turns:
        for n in range(len(left(0, 0))):
            for p in range(2):
                cross(o, p, 0, n)
    for slab in range(1, x.shape[0], 2):
        for way in range(2):

            @pl.when(gets[1 - way])
            def _():
                halo_copy(slab, way).start()

    nearby.wait()
    for wave in range(lats + steps - 1):
        for i in range(steps):
            if 0 <= wave - i < lats:
                if i:
                    for _ in range(ASIDE):
                        next(aside, None)
                for n in range(len(left(0, i))):
                    for p in range(2):
                        add(turns[wave - i], p, i, n)
    for _ in aside:
        pass
    vector_rows((first_sums, second_sums), tiny, first)

    def to_owner(n):
        return pltpu.make_async_remote_copy(
            src_ref=tiny,
            dst_ref=landed.at[n],
            send_sem=tiny_send,
            recv_sem=tiny_recv.at[n],
            device_id=owner,
            device_id_type=MESH,
        )

    @pl.when(jnp.logical_not(mine))
    def _():
        to_owner(d * lats + l).start()

    for p in range(2):
        total = sums[0, slot_of(steps - 1, 0), parts[p]].astype(F32)
        for o in range(1, lats):
            z[o, p].wait_recv()
            total = total + others[o - 1, parts[p]].astype(F32)
        amount = min(parts[p].start + parts[p].size, lines) - parts[p].start
        out[pl.ds(parts[p].start, amount)] = total[:amount]

    @pl.when(mine)
    def _():
        total = tiny[...]
        for a, b in senders:
            to_owner(a * lats + b).wait_recv()
            total = total + landed[a * lats + b]
        out[row : row + count, :] = out[row : row + count, :] + total

    @pl.when(jnp.logical_not(mine))
    def _():
        to_owner(d * lats + l).wait_send()

    for copy in sent:
        copy.wait_send()
    for slab in range(1, x.shape[0], 2):
        for way in range(2):

            @pl.when(gets[1 - way])
            def _():
                halo_copy(slab, way).wait_send()


def scatter(packed, lines, x, gconv, own, lo, hi, to_below, to_above, small, second_sums, width):
    dates, lats, rows, lanes = packed.shape
    slots = dates - 1
    tiny = (vector_home(lines, lats)[3], LANES)
    anywhere, held = pl.BlockSpec(memory_space=pl.ANY), pl.BlockSpec(memory_space=pltpu.VMEM)
    low = pltpu.VMEM((CP, WIDE), BF16)
    row_buffers = [low, low, pltpu.VMEM((CP, WIDE), F32), low, low, low]
    return pl.pallas_call(
        functools.partial(scatter_kernel, dates, lats, lines, width),
        in_specs=[anywhere] * 8 + [held] * 2,
        out_specs=[held, anywhere],
        out_shape=(jax.ShapeDtypeStruct((lines, lanes), F32), jax.ShapeDtypeStruct(x.shape, BF16)),
        scratch_shapes=[
            pltpu.VMEM((lats, slots, rows, lanes), BF16),
            pltpu.VMEM((lats - 1, rows, lanes), BF16),
            pltpu.SemaphoreType.DMA((lats - 1, 2)),
            pltpu.SemaphoreType.DMA((lats - 1, 2)),
            pltpu.SemaphoreType.DMA((lats, 2, slots)),
            pltpu.SemaphoreType.DMA((lats, 2, slots)),
            pltpu.VMEM((2, CP, LANES), F32),
            pltpu.VMEM(tiny, F32),
            pltpu.VMEM((dates * lats,) + tiny, F32),
            pltpu.SemaphoreType.DMA(()),
            pltpu.SemaphoreType.DMA((dates * lats,)),
            pltpu.SemaphoreType.DMA((2, 5)),
            pltpu.SemaphoreType.DMA((2,)),
            pltpu.VMEM((x.shape[0] // 2, 2, CP, WIDE), BF16),
            pltpu.SemaphoreType.DMA((x.shape[0] // 2, 2)),
            pltpu.SemaphoreType.DMA((x.shape[0] // 2, 2)),
            pltpu.VMEM(packed.shape, BF16),
            pltpu.SemaphoreType.DMA(()),
        ]
        + row_buffers * 2,
        compiler_params=pltpu.CompilerParams(
            collective_id=1, has_side_effects=True, vmem_limit_bytes=VMEM
        ),
        name="scatter_grads",
    )(packed, x, gconv, own, lo, hi, to_below, to_above, small, second_sums)


def local(inputs, noise, cotangent, params, psi, step_counts, pixel_mask, offsets, bases):
    samples, steps, rows, width, _ = inputs.shape
    slabs = samples * steps
    dates, lats = lax.axis_size("date"), lax.axis_size("lat")
    lat = rows * lats

    def by_channel(values):
        return jnp.swapaxes(values, 3, 4).reshape(slabs, rows, -1, width)

    def padded(values):
        return jnp.pad(values, ((0, 0), (0, 0), (0, CP - values.shape[2]), (0, WIDE - width)))

    upward = [(i, i + 1) for i in range(lats - 1)]
    downward = [(i + 1, i) for i in range(lats - 1)]
    lines = params.shape[0] // LANES
    held = -(-lines // STEP) * STEP
    shard = jnp.pad(params.reshape(lines, LANES), ((0, held - lines), (0, 0)))
    x = padded(jnp.concatenate([by_channel(inputs), by_channel(noise)], axis=2))
    edges = [(x[s, rows - 1 :], x[s, :1]) for s in range(slabs)]
    gathered, moved, small, halo = gather(shard, x, lines, dates, lats, width)
    gathered = gathered.reshape(dates * lats, held, LANES)
    cot = padded(by_channel(cotangent)).reshape(slabs * rows, CP, WIDE)
    active = jnp.arange(steps, dtype=jnp.int32)[None, :] < step_counts[:, None]
    mask = active.reshape(slabs, 1, 1) * pixel_mask[None]
    mask = jnp.pad(mask.astype(F32), ((0, 0), (0, 0), (0, WIDE - width)))
    matrices = unpack(gathered, lines)
    halos, done = [halo], halo
    for s in range(1, slabs):
        top, bottom, done = lax.optimization_barrier((*edges[s], done))
        done = lax.ppermute(top, "lat", upward), lax.ppermute(bottom, "lat", downward)
        halos += done
    basis = lift(offsets, bases, psi, halos, moved, small, lat, width)
    w, wt, up, upt, dn, dnt = matrices
    basis = basis.reshape(slabs * rows, BASIS * CP, WIDE)
    output, gconv, gup, gdn, second_sums = block(
        basis, x.reshape(slabs * rows, CP, WIDE), cot, mask.reshape(slabs * rows, 1, WIDE),
        wt, upt, up, dnt, dn, small,
    )
    gconv_rows = gconv.reshape(slabs, rows, CP, WIDE)
    own, below_even, above_even, to_below, to_above = lower(offsets, bases, psi, gconv_rows, w, width)
    from_below = lax.ppermute(above_even, "lat", upward)
    from_above = lax.ppermute(below_even, "lat", downward)
    packed = grads(basis, gconv, gup, gdn, dates * lats, lines, held)
    summed, grad = scatter(
        packed.reshape(dates, lats, held, LANES), lines,
        x, gconv_rows, own, from_below, from_above, to_below, to_above, small, second_sums, width,
    )

    def by_pixel(values):
        values = values.reshape(slabs, rows, CP, WIDE)[:, :, :C, :width]
        return jnp.swapaxes(values.reshape(samples, steps, rows, C, width), 3, 4)

    return by_pixel(output), by_pixel(grad), summed.reshape(-1)


def solution(mesh):
    field = P("date", None, "lat", None, None)
    flat = P(("date", "lat"))
    return jax.shard_map(
        local,
        mesh=mesh,
        in_specs=(field, field, field, flat, P(), P("date"), P("lat", None), P(), P()),
        out_specs=(field, field, flat),
        check_vma=False,
    )
```

```python
import functools
import math

import jax
import jax.numpy as jnp
from jax import lax
from jax.experimental import pallas as pl
from jax.experimental.pallas import tpu as pltpu
from jax.sharding import PartitionSpec as P

C = 641
HID = 1282
BASIS = 4
SUPPORT = 12
REACH = 2
CIN = 649
BF16, F32 = jnp.bfloat16, jnp.float32
MESH = pl.DeviceIdType.MESH
LANES = 128
STEP = 16
CP = 656
HP = 1296
WIDE = 768
HL = 1408
UNROLL = 8
ASIDE = 2
PARTS = 2
VMEM = 60 << 20


OFF_G1=BASIS*CIN*C+C; OFF_S1=OFF_G1+CIN; OFF_G2=OFF_S1+CIN; OFF_S2=OFF_G2+C; OFF_UP=OFF_S2+C; OFF_DN=OFF_UP+(C+1)*HID;
SMALL=((OFF_G1,CIN),(OFF_S1,CIN),(OFF_G2,C),(OFF_S2,C))
MATS=((0,C,BASIS*CIN+1,128,3),(OFF_UP,HID,C+1,64,2),(OFF_DN,C,HID+1,128,2))
F_ROWS=29952
def lane_ids(): return lax.broadcasted_iota(jnp.int32,(8,LANES),1)
def place(base,cols,period,b):
    start=base+cols*b
    return start//LANES, start%LANES
def rolled(values, amount):
    out = []
    for n in range(0, len(values), 2):
        pieces = values[n : n + 2]
        if len(pieces) == 2:
            both = jnp.concatenate(pieces, axis=0).astype(BF16)
            both = pltpu.roll(both, amount, axis=1).astype(F32)
            out += [both[:8], both[8:]]
        else:
            out.append(pltpu.roll(pieces[0].astype(BF16).astype(F32), amount, axis=1))
    return out


def flatten(lists):
    return [value for values in lists for value in values]


def unflat(values, width):
    return [values[n : n + width] for n in range(0, len(values), width)]


def unpack_kernel(nrow,pad,g_ref,w_out,wt_out,up_out,upt_out,dn_out,dnt_out,held,w_ref,wt_ref,up_ref,upt_ref,dn_ref,dnt_ref,flat,chunks,in_sems,out_sems):
    shards=held.shape[0]
    parts=[pl.ds(n*shards//4,(n+1)*shards//4-n*shards//4) for n in range(4)]
    loads=[pltpu.make_async_copy(g_ref.at[part],held.at[part],in_sems.at[n]) for n,part in enumerate(parts)]
    for copy in loads:
        copy.start()
    saves=[]
    def save(source,target):
        copy=pltpu.make_async_copy(source,target,out_sems.at[len(saves)])
        copy.start()
        saves.append(copy)
    def fill(s,_):
        flat[pl.ds(nrow*s,pad),:]=held[s].astype(F32); return 0
    for n,copy in enumerate(loads):
        copy.wait()
        lax.fori_loop(n*shards//4,(n+1)*shards//4,fill,0)
    lane=lane_ids()
    def split(base,cols,period,groups):
        J=-(-cols//LANES); pitch=period+8; height=pitch*8*groups+8; last=cols-(J-1)*LANES
        def body(b,_):
            row,s=place(base,cols,period,b)
            back=(LANES-s)%LANES
            found=[[flat[pl.ds(row+641*8*g+j,8,stride=641),:] for g in range(groups)] for j in range(J+1)]
            found=unflat(rolled(flatten(found),back),groups)
            for g in range(groups):
                for j in range(J):
                    val=jnp.where(lane<LANES-s,found[j][g],found[j+1][g])
                    if j==J-1: val=jnp.where(lane<last,val,0.0)
                    chunks[pl.ds(j*height+8*g*pitch+b,8,stride=pitch),:]=val
            return 0
        lax.fori_loop(0,period,body,0,unroll=16)
        def border(a,_):
            for j in range(J): chunks[pl.ds(j*height+a*pitch-8,8),:]=chunks[pl.ds(j*height+a*pitch,8),:]
            return 0
        lax.fori_loop(1,8*groups,border,0)
        return J,height,period
    def convert(dst,dst_row,src_row,rows,pad_rows,J,height,period):
        full=rows//16
        def piece(j,r): return chunks[pl.ds(j*height+r//period*(period+8)+r%period,8),:]
        def pair(j,r): return jnp.concatenate([piece(j,r),piece(j,r+8)],axis=0)
        def body(m,_):
            for j in range(J):
                dst[pl.ds(pl.multiple_of(dst_row+16*m,16),16),j*LANES:(j+1)*LANES]=pair(j,src_row+16*m).astype(BF16)
            return 0
        lax.fori_loop(0,full,body,0,unroll=4)
        keep=lax.broadcasted_iota(jnp.int32,(16,LANES),0)<rows-16*full
        for m in range(full,pad_rows//16):
            for j in range(J):
                v=jnp.where(keep,pair(j,src_row+16*m),0.0) if m==full else jnp.zeros((16,LANES),F32)
                dst[dst_row+16*m:dst_row+16*m+16,j*LANES:(j+1)*LANES]=v.astype(BF16)
    J,h,p=split(*MATS[0][:2],*MATS[0][3:])
    for k in range(BASIS):
        convert(w_ref,k*CP,k*CIN,CIN+(k==BASIS-1),CP,J,h,p)
    save(w_ref,w_out)
    wt_ref[...]=w_ref[:,:CP].T
    save(wt_ref,wt_out)
    J,h,p=split(*MATS[1][:2],*MATS[1][3:])
    convert(up_ref,0,0,C+1,CP,J,h,p)
    save(up_ref,up_out)
    upt_ref[...]=up_ref[:,:HP].T
    save(upt_ref,upt_out)
    J,h,p=split(*MATS[2][:2],*MATS[2][3:])
    convert(dn_ref,0,0,HID+1,HP,J,h,p)
    save(dn_ref,dn_out)
    dnt_ref[...]=dn_ref[:,:CP].T
    save(dnt_ref,dnt_out)
    for copy in saves:
        copy.wait()


def unpack(gathered,nrow):
    shapes=[(BASIS*CP,WIDE),(CP,BASIS*CP),(CP,HL),(HP,CP),(HP,WIDE),(CP,HP)]
    anywhere=pl.BlockSpec(memory_space=pl.ANY)
    return pl.pallas_call(functools.partial(unpack_kernel,nrow,gathered.shape[1]),
        in_specs=[anywhere],
        out_specs=[anywhere]*6,
        out_shape=tuple(jax.ShapeDtypeStruct(shape,BF16) for shape in shapes),
        scratch_shapes=[pltpu.VMEM(gathered.shape,BF16)]+[pltpu.VMEM(shape,BF16) for shape in shapes]
        +[pltpu.VMEM((F_ROWS,LANES),F32),pltpu.VMEM((6*(136*24+8),LANES),F32),pltpu.SemaphoreType.DMA((4,)),pltpu.SemaphoreType.DMA((6,))],
        compiler_params=pltpu.CompilerParams(vmem_limit_bytes=VMEM),name="unpack")(gathered)


def chunk_gather(src, chunks, src_row, dst_row, rows, J, height, last, period):
    lane, sub = lane_ids(), lax.broadcasted_iota(jnp.int32, (8, LANES), 0)

    def step(m):
        at = dst_row + 8 * m
        at = at // period * (period + 8) + at % period
        for j in range(J):
            v = src[pl.ds(src_row + 8 * m, 8), j * LANES : (j + 1) * LANES]
            if j == J - 1:
                v = jnp.where(lane < last, v, 0.0)
            if isinstance(m, int) and 8 * m + 8 > rows:
                v = jnp.where(sub < rows - 8 * m, v, 0.0)
            chunks[pl.ds(j * height + at + 8, 8), :] = v
            chunks[pl.ds(j * height + at, 8), :] = v

    return step


def chunk_clear(chunks, J, height, row, period):
    row = row // period * (period + 8) + row % period

    def body(m, _):
        for j in range(J):
            chunks[pl.ds(j * height + row + 8 * m, 8), :] = jnp.zeros((8, LANES), F32)
        return 0

    lax.fori_loop(0, (height - row) // 8, body, 0)


def line_merge(flat, flat0, chunks, base, cols, period, groups):
    lane, sub = lane_ids(), lax.broadcasted_iota(jnp.int32, (8, LANES), 0)
    J, pitch = -(-cols // LANES), period + 8
    height = pitch * 8 * groups + 8
    row0 = base // LANES - flat0

    def step(b, tails, last=False):
        row, s = place(base, cols, period, b)
        row = row - flat0
        found = [
            chunks[pl.ds(j * height + 8 * g * pitch + b, 8, stride=pitch), :]
            for g in range(groups)
            for j in range(J)
        ]
        found = unflat(rolled(found, s), J)
        new = []
        keep = lane >= s
        for g in range(groups):
            x = found[g]
            for j in range(J):
                v = jnp.where(keep, x[j], tails[g] if j == 0 else x[j - 1])
                if not (last and j == J - 1):
                    flat[pl.ds(row + 641 * 8 * g + j, 8, stride=641), :] = v
            new.append(jnp.where(s == LANES - 1, jnp.where(keep, 0.0, x[J - 1]), v))
        return tuple(new)

    def first():
        init = [jnp.zeros((8, LANES), F32)] * groups
        if base == OFF_DN:
            init[0] = jnp.where(sub == 0, flat[row0 : row0 + 8, :], 0.0)
        return tuple(init)

    def finish(tails):
        if base % LANES:
            for g in range(groups):
                at = pl.ds(row0 + 641 * (8 * g + 1), 8, stride=641)
                flat[at, :] = flat[at, :] + tails[g]

    return step, first, finish


FFN_ROW = OFF_UP // LANES // 8 * 8
FFN_ROWS = OFF_DN // LANES + 641 * 16 + 40 - FFN_ROW
DISCO_ROWS = 641 * 24 + 16


def grads_kernel(nrow, basis, gconv, gup, gdn, out, *refs):
    low, conv, gd, flat, ffn, chunks, gu, gn, stage, in_sems, ffn_sems, out_sems = refs
    count = basis.shape[0]
    shards, pad = out.shape[:2]

    def loads(i):
        return [
            pltpu.make_async_copy(basis.at[i], low.at[i % 2], in_sems.at[i % 2, 0]),
            pltpu.make_async_copy(gconv.at[i], conv.at[i % 2], in_sems.at[i % 2, 1]),
        ]

    weights = [pltpu.make_async_copy(a, b, ffn_sems.at[n]) for n, (a, b) in enumerate(((gup, gu), (gdn, gn)))]
    flying = {}
    for i in range(min(2, count)):
        flying[i] = loads(i)
        for copy in flying[i]:
            copy.start()
        weights[i].start()

    def outer(i, n):
        if n == 0:
            for copy in flying[i]:
                copy.wait()
        at = slice(n * CP, (n + 1) * CP)
        term = lax.dot_general(
            low[i % 2, at, :], conv[i % 2], (((1,), (1,)), ((), ())), preferred_element_type=F32
        )
        if i:
            gd[at, :CP] += term
        else:
            gd[at, :CP] = term
        if n == BASIS - 1 and i + 2 < count:
            flying[i + 2] = loads(i + 2)
            for copy in flying[i + 2]:
                copy.start()

    def lay(n, src, rows, J, height, last, base, cols, period, groups):
        state = {}
        copy = chunk_gather(src, chunks, 0, 0, rows, J, height, last, period)
        step, first, finish = line_merge(ffn, FFN_ROW, chunks, base, cols, period, groups)
        pieces = -(-rows // 8)

        def begin():
            weights[n].wait()

        def gather(start):
            for m in range(start, min(start + 4, pieces)):
                copy(m)

        def ready():
            chunk_clear(chunks, J, height, 8 * pieces, period)
            state["tails"] = first()

        def merge(b):
            state["tails"] = step(b, state["tails"], last=base % LANES and b == period - 1)

        def done():
            finish(state["tails"])

        steps = [begin] + [functools.partial(gather, m) for m in range(0, pieces, 4)] + [ready]
        return steps + [functools.partial(merge, b) for b in range(period)] + [done]

    products = [functools.partial(outer, i, n) for i in range(count) for n in range(BASIS)]
    for n in range(2):
        if n >= count:
            weights[n].start()
    up_steps = lay(0, gu, C + 1, 11, 72 * 16 + 8, 2, OFF_UP, HID, 64, 2)
    down_steps = lay(1, gn, HID + 1, 6, 136 * 16 + 8, 1, OFF_DN, C, 128, 2)
    weave(products, up_steps + down_steps)

    height = 136 * 24 + 8
    for k in range(BASIS):
        rows = CIN + (k == BASIS - 1)
        copy = chunk_gather(gd, chunks, k * CP, k * CIN, rows, 6, height, 1, 128)

        def body(m, _):
            copy(m)
            return 0

        lax.fori_loop(0, rows // 8, body, 0, unroll=8)
        copy(rows // 8)
    chunk_clear(chunks, 6, height, 2600, 128)
    step, first, _ = line_merge(flat, 0, chunks, 0, C, 128, 3)
    lax.fori_loop(0, 128, step, first(), unroll=16)
    seam = OFF_UP // LANES
    for shard in range(shards):
        if nrow * shard < seam < nrow * shard + pad:
            amount = nrow * shard + pad - seam
            flat[seam : seam + amount, :] = ffn[seam - FFN_ROW : seam - FFN_ROW + amount, :]
    slots = stage.shape[0]

    def save(shard, slot):
        return pltpu.make_async_copy(stage.at[slot], out.at[shard], out_sems.at[slot])

    for shard in range(shards):
        slot = shard % slots
        if shard >= slots:
            save(shard - slots, slot).wait()
        source, start = (flat, nrow * shard) if nrow * shard < seam else (ffn, nrow * shard - FFN_ROW)
        stage[slot] = source[start : start + pad, :].astype(BF16)
        save(shard, slot).start()
    for shard in range(max(shards - slots, 0), shards):
        save(shard, shard % slots).wait()


def grads(basis, gconv, gup, gdn, n, nrow, pad):
    anywhere = pl.BlockSpec(memory_space=pl.ANY)
    return pl.pallas_call(
        functools.partial(grads_kernel, nrow),
        in_specs=[anywhere] * 4,
        out_specs=anywhere,
        out_shape=jax.ShapeDtypeStruct((n, pad, LANES), BF16),
        scratch_shapes=[
            pltpu.VMEM((2, BASIS * CP, WIDE), BF16),
            pltpu.VMEM((2, CP, WIDE), BF16),
            pltpu.VMEM((BASIS * CP, WIDE), F32),
            pltpu.VMEM((DISCO_ROWS, LANES), F32),
            pltpu.VMEM((FFN_ROWS, LANES), F32),
            pltpu.VMEM((6 * (136 * 24 + 8), LANES), F32),
            pltpu.VMEM(gup.shape, F32),
            pltpu.VMEM(gdn.shape, F32),
            pltpu.VMEM((8, pad, LANES), BF16),
            pltpu.SemaphoreType.DMA((2, 2)),
            pltpu.SemaphoreType.DMA((2,)),
            pltpu.SemaphoreType.DMA((8,)),
        ],
        compiler_params=pltpu.CompilerParams(vmem_limit_bytes=VMEM),
        name="grads",
    )(basis, gconv, gup, gdn)


def tiled(column):
    return jnp.concatenate([column] * (WIDE // LANES), axis=1)


def lane_of(rows, start=0):
    return lax.broadcasted_iota(jnp.int32, (rows, LANES), 1) + start


def wrapped(chunk, width):
    head, first, last = chunk[:, : WIDE - LANES], chunk[:, :LANES], chunk[:, WIDE - LANES :]
    edge = width - (WIDE - LANES)
    lane = lane_of(chunk.shape[0])
    beyond = jnp.where(
        lane < LANES - REACH, pltpu.roll(first, edge, axis=1), pltpu.roll(last, LANES - edge, axis=1)
    )
    return jnp.concatenate([head, jnp.where(lane < edge, last, beyond)], axis=1)


def cut(chunk, width):
    head, last = chunk[:, : WIDE - LANES], chunk[:, WIDE - LANES :]
    keep = lane_of(chunk.shape[0], WIDE - LANES) < width
    return jnp.concatenate([head, jnp.where(keep, last, 0.0)], axis=1)


def rows_below(count):
    return lax.broadcasted_iota(jnp.int32, (STEP, WIDE), 0) < count


def halves(chunk):
    return chunk[:8] + chunk[8:]


def column_sums(read, channels, count):
    whole = channels // STEP

    def body(m, sums):
        return tuple(a + halves(v) for a, v in zip(sums, read(m)))

    sums = lax.fori_loop(
        0, whole, body, tuple(jnp.zeros((8, WIDE), F32) for _ in range(count)), unroll=UNROLL
    )
    keep = rows_below(channels - whole * STEP)
    sums = [a + halves(jnp.where(keep, v, 0.0)) for a, v in zip(sums, read(whole))]
    return [jnp.sum(a, axis=0, keepdims=True) for a in sums]


def norm_stats(read, channels):
    (total,) = column_sums(lambda m: (read(m),), channels, 1)
    mean = total * (1.0 / channels)

    def squares(m):
        centered = read(m) - mean
        return (centered * centered,)

    (total,) = column_sums(squares, channels, 1)
    return mean, lax.rsqrt(total * (1.0 / channels) + 1e-05)


def each_chunk(body, unroll=None):
    def step(m, _):
        body(m, pl.ds(pl.multiple_of(m * STEP, STEP), STEP))
        return 0

    lax.fori_loop(0, CP // STEP, step, 0, unroll=unroll)


def spread(source, gain, shift, width, moved):
    def read(c):
        return source[pl.ds(pl.multiple_of(c * STEP, STEP), STEP), :].astype(F32)

    mean, scale = norm_stats(read, CIN)
    yield

    def shifts(c, at):
        values = (read(c) - mean) * scale * tiled(gain[at, :]) + tiled(shift[at, :])
        values = wrapped(values, width).astype(BF16)
        for d in range(-REACH, REACH + 1):
            moved[d + REACH, at, :] = pltpu.roll(values, -d % WIDE, axis=1) if d else values

    def step(m, _):
        shifts(m, pl.ds(pl.multiple_of(m * STEP, STEP), STEP))
        return 0

    chunks = CP // STEP
    for n in range(PARTS):
        lax.fori_loop(n * chunks // PARTS, (n + 1) * chunks // PARTS, step, 0, unroll=4)
        yield


def points_of(bases):
    named = [bases[p] for p in range(SUPPORT)]
    ranks = []
    for p in range(SUPPORT):
        rank = jnp.int32(0)
        for before in range(p):
            rank = rank + jnp.where(named[before] == named[p], 1, 0)
        ranks.append(rank)
    picks = {}
    for k in range(BASIS):
        for q in range(3):
            pick = jnp.int32(0)
            for p in range(SUPPORT):
                pick = pick + jnp.where(jnp.logical_and(named[p] == k, ranks[p] == q), p, 0)
            picks[k, q] = pick
    return picks


def combine_row(r, first_row, lat, width, offsets, picks, psi, moved, out):
    for k in range(BASIS):
        parts = []
        for q in range(3):
            p = picks[k, q]
            row = first_row + r + offsets[p, 0]
            inside = jnp.logical_and(row >= 0, row < lat)
            weight = jnp.where(inside, psi[first_row + r, p], 0.0)
            parts.append((weight, r + 1 + offsets[p, 0], offsets[p, 1] + REACH))

        def combine(c, at):
            total = None
            for weight, row, d in parts:
                term = weight * moved[row, d, at, :].astype(F32)
                total = term if total is None else total + term
            to = pl.ds(pl.multiple_of(k * CP + c * STEP, STEP), STEP)
            out[to, :] = cut(total, width).astype(BF16)

        each_chunk(combine, 8)
    last = slice(BASIS * CP - STEP, BASIS * CP)
    bias_row = CIN - (CP - STEP)
    sub = lax.broadcasted_iota(jnp.int32, (STEP, WIDE), 0)
    lane = lax.broadcasted_iota(jnp.int32, (STEP, WIDE), 1)
    ones = jnp.where(lane < width, 1.0, 0.0)
    out[last, :] = jnp.where(sub == bias_row, ones, out[last, :].astype(F32)).astype(BF16)


def lift_kernel(rows, lat, width, offsets, bases, psi, own, small, *refs):
    out, moved, built, ends, sems, out_sems, end_sems = refs[-7:]
    halos = refs[:-7]
    slabs = out.shape[0]
    first_row = lax.axis_index("lat") * rows
    ways = [halos[0].at[0], halos[0].at[1]] + [halo.at[0] for halo in halos[1:]]
    sources = [pltpu.make_async_copy(way, ends.at[n], end_sems.at[n]) for n, way in enumerate(ways)]
    for copy in sources:
        copy.start()

    def inner(s):
        return [pltpu.make_async_copy(own.at[s, r], moved.at[r + 1], sems.at[r]) for r in range(rows)]

    picks = points_of(bases)
    saves = {}
    for s in range(slabs):
        for copy in inner(s):
            copy.start()
        for way, m in ((0, 0), (1, rows + 1)):
            sources[2 * s + way].wait()
            for _ in spread(ends.at[2 * s + way], small.at[0], small.at[1], width, moved.at[m]):
                pass
        for copy in inner(s):
            copy.wait()
        for r in range(rows):
            if s:
                saves[s - 1, r].wait()
            combine_row(r, first_row, lat, width, offsets, picks, psi, moved, built.at[r])
            saves[s, r] = pltpu.make_async_copy(built.at[r], out.at[s, r], out_sems.at[r])
            saves[s, r].start()
    for r in range(rows):
        saves[slabs - 1, r].wait()


def lift(offsets, bases, psi, halos, own, small, lat, width):
    slabs, rows = own.shape[:2]
    smem = pl.BlockSpec(memory_space=pltpu.SMEM)
    anywhere, held = pl.BlockSpec(memory_space=pl.ANY), pl.BlockSpec(memory_space=pltpu.VMEM)
    return pl.pallas_call(
        functools.partial(lift_kernel, rows, lat, width),
        in_specs=[smem, smem, smem, anywhere, held] + [anywhere] * len(halos),
        out_specs=anywhere,
        out_shape=jax.ShapeDtypeStruct((slabs, rows, BASIS * CP, WIDE), BF16),
        scratch_shapes=[
            pltpu.VMEM((rows + 2, 2 * REACH + 1, CP, WIDE), BF16),
            pltpu.VMEM((rows, BASIS * CP, WIDE), BF16),
            pltpu.VMEM((2 * slabs, CP, WIDE), BF16),
            pltpu.SemaphoreType.DMA((rows,)),
            pltpu.SemaphoreType.DMA((rows,)),
            pltpu.SemaphoreType.DMA((2 * slabs,)),
        ],
        compiler_params=pltpu.CompilerParams(vmem_limit_bytes=VMEM),
        cost_estimate=pl.CostEstimate(flops=40 << 20, bytes_accessed=40 << 20, transcendentals=0),
        name="lift",
    )(offsets, bases, psi, own, small, *halos)


GELU_A = math.sqrt(2.0 / math.pi)
GELU_B = 0.044715


TILE = 256


def weave(*lists):
    order = []
    for which, steps in enumerate(lists):
        for n, step in enumerate(steps):
            order.append(((n + 0.5) / len(steps), which, n, step))
    for _, _, _, step in sorted(order, key=lambda entry: entry[:3]):
        step()


class Job:
    def __init__(self, buffers, weights, totals, mask):
        self.basis, self.x, self.cot, self.out, self.gconv = buffers[:5]
        self.res, self.second, self.pre, self.act, self.mid, self.gact, self.gb, self.gpre = buffers[5:]
        self.wt, self.upt, self.up, self.dnt, self.dn, self.gain, self.shift = weights
        self.gup, self.gdn, self.sums = totals
        self.mask = mask

    @staticmethod
    def at(c):
        return slice(c * STEP, (c + 1) * STEP)

    @staticmethod
    def wide(column):
        return jnp.concatenate([column] * (TILE // LANES), axis=1)

    @staticmethod
    def only(c, values, channels, other=0.0):
        if (c + 1) * STEP <= channels:
            return values
        row = lax.broadcasted_iota(jnp.int32, (STEP, TILE), 0)
        return jnp.where(row < channels - c * STEP, values, other)

    def product(self, out, left, right, count):
        rows = left.shape[0]
        size = -(-rows // (count * STEP)) * STEP

        def step(start):
            at = slice(start, min(start + size, rows))
            values = left[at, : right.shape[0]]
            out[at, :] = jnp.dot(values, right[...], preferred_element_type=F32)

        return [functools.partial(step, start) for start in range(0, rows, size)]

    def outer(self, out, left, right, count):
        rows = left.shape[0]
        size = -(-rows // (count * STEP)) * STEP

        def step(start):
            at = slice(start, min(start + size, rows))
            term = lax.dot_general(
                left[at, :], right[...], (((1,), (1,)), ((), ())), preferred_element_type=F32
            )
            out[at, : right.shape[0]] += term

        return [functools.partial(step, start) for start in range(0, rows, size)]

    def m1(self):
        return self.product(self.res, self.wt, self.basis, 4)

    def v1(self):
        state = {"sum": jnp.zeros((8, TILE), F32), "square": jnp.zeros((8, TILE), F32)}
        mask = self.mask()

        def add(c):
            at = self.at(c)
            value = self.res[at, :] + self.only(c, self.x[at, :].astype(F32), C)
            self.res[at, :] = value
            self.gb[at, :] = (self.cot[at, :].astype(F32) * mask).astype(BF16)
            state["sum"] = state["sum"] + halves(self.only(c, value, C))

        def mean():
            self.mean = jnp.sum(state["sum"], axis=0, keepdims=True) * (1.0 / C)

        def square(c):
            value = self.res[self.at(c), :] - self.mean
            state["square"] = state["square"] + halves(self.only(c, value * value, C))

        def scale():
            total = jnp.sum(state["square"], axis=0, keepdims=True)
            self.scale = lax.rsqrt(total * (1.0 / C) + 1e-05)

        def normalize(c):
            at = self.at(c)
            value = (self.res[at, :] - self.mean) * self.scale
            value = value * self.wide(self.gain[at, :]) + self.wide(self.shift[at, :])
            row = lax.broadcasted_iota(jnp.int32, (STEP, TILE), 0)
            if c == C // STEP:
                value = jnp.where(row == C % STEP, 1.0, value)
            self.second[at, :] = value.astype(BF16)

        chunks = range(CP // STEP)
        steps = [functools.partial(add, c) for c in chunks] + [mean]
        steps += [functools.partial(square, c) for c in chunks] + [scale]
        return steps + [functools.partial(normalize, c) for c in chunks]

    def m2(self):
        return self.product(self.pre, self.upt, self.second, 9)

    def v2(self):
        def gelu(c):
            at = self.at(c)
            v = self.pre[at, :]
            square = v * v
            bend = jnp.tanh(GELU_A * v * (1.0 + GELU_B * square))
            half = 0.5 * (1.0 + bend)
            value = v * half
            if c == HID // STEP:
                row = lax.broadcasted_iota(jnp.int32, (STEP, TILE), 0)
                value = jnp.where(row == HID % STEP, 1.0, value)
            self.act[at, :] = value.astype(BF16)
            rise = GELU_A * (1.0 + 3.0 * GELU_B * square)
            self.pre[at, :] = half + 0.5 * v * (1.0 - bend * bend) * rise

        return [functools.partial(gelu, c) for c in range(HP // STEP)]

    def m3(self):
        back = self.product(self.gact, self.dn, self.gb, 9)
        return self.product(self.mid, self.dnt, self.act, 4) + back

    def v3(self):
        def finish(c):
            at = self.at(c)
            self.out[at, :] = (self.res[at, :] + self.mid[at, :]).astype(BF16)

        def back(c):
            at = self.at(c)
            self.gpre[at, :] = (self.gact[at, :] * self.pre[at, :]).astype(BF16)

        steps = [functools.partial(finish, c) for c in range(CP // STEP)]
        return steps + [functools.partial(back, c) for c in range(HP // STEP)]

    def m4(self):
        return self.product(self.mid, self.up, self.gpre, 4)

    def v4(self):
        state = {"flat": jnp.zeros((8, TILE), F32), "along": jnp.zeros((8, TILE), F32)}

        def terms(c):
            at = self.at(c)
            dm = self.mid[at, :]
            xhat = (self.res[at, :] - self.mean) * self.scale
            return dm, xhat, dm * self.wide(self.gain[at, :])

        def means(c):
            _, xhat, g = terms(c)
            g = self.only(c, g, C)
            state["flat"] = state["flat"] + halves(g)
            state["along"] = state["along"] + halves(g * xhat)

        def join():
            for name in state:
                state[name] = jnp.sum(state[name], axis=0, keepdims=True) * (1.0 / C)

        def backward(c):
            at = self.at(c)
            dm, xhat, g = terms(c)
            value = g - state["flat"] - xhat * state["along"]
            value = self.gb[at, :].astype(F32) + self.scale * value
            self.gconv[at, :] = self.only(c, value, C).astype(BF16)
            for n, term in enumerate((dm * xhat, dm)):
                self.sums[n, at, :] += term[:, :LANES] + term[:, LANES:]

        chunks = range(CP // STEP)
        steps = [functools.partial(means, c) for c in chunks] + [join]
        return steps + [functools.partial(backward, c) for c in chunks]

    def m5(self):
        first = self.outer(self.gdn, self.act, self.gb, 3)
        return first + self.outer(self.gup, self.second, self.gpre, 2)


def block_kernel(
    basis, x, cot, mask, wt, upt, up, dnt, dn, small, out, gconv, gup, gdn, sums, *scratch
):
    gain, shift = small.at[2], small.at[3]
    count = basis.shape[0]
    tiles = WIDE // TILE
    in_sems, out_sems = scratch[-2:]
    per_job = (len(scratch) - 2) // 2
    sets = [scratch[:per_job], scratch[per_job : 2 * per_job]]
    for total in (gup, gdn, sums):
        total[...] = jnp.zeros_like(total)

    def place(i, j):
        return i // tiles * 2 + j, pl.ds(pl.multiple_of(i % tiles * TILE, TILE), TILE)

    def arrive(i, j):
        row, lanes = place(i, j)
        return [
            pltpu.make_async_copy(source.at[row, :, lanes], sets[j][n], in_sems.at[j, n])
            for n, source in enumerate((basis, x, cot))
        ]

    def leave(i, j):
        row, lanes = place(i, j)
        return [
            pltpu.make_async_copy(sets[j][3 + n], target.at[row, :, lanes], out_sems.at[j, n])
            for n, target in enumerate((out, gconv))
        ]

    last = count // 2 * tiles - 1
    for j in range(2):
        for copy in arrive(0, j):
            copy.start()

    def pair(i, _):
        def row_mask(j):
            row, lanes = place(i, j)
            return lambda: mask[row, :, lanes]

        weights, totals = (wt, upt, up, dnt, dn, gain, shift), (gup, gdn, sums)
        a, b = (Job(sets[j], weights, totals, row_mask(j)) for j in range(2))
        after = jnp.minimum(i + 1, last)
        coming = [arrive(after, j) for j in range(2)]
        leaving = [leave(i, j) for j in range(2)]
        for j in range(2):
            for copy in arrive(i, j):
                copy.wait()
        weave(a.m1())
        coming[0][0].start()
        weave(a.v1(), b.m1())
        coming[1][0].start()
        for n in (1, 2):
            coming[0][n].start()
        weave(a.m2(), b.v1())
        for n in (1, 2):
            coming[1][n].start()
        weave(a.v2(), b.m2())
        weave(a.m3(), b.v2())
        weave(a.v3(), b.m3())
        leaving[0][0].start()
        weave(a.m4(), b.v3())
        leaving[1][0].start()
        weave(a.v4(), b.m4())
        leaving[0][1].start()
        weave(a.m5(), b.v4())
        leaving[1][1].start()
        weave(b.m5())
        for copies in leaving:
            for copy in copies:
                copy.wait()
        return 0

    lax.fori_loop(0, last + 1, pair, 0)
    for j in range(2):
        for copy in arrive(last, j):
            copy.wait()


def block(basis, x, cot, mask, wt, upt, up, dnt, dn, small):
    count = x.shape[0]
    anywhere = pl.BlockSpec(memory_space=pl.ANY)
    held = pl.BlockSpec(memory_space=pltpu.VMEM)
    low, high = pltpu.VMEM((CP, TILE), BF16), pltpu.VMEM((CP, TILE), F32)
    hidden_low, hidden_high = pltpu.VMEM((HP, TILE), BF16), pltpu.VMEM((HP, TILE), F32)
    per_job = [pltpu.VMEM((BASIS * CP, TILE), BF16), low, low, low, low]
    per_job += [high, low, hidden_high, hidden_low, high, hidden_high, low, hidden_low]
    return pl.pallas_call(
        block_kernel,
        in_specs=[anywhere] * 3 + [held] * 7,
        out_specs=[anywhere] * 2 + [held] * 3,
        out_shape=(
            jax.ShapeDtypeStruct((count, CP, WIDE), BF16),
            jax.ShapeDtypeStruct((count, CP, WIDE), BF16),
            jax.ShapeDtypeStruct((CP, HL), F32),
            jax.ShapeDtypeStruct((HP, WIDE), F32),
            jax.ShapeDtypeStruct((2, CP, LANES), F32),
        ),
        scratch_shapes=per_job * 2 + [pltpu.SemaphoreType.DMA((2, 3)), pltpu.SemaphoreType.DMA((2, 2))],
        compiler_params=pltpu.CompilerParams(vmem_limit_bytes=VMEM),
        name="block",
    )(basis, x, cot, mask, wt, upt, up, dnt, dn, small)


def along_lanes(ref, at, values):
    total = values[:, :LANES]
    for j in range(1, WIDE // LANES):
        total = total + values[:, j * LANES : (j + 1) * LANES]
    ref[at, :] = ref[at, :] + total


GROUP = 7 * STEP


def lower_kernel(rows, width, offsets, bases, psi, gconv, w, own, lo0, hi0, lo1, hi1, *scratch):
    place, coef, in_sems, w_sems, out_sems = scratch[-5:]
    per_slab = (len(scratch) - 5) // 2
    sets = [scratch[:per_slab], scratch[per_slab : 2 * per_slab]]
    first_row = lax.axis_index("lat") * rows
    span = 2 * REACH + 1
    groups = -(-CP // GROUP)
    for n in range(3 * span):
        place[n] = 0
        for r in range(rows):
            coef[r, n] = 0.0
    for p in range(SUPPORT):
        n = (offsets[p, 0] + 1) * span + offsets[p, 1] + REACH
        place[n] = bases[p]
        for r in range(rows):
            coef[r, n] = psi[first_row + r, p]

    def channels(g):
        return pl.ds(pl.multiple_of(jnp.minimum(g * GROUP, CP - GROUP), STEP), GROUP)

    def weights(j, g):
        return pltpu.make_async_copy(w.at[:, channels(g), :], sets[j][1], w_sems.at[j])

    def products(j):
        ring, part, lifted = sets[j][:3]

        def step(r, k):
            values = jnp.dot(part[k, :, :CP], ring[r], preferred_element_type=F32)
            lifted[r, k] = values.astype(BF16)

        return [functools.partial(step, r, k) for r in range(rows) for k in range(BASIS)]

    def gathers(j):
        lifted, inner, below, above = sets[j][2:]

        def step(c, target):
            at = slice(c * STEP, (c + 1) * STEP)
            total = None
            for d in range(-REACH, REACH + 1):
                part = None
                for o in (-1, 0, 1):
                    r = target - o
                    if 0 <= r < rows:
                        n = (o + 1) * span + d + REACH
                        term = coef[r, n] * lifted[r, place[n], at, :].astype(F32)
                        part = term if part is None else part + term
                if d:
                    part = pltpu.roll(part.astype(BF16), d % WIDE, axis=1).astype(F32)
                total = part if total is None else total + part
            if target < 0:
                below[at, :] = total.astype(BF16)
            elif target == rows:
                above[at, :] = total.astype(BF16)
            else:
                inner[target, at, :] = total

        return [functools.partial(step, c, t) for c in range(GROUP // STEP) for t in range(-1, rows + 1)]

    def pair_of_slabs(both, _):
        def leaving(j, g):
            slab = both * 2 + j
            lo, hi = ((lo0, hi0), (lo1, hi1))[j]
            targets = (own.at[slab, :, channels(g), :], lo.at[both, channels(g), :], hi.at[both, channels(g), :])
            return [
                pltpu.make_async_copy(sets[j][3 + n], target, out_sems.at[j, n])
                for n, target in enumerate(targets)
            ]

        rings = [pltpu.make_async_copy(gconv.at[both * 2 + j], sets[j][0], in_sems.at[j]) for j in range(2)]
        for j in range(2):
            rings[j].start()
            weights(j, 0).start()
        for j in range(2):
            rings[j].wait()
            ring = sets[j][0]
            edge = width - (WIDE - LANES)
            lane = lane_of(CP)
            for r in range(rows):
                first, last = ring[r, :, :LANES].astype(F32), ring[r, :, WIDE - LANES :].astype(F32)
                beyond = jnp.where(
                    lane < LANES - REACH,
                    pltpu.roll(first, edge, axis=1),
                    pltpu.roll(last, LANES - edge, axis=1),
                )
                ring[r, :, WIDE - LANES :] = jnp.where(lane < edge, last, beyond).astype(BF16)
        weights(0, 0).wait()
        weave(products(0))
        weights(0, min(1, groups - 1)).start()

        def group(g, _):
            after, later = jnp.minimum(g + 1, groups - 1), jnp.minimum(g + 2, groups - 1)
            def free(j):
                @pl.when(g > 0)
                def _():
                    for copy in leaving(j, jnp.maximum(g - 1, 0)):
                        copy.wait()

            weights(1, g).wait()
            free(0)
            weave(products(1), gathers(0))
            weights(1, after).start()
            for copy in leaving(0, g):
                copy.start()
            weights(0, after).wait()
            free(1)
            weave(products(0), gathers(1))
            weights(0, later).start()
            for copy in leaving(1, g):
                copy.start()
            return 0

        lax.fori_loop(0, groups, group, 0)
        for j in range(2):
            weights(j, groups - 1).wait()
            for copy in leaving(j, groups - 1):
                copy.wait()
        return 0

    lax.fori_loop(0, gconv.shape[0] // 2, pair_of_slabs, 0)


def lower(offsets, bases, psi, gconv, w, width):
    slabs, rows = gconv.shape[:2]
    smem = pl.BlockSpec(memory_space=pltpu.SMEM)
    anywhere = pl.BlockSpec(memory_space=pl.ANY)
    edge = jax.ShapeDtypeStruct((slabs // 2, CP, WIDE), BF16)
    per_slab = [
        pltpu.VMEM((rows, CP, WIDE), BF16),
        pltpu.VMEM((BASIS, GROUP, WIDE), BF16),
        pltpu.VMEM((rows, BASIS, GROUP, WIDE), BF16),
        pltpu.VMEM((rows, GROUP, WIDE), F32),
        pltpu.VMEM((GROUP, WIDE), BF16),
        pltpu.VMEM((GROUP, WIDE), BF16),
    ]
    return pl.pallas_call(
        functools.partial(lower_kernel, rows, width),
        in_specs=[smem, smem, smem, anywhere, anywhere],
        out_specs=[anywhere] * 5,
        out_shape=(jax.ShapeDtypeStruct((slabs, rows, CP, WIDE), F32),) + (edge,) * 4,
        scratch_shapes=per_slab * 2
        + [
            pltpu.SMEM((3 * (2 * REACH + 1),), jnp.int32),
            pltpu.SMEM((rows, 3 * (2 * REACH + 1)), F32),
            pltpu.SemaphoreType.DMA((2,)),
            pltpu.SemaphoreType.DMA((2,)),
            pltpu.SemaphoreType.DMA((2, 3)),
        ],
        compiler_params=pltpu.CompilerParams(vmem_limit_bytes=VMEM),
        name="lower",
    )(offsets, bases, psi, gconv, w.reshape(BASIS, CP, WIDE))


def input_rows(width, x, gconv, own, lo, hi, gain, grad, sums, buffers, in_sems, out_sems, arrived):
    rows = x.shape[1]
    places = [(s, r) for s in range(x.shape[0]) for r in range(rows)]
    saves = []

    def loads(n):
        s, r = places[n]
        sources = [x.at[s, r], gconv.at[s, r], own.at[s, r]]
        sources += [lo.at[s // 2]] if r == 0 and s % 2 == 0 else []
        sources += [hi.at[s // 2]] if r == rows - 1 and s % 2 == 0 else []
        slots = [0, 1, 2] + ([3] if r == 0 else []) + ([4] if r == rows - 1 else [])
        return [
            pltpu.make_async_copy(source, buffers[n % 2][slot], in_sems.at[n % 2, slot])
            for source, slot in zip(sources, slots)
        ]

    flying = loads(0)
    for copy in flying:
        copy.start()
    sums[...] = jnp.zeros_like(sums)
    for n, (s, r) in enumerate(places):
        for copy in flying:
            copy.wait()
        if n + 1 < len(places):
            flying = loads(n + 1)
            for copy in flying:
                copy.start()
        here, conv, total, below, above, result = buffers[n % 2]
        if s % 2:
            below = arrived(s, 0) if r == 0 else None
            above = arrived(s, 1) if r == rows - 1 else None

        def read(c):
            return here[pl.ds(pl.multiple_of(c * STEP, STEP), STEP), :].astype(F32)

        mean, scale = norm_stats(read, CIN)
        yield

        if r == 0 or r == rows - 1:

            def join(c, at):
                value = total[at, :]
                if r == 0:
                    value = value + below[at, :].astype(F32)
                if r == rows - 1:
                    value = value + above[at, :].astype(F32)
                total[at, :] = value

            each_chunk(join, 8)
            yield

        def means(c):
            at = pl.ds(pl.multiple_of(c * STEP, STEP), STEP)
            g = total[at, :] * tiled(gain[at, :])
            return g, g * ((read(c) - mean) * scale)

        flat, along = [v * (1.0 / CIN) for v in column_sums(means, CIN, 2)]
        yield
        if n >= 2:
            saves[n - 2].wait()

        def backward(c, at):
            dm = cut(total[at, :], width)
            xhat = (read(c) - mean) * scale
            g = dm * tiled(gain[at, :])
            value = scale * (g - flat - xhat * along) + conv[at, :].astype(F32)
            result[at, :] = value.astype(BF16)
            along_lanes(sums.at[0], at, dm * xhat)
            along_lanes(sums.at[1], at, dm)

        each_chunk(backward, 8)
        save = pltpu.make_async_copy(result, grad.at[s, r], out_sems.at[n % 2])
        save.start()
        saves.append(save)
        yield
    for save in saves[-2:]:
        save.wait()


def flip(value, bit):
    return value + (1 - 2 * ((value // (1 << bit)) % 2)) * (1 << bit)


def flipped(value, mask):
    bit = 0
    while mask >> bit:
        if mask >> bit & 1:
            value = flip(value, bit)
        bit += 1
    return value


def span(bits):
    masks = [0]
    for b in bits:
        masks = masks + [m | 1 << b for m in masks]
    return masks


def orders(dates):
    bits = list(range(1, dates.bit_length() - 1))
    return bits + [0], bits[::-1] + [0]


def pieces(rows):
    cut = rows // (2 * STEP) * STEP
    return pl.ds(0, cut), pl.ds(cut, rows - cut)


def greet(dates, lats, d, l, owner):
    barrier = pltpu.get_barrier_semaphore()
    bits = range(dates.bit_length() - 1)
    peers = [(d, lax.rem(l + o, lats)) for o in range(1, lats)] + [(flip(d, b), l) for b in bits]
    for peer in peers:
        pl.semaphore_signal(barrier, inc=1, device_id=peer, device_id_type=MESH)
    next_to = [(owner[0], b) for b in range(lats) if b != owner[1]] + [(flip(owner[0], b), owner[1]) for b in bits]
    away = [(a, b) for a in range(dates) for b in range(lats) if (a, b) not in next_to + [owner]]
    mine = jnp.logical_and(d == owner[0], l == owner[1])
    near = functools.reduce(jnp.logical_or, [jnp.logical_and(d == a, l == b) for a, b in next_to])
    far = jnp.logical_not(jnp.logical_or(mine, near))

    @pl.when(mine)
    def _():
        for peer in away:
            pl.semaphore_signal(barrier, inc=1, device_id=peer, device_id_type=MESH)
        pl.semaphore_wait(barrier, len(peers) + len(away))

    @pl.when(near)
    def _():
        pl.semaphore_wait(barrier, len(peers))

    @pl.when(far)
    def _():
        pl.semaphore_signal(barrier, inc=1, device_id=owner, device_id_type=MESH)
        pl.semaphore_wait(barrier, len(peers) + 1)


def read_norms(landed, first, out):
    lane = lane_ids()
    sub = lax.broadcasted_iota(jnp.int32, (8, LANES), 0)
    lines = landed[...].astype(F32)
    for i, (off, n) in enumerate(SMALL):
        row, s = divmod(off - first * LANES, LANES)
        r = pltpu.roll(lines[row : row + 8], (LANES - s) % LANES, axis=1)
        v = jnp.where(lane < LANES - s, r, pltpu.roll(r, 7, axis=0))
        t = jnp.where(sub * LANES + lane < n, v, 0.0).T
        for j in range(6):
            rows = min(LANES, CP - j * LANES)
            out[i, j * LANES : j * LANES + rows, :] = jnp.broadcast_to(t[:rows, j : j + 1], (rows, LANES))


def norm_home(lines, lats):
    start, end = OFF_G1 // LANES, (OFF_UP - 1) // LANES + 3
    owner = start // lines
    row = (start - owner * lines) // STEP * STEP
    count = -(-(end - owner * lines - row) // STEP) * STEP
    assert row + count <= -(-lines // STEP) * STEP
    return divmod(owner, lats), owner * lines + row, row, count


def gather_kernel(
    dates, lats, lines, width, src, x, out, moved, small, halo, local_sem, z_send, z_recv, send, recv,
    buffers, buffer_sems, landed, norm_sem, norm_send, norm_recv, halo_send, halo_recv, near, near_sem,
):
    d, l = lax.axis_index("date"), lax.axis_index("lat")
    steps = dates.bit_length() - 1
    parts = pieces(src.shape[0])
    owner, first, row, count = norm_home(lines, lats)
    mine = jnp.logical_and(d == owner[0], l == owner[1])
    others = [(a, b) for a in range(dates) for b in range(lats) if (a, b) != owner]
    window = src.at[pl.ds(row, count)]
    nearby = pltpu.make_async_copy(x, near, near_sem)
    nearby.start()

    greet(dates, lats, d, l, owner)

    def norms_to(n):
        return pltpu.make_async_remote_copy(
            src_ref=window,
            dst_ref=landed,
            send_sem=norm_send.at[n],
            recv_sem=norm_recv,
            device_id=others[n],
            device_id_type=MESH,
        )

    @pl.when(mine)
    def _():
        for n in range(len(others)):
            norms_to(n).start()
        pltpu.make_async_copy(window, landed, norm_sem).start()

    own = pltpu.make_async_copy(src, out.at[d, l], local_sem)
    own.start()
    sent, arriving, flights = [], {}, {}

    def along(o):
        copy = pltpu.make_async_remote_copy(
            src_ref=src,
            dst_ref=out.at[d, l],
            send_sem=z_send.at[o - 1],
            recv_sem=z_recv.at[o - 1],
            device_id=(d, lax.rem(l + o, lats)),
            device_id_type=MESH,
        )
        copy.start()
        sent.append(copy)
        arriving[o] = copy

    def cross(o, p, i, n):
        order = orders(dates)[p]
        block = out.at[flipped(d, span(order[:i])[n]), lax.rem(l - o + lats, lats), parts[p]]
        slot = (1 << i) - 1 + n
        copy = pltpu.make_async_remote_copy(
            src_ref=src.at[parts[p]] if o == 0 and n == 0 else block,
            dst_ref=block,
            send_sem=send.at[o, p, slot],
            recv_sem=recv.at[o, p, slot],
            device_id=(flip(d, order[i]), l),
            device_id_type=MESH,
        )
        copy.start()
        sent.append(copy)
        flights[o, p, i, n] = copy

    rows = [(s, r) for s in range(x.shape[0]) for r in range(x.shape[1])]
    saves = []

    def spread_rows():
        @pl.when(mine)
        def _():
            pltpu.make_async_copy(window, landed, norm_sem).wait()

        @pl.when(jnp.logical_not(mine))
        def _():
            norms_to(0).wait_recv()

        read_norms(landed, first, small)
        nearby.wait()
        for n, (s, r) in enumerate(rows):
            if n >= 2:
                saves[n - 2].wait()
            yield from spread(near.at[s, r], small.at[0], small.at[1], width, buffers.at[n % 2])
            save = pltpu.make_async_copy(buffers.at[n % 2], moved.at[s, r], buffer_sems.at[n % 2])
            save.start()
            saves.append(save)
            yield

    def halo_copy(way):
        return pltpu.make_async_remote_copy(
            src_ref=x.at[0, 0 if way else x.shape[1] - 1],
            dst_ref=halo.at[way],
            send_sem=halo_send.at[way],
            recv_sem=halo_recv.at[way],
            device_id=(d, lax.rem(l + (lats - 1 if way else 1), lats)),
            device_id_type=MESH,
        )

    sends = [l < lats - 1, l > 0]
    aside = spread_rows()
    for wave in range(lats + steps):
        if wave < lats:
            if wave:
                arriving[wave].wait_recv()
            if wave == 0:
                for o in range(1, lats):
                    along(o)
            for i in range(steps):
                for p in range(2):
                    cross(wave, p, i, 0)
            if wave == 0:
                for way in range(2):

                    @pl.when(sends[way])
                    def _():
                        halo_copy(way).start()

        next(aside, None)
        for i in range(steps)[::-1]:
            o = wave - 1 - i
            if 0 <= o < lats:
                next(aside, None)
                for n in range(1 << i):
                    for p in range(2):
                        flights[o, p, i, n].wait_recv()
                        for later in range(i + 1, steps):
                            cross(o, p, later, n + (1 << i))
    for _ in aside:
        pass
    for save in saves[-2:]:
        save.wait()
    blank = buffers.at[0, 0]
    blank[...] = jnp.zeros_like(blank)
    for way in range(2):

        @pl.when(sends[1 - way])
        def _():
            halo_copy(way).wait_recv()

        @pl.when(jnp.logical_not(sends[1 - way]))
        def _():
            pltpu.sync_copy(blank, halo.at[way])

        @pl.when(sends[way])
        def _():
            halo_copy(way).wait_send()

    own.wait()
    for copy in sent:
        copy.wait_send()

    @pl.when(mine)
    def _():
        for n in range(len(others)):
            norms_to(n).wait_send()


def gather(shard, x, lines, dates, lats, width):
    slots = dates - 1
    moved = x.shape[:2] + (2 * REACH + 1,) + x.shape[2:]
    anywhere = pl.BlockSpec(memory_space=pl.ANY)
    return pl.pallas_call(
        functools.partial(gather_kernel, dates, lats, lines, width),
        in_specs=[anywhere, anywhere],
        out_specs=[anywhere, anywhere, pl.BlockSpec(memory_space=pltpu.VMEM), anywhere],
        out_shape=(
            jax.ShapeDtypeStruct((dates, lats) + shard.shape, shard.dtype),
            jax.ShapeDtypeStruct(moved, BF16),
            jax.ShapeDtypeStruct((4, CP, LANES), F32),
            jax.ShapeDtypeStruct((2,) + x.shape[2:], BF16),
        ),
        scratch_shapes=[
            pltpu.SemaphoreType.DMA(()),
            pltpu.SemaphoreType.DMA((lats - 1,)),
            pltpu.SemaphoreType.DMA((lats - 1,)),
            pltpu.SemaphoreType.DMA((lats, 2, slots)),
            pltpu.SemaphoreType.DMA((lats, 2, slots)),
            pltpu.VMEM((2,) + moved[2:], BF16),
            pltpu.SemaphoreType.DMA((2,)),
            pltpu.VMEM((norm_home(lines, lats)[3], LANES), BF16),
            pltpu.SemaphoreType.DMA(()),
            pltpu.SemaphoreType.DMA((dates * lats - 1,)),
            pltpu.SemaphoreType.DMA(()),
            pltpu.SemaphoreType.DMA((2,)),
            pltpu.SemaphoreType.DMA((2,)),
            pltpu.VMEM(x.shape, BF16),
            pltpu.SemaphoreType.DMA(()),
        ],
        compiler_params=pltpu.CompilerParams(
            collective_id=2, has_side_effects=True, vmem_limit_bytes=VMEM
        ),
        name="gather_params",
    )(shard, x)


def vector_rows(sums, tiny, first):
    lane = lane_ids()
    sub = lax.broadcasted_iota(jnp.int32, (8, LANES), 0)
    tiny[...] = jnp.zeros_like(tiny)
    for n, (off, channels) in enumerate(SMALL):
        lines = []
        for j in range(6):
            height = min(LANES, CP - j * LANES)
            block = sums[n // 2][n % 2, j * LANES : j * LANES + height, :]
            if height < LANES:
                block = jnp.concatenate([block, jnp.zeros((LANES - height, LANES), F32)], axis=0)
            lines.append(jnp.sum(block.T, axis=0, keepdims=True))
        lines = jnp.concatenate(lines + [jnp.zeros((2, LANES), F32)], axis=0)
        lines = jnp.where(sub * LANES + lane < channels, lines, 0.0)
        row, s = divmod(off - first * LANES, LANES)
        r = pltpu.roll(lines, s, axis=1)
        moved = jnp.where(lane >= s, r, jnp.where(sub == 0, 0.0, pltpu.roll(r, 1, axis=0)))
        tiny[row : row + 8, :] = tiny[row : row + 8, :] + moved


def vector_home(lines, lats):
    start, end = OFF_G1 // LANES, (OFF_UP - 1) // LANES + 1
    owner = start // lines
    row = (start - owner * lines) // 8 * 8
    count = -(-(end + 8 - owner * lines - row) // 8) * 8
    assert end <= (owner + 1) * lines
    return divmod(owner, lats), owner * lines + row, row, count


def scatter_kernel(
    dates, lats, lines, width, src, x, gconv, own, lo, hi, to_below, to_above, small, second_sums, out, grad,
    sums, others, z_send, z_recv, send, recv, first_sums, tiny, landed, tiny_send, tiny_recv,
    in_sems, out_sems, halo, halo_send, halo_recv, near, near_sem, *row_buffers
):
    d, l = lax.axis_index("date"), lax.axis_index("lat")
    steps = dates.bit_length() - 1
    paths = [order[::-1] for order in orders(dates)]
    parts = pieces(src.shape[2])
    owner, first, row, count = vector_home(lines, lats)
    mine = jnp.logical_and(d == owner[0], l == owner[1])
    senders = [(a, b) for a in range(dates) for b in range(lats) if (a, b) != owner]

    nearby = pltpu.make_async_copy(src, near, near_sem)
    nearby.start()
    greet(dates, lats, d, l, owner)
    sent, flights, z = [], {}, {}
    half = len(row_buffers) // 2
    gets = [l > 0, l < lats - 1]

    def halo_copy(slab, way):
        return pltpu.make_async_remote_copy(
            src_ref=(to_below if way else to_above).at[slab // 2],
            dst_ref=halo.at[slab // 2, way],
            send_sem=halo_send.at[slab // 2, way],
            recv_sem=halo_recv.at[slab // 2, way],
            device_id=(d, lax.rem(l + (lats - 1 if way else 1), lats)),
            device_id_type=MESH,
        )

    def arrived(slab, way):
        @pl.when(gets[way])
        def _():
            halo_copy(slab, way).wait_recv()

        @pl.when(jnp.logical_not(gets[way]))
        def _():
            halo[slab // 2, way] = jnp.zeros_like(halo[slab // 2, way])

        return halo.at[slab // 2, way]

    aside = input_rows(
        width, x, gconv, own, lo, hi, small.at[0], grad, first_sums,
        [row_buffers[:half], row_buffers[half:]], in_sems, out_sems, arrived,
    )

    def left(p, i):
        return span(paths[p][i + 1 :][::-1])[::-1]

    def slot_of(i, n):
        return sum(1 << (steps - 1 - e) for e in range(i)) + n

    def held(o, p, i, mask):
        if i == 0:
            return near.at[flipped(d, mask), lax.rem(l + o, lats), parts[p]]
        return sums.at[o, slot_of(i - 1, left(p, i - 1).index(mask)), parts[p]]

    def first_block(o, p, mask):
        return src.at[flipped(d, mask), lax.rem(l + o, lats), parts[p]]

    def cross(o, p, i, n):
        bit = paths[p][i]
        slot = slot_of(i, n)
        copy = pltpu.make_async_remote_copy(
            src_ref=held(o, p, i, left(p, i)[n] | 1 << bit) if i else first_block(o, p, left(p, i)[n] | 1 << bit),
            dst_ref=sums.at[o, slot, parts[p]],
            send_sem=send.at[o, p, slot],
            recv_sem=recv.at[o, p, slot],
            device_id=(flip(d, bit), l),
            device_id_type=MESH,
        )
        copy.start()
        sent.append(copy)
        flights[o, p, i, n] = copy

    def add(o, p, i, n):
        flights[o, p, i, n].wait_recv()
        have = held(o, p, i, left(p, i)[n])
        got = sums.at[o, slot_of(i, n), parts[p]]
        got[...] = (have[...].astype(F32) + got[...].astype(F32)).astype(BF16)
        if i + 1 < steps:
            if n < len(left(p, i + 1)):
                cross(o, p, i + 1, n)
        elif o:
            copy = pltpu.make_async_remote_copy(
                src_ref=got,
                dst_ref=others.at[o - 1, parts[p]],
                send_sem=z_send.at[o - 1, p],
                recv_sem=z_recv.at[o - 1, p],
                device_id=(d, lax.rem(l + o, lats)),
                device_id_type=MESH,
            )
            copy.start()
            sent.append(copy)
            z[o, p] = copy

    turns = list(range(1, lats)) + [0]
    for o in turns:
        for n in range(len(left(0, 0))):
            for p in range(2):
                cross(o, p, 0, n)
    for slab in range(1, x.shape[0], 2):
        for way in range(2):

            @pl.when(gets[1 - way])
            def _():
                halo_copy(slab, way).start()

    nearby.wait()
    for wave in range(lats + steps - 1):
        for i in range(steps):
            if 0 <= wave - i < lats:
                if i:
                    for _ in range(ASIDE):
                        next(aside, None)
                for n in range(len(left(0, i))):
                    for p in range(2):
                        add(turns[wave - i], p, i, n)
    for _ in aside:
        pass
    vector_rows((first_sums, second_sums), tiny, first)

    def to_owner(n):
        return pltpu.make_async_remote_copy(
            src_ref=tiny,
            dst_ref=landed.at[n],
            send_sem=tiny_send,
            recv_sem=tiny_recv.at[n],
            device_id=owner,
            device_id_type=MESH,
        )

    @pl.when(jnp.logical_not(mine))
    def _():
        to_owner(d * lats + l).start()

    for p in range(2):
        total = sums[0, slot_of(steps - 1, 0), parts[p]].astype(F32)
        for o in range(1, lats):
            z[o, p].wait_recv()
            total = total + others[o - 1, parts[p]].astype(F32)
        amount = min(parts[p].start + parts[p].size, lines) - parts[p].start
        out[pl.ds(parts[p].start, amount)] = total[:amount]

    @pl.when(mine)
    def _():
        total = tiny[...]
        for a, b in senders:
            to_owner(a * lats + b).wait_recv()
            total = total + landed[a * lats + b]
        out[row : row + count, :] = out[row : row + count, :] + total

    @pl.when(jnp.logical_not(mine))
    def _():
        to_owner(d * lats + l).wait_send()

    for copy in sent:
        copy.wait_send()
    for slab in range(1, x.shape[0], 2):
        for way in range(2):

            @pl.when(gets[1 - way])
            def _():
                halo_copy(slab, way).wait_send()


def scatter(packed, lines, x, gconv, own, lo, hi, to_below, to_above, small, second_sums, width):
    dates, lats, rows, lanes = packed.shape
    slots = dates - 1
    tiny = (vector_home(lines, lats)[3], LANES)
    anywhere, held = pl.BlockSpec(memory_space=pl.ANY), pl.BlockSpec(memory_space=pltpu.VMEM)
    low = pltpu.VMEM((CP, WIDE), BF16)
    row_buffers = [low, low, pltpu.VMEM((CP, WIDE), F32), low, low, low]
    return pl.pallas_call(
        functools.partial(scatter_kernel, dates, lats, lines, width),
        in_specs=[anywhere] * 8 + [held] * 2,
        out_specs=[held, anywhere],
        out_shape=(jax.ShapeDtypeStruct((lines, lanes), F32), jax.ShapeDtypeStruct(x.shape, BF16)),
        scratch_shapes=[
            pltpu.VMEM((lats, slots, rows, lanes), BF16),
            pltpu.VMEM((lats - 1, rows, lanes), BF16),
            pltpu.SemaphoreType.DMA((lats - 1, 2)),
            pltpu.SemaphoreType.DMA((lats - 1, 2)),
            pltpu.SemaphoreType.DMA((lats, 2, slots)),
            pltpu.SemaphoreType.DMA((lats, 2, slots)),
            pltpu.VMEM((2, CP, LANES), F32),
            pltpu.VMEM(tiny, F32),
            pltpu.VMEM((dates * lats,) + tiny, F32),
            pltpu.SemaphoreType.DMA(()),
            pltpu.SemaphoreType.DMA((dates * lats,)),
            pltpu.SemaphoreType.DMA((2, 5)),
            pltpu.SemaphoreType.DMA((2,)),
            pltpu.VMEM((x.shape[0] // 2, 2, CP, WIDE), BF16),
            pltpu.SemaphoreType.DMA((x.shape[0] // 2, 2)),
            pltpu.SemaphoreType.DMA((x.shape[0] // 2, 2)),
            pltpu.VMEM(packed.shape, BF16),
            pltpu.SemaphoreType.DMA(()),
        ]
        + row_buffers * 2,
        compiler_params=pltpu.CompilerParams(
            collective_id=1, has_side_effects=True, vmem_limit_bytes=VMEM
        ),
        name="scatter_grads",
    )(packed, x, gconv, own, lo, hi, to_below, to_above, small, second_sums)


def local(inputs, noise, cotangent, params, psi, step_counts, pixel_mask, offsets, bases):
    samples, steps, rows, width, _ = inputs.shape
    slabs = samples * steps
    dates, lats = lax.axis_size("date"), lax.axis_size("lat")
    lat = rows * lats

    def by_channel(values):
        return jnp.swapaxes(values, 3, 4).reshape(slabs, rows, -1, width)

    def padded(values):
        return jnp.pad(values, ((0, 0), (0, 0), (0, CP - values.shape[2]), (0, WIDE - width)))

    upward = [(i, i + 1) for i in range(lats - 1)]
    downward = [(i + 1, i) for i in range(lats - 1)]
    lines = params.shape[0] // LANES
    held = -(-lines // STEP) * STEP
    shard = jnp.pad(params.reshape(lines, LANES), ((0, held - lines), (0, 0)))
    x = padded(jnp.concatenate([by_channel(inputs), by_channel(noise)], axis=2))
    edges = [(x[s, rows - 1 :], x[s, :1]) for s in range(slabs)]
    gathered, moved, small, halo = gather(shard, x, lines, dates, lats, width)
    gathered = gathered.reshape(dates * lats, held, LANES)
    cot = padded(by_channel(cotangent)).reshape(slabs * rows, CP, WIDE)
    active = jnp.arange(steps, dtype=jnp.int32)[None, :] < step_counts[:, None]
    mask = active.reshape(slabs, 1, 1) * pixel_mask[None]
    mask = jnp.pad(mask.astype(F32), ((0, 0), (0, 0), (0, WIDE - width)))
    matrices = unpack(gathered, lines)
    halos, done = [halo], halo
    for s in range(1, slabs):
        top, bottom, done = lax.optimization_barrier((*edges[s], done))
        done = lax.ppermute(top, "lat", upward), lax.ppermute(bottom, "lat", downward)
        halos += done
    basis = lift(offsets, bases, psi, halos, moved, small, lat, width)
    w, wt, up, upt, dn, dnt = matrices
    basis = basis.reshape(slabs * rows, BASIS * CP, WIDE)
    output, gconv, gup, gdn, second_sums = block(
        basis, x.reshape(slabs * rows, CP, WIDE), cot, mask.reshape(slabs * rows, 1, WIDE),
        wt, upt, up, dnt, dn, small,
    )
    gconv_rows = gconv.reshape(slabs, rows, CP, WIDE)
    own, below_even, above_even, to_below, to_above = lower(offsets, bases, psi, gconv_rows, w, width)
    from_below = lax.ppermute(above_even, "lat", upward)
    from_above = lax.ppermute(below_even, "lat", downward)
    packed = grads(basis, gconv, gup, gdn, dates * lats, lines, held)
    summed, grad = scatter(
        packed.reshape(dates, lats, held, LANES), lines,
        x, gconv_rows, own, from_below, from_above, to_below, to_above, small, second_sums, width,
    )

    def by_pixel(values):
        values = values.reshape(slabs, rows, CP, WIDE)[:, :, :C, :width]
        return jnp.swapaxes(values.reshape(samples, steps, rows, C, width), 3, 4)

    return by_pixel(output), by_pixel(grad), summed.reshape(-1)


def solution(mesh):
    field = P("date", None, "lat", None, None)
    flat = P(("date", "lat"))
    return jax.shard_map(
        local,
        mesh=mesh,
        in_specs=(field, field, field, flat, P(), P("date"), P("lat", None), P(), P()),
        out_specs=(field, field, flat),
        check_vma=False,
    )
```
